32 devices in a mesh: lon: 4 (over z), lat: 4 (over y, core), lev: 2 (over x).
Axes of the slice: x: 2, y: 2, z: 4, core: 2. Of those that a mesh axis runs over, the one named last changes fastest.
Arguments:
- state: float32 [5, 16, 64, 2048], P(None, 'lev', 'lat', 'lon'), may hold values from -6 to 6
- mask: int32 [16, 64, 2048], P('lev', 'lat', 'lon'), may hold values 0 or 1
- coriolis: float32 [64], P('lat'), may hold values from 0.05 to 0.3
- penetration: float32 [16], P('lev'), may hold values from 0.05 to 1
- flux_tiles: float32 [2048, 3, 512], P(('lon', 'lat')), may hold values from -4 to 4
- flux_owner: int32 [2048, 1], P(('lon', 'lat')), may hold values from 0 to 15; in each aligned block of 128 rows (0 to 127, 128 to 255, ...) at most 16 rows name the same one
- flux_row: int32 [2048], P(('lon', 'lat')), may hold values from 0 to 15
- fold_partner: int32 [2048], replicated, may hold values from 0 to 2047, as said below
Outputs:
- new_state: float32 [5, 16, 64, 2048], P(None, 'lev', 'lat', 'lon')
The draws below stay inside these ranges and needn't reach their ends.
Inputs may be any that keep to these rules, and one draw needn't show every extreme that they name: `flux_owner`: among the 128 tiles of one device at most 16 name the same owner, and some owner receives exactly 16 from some device. fold_partner[i] = (h - i) mod 2048 for one hinge column h.
All inputs are finite; a program needn't handle non-finite values. No bound on the sum of `mask` on one device may be relied on, other than what follows from the above.
Results may differ from the reference program's by a relative error of at most 0.0003.
Values sent between devices are 32-bit elements; how exact they have to be, the bound alone decides.
No kernel may reach another device: no remote copies, remote signals or barrier semaphores. Data moves between devices by JAX's collectives and lax.ppermute only.
A program may use at most 192 MiB of HBM per device.

```python
import math
import jax
import jax.numpy as jnp
import numpy as np

CLON = 512
CLAT = 16
XT = 128
STEPS = 2
LEVELS = 16
NLAT = 64
NLON = 2048
CAP = 16
TILES = 2048
N_LON = 4
N_LAT = 4


def draw_fold_partner(key, part):
    hinge = jax.random.randint(key, (), 0, NLON, dtype=jnp.int32)
    return ((hinge - jnp.arange(NLON, dtype=jnp.int32)) % NLON).astype(jnp.int32)


def touch_ends(drawn, stream_key, low, largest):
    longest = drawn.shape.index(max(drawn.shape))
    spots = []
    for shift in (0, 1):
        where = [jax.random.randint(jax.random.fold_in(stream_key, axis), (), 0, length) for axis, length in enumerate(drawn.shape)]
        where[longest] = (where[longest] + shift) % drawn.shape[longest]
        spots.append(tuple(where))
    return drawn.at[spots[0]].set(low).at[spots[1]].set(largest)


def levels(key, shape, shards, least, largest):
    factor_of, own = 1.0, jax.random.fold_in(key, 6)
    for axis_at, shards_of in shards:
        heights = jnp.exp(jax.random.uniform(jax.random.fold_in(own, axis_at), (shards_of,), jnp.float32, least / len(shards), largest / len(shards)))
        factor_of = factor_of * jnp.repeat(heights, shape[axis_at] // shards_of).reshape([-1 if axis == axis_at else 1 for axis in range(len(shape))])
    return factor_of


def routed_block(stream_key, own, number, rows, count, top, reach, lean):
    ranking = jax.random.permutation(stream_key, count)
    crowded, usual = load_shares(count, rows * top, reach, lean, True), load_shares(count, rows * top, reach, lean, False)
    places = jnp.arange(count)

    def named(tallies, rotation):
        used = int((tallies > 0).sum())
        fixed = max(1, used // 4)
        shifted = fixed + (places - fixed + rotation * (used - fixed)) % max(1, count - fixed)
        return jnp.zeros((count,), jnp.int32).at[ranking[jnp.where(places < fixed, places, shifted)]].set(jnp.asarray(tallies, jnp.int32))

    tallies = jnp.where(number % 4 == 0, named(crowded, number // 4), named(usual, number - number // 4 - 1))
    mixed = jax.random.permutation(jax.random.fold_in(own, 3), count)
    giver, taker = mixed[0:count // 2 * 2:2], mixed[1:count // 2 * 2:2]
    slack = jnp.minimum(tallies[giver] - 1, reach - tallies[taker]) // 2
    slack = jnp.where((giver == ranking[0]) | (taker == ranking[0]) | (tallies[taker] == 0), 0, jnp.maximum(slack, 0))
    shifted = jax.random.randint(jax.random.fold_in(own, 4), (count // 2,), 0, 1 << 20) % (slack + 1)
    tallies = tallies.at[giver].add(-shifted).at[taker].add(shifted)
    items = jnp.searchsorted(jnp.cumsum(tallies), jnp.arange(rows * top), side="right").astype(jnp.int32)
    grid = items.reshape(top, rows).T
    grid = grid[jax.random.permutation(jax.random.fold_in(own, 1), rows)]
    rotation = jax.random.randint(jax.random.fold_in(own, 2), (rows, 1), 0, top)
    return jnp.take_along_axis(grid, (jnp.arange(top)[None, :] + rotation) % top, axis=1)


def load_shares(number_of, total, bound, slope, full):
    weights = [(1 << 20) // math.isqrt(rank ** slope) + 1 for rank in range(1, number_of + 1)]
    largest = bound if full else min(bound, max(-(-total // number_of), total * weights[0] // sum(weights)))
    least = 1 if total - largest >= number_of - 1 else 0
    given, spare = [largest] + [least] * (number_of - 1), total - largest - least * (number_of - 1)
    while spare > 0:
        candidates = [i for i in range(1, number_of) if given[i] < largest] or [i for i in range(1, number_of) if given[i] < bound]
        pool, left = sum([weights[i] for i in candidates]), spare
        for i in candidates:
            more = min(bound - given[i], max(1, left * weights[i] // pool), spare)
            given[i] = given[i] + more
            spare = spare - more
    return np.array(given)


def normal_values(stream_key, shape, spread, limit, pieces=(), kind=jnp.bfloat16):
    values = jax.random.normal(stream_key, shape, jnp.float32) * spread
    if len(pieces) > 0:
        values = levels(stream_key, shape, pieces, -0.22, 0.18) * values
    return jnp.clip(values, min=-limit, max=limit).astype(kind)


def setup_inputs(seed: int = 0) -> dict:
    key_list = jax.random.split(jax.random.key(seed), 9)
    state = normal_values(key_list[0], (5, LEVELS, NLAT, NLON), 1.0, 6.0, ((1, 2), (2, 4), (3, 4)), jnp.float32)
    mask = touch_ends((jax.random.randint(key_list[1], (LEVELS, NLAT, NLON), 0, 4) < 3).astype(jnp.int32), jax.random.fold_in(key_list[1], 1), 0, 1)
    coriolis = jnp.clip(jnp.exp(math.log(0.3) - 1.7917595 * jax.random.uniform(key_list[2], (NLAT,), jnp.float32) ** levels(key_list[2], (NLAT,), ((0, 4),), -0.2, 0.2)), 0.05, 0.3)
    penetration = jnp.clip(jnp.exp(math.log(1.0) - 2.9957323 * jax.random.uniform(key_list[3], (LEVELS,), jnp.float32) ** levels(key_list[3], (LEVELS,), ((0, 2),), -0.2, 0.2)), 0.05, 1.0)
    flux_tiles = normal_values(key_list[4], (TILES, 3, CLON), 0.5, 4.0, ((0, 16),), jnp.float32)
    flux_owner_keys = jax.random.split(jax.random.fold_in(key_list[5], 1), TILES // XT)
    flux_owner_turns = jax.random.permutation(jax.random.fold_in(key_list[5], 3), TILES // XT)
    flux_owner = jax.vmap(lambda own, number: routed_block(jax.random.fold_in(key_list[5], 2), own, number, XT, N_LON * N_LAT, 1, CAP, 2))(flux_owner_keys, flux_owner_turns).reshape((TILES, 1))
    flux_row = touch_ends(jax.random.randint(key_list[6], (TILES,), 0, CLAT), jax.random.fold_in(key_list[6], 1), 0, CLAT - 1).astype(jnp.int32)
    fold_partner = draw_fold_partner(jax.random.fold_in(key_list[8], 71), 0)
    return dict(state=state, mask=mask, coriolis=coriolis, penetration=penetration, flux_tiles=flux_tiles, flux_owner=flux_owner, flux_row=flux_row, fold_partner=fold_partner)


ALPHA = 0.2
BETA = 0.15
PRESS = 0.1
VISCOUS = 0.1
DIFFUSE = 0.1
ADVECT = 0.1


def surface_flux(flux_tiles, flux_owner, flux_row):
    owners = N_LON * N_LAT
    where_to = flux_owner[:, 0] * CLAT + flux_row
    total = jnp.zeros((owners * CLAT, 3, CLON), jnp.float32).at[where_to].add(flux_tiles)
    total = total.reshape(N_LON, N_LAT, CLAT, 3, CLON)
    return total.transpose(3, 1, 2, 0, 4).reshape(3, N_LAT * CLAT, N_LON * CLON)


def neighbours(field, sign, partner):
    east = jnp.roll(field, -1, axis=2)
    west = jnp.roll(field, 1, axis=2)
    north_row = sign * field[:, -1, :][:, partner]
    north = jnp.concatenate([field[:, 1:, :], north_row[:, None, :]], axis=1)
    south = jnp.concatenate([field[:, :1, :], field[:, :-1, :]], axis=1)
    return east, west, north, south


def pressure_of(temper, saline):
    buoyancy = ALPHA * temper - BETA * saline
    return PRESS * (jnp.cumsum(buoyancy, axis=0) - 0.5 * buoyancy)


def advance(state, wet, turning, absorb, forcing, partner):
    signs = (-1.0, -1.0, 1.0, 1.0, 1.0)
    pressure = pressure_of(state[2], state[3])
    east_p, west_p, north_p, south_p = neighbours(pressure, 1.0, partner)
    slope_x = 0.5 * (east_p - west_p)
    slope_y = 0.5 * (north_p - south_p)
    zonal, merid = state[0], state[1]
    result = []
    for field in range(5):
        value = state[field]
        east, west, north, south = neighbours(value, signs[field], partner)
        laplace = east + west + north + south - 4.0 * value
        if field == 0:
            trend = turning * merid - slope_x + VISCOUS * laplace
        elif field == 1:
            trend = -turning * zonal - slope_y + VISCOUS * laplace
        else:
            trend = DIFFUSE * laplace - ADVECT * (zonal * (0.5 * (east - west)) + merid * (0.5 * (north - south))) + absorb * forcing[field - 2][None]
        result.append(value + wet * trend)
    return jnp.stack(result)


def reference(state, mask, coriolis, penetration, flux_tiles, flux_owner, flux_row, fold_partner):
    forcing = surface_flux(flux_tiles, flux_owner, flux_row)
    wet = mask.astype(jnp.float32)
    turning = coriolis[None, :, None]
    absorb = penetration[:, None, None]
    for substep in range(STEPS):
        state = advance(state, wet, turning, absorb, forcing, fold_partner)
    return state
```

```python
import functools

import jax
import jax.numpy as jnp
from jax import lax
from jax.experimental import pallas as pl
from jax.experimental.pallas import tpu as pltpu
from jax.sharding import PartitionSpec as P

ALPHA = 0.2
BETA = 0.15
PRESS = 0.1
VISCOUS = 0.1
DIFFUSE = 0.1
ADVECT = 0.1

F32 = jnp.float32
I32 = jnp.int32
LANES = 128
DEEP = 8
FAR = 64
WET = 48
SLABS = 11
CORNERS = SLABS
VMEM_BYTES = 24 * 1024 * 1024
PREPARE_BYTES = 58 * 1024 * 1024

VMEM = pl.BlockSpec(memory_space=pltpu.VMEM)
SMEM = pl.BlockSpec(memory_space=pltpu.SMEM)
ANY = pl.BlockSpec(memory_space=pl.ANY)
HBM = pl.BlockSpec(memory_space=pltpu.HBM)


def iota(shape, dim):
    return lax.broadcasted_iota(I32, shape, dim)


def roll(value, shift, axis):
    return pltpu.roll(value, shift % value.shape[axis], axis)


def call(kernel, out_shape, in_specs, args, scratch=(), name=None, vmem=VMEM_BYTES):
    return pl.pallas_call(
        kernel,
        out_shape=out_shape,
        in_specs=in_specs,
        out_specs=jax.tree.map(lambda _: VMEM, out_shape),
        scratch_shapes=list(scratch),
        compiler_params=pltpu.CompilerParams(vmem_limit_bytes=vmem),
        name=name,
    )(*args)


def after(values, *others):
    return lax.optimization_barrier((values, others))[0]


def shape(*dims):
    return jax.ShapeDtypeStruct(dims, F32)


def prepare_kernel(
    n_lon, n_lat, state_hbm, mask_hbm, tiles_hbm, owner_hbm, row_hbm, partner_hbm, keep_ref, send_ref, west_ref, east_ref,
    top_ref, state_ref, mask_ref, x_ref, owners_ref, rows_ref, hinge_ref, sem,
):
    tiles, cols = tiles_hbm.shape[1], tiles_hbm.shape[2]
    half_cols = cols // 2
    rows = 2 * DEEP
    n_y = n_lat // 2
    half = lax.axis_index("lev")
    lat = lax.axis_index("lat")
    core = lax.rem(lat, 2)
    begin = pl.multiple_of(half * half_cols, LANES)
    indices = [
        pltpu.make_async_copy(owner_hbm, owners_ref, sem.at[0]),
        pltpu.make_async_copy(row_hbm, rows_ref, sem.at[1]),
        pltpu.make_async_copy(partner_hbm, hinge_ref, sem.at[2]),
    ]
    fluxes = [
        pltpu.make_async_copy(
            tiles_hbm.at[c, :, pl.ds(begin, half_cols)], x_ref.at[:, pl.ds(c * half_cols, half_cols)], sem.at[3 + c]
        )
        for c in range(3)
    ]
    fields = [
        pltpu.make_async_copy(state_hbm, state_ref, sem.at[6]),
        pltpu.make_async_copy(mask_hbm, mask_ref, sem.at[7]),
    ]
    for copy in indices + fluxes + fields:
        copy.start()
    for copy in indices:
        copy.wait()

    key = owners_ref[...] * rows + rows_ref[...]
    hinge_block = hinge_ref[0] // cols
    slots = keep_ref.shape[0]
    slot = iota((slots, tiles), 0)
    group, sub = slot >> 3, slot & 7
    at_y = (group >> (n_lon.bit_length() - 1)) ^ (lat // 2)
    at_lon = (group & (n_lon - 1)) ^ lax.axis_index("lon")

    def wrapped(lon):
        return jnp.where(lon < 0, lon + n_lon, jnp.where(lon >= n_lon, lon - n_lon, lon))

    def one_hot(hit):
        return jnp.where(hit, 1.0, 0.0).astype(jnp.bfloat16)

    def weights(to_core):
        lat = 2 * at_y + to_core
        owner = at_lon * n_lat + lat
        last = lat == n_lat - 1
        top = n_lat * rows - 1
        south = jnp.where(lat == 0, owner * rows, owner * rows - 1)
        north = jnp.where(last, wrapped(hinge_block - at_lon) * (n_lat * rows) + top, (owner + 1) * rows)
        third = jnp.where(last, wrapped(hinge_block - at_lon - 1) * (n_lat * rows) + top, -1)
        kind = sub >> 1
        extra_key = jnp.where(kind == 0, south, jnp.where(kind == 1, north, jnp.where(kind == 2, third, -1)))
        extra = key == extra_key
        beside = wrapped(at_lon + 1 - 2 * half) * n_lat + lat
        return (
            one_hot(key == owner * rows + sub),
            one_hot(key == owner * rows + DEEP + sub),
            one_hot(extra & ((sub & 1) == 0)),
            one_hot(extra & ((sub & 1) == 1)),
            one_hot(((key >> 4) == beside) & (sub == 6)),
        )

    def split(x):
        first = x.astype(jnp.bfloat16)
        rest = x - first.astype(F32)
        second = rest.astype(jnp.bfloat16)
        third = (rest - second.astype(F32)).astype(jnp.bfloat16)
        return first, second, third

    square = iota((tiles, tiles), 0) == iota((tiles, tiles), 1)
    row_of = jnp.sum(jnp.where(square, (key & (rows - 1)).astype(F32), 0.0), axis=1, keepdims=True).astype(I32)

    for copy in fluxes:
        copy.wait()
    x = x_ref[...]
    lane = iota((tiles, LANES), 1)
    edge = jnp.zeros((tiles, LANES), F32)
    for c in range(3):
        begin = c * half_cols
        value = jnp.where(half == 0, x[:, begin : begin + 1], x[:, begin + half_cols - 1 : begin + half_cols])
        edge = jnp.where(((lane >> 4) == c) & ((lane & 15) == row_of), value, edge)
    parts, edges = split(x), split(edge)
    wide = 3 * half_cols
    quarter = wide // 2

    def dot(hot, terms, begin, end):
        products = [
            jnp.dot(hot, term[:, begin:end], preferred_element_type=F32) for term in reversed(terms)
        ]
        return products[0] + products[1] + products[2]

    for out_ref, to_core in ((keep_ref, core), (send_ref, 1 - core)):
        low, high, even, odd, ring = weights(to_core)
        out_ref[:, 0:wide] = dot(low, parts, 0, wide)
        out_ref[:, wide : 2 * wide] = dot(high, parts, 0, wide)
        rest = dot(even, parts, 0, quarter) + dot(odd, parts, quarter, wide)
        beside = dot(ring, edges, 0, LANES)
        out_ref[:, 2 * wide : 2 * wide + LANES] = rest[:, 0:LANES] + beside
        out_ref[:, 2 * wide + LANES :] = rest[:, LANES:]

    for copy in fields:
        copy.wait()
    edge_rows(state_ref, mask_ref, top_ref, rows, rows - 1, rows - 2)
    edge_columns(state_ref, mask_ref, west_ref, east_ref)


def merge_kernel(kept_ref, got_ref, keep_ref, send_ref):
    half = keep_ref.shape[0]
    send_ref[...] = kept_ref[half:, :] + got_ref[half:, :]
    keep_ref[...] = kept_ref[0:half, :] + got_ref[0:half, :]


def prepare(state, mask, flux_tiles, flux_owner, flux_row, fold_partner, n_lon, n_lat):
    tiles, _, cols = flux_tiles.shape
    wide = 3 * (cols // 2)
    slots = shape(n_lon * n_lat // 2 * DEEP, 2 * wide + wide // 2)
    side = shape(2 * DEEP, LANES)
    return call(
        functools.partial(prepare_kernel, n_lon, n_lat),
        (slots, slots, side, side, shape(SLABS, DEEP, cols)),
        [HBM] * 6,
        (
            state,
            mask,
            flux_tiles.transpose(1, 0, 2),
            flux_owner.reshape(1, tiles),
            flux_row.reshape(1, tiles),
            fold_partner,
        ),
        [
            pltpu.VMEM(state.shape, F32),
            pltpu.VMEM(mask.shape, I32),
            pltpu.VMEM((tiles, wide), F32),
            pltpu.VMEM((1, tiles), I32),
            pltpu.VMEM((1, tiles), I32),
            pltpu.SMEM(fold_partner.shape, I32),
            pltpu.SemaphoreType.DMA((8,)),
        ],
        name="prepare",
        vmem=PREPARE_BYTES,
    )


def level_rows(ref, row, rows):
    return jnp.concatenate([ref[k * rows + row : k * rows + row + 1, :] for k in range(DEEP)], axis=0)


def buoyancy_of(temper, saline):
    return ALPHA * temper - BETA * saline


def edge_rows(state_ref, mask_ref, out_ref, rows, near, far):
    for f in range(5):
        out_ref[2 * f] = level_rows(state_ref.at[f], near, rows)
        out_ref[2 * f + 1] = level_rows(state_ref.at[f], far, rows)
    out_ref[10] = level_rows(mask_ref, near, rows).astype(F32)


def edge_columns(state_ref, mask_ref, west_ref, east_ref):
    rows, cols = west_ref.shape[0], state_ref.shape[2]
    lane = iota((rows, LANES), 1)
    last = slice(cols - LANES, cols)
    west = jnp.zeros((rows, LANES), F32)
    east = jnp.zeros((rows, LANES), F32)
    for k in range(DEEP):
        at = slice(k * rows, (k + 1) * rows)
        for f in range(5):
            to = f * DEEP + k
            left, right = state_ref[f, at, 0:LANES], state_ref[f, at, last]
            west = jnp.where(lane == to, roll(left, to, 1), west)
            west = jnp.where(lane == FAR + to, roll(left, FAR + to - 1, 1), west)
            east = jnp.where(lane == to, roll(right, to + 1, 1), east)
            east = jnp.where(lane == FAR + to, roll(right, FAR + to + 2, 1), east)
        west = jnp.where(lane == WET + k, roll(mask_ref[at, 0:LANES].astype(F32), WET + k, 1), west)
        east = jnp.where(lane == WET + k, roll(mask_ref[at, last].astype(F32), WET + k + 1, 1), east)
    west_ref[...] = west
    east_ref[...] = east


def rows_kernel(state_ref, mask_ref, turn_ref, from_west_ref, from_east_ref, pair_ref, cross_ref):
    rows, cols = from_west_ref.shape[0], state_ref.shape[2]
    odd = lax.rem(lax.axis_index("lat"), 2) == 1

    def fill(out_ref, near, far):
        edge_rows(state_ref, mask_ref, out_ref, rows, near, far)
        out_ref[CORNERS] = jnp.full((DEEP, cols), turn_ref[near], F32)
        out_ref[CORNERS, 0:1, 0:LANES] = from_west_ref[near : near + 1, :]
        out_ref[CORNERS, 1:2, 0:LANES] = from_east_ref[near : near + 1, :]

    @pl.when(odd)
    def _():
        fill(pair_ref, 0, 1)
        fill(cross_ref, rows - 1, rows - 2)

    @pl.when(jnp.logical_not(odd))
    def _():
        fill(pair_ref, rows - 1, rows - 2)
        fill(cross_ref, 0, 1)


def around(value, west, east, south, north):
    rows, cols = value.shape
    row, col = iota((rows, cols), 0), iota((rows, cols), 1)
    return (
        jnp.where(col == cols - 1, east, roll(value, -1, 1)),
        jnp.where(col == 0, west, roll(value, 1, 1)),
        jnp.where(row == rows - 1, north, roll(value, -1, 0)),
        jnp.where(row == 0, south, roll(value, 1, 0)),
    )


def advanced(values, sides, wet, turn, pressed, heat=None):
    zonal, merid = values[0], values[1]
    sums = [(e + w) + (n + s) for e, w, n, s in sides]
    across = [(e - w, n - s) for e, w, n, s in sides]
    press_x, press_y = pressed(
        0.5 * buoyancy_of(across[2][0], across[3][0]), 0.5 * buoyancy_of(across[2][1], across[3][1])
    )
    out = []
    carry_x, carry_y = (0.5 * ADVECT) * zonal, (0.5 * ADVECT) * merid
    for f in range(5):
        spread = (VISCOUS if f < 2 else DIFFUSE) * (sums[f] - 4.0 * values[f])
        if f == 0:
            trend = spread + (turn * merid - press_x)
        elif f == 1:
            trend = spread - (turn * zonal + press_y)
        else:
            trend = spread - (carry_x * across[f][0] + carry_y * across[f][1])
        new = values[f] + wet * trend
        out.append(new if heat is None or f < 2 else new + heat[f - 2])
    return out


class Tiles:
    def __init__(self, grid, west=None, east=None, south=None, north=None):
        self.grid, self.ghosts, self.turned = grid, (west, east, south, north), {}
        self.lane, self.sub = iota((DEEP, LANES), 1), iota((DEEP, LANES), 0)

    def rolled(self, r, j, shift, axis):
        at = (r, j, shift, axis)
        if at not in self.turned:
            self.turned[at] = roll(self.grid[r][j], shift, axis)
        return self.turned[at]

    def side(self, r, j, shift, axis):
        here = self.rolled(r, j, shift, axis)
        r_from, j_from = (r, j - shift) if axis else (r - shift, j)
        edge = (0 if shift == 1 else LANES - 1) if axis else (0 if shift == 1 else DEEP - 1)
        if 0 <= r_from < len(self.grid) and 0 <= j_from < len(self.grid[0]):
            other = self.rolled(r_from, j_from, shift, axis)
        else:
            ghost = self.ghosts[(0 if shift == 1 else 1) + (0 if axis else 2)]
            if ghost is None:
                return here
            other = ghost[r if axis else j]
        return jnp.where((self.lane if axis else self.sub) == edge, other, here)

    def around(self, r, j):
        return self.side(r, j, -1, 1), self.side(r, j, 1, 1), self.side(r, j, -1, 0), self.side(r, j, 1, 0)


def tile(r, j, k, rows):
    return slice(k * rows + r * DEEP, k * rows + (r + 1) * DEEP), slice(j * LANES, (j + 1) * LANES)


def turn_column(turn_ref, rows):
    row = iota((rows, LANES), 0)
    column = jnp.zeros((rows, LANES), F32)
    for j in range(rows):
        column = jnp.where(row == j, turn_ref[j], column)
    return column


def mirrored(value, width):
    back = LANES - 1 - iota((value.shape[0], LANES), 1)
    blocks = [
        jnp.take_along_axis(value[:, begin : begin + LANES], back, axis=1)
        for begin in range(width - LANES, -1, -LANES)
    ]
    return jnp.concatenate(blocks, axis=1)


def scan_down(value):
    row = iota(value.shape, 0)
    for step in (1, 2, 4):
        value = value + jnp.where(row >= step, roll(value, step, 0), 0.0)
    return value


def scan_lanes(value):
    lane = iota(value.shape, 1) & 7
    for step in (1, 2, 4):
        value = value + jnp.where(lane >= step, roll(value, step, 1), 0.0)
    return value


def lanes_between(value, begin, end):
    lane = iota(value.shape, 1)
    return jnp.where((lane >= begin) & (lane < end), value, 0.0)


def buoyancy_sum(column):
    here = lanes_between(buoyancy_of(roll(column, -16, 1), roll(column, -24, 1)), 0, 8)
    return jnp.sum(here, axis=1, keepdims=True)


def interior_kernel(state_ref, mask_ref, turn_ref, share_ref, new_ref, sums_ref):
    rows, cols = sums_ref.shape[0], state_ref.shape[2]
    n_r, n_j = rows // DEEP, cols // LANES
    turn = turn_column(turn_ref, rows)
    grid = [(r, j) for r in range(n_r) for j in range(n_j)]
    zero = jnp.zeros((DEEP, LANES), F32)
    run = {at: [zero] * 5 for at in grid}
    for k in range(DEEP):
        fields = [Tiles([[state_ref[(f, *tile(r, j, k, rows))] for j in range(n_j)] for r in range(n_r)]) for f in range(5)]
        for r, j in grid:
            at = tile(r, j, k, rows)
            above_x, above_y, before, total, absorbed = run[r, j]
            slopes = []

            def pressed(x, y):
                slopes.extend((x, y))
                return PRESS * (above_x + 0.5 * x), PRESS * (above_y + 0.5 * y)

            values = [field.grid[r][j] for field in fields]
            wet = mask_ref[at].astype(F32)
            new = advanced(
                values, [field.around(r, j) for field in fields], wet, turn[r * DEEP : (r + 1) * DEEP, 0:1], pressed
            )
            for f in range(5):
                new_ref[(f, *at)] = new[f]
            run[r, j] = [
                above_x + slopes[0],
                above_y + slopes[1],
                before + buoyancy_of(values[2], values[3]),
                total + buoyancy_of(new[2], new[3]),
                absorbed + wet * share_ref[k],
            ]
    for r, j in grid:
        for kind in range(3):
            at = slice(kind * cols + j * LANES, kind * cols + (j + 1) * LANES)
            sums_ref[r * DEEP : (r + 1) * DEEP, at] = run[r, j][2 + kind]


def rim_kernel(
    n_lon, n_lat, state_ref, mask_ref, turn_ref, share_ref, partner_ref, own_west_ref, own_east_ref,
    from_west_ref, from_east_ref, pair_ref, cross_ref, inside_ref, *refs,
):
    blocks = refs[:n_lon]
    ring_rows_ref, ring_cols_ref, edge_rows_ref, edge_cols_ref, sums_ref, south_ref, north_ref, fold_ref, sem = refs[n_lon:]
    rows, cols = from_west_ref.shape[0], state_ref.shape[2]
    lon, lat = lax.axis_index("lon"), lax.axis_index("lat")
    odd = lax.rem(lat, 2) == 1
    hinge = partner_ref[0]
    hinge_block = hinge // cols
    within = hinge - hinge_block * cols
    at_top = lat == n_lat - 1
    wanted = [lax.rem(2 * lon - hinge_block + offset + 2 * n_lon, n_lon) for offset in (1, 0, -1)]

    @pl.when(at_top)
    def _():
        for place in range(3):
            for d in range(n_lon):

                @pl.when(wanted[place] == d)
                def _(place=place, d=d):
                    pltpu.make_async_copy(blocks[d], fold_ref.at[place], sem.at[place]).start()

    @pl.when(odd)
    def _():
        south_ref[...] = pair_ref[...]

    @pl.when(jnp.logical_not(odd))
    def _():
        north_ref[...] = pair_ref[...]

    @pl.when(jnp.logical_not(odd) & (lat > 0))
    def _():
        south_ref[...] = cross_ref[...]

    @pl.when(odd & (lat < n_lat - 1))
    def _():
        north_ref[...] = cross_ref[...]

    @pl.when(lat == 0)
    def _():
        edge_rows(state_ref, mask_ref, south_ref, rows, 0, 0)
        south_ref[CORNERS] = jnp.full((DEEP, cols), turn_ref[0], F32)
        south_ref[CORNERS, 0:1, 0:LANES] = from_west_ref[0:1, :]
        south_ref[CORNERS, 1:2, 0:LANES] = from_east_ref[0:1, :]

    sub8, lane8 = iota((DEEP, LANES), 0), iota((DEEP, LANES), 1)

    @pl.when(at_top)
    def _():
        for place in range(3):
            pltpu.make_async_copy(blocks[0], fold_ref.at[place], sem.at[place]).wait()
        west = jnp.zeros((DEEP, LANES), F32)
        east = jnp.zeros((DEEP, LANES), F32)
        for slab in range(SLABS):
            row = jnp.concatenate([fold_ref[0, slab], fold_ref[1, slab], fold_ref[2, slab]], axis=1)
            row = pltpu.roll(row, 3 * cols - 1 - within, 1)
            if slab < 4:
                row = -row
            north_ref[slab] = mirrored(row, cols)
            if slab < 10 and slab % 2 == 0:
                here = lane8 == (slab // 2) * DEEP + sub8
                west = jnp.where(here, row[:, cols : cols + 1], west)
                east = jnp.where(here, row[:, 3 * cols - 1 :], east)
        north_ref[CORNERS] = jnp.full((DEEP, cols), turn_ref[rows - 1], F32)
        north_ref[CORNERS, 0:1, 0:LANES] = jnp.sum(west, axis=0, keepdims=True)
        north_ref[CORNERS, 1:2, 0:LANES] = jnp.sum(east, axis=0, keepdims=True)

    tail = slice(3 * cols, 3 * cols + LANES)
    sums_ref[rows:, :] = jnp.zeros((DEEP, sums_ref.shape[1]), F32)
    sums_ref[0:rows, 0 : 3 * cols] = inside_ref[...]

    share_down = jnp.zeros((DEEP, LANES), F32)
    for k in range(DEEP):
        share_down = jnp.where(sub8 == k, share_ref[k], share_down)

    def down(line, f):
        return jnp.sum(jnp.where(lane8 == f * DEEP + sub8, line, 0.0), axis=1, keepdims=True)

    def pressed_rows(x, y):
        return PRESS * (scan_down(x) - 0.5 * x), PRESS * (scan_down(y) - 0.5 * y)

    def row_step(near, south, north, west_line, east_line, wet, turn):
        col = iota((DEEP, cols), 1)
        sides = [
            (
                jnp.where(col == cols - 1, down(east_line, f), roll(near[f], -1, 1)),
                jnp.where(col == 0, down(west_line, f), roll(near[f], 1, 1)),
                north[f],
                south[f],
            )
            for f in range(5)
        ]
        return advanced(near, sides, wet, turn, pressed_rows)

    for side, ghost_ref, edge, inner in ((0, south_ref, 0, 1), (1, north_ref, rows - 1, rows - 2)):
        near = [ghost_ref[2 * f] for f in range(5)]
        far = [ghost_ref[2 * f + 1] for f in range(5)]
        own = [level_rows(state_ref.at[f], edge, rows) for f in range(5)]
        own_next = [level_rows(state_ref.at[f], inner, rows) for f in range(5)]
        ring_wet = ghost_ref[10]
        corners = ghost_ref[CORNERS, :, 0:LANES]
        south, north = (far, own) if side == 0 else (own, far)
        ring = row_step(near, south, north, corners[0:1, :], corners[1:2, :], ring_wet, corners[2:3, 0:1])
        south, north = (near, own_next) if side == 0 else (own_next, near)
        wet = level_rows(mask_ref, edge, rows).astype(F32)
        edge_line = slice(edge, edge + 1)
        new = row_step(own, south, north, from_west_ref[edge_line, :], from_east_ref[edge_line, :], wet, turn_ref[edge])
        for f in range(5):
            edge_rows_ref[side, f] = new[f]
            ring_rows_ref[side, f] = jnp.where(lat == 0, new[f], ring[f]) if side == 0 else ring[f]
        ring_rows_ref[side, 5] = ring_wet
        at = slice(rows + side, rows + side + 1)
        below = slice(rows + 2 + side, rows + 3 + side)
        sums_ref[at, 0:cols] = jnp.sum(buoyancy_of(near[2], near[3]), axis=0, keepdims=True)
        sums_ref[below, 0:cols] = jnp.sum(buoyancy_of(far[2], far[3]), axis=0, keepdims=True)
        here = buoyancy_of(ring_rows_ref[side, 2], ring_rows_ref[side, 3])
        sums_ref[at, cols : 2 * cols] = jnp.sum(here, axis=0, keepdims=True)
        sums_ref[at, 2 * cols : 3 * cols] = jnp.sum(ring_wet * share_down[:, 0:1], axis=0, keepdims=True)
        corner_sums = buoyancy_sum(corners)
        for at_col in range(2):
            sums_ref[at, 3 * cols + at_col : 3 * cols + at_col + 1] = corner_sums[at_col : at_col + 1, :]

    row, lane = iota((rows, LANES), 0), iota((rows, LANES), 1)
    turn = turn_column(turn_ref, rows)
    share_lanes = jnp.zeros((rows, LANES), F32)
    for k in range(DEEP):
        share_lanes = jnp.where((lane & 7) == k, share_ref[k], share_lanes)

    def column_step(near, east, west, north, south):
        dx, dy = 0.5 * (east - west), 0.5 * (north - south)
        lap = (east + west) + (north + south) - 4.0 * near
        zonal, merid = lanes_between(near, 0, 8), lanes_between(near, 8, 16)
        wet = lanes_between(near, WET, WET + 8)
        wet_all = sum(roll(wet, -8 * n, 1) for n in range(2, 7))
        zonal_all = sum(roll(zonal, 8 * n, 1) for n in (2, 3, 4))
        merid_all = sum(roll(merid, 8 * n, 1) for n in (1, 2, 3))
        bx = lanes_between(buoyancy_of(roll(dx, -16, 1), roll(dx, -24, 1)), 0, 8)
        by = lanes_between(buoyancy_of(roll(dy, -8, 1), roll(dy, -16, 1)), 8, 16)
        press_x, press_y = PRESS * (scan_lanes(bx) - 0.5 * bx), PRESS * (scan_lanes(by) - 0.5 * by)
        trend = VISCOUS * lap - ADVECT * (zonal_all * dx + merid_all * dy) - press_x - press_y
        trend = trend + lanes_between(turn * roll(near, -8, 1), 0, 8) - lanes_between(turn * roll(near, 8, 1), 8, 16)
        return near + wet_all * trend, wet

    block = jnp.zeros((rows, LANES), F32)
    sides = ((0, from_west_ref, own_west_ref), (1, from_east_ref, own_east_ref))
    for side, ghost_ref, own_ref in sides:
        near, own = ghost_ref[...], own_ref[...]
        far, own_next = roll(near, -FAR, 1), roll(own, -FAR, 1)
        north = jnp.where(row == rows - 1, north_ref[CORNERS, side : side + 1, 0:LANES], roll(near, -1, 0))
        south = jnp.where(row == 0, south_ref[CORNERS, side : side + 1, 0:LANES], roll(near, 1, 0))
        east, west = (own, far) if side == 0 else (far, own)
        new, wet = column_step(near, east, west, north, south)
        ring_cols_ref[side] = new
        found = (buoyancy_sum(near), buoyancy_sum(far), buoyancy_sum(new), jnp.sum(wet * share_lanes, axis=1, keepdims=True))
        for kind in range(4):
            block = jnp.where(lane == 2 * kind + side, found[kind], block)
        east, west = (own_next, near) if side == 0 else (near, own_next)
        new, _ = column_step(own, east, west, roll(own, -1, 0), roll(own, 1, 0))
        edge_cols_ref[side] = new
        column = cols if side == 0 else 2 * cols - 1
        sums_ref[0:rows, column : column + 1] = buoyancy_sum(new)
    sums_ref[0:rows, tail] = block
    for side, edge in ((0, 0), (1, rows - 1)):
        here = buoyancy_of(edge_rows_ref[side, 2], edge_rows_ref[side, 3])
        sums_ref[edge : edge + 1, cols : 2 * cols] = jnp.sum(here, axis=0, keepdims=True)


def last_kernel(
    n_lon, n_lat, state_ref, mask_ref, ring_rows_ref, ring_cols_ref, edge_rows_ref, edge_cols_ref, sums_ref, mine_ref,
    theirs_ref, turn_ref, share_ref, partner_ref, out_ref,
):
    rows, cols = mask_ref.shape[0] // DEEP, mask_ref.shape[1]
    n_r, n_j = rows // DEEP, cols // LANES
    half_cols = cols // 2
    wide = 3 * half_cols
    mine, theirs = mine_ref[...], theirs_ref[...]
    first = lax.axis_index("lev") == 0
    halves = (jnp.where(first, mine, theirs), jnp.where(first, theirs, mine))
    lat = lax.axis_index("lat")
    at_top, at_bottom = lat == n_lat - 1, lat == 0
    hinge = partner_ref[0]
    within = hinge - (hinge // cols) * cols

    def extra(kind, c):
        found = []
        for part in halves:
            line = jnp.concatenate(
                [part[2 * kind : 2 * kind + 1, 2 * wide :], part[2 * kind + 1 : 2 * kind + 2, 2 * wide :]], axis=1
            )
            found.append(line[:, c * half_cols : (c + 1) * half_cols])
        return jnp.concatenate(found, axis=1)

    flux, flux_south, flux_north, flux_west, flux_east = [], [], [], [], []
    sub8 = iota((DEEP, LANES), 0)
    lane8 = iota((DEEP, LANES), 1)
    crossed = jnp.zeros((DEEP, 2 * cols), F32)
    for c in range(3):
        pair = jnp.concatenate([extra(2, c), extra(1, c)], axis=1)
        crossed = jnp.where(iota(crossed.shape, 0) == c, pair, crossed)
    crossed = mirrored(pltpu.roll(crossed, 2 * cols - 1 - within, 1), cols)
    row, lane = iota((rows, LANES), 0), iota((rows, LANES), 1)
    for c in range(3):
        bands = [
            jnp.concatenate([part[:, b * wide + c * half_cols : b * wide + (c + 1) * half_cols] for part in halves], axis=1)
            for b in range(2)
        ]
        flux.append(jnp.concatenate(bands, axis=0))
        flux_south.append(extra(0, c))
        flux_north.append(jnp.where(at_top, crossed[c : c + 1, :], extra(1, c)))
        here = lane == c * 16 + row
        for side, part in ((flux_west, halves[1]), (flux_east, halves[0])):
            line = part[6:7, 2 * wide : 2 * wide + LANES]
            side.append(jnp.sum(jnp.where(here, line, 0.0), axis=1, keepdims=True))

    turn = turn_column(turn_ref, rows)
    share_down = jnp.zeros((DEEP, LANES), F32)
    share_lanes = jnp.zeros((rows, LANES), F32)
    for k in range(DEEP):
        share_down = jnp.where(sub8 == k, share_ref[k], share_down)
        share_lanes = jnp.where((lane & 7) == k, share_ref[k], share_lanes)

    shallow = sums_ref[0:rows, 0:cols]
    tail = sums_ref[:, 3 * cols : 3 * cols + LANES]
    shallow_rows = [sums_ref[rows + n : rows + n + 1, 0:cols] for n in range(4)]
    east, west, north, south = around(shallow, tail[0:rows, 0:1], tail[0:rows, 1:2], shallow_rows[0], shallow_rows[1])
    half_press = 0.5 * PRESS
    push_x, push_y = half_press * (east - west), half_press * (north - south)
    col_row = iota((1, cols), 1)
    push_rows, push_cols = [], []
    for side in range(2):
        near, far = shallow_rows[side], shallow_rows[2 + side]
        west = jnp.where(col_row == 0, tail[rows + side : rows + side + 1, 0:1], roll(near, 1, 1))
        east = jnp.where(col_row == cols - 1, tail[rows + side : rows + side + 1, 1:2], roll(near, -1, 1))
        inner = shallow[0:1, :] if side == 0 else shallow[rows - 1 :, :]
        rise = inner - far if side == 0 else far - inner
        along, across = half_press * (east - west), half_press * rise
        if side == 0:
            along = jnp.where(at_bottom, push_x[0:1, :], along)
            across = jnp.where(at_bottom, push_y[0:1, :], across)
        push_rows.append((along, across))
    for side in range(2):
        near = jnp.broadcast_to(tail[0:rows, side : side + 1], (rows, LANES))
        far = tail[0:rows, 2 + side : 3 + side]
        inner = shallow[:, 0:1] if side == 0 else shallow[:, cols - 1 :]
        north = jnp.where(row == rows - 1, tail[rows + 1 : rows + 2, side : side + 1], roll(near, -1, 0))
        south = jnp.where(row == 0, tail[rows : rows + 1, side : side + 1], roll(near, 1, 0))
        push_cols.append((half_press * (inner - far if side == 0 else far - inner), half_press * (north - south)))

    ring_rows, above_rows = [], []
    for side, source in ((0, flux_south), (1, flux_north)):
        at = slice(rows + side, rows + side + 1)
        wet = ring_rows_ref[side, 5]
        taken = wet * share_down[:, 0:1]
        values = [ring_rows_ref[side, f] - wet * push_rows[side][f] for f in range(2)]
        values += [ring_rows_ref[side, 2 + c] + taken * source[c] for c in range(3)]
        ring_rows.append(values)
        above_rows.append(
            sums_ref[at, cols : 2 * cols] + sums_ref[at, 2 * cols : 3 * cols] * buoyancy_of(source[0], source[1])
        )
    ring_cols, above_cols = [], []
    for side, source in ((0, flux_west), (1, flux_east)):
        found = ring_cols_ref[side]
        wet = lanes_between(found, WET, WET + 8)
        taken = wet * share_lanes
        found = found - roll(wet, -WET, 1) * push_cols[side][0] - roll(wet, 8 - WET, 1) * push_cols[side][1]
        for c in range(3):
            found = found + roll(taken, 8 * (2 + c) - WET, 1) * source[c]
        ring_cols.append(found)
        above_cols.append(tail[0:rows, 4 + side : 5 + side] + tail[0:rows, 6 + side : 7 + side] * buoyancy_of(source[0], source[1]))
    above = sums_ref[0:rows, cols : 2 * cols] + sums_ref[0:rows, 2 * cols : 3 * cols] * buoyancy_of(flux[0], flux[1])
    east, west, north, south = around(above, above_cols[0], above_cols[1], above_rows[0], above_rows[1])
    above_x, above_y = 0.5 * (east - west), 0.5 * (north - south)

    grid = [(r, j) for r in range(n_r) for j in range(n_j)]

    def cut(value, r, j):
        return value[r * DEEP : (r + 1) * DEEP, j * LANES : (j + 1) * LANES]

    run = {at: (cut(above_x, *at), cut(above_y, *at)) for at in grid}
    edge_cols = [edge_cols_ref[side] for side in range(2)]

    def column(value, r, n):
        return jnp.broadcast_to(value[r * DEEP : (r + 1) * DEEP, n : n + 1], (DEEP, LANES))

    for k in range(DEEP):
        wets, heats, grids = {}, {}, [[[None] * n_j for _ in range(n_r)] for _ in range(5)]
        for r, j in grid:
            at = tile(r, j, k, rows)
            wet = mask_ref[at].astype(F32)
            taken = wet * share_ref[k]
            wets[r, j] = wet
            heats[r, j] = [taken * cut(flux[c], r, j) for c in range(3)]
            for f in range(5):
                value = state_ref[(f, *at)]
                if j == 0:
                    value = jnp.where(lane8 == 0, column(edge_cols[0], r, f * DEEP + k), value)
                if j == n_j - 1:
                    value = jnp.where(lane8 == LANES - 1, column(edge_cols[1], r, f * DEEP + k), value)
                if r == 0:
                    value = jnp.where(sub8 == 0, edge_rows_ref[0, f, k : k + 1, at[1]], value)
                if r == n_r - 1:
                    value = jnp.where(sub8 == DEEP - 1, edge_rows_ref[1, f, k : k + 1, at[1]], value)
                if f < 2:
                    value = value - wet * cut((push_x, push_y)[f], r, j)
                else:
                    value = value + heats[r, j][f - 2]
                grids[f][r][j] = value
        fields = [
            Tiles(
                grids[f],
                [column(ring_cols[0], r, f * DEEP + k) for r in range(n_r)],
                [column(ring_cols[1], r, f * DEEP + k) for r in range(n_r)],
                [ring_rows[0][f][k : k + 1, j * LANES : (j + 1) * LANES] for j in range(n_j)],
                [ring_rows[1][f][k : k + 1, j * LANES : (j + 1) * LANES] for j in range(n_j)],
            )
            for f in range(5)
        ]
        for r, j in grid:
            at = tile(r, j, k, rows)
            over_x, over_y = run[r, j]

            def pressed(x, y):
                run[r, j] = (over_x + x, over_y + y)
                return PRESS * (over_x + 0.5 * x), PRESS * (over_y + 0.5 * y)

            new = advanced(
                [field.grid[r][j] for field in fields],
                [field.around(r, j) for field in fields],
                wets[r, j],
                turn[r * DEEP : (r + 1) * DEEP, 0:1],
                pressed,
                heats[r, j],
            )
            for f in range(5):
                out_ref[(f, *at)] = new[f]


def body(n_lon, n_lat, state, mask, coriolis, penetration, flux_tiles, flux_owner, flux_row, fold_partner):
    fields, levels, rows, cols = state.shape
    flat_state = state.reshape(fields, levels * rows, cols)
    flat_mask = mask.reshape(levels * rows, cols)
    last = n_lat - 1

    def across(d):
        return [(a * n_lat + last, (a + d) % n_lon * n_lat + last) for a in range(n_lon)]

    keep, send, west, east, top = prepare(
        flat_state, flat_mask, flux_tiles, flux_owner, flux_row, fold_partner, n_lon, n_lat
    )

    stages = []
    for axis, size, least in (("lat", n_lat, 2), ("lon", n_lon, 1)):
        bit = size // 2
        while bit >= least:
            stages.append((axis, size, bit))
            bit //= 2
    got = lax.ppermute(send, "lat", [(i, i ^ 1) for i in range(n_lat)])

    def merged(keep, got):
        half = shape(keep.shape[0] // 2, keep.shape[1])
        return call(merge_kernel, (half, half), [VMEM] * 2, (keep, got), name="merge_flux")

    def passed_on(send, stage):
        axis, size, bit = stage
        return lax.ppermute(send, axis, [(i, i ^ bit) for i in range(size)])

    keep, send = merged(keep, got)
    got = passed_on(send, stages[0])

    west, east, top = after((west, east, top), send)
    from_west = lax.ppermute(east, "lon", [(i, (i + 1) % n_lon) for i in range(n_lon)])
    from_east = lax.ppermute(west, "lon", [((i + 1) % n_lon, i) for i in range(n_lon)])
    folded = {d: lax.ppermute(top, ("lon", "lat"), across(d)) for d in (1, n_lon - 1)}
    message = shape(SLABS + 1, DEEP, cols)
    pair, cross = call(
        rows_kernel,
        (message, message),
        [VMEM, VMEM, SMEM, VMEM, VMEM],
        (flat_state, flat_mask, coriolis, from_west, from_east),
        name="edge_rows",
    )
    keep = after(keep, (pair, cross, folded))
    keep, send = merged(keep, got)
    got = passed_on(send, stages[1])

    pair, cross, top = after((pair, cross, top), send)
    folded.update({d: lax.ppermute(top, ("lon", "lat"), across(d)) for d in range(2, n_lon - 1)})
    from_pair = lax.ppermute(pair, "lat", [(i, i ^ 1) for i in range(n_lat)])
    from_cross = lax.ppermute(cross, "lat", [(i, i + 1 if i % 2 else i - 1) for i in range(1, last)])
    keep = after(keep, (from_pair, from_cross, folded))
    for stage in stages[2:]:
        keep, send = merged(keep, got)
        got = passed_on(send, stage)

    near_state, near_mask = after((flat_state, flat_mask), send)
    new_state, inside = call(
        interior_kernel,
        (shape(fields, levels * rows, cols), shape(rows, 3 * cols)),
        [VMEM, VMEM, SMEM, SMEM],
        (near_state, near_mask, coriolis, penetration),
        name="first_inside",
    )
    keep = after(keep, inside)
    mine = keep + got
    theirs = lax.ppermute(mine, "lev", [(0, 1), (1, 0)])

    inside = after(inside, mine)
    ring = (shape(2, 6, DEEP, cols), shape(2, rows, LANES), shape(2, 5, DEEP, cols), shape(2, rows, LANES))
    blocks = [top] + [folded[d] for d in range(1, n_lon)]
    *ring, sums = call(
        functools.partial(rim_kernel, n_lon, n_lat),
        (*ring, shape(rows + DEEP, 3 * cols + LANES)),
        [VMEM, VMEM, SMEM, SMEM, SMEM] + [VMEM] * 7 + [ANY] * n_lon,
        (
            flat_state, flat_mask, coriolis, penetration, fold_partner, west, east, from_west, from_east, from_pair,
            from_cross, inside, *blocks,
        ),
        [
            pltpu.VMEM((SLABS + 1, DEEP, cols), F32),
            pltpu.VMEM((SLABS + 1, DEEP, cols), F32),
            pltpu.VMEM((3, SLABS, DEEP, cols), F32),
            pltpu.SemaphoreType.DMA((3,)),
        ],
        name="first_rim",
    )
    sums = lax.ppermute(sums, "lev", [(0, 1)])

    out = call(
        functools.partial(last_kernel, n_lon, n_lat),
        shape(fields, levels * rows, cols),
        [VMEM] * 9 + [SMEM] * 3,
        (new_state, flat_mask, *ring, sums, mine, theirs, coriolis, penetration, fold_partner),
        name="last_substep",
    )
    return out.reshape(fields, levels, rows, cols)


def solution(mesh):
    n_lon, n_lat = mesh.shape["lon"], mesh.shape["lat"]
    assert mesh.shape["lev"] == 2 and n_lat % 2 == 0 and n_lon > 2
    return jax.shard_map(
        functools.partial(body, n_lon, n_lat),
        mesh=mesh,
        in_specs=(
            P(None, "lev", "lat", "lon"),
            P("lev", "lat", "lon"),
            P("lat"),
            P("lev"),
            P(("lon", "lat"), None, None),
            P(("lon", "lat"), None),
            P(("lon", "lat")),
            P(),
        ),
        out_specs=P(None, "lev", "lat", "lon"),
        check_vma=False,
    )
```

```python
import functools

import jax
import jax.numpy as jnp
from jax import lax
from jax.experimental import pallas as pl
from jax.experimental.pallas import tpu as pltpu
from jax.sharding import PartitionSpec as P

ALPHA = 0.2
BETA = 0.15
PRESS = 0.1
VISCOUS = 0.1
DIFFUSE = 0.1
ADVECT = 0.1

F32 = jnp.float32
I32 = jnp.int32
LANES = 128
DEEP = 8
FAR = 64
WET = 48
ABOVE = 56
SLABS = 11
CORNERS = SLABS
VMEM_BYTES = 24 * 1024 * 1024

VMEM = pl.BlockSpec(memory_space=pltpu.VMEM)
SMEM = pl.BlockSpec(memory_space=pltpu.SMEM)
ANY = pl.BlockSpec(memory_space=pl.ANY)
HBM = pl.BlockSpec(memory_space=pltpu.HBM)


def iota(shape, dim):
    return lax.broadcasted_iota(I32, shape, dim)


def roll(value, shift, axis):
    return pltpu.roll(value, shift % value.shape[axis], axis)


def call(kernel, out_shape, in_specs, args, scratch=(), name=None, out_specs=None, aliases=None):
    return pl.pallas_call(
        kernel,
        out_shape=out_shape,
        in_specs=in_specs,
        out_specs=out_specs or jax.tree.map(lambda _: VMEM, out_shape),
        input_output_aliases=aliases or {},
        scratch_shapes=list(scratch),
        compiler_params=pltpu.CompilerParams(vmem_limit_bytes=VMEM_BYTES),
        name=name,
    )(*args)


def after(values, *others):
    return lax.optimization_barrier((values, others))[0]


def shape(*dims):
    return pltpu.VMEM(dims, F32)


def in_hbm(*arrays):
    return tuple(pltpu.with_memory_space_constraint(array, pltpu.HBM) for array in arrays)


def prepare_kernel(
    n_lon, n_lat, state_hbm, mask_hbm, tiles_hbm, owner_hbm, row_hbm, partner_hbm, keep_ref, send_ref, west_ref, east_ref,
    total_ref, state_ref, mask_ref, x_ref, owners_ref, rows_ref, hinge_ref, sem,
):
    tiles, cols = tiles_hbm.shape[1], tiles_hbm.shape[2]
    half_cols = cols // 2
    rows = 2 * DEEP
    n_y = n_lat // 2
    half = lax.axis_index("lev")
    lat = lax.axis_index("lat")
    core = lax.rem(lat, 2)
    begin = pl.multiple_of(half * half_cols, LANES)
    indices = [
        pltpu.make_async_copy(owner_hbm, owners_ref, sem.at[0]),
        pltpu.make_async_copy(row_hbm, rows_ref, sem.at[1]),
        pltpu.make_async_copy(partner_hbm, hinge_ref, sem.at[2]),
    ]
    fluxes = [
        pltpu.make_async_copy(
            tiles_hbm.at[c, :, pl.ds(begin, half_cols)], x_ref.at[:, pl.ds(c * half_cols, half_cols)], sem.at[3 + c]
        )
        for c in range(3)
    ]
    fields = [
        pltpu.make_async_copy(state_hbm, state_ref, sem.at[6]),
        pltpu.make_async_copy(mask_hbm, mask_ref, sem.at[7]),
    ]
    for copy in indices + fluxes + fields:
        copy.start()
    for copy in indices:
        copy.wait()

    key = owners_ref[...] * rows + rows_ref[...]
    hinge_block = hinge_ref[0] // cols
    slots = keep_ref.shape[0]
    slot = iota((slots, tiles), 0)
    group, sub = slot >> 3, slot & 7
    at_y = (group >> (n_lon.bit_length() - 1)) ^ (lat // 2)
    at_lon = (group & (n_lon - 1)) ^ lax.axis_index("lon")

    def wrapped(lon):
        return jnp.where(lon < 0, lon + n_lon, jnp.where(lon >= n_lon, lon - n_lon, lon))

    def one_hot(hit):
        return jnp.where(hit, 1.0, 0.0).astype(jnp.bfloat16)

    def weights(to_core):
        lat = 2 * at_y + to_core
        owner = at_lon * n_lat + lat
        last = lat == n_lat - 1
        top = n_lat * rows - 1
        south = jnp.where(lat == 0, owner * rows, owner * rows - 1)
        north = jnp.where(last, wrapped(hinge_block - at_lon) * (n_lat * rows) + top, (owner + 1) * rows)
        third = jnp.where(last, wrapped(hinge_block - at_lon - 1) * (n_lat * rows) + top, -1)
        kind = sub >> 1
        extra_key = jnp.where(kind == 0, south, jnp.where(kind == 1, north, jnp.where(kind == 2, third, -1)))
        extra = key == extra_key
        beside = wrapped(at_lon + 1 - 2 * half) * n_lat + lat
        return (
            one_hot(key == owner * rows + sub),
            one_hot(key == owner * rows + DEEP + sub),
            one_hot(extra & ((sub & 1) == 0)),
            one_hot(extra & ((sub & 1) == 1)),
            one_hot(((key >> 4) == beside) & (sub == 6)),
        )

    def split(x):
        first = x.astype(jnp.bfloat16)
        rest = x - first.astype(F32)
        second = rest.astype(jnp.bfloat16)
        third = (rest - second.astype(F32)).astype(jnp.bfloat16)
        return first, second, third

    square = iota((tiles, tiles), 0) == iota((tiles, tiles), 1)
    row_of = jnp.sum(jnp.where(square, (key & (rows - 1)).astype(F32), 0.0), axis=1, keepdims=True).astype(I32)

    for copy in fluxes:
        copy.wait()
    x = x_ref[...]
    lane = iota((tiles, LANES), 1)
    edge = jnp.zeros((tiles, LANES), F32)
    for c in range(3):
        begin = c * half_cols
        value = jnp.where(half == 0, x[:, begin : begin + 1], x[:, begin + half_cols - 1 : begin + half_cols])
        edge = jnp.where(((lane >> 4) == c) & ((lane & 15) == row_of), value, edge)
    parts, edges = split(x), split(edge)
    wide = 3 * half_cols
    quarter = wide // 2

    def dot(hot, terms, begin, end):
        products = [
            jnp.dot(hot, term[:, begin:end], preferred_element_type=F32) for term in reversed(terms)
        ]
        return products[0] + products[1] + products[2]

    for out_ref, to_core in ((keep_ref, core), (send_ref, 1 - core)):
        low, high, even, odd, ring = weights(to_core)
        out_ref[:, 0:wide] = dot(low, parts, 0, wide)
        out_ref[:, wide : 2 * wide] = dot(high, parts, 0, wide)
        rest = dot(even, parts, 0, quarter) + dot(odd, parts, quarter, wide)
        beside = dot(ring, edges, 0, LANES)
        out_ref[:, 2 * wide : 2 * wide + LANES] = rest[:, 0:LANES] + beside
        out_ref[:, 2 * wide + LANES :] = rest[:, LANES:]

    for copy in fields:
        copy.wait()
    total = jnp.zeros(total_ref.shape, F32)
    for k in range(DEEP):
        at = slice(k * rows, (k + 1) * rows)
        total = total + buoyancy_of(state_ref[2, at, :], state_ref[3, at, :])
    total_ref[...] = total
    edge_columns(state_ref, mask_ref, west_ref, east_ref)


def merge_kernel(kept_ref, got_ref, keep_ref, send_ref):
    half = keep_ref.shape[0]
    send_ref[...] = kept_ref[half:, :] + got_ref[half:, :]
    keep_ref[...] = kept_ref[0:half, :] + got_ref[0:half, :]


def prepare(state, mask, flux_tiles, flux_owner, flux_row, fold_partner, n_lon, n_lat):
    tiles, _, cols = flux_tiles.shape
    wide = 3 * (cols // 2)
    slots = shape(n_lon * n_lat // 2 * DEEP, 2 * wide + wide // 2)
    side = shape(2 * DEEP, LANES)
    return call(
        functools.partial(prepare_kernel, n_lon, n_lat),
        (slots, slots, side, side, shape(2 * DEEP, cols)),
        [HBM] * 6,
        in_hbm(
            state,
            mask,
            flux_tiles.transpose(1, 0, 2),
            flux_owner.reshape(1, tiles),
            flux_row.reshape(1, tiles),
            fold_partner,
        ),
        [
            pltpu.VMEM(state.shape, F32),
            pltpu.VMEM(mask.shape, I32),
            pltpu.VMEM((tiles, wide), F32),
            pltpu.VMEM((1, tiles), I32),
            pltpu.VMEM((1, tiles), I32),
            pltpu.SMEM(fold_partner.shape, I32),
            pltpu.SemaphoreType.DMA((8,)),
        ],
        name="prepare",
    )


def level_rows(ref, row, rows):
    return jnp.concatenate([ref[k * rows + row : k * rows + row + 1, :] for k in range(DEEP)], axis=0)


def buoyancy_of(temper, saline):
    return ALPHA * temper - BETA * saline


def edge_rows(state_ref, mask_ref, out_ref, rows, near, far):
    for f in range(5):
        out_ref[2 * f] = level_rows(state_ref.at[f], near, rows)
        out_ref[2 * f + 1] = level_rows(state_ref.at[f], far, rows)
    out_ref[10] = level_rows(mask_ref, near, rows).astype(F32)


def edge_columns(state_ref, mask_ref, west_ref, east_ref):
    rows, cols = west_ref.shape[0], state_ref.shape[2]
    lane = iota((rows, LANES), 1)
    last = slice(cols - LANES, cols)
    west = jnp.zeros((rows, LANES), F32)
    east = jnp.zeros((rows, LANES), F32)
    for k in range(DEEP):
        at = slice(k * rows, (k + 1) * rows)
        for f in range(5):
            to = f * DEEP + k
            left, right = state_ref[f, at, 0:LANES], state_ref[f, at, last]
            west = jnp.where(lane == to, roll(left, to, 1), west)
            west = jnp.where(lane == FAR + to, roll(left, FAR + to - 1, 1), west)
            east = jnp.where(lane == to, roll(right, to + 1, 1), east)
            east = jnp.where(lane == FAR + to, roll(right, FAR + to + 2, 1), east)
        west = jnp.where(lane == WET + k, roll(mask_ref[at, 0:LANES].astype(F32), WET + k, 1), west)
        east = jnp.where(lane == WET + k, roll(mask_ref[at, last].astype(F32), WET + k + 1, 1), east)
    west_ref[...] = west
    east_ref[...] = east


def columns_kernel(west_ref, east_ref, prefix_ref, west_out_ref, east_out_ref):
    rows, cols = prefix_ref.shape
    lane = iota((rows, LANES), 1)
    for side, in_ref, out_ref in ((0, west_ref, west_out_ref), (1, east_ref, east_out_ref)):
        near, far = (0, 1) if side == 0 else (cols - 1, cols - 2)
        value = jnp.where(lane == ABOVE, prefix_ref[:, near : near + 1], in_ref[...])
        out_ref[...] = jnp.where(lane == FAR + ABOVE, prefix_ref[:, far : far + 1], value)


def corner_slab(out_ref, prefix_ref, turn_ref, from_west_ref, from_east_ref, near, far):
    out_ref[CORNERS] = jnp.full(out_ref.shape[1:], turn_ref[near], F32)
    out_ref[CORNERS, 0:1, 0:LANES] = from_west_ref[near : near + 1, :]
    out_ref[CORNERS, 1:2, 0:LANES] = from_east_ref[near : near + 1, :]
    out_ref[CORNERS, 3:4, :] = prefix_ref[near : near + 1, :]
    out_ref[CORNERS, 4:5, :] = prefix_ref[far : far + 1, :]


def rows_kernel(state_ref, mask_ref, prefix_ref, turn_ref, from_west_ref, from_east_ref, pair_ref, cross_ref):
    rows = prefix_ref.shape[0]
    odd = lax.rem(lax.axis_index("lat"), 2) == 1

    def fill(out_ref, near, far):
        edge_rows(state_ref, mask_ref, out_ref, rows, near, far)
        corner_slab(out_ref, prefix_ref, turn_ref, from_west_ref, from_east_ref, near, far)

    @pl.when(odd)
    def _():
        fill(pair_ref, 0, 1)
        fill(cross_ref, rows - 1, rows - 2)

    @pl.when(jnp.logical_not(odd))
    def _():
        fill(pair_ref, rows - 1, rows - 2)
        fill(cross_ref, 0, 1)


def around(value, west, east, south, north):
    rows, cols = value.shape
    row, col = iota((rows, cols), 0), iota((rows, cols), 1)
    return (
        jnp.where(col == cols - 1, east, roll(value, -1, 1)),
        jnp.where(col == 0, west, roll(value, 1, 1)),
        jnp.where(row == rows - 1, north, roll(value, -1, 0)),
        jnp.where(row == 0, south, roll(value, 1, 0)),
    )


def advanced(values, sides, wet, turn, pressed, heat=None):
    zonal, merid = values[0], values[1]
    sums = [(e + w) + (n + s) for e, w, n, s in sides]
    across = [(e - w, n - s) for e, w, n, s in sides]
    press_x, press_y = pressed(
        0.5 * buoyancy_of(across[2][0], across[3][0]), 0.5 * buoyancy_of(across[2][1], across[3][1])
    )
    out = []
    carry_x, carry_y = (0.5 * ADVECT) * zonal, (0.5 * ADVECT) * merid
    for f in range(5):
        spread = (VISCOUS if f < 2 else DIFFUSE) * (sums[f] - 4.0 * values[f])
        if f == 0:
            trend = spread + (turn * merid - press_x)
        elif f == 1:
            trend = spread - (turn * zonal + press_y)
        else:
            trend = spread - (carry_x * across[f][0] + carry_y * across[f][1])
        new = values[f] + wet * trend
        out.append(new if heat is None or f < 2 else new + heat[f - 2])
    return out


class Tiles:
    def __init__(self, grid, west=None, east=None, south=None, north=None):
        self.grid, self.ghosts, self.turned = grid, (west, east, south, north), {}
        self.lane, self.sub = iota((DEEP, LANES), 1), iota((DEEP, LANES), 0)

    def rolled(self, r, j, shift, axis):
        at = (r, j, shift, axis)
        if at not in self.turned:
            self.turned[at] = roll(self.grid[r][j], shift, axis)
        return self.turned[at]

    def side(self, r, j, shift, axis):
        here = self.rolled(r, j, shift, axis)
        r_from, j_from = (r, j - shift) if axis else (r - shift, j)
        edge = (0 if shift == 1 else LANES - 1) if axis else (0 if shift == 1 else DEEP - 1)
        if 0 <= r_from < len(self.grid) and 0 <= j_from < len(self.grid[0]):
            other = self.rolled(r_from, j_from, shift, axis)
        else:
            ghost = self.ghosts[(0 if shift == 1 else 1) + (0 if axis else 2)]
            if ghost is None:
                return here
            other = ghost[r if axis else j]
        return jnp.where((self.lane if axis else self.sub) == edge, other, here)

    def around(self, r, j):
        return self.side(r, j, -1, 1), self.side(r, j, 1, 1), self.side(r, j, -1, 0), self.side(r, j, 1, 0)


def tile(r, j, k, rows):
    return slice(k * rows + r * DEEP, k * rows + (r + 1) * DEEP), slice(j * LANES, (j + 1) * LANES)


def turn_column(turn_ref, rows):
    row = iota((rows, LANES), 0)
    column = jnp.zeros((rows, LANES), F32)
    for j in range(rows):
        column = jnp.where(row == j, turn_ref[j], column)
    return column


def mirrored(value, width):
    back = LANES - 1 - iota((value.shape[0], LANES), 1)
    blocks = [
        jnp.take_along_axis(value[:, begin : begin + LANES], back, axis=1)
        for begin in range(width - LANES, -1, -LANES)
    ]
    return jnp.concatenate(blocks, axis=1)


def scan_down(value):
    row = iota(value.shape, 0)
    for step in (1, 2, 4):
        value = value + jnp.where(row >= step, roll(value, step, 0), 0.0)
    return value


def scan_lanes(value):
    lane = iota(value.shape, 1) & 7
    for step in (1, 2, 4):
        value = value + jnp.where(lane >= step, roll(value, step, 1), 0.0)
    return value


def lanes_between(value, begin, end):
    lane = iota(value.shape, 1)
    return jnp.where((lane >= begin) & (lane < end), value, 0.0)


def buoyancy_sum(column):
    here = lanes_between(buoyancy_of(roll(column, -16, 1), roll(column, -24, 1)), 0, 8)
    return jnp.sum(here, axis=1, keepdims=True)


def inside_kernel(state_ref, mask_ref, prefix_ref, turn_ref, share_ref, new_ref, sums_ref):
    rows, cols = prefix_ref.shape
    n_r, n_j = rows // DEEP, cols // LANES
    turn = turn_column(turn_ref, rows)
    grid = [(r, j) for r in range(n_r) for j in range(n_j)]
    zero = jnp.zeros((DEEP, LANES), F32)
    prefix = Tiles([[prefix_ref[tile(r, j, 0, rows)] for j in range(n_j)] for r in range(n_r)])
    run = {}
    for at in grid:
        east, west, north, south = prefix.around(*at)
        run[at] = [0.5 * (east - west), 0.5 * (north - south), zero, zero]
    for k in range(DEEP):
        fields = [Tiles([[state_ref[(f, *tile(r, j, k, rows))] for j in range(n_j)] for r in range(n_r)]) for f in range(5)]
        for r, j in grid:
            at = tile(r, j, k, rows)
            above_x, above_y, total, absorbed = run[r, j]
            slopes = []

            def pressed(x, y):
                slopes.extend((x, y))
                return PRESS * (above_x + 0.5 * x), PRESS * (above_y + 0.5 * y)

            values = [field.grid[r][j] for field in fields]
            wet = mask_ref[at].astype(F32)
            new = advanced(
                values, [field.around(r, j) for field in fields], wet, turn[r * DEEP : (r + 1) * DEEP, 0:1], pressed
            )
            for f in range(5):
                new_ref[(f, *at)] = new[f]
            run[r, j] = [
                above_x + slopes[0],
                above_y + slopes[1],
                total + buoyancy_of(new[2], new[3]),
                absorbed + wet * share_ref[k],
            ]
    for r, j in grid:
        for kind in range(2):
            at = slice(kind * cols + j * LANES, kind * cols + (j + 1) * LANES)
            sums_ref[r * DEEP : (r + 1) * DEEP, at] = run[r, j][2 + kind]


def rim_kernel(
    n_lat, state_ref, mask_ref, prefix_ref, turn_ref, share_ref, partner_ref, own_west_ref, own_east_ref,
    from_west_ref, from_east_ref, pair_ref, cross_ref, first_ref, second_ref, inside_ref, ring_rows_ref, ring_cols_ref,
    edge_rows_ref, edge_cols_ref, sums_ref, south_ref, north_ref,
):
    rows, cols = prefix_ref.shape
    lat = lax.axis_index("lat")
    odd = lax.rem(lat, 2) == 1
    hinge = partner_ref[0]
    within = hinge - (hinge // cols) * cols
    at_top = lat == n_lat - 1

    @pl.when(odd)
    def _():
        south_ref[...] = pair_ref[...]

    @pl.when(jnp.logical_not(odd))
    def _():
        north_ref[...] = pair_ref[...]

    @pl.when(jnp.logical_not(odd) & (lat > 0))
    def _():
        south_ref[...] = cross_ref[...]

    @pl.when(odd & (lat < n_lat - 1))
    def _():
        north_ref[...] = cross_ref[...]

    @pl.when(lat == 0)
    def _():
        edge_rows(state_ref, mask_ref, south_ref, rows, 0, 0)
        corner_slab(south_ref, prefix_ref, turn_ref, from_west_ref, from_east_ref, 0, 0)

    sub8, lane8 = iota((DEEP, LANES), 0), iota((DEEP, LANES), 1)

    @pl.when(at_top)
    def _():
        west = jnp.zeros((DEEP, LANES), F32)
        east = jnp.zeros((DEEP, LANES), F32)
        for slab in range(SLABS + 1):
            row = jnp.concatenate([second_ref[slab], first_ref[slab]], axis=1)
            row = pltpu.roll(row, 2 * cols - 1 - within, 1)
            if slab < 4:
                row = -row
            north_ref[slab] = mirrored(row, cols)
            if slab < 10 and slab % 2 == 0:
                here = lane8 == (slab // 2) * DEEP + sub8
            elif slab == CORNERS:
                here = (lane8 == ABOVE) & (sub8 == 3)
            else:
                continue
            west = jnp.where(here, row[:, cols : cols + 1], west)
            east = jnp.where(here, row[:, 2 * cols - 1 :], east)
        beyond = first_ref[CORNERS, 1:2, 0:LANES]
        beyond = jnp.where(iota((1, LANES), 1) < 16, -beyond, beyond)
        west = jnp.where(within == cols - 1, beyond, jnp.sum(west, axis=0, keepdims=True))
        north_ref[CORNERS, 0:1, 0:LANES] = west
        north_ref[CORNERS, 1:2, 0:LANES] = jnp.sum(east, axis=0, keepdims=True)
        north_ref[CORNERS, 2:3, :] = jnp.full((1, cols), turn_ref[rows - 1], F32)

    wide = cols + LANES
    sums_ref[rows:, :] = jnp.zeros((DEEP, 2 * wide), F32)
    for kind in range(2):
        sums_ref[0:rows, kind * wide : kind * wide + cols] = inside_ref[:, kind * cols : (kind + 1) * cols]

    share_down = jnp.zeros((DEEP, LANES), F32)
    for k in range(DEEP):
        share_down = jnp.where(sub8 == k, share_ref[k], share_down)

    def down(line, f):
        return jnp.sum(jnp.where(lane8 == f * DEEP + sub8, line, 0.0), axis=1, keepdims=True)

    def row_step(near, south, north, west_line, east_line, wet, turn, above, above_south, above_north):
        col = iota((DEEP, cols), 1)
        sides = [
            (
                jnp.where(col == cols - 1, down(east_line, f), roll(near[f], -1, 1)),
                jnp.where(col == 0, down(west_line, f), roll(near[f], 1, 1)),
                north[f],
                south[f],
            )
            for f in range(5)
        ]
        east = jnp.where(col[0:1] == cols - 1, east_line[:, ABOVE : ABOVE + 1], roll(above, -1, 1))
        west = jnp.where(col[0:1] == 0, west_line[:, ABOVE : ABOVE + 1], roll(above, 1, 1))
        above_x, above_y = 0.5 * (east - west), 0.5 * (above_north - above_south)

        def pressed(x, y):
            return PRESS * (above_x + scan_down(x) - 0.5 * x), PRESS * (above_y + scan_down(y) - 0.5 * y)

        return advanced(near, sides, wet, turn, pressed)

    for side, ghost_ref, edge, inner in ((0, south_ref, 0, 1), (1, north_ref, rows - 1, rows - 2)):
        near = [ghost_ref[2 * f] for f in range(5)]
        far = [ghost_ref[2 * f + 1] for f in range(5)]
        own = [level_rows(state_ref.at[f], edge, rows) for f in range(5)]
        own_next = [level_rows(state_ref.at[f], inner, rows) for f in range(5)]
        ring_wet = ghost_ref[10]
        corners = ghost_ref[CORNERS, :, 0:LANES]
        above_near, above_far = ghost_ref[CORNERS, 3:4, :], ghost_ref[CORNERS, 4:5, :]
        above_own, above_next = prefix_ref[edge : edge + 1, :], prefix_ref[inner : inner + 1, :]
        outward, inward = (far, above_far), (own, above_own)
        (south, above_south), (north, above_north) = (outward, inward) if side == 0 else (inward, outward)
        ring = row_step(
            near, south, north, corners[0:1, :], corners[1:2, :], ring_wet, corners[2:3, 0:1], above_near, above_south, above_north
        )
        outward, inward = (near, above_near), (own_next, above_next)
        (south, above_south), (north, above_north) = (outward, inward) if side == 0 else (inward, outward)
        wet = level_rows(mask_ref, edge, rows).astype(F32)
        edge_line = slice(edge, edge + 1)
        new = row_step(
            own, south, north, from_west_ref[edge_line, :], from_east_ref[edge_line, :], wet, turn_ref[edge],
            above_own, above_south, above_north,
        )
        for f in range(5):
            edge_rows_ref[side, f] = new[f]
            ring_rows_ref[side, f] = jnp.where(lat == 0, new[f], ring[f]) if side == 0 else ring[f]
        ring_rows_ref[side, 5] = ring_wet
        at = slice(rows + side, rows + side + 1)
        here = buoyancy_of(ring_rows_ref[side, 2], ring_rows_ref[side, 3])
        sums_ref[at, 0:cols] = jnp.sum(here, axis=0, keepdims=True)
        sums_ref[at, wide : wide + cols] = jnp.sum(ring_wet * share_down[:, 0:1], axis=0, keepdims=True)

    row, lane = iota((rows, LANES), 0), iota((rows, LANES), 1)
    turn = turn_column(turn_ref, rows)
    share_lanes = jnp.zeros((rows, LANES), F32)
    for k in range(DEEP):
        share_lanes = jnp.where((lane & 7) == k, share_ref[k], share_lanes)

    def column_step(near, east, west, north, south):
        dx, dy = 0.5 * (east - west), 0.5 * (north - south)
        lap = (east + west) + (north + south) - 4.0 * near
        zonal, merid = lanes_between(near, 0, 8), lanes_between(near, 8, 16)
        wet = lanes_between(near, WET, WET + 8)
        wet_all = sum(roll(wet, -8 * n, 1) for n in range(2, 7))
        zonal_all = sum(roll(zonal, 8 * n, 1) for n in (2, 3, 4))
        merid_all = sum(roll(merid, 8 * n, 1) for n in (1, 2, 3))
        bx = lanes_between(buoyancy_of(roll(dx, -16, 1), roll(dx, -24, 1)), 0, 8)
        by = lanes_between(buoyancy_of(roll(dy, -8, 1), roll(dy, -16, 1)), 8, 16)
        press_x = lanes_between(PRESS * (dx[:, ABOVE : ABOVE + 1] + scan_lanes(bx) - 0.5 * bx), 0, 8)
        press_y = lanes_between(PRESS * (dy[:, ABOVE : ABOVE + 1] + scan_lanes(by) - 0.5 * by), 8, 16)
        trend = VISCOUS * lap - ADVECT * (zonal_all * dx + merid_all * dy) - press_x - press_y
        trend = trend + lanes_between(turn * roll(near, -8, 1), 0, 8) - lanes_between(turn * roll(near, 8, 1), 8, 16)
        return near + wet_all * trend, wet

    blocks = [jnp.zeros((rows, LANES), F32)] * 2
    sides = ((0, from_west_ref, own_west_ref), (1, from_east_ref, own_east_ref))
    for side, ghost_ref, own_ref in sides:
        near, own = ghost_ref[...], own_ref[...]
        far, own_next = roll(near, -FAR, 1), roll(own, -FAR, 1)
        north = jnp.where(row == rows - 1, north_ref[CORNERS, side : side + 1, 0:LANES], roll(near, -1, 0))
        south = jnp.where(row == 0, south_ref[CORNERS, side : side + 1, 0:LANES], roll(near, 1, 0))
        east, west = (own, far) if side == 0 else (far, own)
        new, wet = column_step(near, east, west, north, south)
        ring_cols_ref[side] = new
        blocks[0] = jnp.where(lane == side, buoyancy_sum(new), blocks[0])
        blocks[1] = jnp.where(lane == side, jnp.sum(wet * share_lanes, axis=1, keepdims=True), blocks[1])
        east, west = (own_next, near) if side == 0 else (near, own_next)
        new, _ = column_step(own, east, west, roll(own, -1, 0), roll(own, 1, 0))
        edge_cols_ref[side] = new
        column = 0 if side == 0 else cols - 1
        sums_ref[0:rows, column : column + 1] = buoyancy_sum(new)
    for kind in range(2):
        sums_ref[0:rows, kind * wide + cols : (kind + 1) * wide] = blocks[kind]
    for side, edge in ((0, 0), (1, rows - 1)):
        here = buoyancy_of(edge_rows_ref[side, 2], edge_rows_ref[side, 3])
        sums_ref[edge : edge + 1, 0:cols] = jnp.sum(here, axis=0, keepdims=True)


def second_kernel(
    n_lat, state_ref, mask_ref, ring_rows_ref, ring_cols_ref, edge_rows_ref, edge_cols_ref, mine_ref, theirs_ref,
    turn_ref, share_ref, partner_ref, out_hbm, flow_ref, drive_ref, tracers_ref, sem,
):
    rows, cols = mask_ref.shape[0] // DEEP, mask_ref.shape[1]
    n_r, n_j = rows // DEEP, cols // LANES
    half_cols = cols // 2
    wide = 3 * half_cols
    mine, theirs = mine_ref[...], theirs_ref[...]
    first = lax.axis_index("lev") == 0
    halves = (jnp.where(first, mine, theirs), jnp.where(first, theirs, mine))
    at_top = lax.axis_index("lat") == n_lat - 1
    hinge = partner_ref[0]
    within = hinge - (hinge // cols) * cols

    def extra(kind, c):
        found = []
        for part in halves:
            line = jnp.concatenate(
                [part[2 * kind : 2 * kind + 1, 2 * wide :], part[2 * kind + 1 : 2 * kind + 2, 2 * wide :]], axis=1
            )
            found.append(line[:, c * half_cols : (c + 1) * half_cols])
        return jnp.concatenate(found, axis=1)

    flux, flux_south, flux_north, flux_west, flux_east = [], [], [], [], []
    sub8 = iota((DEEP, LANES), 0)
    lane8 = iota((DEEP, LANES), 1)
    crossed = jnp.zeros((DEEP, 2 * cols), F32)
    for c in range(3):
        pair = jnp.concatenate([extra(2, c), extra(1, c)], axis=1)
        crossed = jnp.where(iota(crossed.shape, 0) == c, pair, crossed)
    crossed = mirrored(pltpu.roll(crossed, 2 * cols - 1 - within, 1), cols)
    row, lane = iota((rows, LANES), 0), iota((rows, LANES), 1)
    for c in range(3):
        bands = [
            jnp.concatenate([part[:, b * wide + c * half_cols : b * wide + (c + 1) * half_cols] for part in halves], axis=1)
            for b in range(2)
        ]
        flux.append(jnp.concatenate(bands, axis=0))
        flux_south.append(extra(0, c))
        flux_north.append(jnp.where(at_top, crossed[c : c + 1, :], extra(1, c)))
        here = lane == c * 16 + row
        for side, part in ((flux_west, halves[1]), (flux_east, halves[0])):
            line = part[6:7, 2 * wide : 2 * wide + LANES]
            side.append(jnp.sum(jnp.where(here, line, 0.0), axis=1, keepdims=True))

    turn = turn_column(turn_ref, rows)
    share_down = jnp.zeros((DEEP, LANES), F32)
    share_lanes = jnp.zeros((rows, LANES), F32)
    for k in range(DEEP):
        share_down = jnp.where(sub8 == k, share_ref[k], share_down)
        share_lanes = jnp.where((lane & 7) == k, share_ref[k], share_lanes)

    drive_ref[...] = jnp.zeros(drive_ref.shape, F32)
    drive_ref[0:rows, 0:cols] = buoyancy_of(flux[0], flux[1])

    ring_rows, ring_cols = [], []
    for side, source in ((0, flux_south), (1, flux_north)):
        taken = ring_rows_ref[side, 5] * share_down[:, 0:1]
        values = [ring_rows_ref[side, f] for f in range(2)]
        ring_rows.append(values + [ring_rows_ref[side, 2 + c] + taken * source[c] for c in range(3)])
        drive_ref[rows + side : rows + side + 1, 0:cols] = buoyancy_of(source[0], source[1])
    for side, source in ((0, flux_west), (1, flux_east)):
        found = ring_cols_ref[side]
        taken = lanes_between(found, WET, WET + 8) * share_lanes
        for c in range(3):
            found = found + roll(taken, 8 * (2 + c) - WET, 1) * source[c]
        ring_cols.append(found)
        drive_ref[0:rows, cols + side : cols + side + 1] = buoyancy_of(source[0], source[1])

    grid = [(r, j) for r in range(n_r) for j in range(n_j)]

    def cut(value, r, j):
        return value[r * DEEP : (r + 1) * DEEP, j * LANES : (j + 1) * LANES]

    zero = jnp.zeros((DEEP, LANES), F32)
    run = {at: (zero, zero) for at in grid}
    edge_cols = [edge_cols_ref[side] for side in range(2)]
    copies = []

    def column(value, r, n):
        return jnp.broadcast_to(value[r * DEEP : (r + 1) * DEEP, n : n + 1], (DEEP, LANES))

    for k in range(DEEP):
        wets, heats, grids = {}, {}, [[[None] * n_j for _ in range(n_r)] for _ in range(5)]
        for r, j in grid:
            at = tile(r, j, k, rows)
            wet = mask_ref[at].astype(F32)
            taken = wet * share_ref[k]
            wets[r, j] = wet
            heats[r, j] = [taken * cut(flux[c], r, j) for c in range(3)]
            for f in range(5):
                value = state_ref[(f, *at)]
                if j == 0:
                    value = jnp.where(lane8 == 0, column(edge_cols[0], r, f * DEEP + k), value)
                if j == n_j - 1:
                    value = jnp.where(lane8 == LANES - 1, column(edge_cols[1], r, f * DEEP + k), value)
                if r == 0:
                    value = jnp.where(sub8 == 0, edge_rows_ref[0, f, k : k + 1, at[1]], value)
                if r == n_r - 1:
                    value = jnp.where(sub8 == DEEP - 1, edge_rows_ref[1, f, k : k + 1, at[1]], value)
                if f >= 2:
                    value = value + heats[r, j][f - 2]
                grids[f][r][j] = value
        fields = [
            Tiles(
                grids[f],
                [column(ring_cols[0], r, f * DEEP + k) for r in range(n_r)],
                [column(ring_cols[1], r, f * DEEP + k) for r in range(n_r)],
                [ring_rows[0][f][k : k + 1, j * LANES : (j + 1) * LANES] for j in range(n_j)],
                [ring_rows[1][f][k : k + 1, j * LANES : (j + 1) * LANES] for j in range(n_j)],
            )
            for f in range(5)
        ]
        for r, j in grid:
            at = tile(r, j, k, rows)
            over_x, over_y = run[r, j]

            def pressed(x, y):
                run[r, j] = (over_x + x, over_y + y)
                return PRESS * (over_x + 0.5 * x), PRESS * (over_y + 0.5 * y)

            new = advanced(
                [field.grid[r][j] for field in fields],
                [field.around(r, j) for field in fields],
                wets[r, j],
                turn[r * DEEP : (r + 1) * DEEP, 0:1],
                pressed,
                heats[r, j],
            )
            for f in range(5):
                if f < 2:
                    flow_ref[(f, *at)] = new[f]
                else:
                    tracers_ref[(f - 2, *at)] = new[f]
        whole = pl.ds(k * rows, rows)
        copies.append(
            pltpu.make_async_copy(tracers_ref.at[:, whole, :], out_hbm.at[pl.ds(2, 3), whole, :], sem.at[k])
        )
        copies[-1].start()
    for copy in copies:
        copy.wait()


def last_kernel(out_in_hbm, flow_ref, mask_ref, sums_ref, drive_ref, out_hbm, moved_ref, sem):
    del out_in_hbm
    rows, cols = mask_ref.shape[0] // DEEP, mask_ref.shape[1]
    wide = cols + LANES
    above = sums_ref[:, 0:wide] + sums_ref[:, wide : 2 * wide] * drive_ref[...]
    east, west, north, south = around(
        above[0:rows, 0:cols],
        above[0:rows, cols : cols + 1],
        above[0:rows, cols + 1 : cols + 2],
        above[rows : rows + 1, 0:cols],
        above[rows + 1 : rows + 2, 0:cols],
    )
    push_x, push_y = (0.5 * PRESS) * (east - west), (0.5 * PRESS) * (north - south)
    copies = []
    for k in range(DEEP):
        whole = pl.ds(k * rows, rows)
        wet = mask_ref[whole, :].astype(F32)
        moved_ref[0, whole, :] = flow_ref[0, whole, :] - wet * push_x
        moved_ref[1, whole, :] = flow_ref[1, whole, :] - wet * push_y
        copies.append(pltpu.make_async_copy(moved_ref.at[:, whole, :], out_hbm.at[pl.ds(0, 2), whole, :], sem.at[k]))
        copies[-1].start()
    for copy in copies:
        copy.wait()


def body(n_lon, n_lat, state, mask, coriolis, penetration, flux_tiles, flux_owner, flux_row, fold_partner):
    fields, levels, rows, cols = state.shape
    flat_state = state.reshape(fields, levels * rows, cols)
    flat_mask = mask.reshape(levels * rows, cols)
    last = n_lat - 1

    keep, send, west, east, total = prepare(
        flat_state, flat_mask, flux_tiles, flux_owner, flux_row, fold_partner, n_lon, n_lat
    )

    stages = []
    for axis, size, least in (("lat", n_lat, 2), ("lon", n_lon, 1)):
        bit = size // 2
        while bit >= least:
            stages.append((axis, size, bit))
            bit //= 2
    got = lax.ppermute(send, "lat", [(i, i ^ 1) for i in range(n_lat)])
    prefix = lax.ppermute(total, "lev", [(0, 1)])

    def merged(keep, got):
        half = shape(keep.shape[0] // 2, keep.shape[1])
        return call(merge_kernel, (half, half), [VMEM] * 2, (keep, got), name="merge_flux")

    def passed_on(send, stage):
        axis, size, bit = stage
        return lax.ppermute(send, axis, [(i, i ^ bit) for i in range(size)])

    keep, send = merged(keep, got)
    got = passed_on(send, stages[0])

    prefix = after(prefix, send)
    side = shape(rows, LANES)
    west, east = call(columns_kernel, (side, side), [VMEM] * 3, (west, east, prefix), name="edge_columns")
    from_west = lax.ppermute(east, "lon", [(i, (i + 1) % n_lon) for i in range(n_lon)])
    from_east = lax.ppermute(west, "lon", [((i + 1) % n_lon, i) for i in range(n_lon)])
    message = shape(SLABS + 1, DEEP, cols)
    pair, cross = call(
        rows_kernel,
        (message, message),
        [VMEM, VMEM, VMEM, SMEM, VMEM, VMEM],
        (flat_state, flat_mask, prefix, coriolis, from_west, from_east),
        name="edge_rows",
    )
    hinge_block = fold_partner[0] >> (cols.bit_length() - 1)
    keep = after(keep, (pair, cross, hinge_block))
    keep, send = merged(keep, got)
    got = passed_on(send, stages[1])

    pair, cross = after((pair, cross), send)
    from_pair = lax.ppermute(pair, "lat", [(i, i ^ 1) for i in range(n_lat)])
    from_cross = lax.ppermute(cross, "lat", [(i, i + 1 if i % 2 else i - 1) for i in range(1, last)])

    def folded(block):
        def swap(rows_out):
            return tuple(
                lax.ppermute(
                    rows_out,
                    ("lon", "lat"),
                    [(a * n_lat + last, (block - more - a) % n_lon * n_lat + last) for a in range(n_lon)],
                )
                for more in (0, 1)
            )

        return swap

    first, second = lax.switch(hinge_block, [folded(block) for block in range(n_lon)], cross)
    keep = after(keep, (from_pair, from_cross, first, second))
    for stage in stages[2:]:
        keep, send = merged(keep, got)
        got = passed_on(send, stage)

    near_state, near_mask = after((flat_state, flat_mask), send)
    new_state, inside = call(
        inside_kernel,
        (shape(fields, levels * rows, cols), shape(rows, 2 * cols)),
        [VMEM, VMEM, VMEM, SMEM, SMEM],
        (near_state, near_mask, prefix, coriolis, penetration),
        name="first_inside",
    )
    keep = after(keep, inside)
    mine = keep + got
    theirs = lax.ppermute(mine, "lev", [(0, 1), (1, 0)])

    inside = after(inside, mine)
    wide = cols + LANES
    *ring, sums = call(
        functools.partial(rim_kernel, n_lat),
        (
            shape(2, 6, DEEP, cols),
            shape(2, rows, LANES),
            shape(2, 5, DEEP, cols),
            shape(2, rows, LANES),
            shape(rows + DEEP, 2 * wide),
        ),
        [VMEM, VMEM, VMEM, SMEM, SMEM, SMEM] + [VMEM] * 9,
        (
            flat_state, flat_mask, prefix, coriolis, penetration, fold_partner, west, east, from_west, from_east, from_pair,
            from_cross, first, second, inside,
        ),
        [pltpu.VMEM((SLABS + 1, DEEP, cols), F32), pltpu.VMEM((SLABS + 1, DEEP, cols), F32)],
        name="first_rim",
    )
    sums = after(sums, theirs)
    sums = lax.ppermute(sums, "lev", [(0, 1)])

    out = jax.ShapeDtypeStruct(flat_state.shape, F32)
    result, flow, drive = call(
        functools.partial(second_kernel, n_lat),
        (out, shape(2, levels * rows, cols), shape(rows + DEEP, wide)),
        [VMEM] * 8 + [SMEM] * 3,
        (new_state, flat_mask, *ring, mine, theirs, coriolis, penetration, fold_partner),
        [pltpu.VMEM((3, levels * rows, cols), F32), pltpu.SemaphoreType.DMA((DEEP,))],
        name="second_substep",
        out_specs=(ANY, VMEM, VMEM),
    )
    result = call(
        last_kernel,
        out,
        [ANY] + [VMEM] * 4,
        (result, flow, flat_mask, sums, drive),
        [pltpu.VMEM((2, levels * rows, cols), F32), pltpu.SemaphoreType.DMA((DEEP,))],
        name="deeper_pressure",
        out_specs=ANY,
        aliases={0: 0},
    )
    return result.reshape(fields, levels, rows, cols)


def solution(mesh):
    n_lon, n_lat = mesh.shape["lon"], mesh.shape["lat"]
    assert mesh.shape["lev"] == 2 and n_lat % 2 == 0 and n_lon > 2
    return jax.shard_map(
        functools.partial(body, n_lon, n_lat),
        mesh=mesh,
        in_specs=(
            P(None, "lev", "lat", "lon"),
            P("lev", "lat", "lon"),
            P("lat"),
            P("lev"),
            P(("lon", "lat"), None, None),
            P(("lon", "lat"), None),
            P(("lon", "lat")),
            P(),
        ),
        out_specs=P(None, "lev", "lat", "lon"),
        check_vma=False,
    )
```

```python
import functools

import jax
import jax.numpy as jnp
from jax import lax
from jax.experimental import pallas as pl
from jax.experimental.pallas import tpu as pltpu
from jax.sharding import PartitionSpec as P

ALPHA = 0.2
BETA = 0.15
PRESS = 0.1
VISCOUS = 0.1
DIFFUSE = 0.1
ADVECT = 0.1

F32 = jnp.float32
I32 = jnp.int32
LANES = 128
DEEP = 8
FAR = 64
WET = 48
ABOVE = 56
SLABS = 11
CORNERS = SLABS
VMEM_BYTES = 24 * 1024 * 1024

VMEM = pl.BlockSpec(memory_space=pltpu.VMEM)
SMEM = pl.BlockSpec(memory_space=pltpu.SMEM)
ANY = pl.BlockSpec(memory_space=pl.ANY)
HBM = pl.BlockSpec(memory_space=pltpu.HBM)


def iota(shape, dim):
    return lax.broadcasted_iota(I32, shape, dim)


def roll(value, shift, axis):
    return pltpu.roll(value, shift % value.shape[axis], axis)


def call(kernel, out_shape, in_specs, args, scratch=(), name=None, out_specs=None, aliases=None):
    return pl.pallas_call(
        kernel,
        out_shape=out_shape,
        in_specs=in_specs,
        out_specs=out_specs or jax.tree.map(lambda _: VMEM, out_shape),
        input_output_aliases=aliases or {},
        scratch_shapes=list(scratch),
        compiler_params=pltpu.CompilerParams(vmem_limit_bytes=VMEM_BYTES),
        name=name,
    )(*args)


def after(values, *others):
    return lax.optimization_barrier((values, others))[0]


def shape(*dims):
    return pltpu.VMEM(dims, F32)


def in_hbm(*arrays):
    return tuple(pltpu.with_memory_space_constraint(array, pltpu.HBM) for array in arrays)


def prepare_kernel(
    n_lon, n_lat, state_hbm, mask_hbm, tiles_hbm, owner_hbm, row_hbm, partner_hbm, keep_ref, send_ref, west_ref, east_ref,
    total_ref, state_ref, mask_ref, x_ref, owners_ref, rows_ref, hinge_ref, sem,
):
    tiles, cols = tiles_hbm.shape[1], tiles_hbm.shape[2]
    half_cols = cols // 2
    rows = 2 * DEEP
    n_y = n_lat // 2
    half = lax.axis_index("lev")
    lat = lax.axis_index("lat")
    core = lax.rem(lat, 2)
    begin = pl.multiple_of(half * half_cols, LANES)
    indices = [
        pltpu.make_async_copy(owner_hbm, owners_ref, sem.at[0]),
        pltpu.make_async_copy(row_hbm, rows_ref, sem.at[1]),
        pltpu.make_async_copy(partner_hbm, hinge_ref, sem.at[2]),
    ]
    fluxes = [
        pltpu.make_async_copy(
            tiles_hbm.at[c, :, pl.ds(begin, half_cols)], x_ref.at[:, pl.ds(c * half_cols, half_cols)], sem.at[3 + c]
        )
        for c in range(3)
    ]
    fields = [
        pltpu.make_async_copy(state_hbm, state_ref, sem.at[6]),
        pltpu.make_async_copy(mask_hbm, mask_ref, sem.at[7]),
    ]
    for copy in indices + fluxes + fields:
        copy.start()
    for copy in indices:
        copy.wait()

    key = owners_ref[...] * rows + rows_ref[...]
    hinge_block = hinge_ref[0] // cols
    slots = keep_ref.shape[0]
    slot = iota((slots, tiles), 0)
    group, sub = slot >> 3, slot & 7
    at_y = (group >> (n_lon.bit_length() - 1)) ^ (lat // 2)
    at_lon = (group & (n_lon - 1)) ^ lax.axis_index("lon")

    def wrapped(lon):
        return jnp.where(lon < 0, lon + n_lon, jnp.where(lon >= n_lon, lon - n_lon, lon))

    def one_hot(hit):
        return jnp.where(hit, 1.0, 0.0).astype(jnp.bfloat16)

    def weights(to_core):
        lat = 2 * at_y + to_core
        owner = at_lon * n_lat + lat
        last = lat == n_lat - 1
        top = n_lat * rows - 1
        south = jnp.where(lat == 0, owner * rows, owner * rows - 1)
        north = jnp.where(last, wrapped(hinge_block - at_lon) * (n_lat * rows) + top, (owner + 1) * rows)
        third = jnp.where(last, wrapped(hinge_block - at_lon - 1) * (n_lat * rows) + top, -1)
        kind = sub >> 1
        extra_key = jnp.where(kind == 0, south, jnp.where(kind == 1, north, jnp.where(kind == 2, third, -1)))
        extra = key == extra_key
        beside = wrapped(at_lon + 1 - 2 * half) * n_lat + lat
        return (
            one_hot(key == owner * rows + sub),
            one_hot(key == owner * rows + DEEP + sub),
            one_hot(extra & ((sub & 1) == 0)),
            one_hot(extra & ((sub & 1) == 1)),
            one_hot(((key >> 4) == beside) & (sub == 6)),
        )

    def split(x):
        first = x.astype(jnp.bfloat16)
        rest = x - first.astype(F32)
        second = rest.astype(jnp.bfloat16)
        third = (rest - second.astype(F32)).astype(jnp.bfloat16)
        return first, second, third

    square = iota((tiles, tiles), 0) == iota((tiles, tiles), 1)
    row_of = jnp.sum(jnp.where(square, (key & (rows - 1)).astype(F32), 0.0), axis=1, keepdims=True).astype(I32)

    for copy in fluxes:
        copy.wait()
    x = x_ref[...]
    lane = iota((tiles, LANES), 1)
    edge = jnp.zeros((tiles, LANES), F32)
    for c in range(3):
        begin = c * half_cols
        value = jnp.where(half == 0, x[:, begin : begin + 1], x[:, begin + half_cols - 1 : begin + half_cols])
        edge = jnp.where(((lane >> 4) == c) & ((lane & 15) == row_of), value, edge)
    parts, edges = split(x), split(edge)
    wide = 3 * half_cols
    quarter = wide // 2

    def dot(hot, terms, begin, end):
        products = [
            jnp.dot(hot, term[:, begin:end], preferred_element_type=F32) for term in reversed(terms)
        ]
        return products[0] + products[1] + products[2]

    for out_ref, to_core in ((keep_ref, core), (send_ref, 1 - core)):
        low, high, even, odd, ring = weights(to_core)
        out_ref[:, 0:wide] = dot(low, parts, 0, wide)
        out_ref[:, wide : 2 * wide] = dot(high, parts, 0, wide)
        rest = dot(even, parts, 0, quarter) + dot(odd, parts, quarter, wide)
        beside = dot(ring, edges, 0, LANES)
        out_ref[:, 2 * wide : 2 * wide + LANES] = rest[:, 0:LANES] + beside
        out_ref[:, 2 * wide + LANES :] = rest[:, LANES:]

    for copy in fields:
        copy.wait()
    total = jnp.zeros(total_ref.shape, F32)
    for k in range(DEEP):
        at = slice(k * rows, (k + 1) * rows)
        total = total + buoyancy_of(state_ref[2, at, :], state_ref[3, at, :])
    total_ref[...] = total
    edge_columns(state_ref, mask_ref, west_ref, east_ref)


def merge_kernel(kept_ref, got_ref, keep_ref, send_ref):
    half = keep_ref.shape[0]
    send_ref[...] = kept_ref[half:, :] + got_ref[half:, :]
    keep_ref[...] = kept_ref[0:half, :] + got_ref[0:half, :]


def prepare(state, mask, flux_tiles, flux_owner, flux_row, fold_partner, n_lon, n_lat):
    tiles, _, cols = flux_tiles.shape
    wide = 3 * (cols // 2)
    slots = shape(n_lon * n_lat // 2 * DEEP, 2 * wide + wide // 2)
    side = shape(2 * DEEP, LANES)
    return call(
        functools.partial(prepare_kernel, n_lon, n_lat),
        (slots, slots, side, side, shape(2 * DEEP, cols)),
        [HBM] * 6,
        in_hbm(
            state,
            mask,
            flux_tiles.transpose(1, 0, 2),
            flux_owner.reshape(1, tiles),
            flux_row.reshape(1, tiles),
            fold_partner,
        ),
        [
            pltpu.VMEM(state.shape, F32),
            pltpu.VMEM(mask.shape, I32),
            pltpu.VMEM((tiles, wide), F32),
            pltpu.VMEM((1, tiles), I32),
            pltpu.VMEM((1, tiles), I32),
            pltpu.SMEM(fold_partner.shape, I32),
            pltpu.SemaphoreType.DMA((8,)),
        ],
        name="prepare",
    )


def level_rows(ref, row, rows):
    return jnp.concatenate([ref[k * rows + row : k * rows + row + 1, :] for k in range(DEEP)], axis=0)


def buoyancy_of(temper, saline):
    return ALPHA * temper - BETA * saline


def edge_rows(state_ref, mask_ref, out_ref, rows, near, far):
    for f in range(5):
        out_ref[2 * f] = level_rows(state_ref.at[f], near, rows)
        out_ref[2 * f + 1] = level_rows(state_ref.at[f], far, rows)
    out_ref[10] = level_rows(mask_ref, near, rows).astype(F32)


def edge_columns(state_ref, mask_ref, west_ref, east_ref):
    rows, cols = west_ref.shape[0], state_ref.shape[2]
    lane = iota((rows, LANES), 1)
    last = slice(cols - LANES, cols)
    west = jnp.zeros((rows, LANES), F32)
    east = jnp.zeros((rows, LANES), F32)
    for k in range(DEEP):
        at = slice(k * rows, (k + 1) * rows)
        for f in range(5):
            to = f * DEEP + k
            left, right = state_ref[f, at, 0:LANES], state_ref[f, at, last]
            west = jnp.where(lane == to, roll(left, to, 1), west)
            west = jnp.where(lane == FAR + to, roll(left, FAR + to - 1, 1), west)
            east = jnp.where(lane == to, roll(right, to + 1, 1), east)
            east = jnp.where(lane == FAR + to, roll(right, FAR + to + 2, 1), east)
        west = jnp.where(lane == WET + k, roll(mask_ref[at, 0:LANES].astype(F32), WET + k, 1), west)
        east = jnp.where(lane == WET + k, roll(mask_ref[at, last].astype(F32), WET + k + 1, 1), east)
    west_ref[...] = west
    east_ref[...] = east


def top_kernel(state_ref, mask_ref, prefix_ref, top_ref):
    rows = prefix_ref.shape[0]
    edge_rows(state_ref, mask_ref, top_ref, rows, rows - 1, rows - 2)
    top_ref[CORNERS] = jnp.zeros(top_ref.shape[1:], F32)
    for n in (1, 2):
        top_ref[CORNERS, 2 + n : 3 + n, :] = prefix_ref[rows - n : rows - n + 1, :]


def columns_kernel(n_lat, west_ref, east_ref, prefix_ref, first_ref, second_ref, partner_ref, west_out_ref, east_out_ref):
    rows, cols = prefix_ref.shape
    lane = iota((rows, LANES), 1)
    for side, in_ref, out_ref in ((0, west_ref, west_out_ref), (1, east_ref, east_out_ref)):
        near, far = (0, 1) if side == 0 else (cols - 1, cols - 2)
        value = jnp.where(lane == ABOVE, prefix_ref[:, near : near + 1], in_ref[...])
        out_ref[0:rows, :] = jnp.where(lane == FAR + ABOVE, prefix_ref[:, far : far + 1], value)
        out_ref[rows:, :] = jnp.zeros((DEEP, LANES), F32)

    @pl.when(lax.axis_index("lat") == n_lat - 1)
    def _():
        within = partner_ref[0] & (cols - 1)
        sub8, lane8 = iota((DEEP, LANES), 0), iota((DEEP, LANES), 1)
        col = iota((DEEP, 2 * cols), 1)
        for place, out_ref in ((cols + within, west_out_ref), (within + 1, east_out_ref)):
            line = jnp.zeros((DEEP, LANES), F32)
            for slab in (0, 2, 4, 6, 8, CORNERS):
                both = jnp.concatenate([second_ref[slab], first_ref[slab]], axis=1)
                cell = jnp.sum(jnp.where(col == place, both, 0.0), axis=1, keepdims=True)
                here = (lane8 == ABOVE) & (sub8 == 3) if slab == CORNERS else lane8 == (slab // 2) * DEEP + sub8
                line = jnp.where(here, -cell if slab < 4 else cell, line)
            out_ref[rows : rows + 1, :] = jnp.sum(line, axis=0, keepdims=True)


def corner_slab(out_ref, prefix_ref, turn_ref, from_west_ref, from_east_ref, near, far):
    out_ref[CORNERS] = jnp.full(out_ref.shape[1:], turn_ref[near], F32)
    out_ref[CORNERS, 0:1, 0:LANES] = from_west_ref[near : near + 1, :]
    out_ref[CORNERS, 1:2, 0:LANES] = from_east_ref[near : near + 1, :]
    out_ref[CORNERS, 3:4, :] = prefix_ref[near : near + 1, :]
    out_ref[CORNERS, 4:5, :] = prefix_ref[far : far + 1, :]


def rows_kernel(state_ref, mask_ref, prefix_ref, turn_ref, from_west_ref, from_east_ref, pair_ref, cross_ref):
    rows = prefix_ref.shape[0]
    odd = lax.rem(lax.axis_index("lat"), 2) == 1

    def fill(out_ref, near, far):
        edge_rows(state_ref, mask_ref, out_ref, rows, near, far)
        corner_slab(out_ref, prefix_ref, turn_ref, from_west_ref, from_east_ref, near, far)

    @pl.when(odd)
    def _():
        fill(pair_ref, 0, 1)
        fill(cross_ref, rows - 1, rows - 2)

    @pl.when(jnp.logical_not(odd))
    def _():
        fill(pair_ref, rows - 1, rows - 2)
        fill(cross_ref, 0, 1)


def around(value, west, east, south, north):
    rows, cols = value.shape
    row, col = iota((rows, cols), 0), iota((rows, cols), 1)
    return (
        jnp.where(col == cols - 1, east, roll(value, -1, 1)),
        jnp.where(col == 0, west, roll(value, 1, 1)),
        jnp.where(row == rows - 1, north, roll(value, -1, 0)),
        jnp.where(row == 0, south, roll(value, 1, 0)),
    )


def advanced(values, sides, wet, turn, pressed, heat=None):
    zonal, merid = values[0], values[1]
    sums = [(e + w) + (n + s) for e, w, n, s in sides]
    across = [(e - w, n - s) for e, w, n, s in sides]
    press_x, press_y = pressed(
        0.5 * buoyancy_of(across[2][0], across[3][0]), 0.5 * buoyancy_of(across[2][1], across[3][1])
    )
    out = []
    carry_x, carry_y = (0.5 * ADVECT) * zonal, (0.5 * ADVECT) * merid
    for f in range(5):
        spread = (VISCOUS if f < 2 else DIFFUSE) * (sums[f] - 4.0 * values[f])
        if f == 0:
            trend = spread + (turn * merid - press_x)
        elif f == 1:
            trend = spread - (turn * zonal + press_y)
        else:
            trend = spread - (carry_x * across[f][0] + carry_y * across[f][1])
        new = values[f] + wet * trend
        out.append(new if heat is None or f < 2 else new + heat[f - 2])
    return out


class Tiles:
    def __init__(self, grid, west=None, east=None, south=None, north=None):
        self.grid, self.ghosts, self.turned = grid, (west, east, south, north), {}
        self.lane, self.sub = iota((DEEP, LANES), 1), iota((DEEP, LANES), 0)

    def rolled(self, r, j, shift, axis):
        at = (r, j, shift, axis)
        if at not in self.turned:
            self.turned[at] = roll(self.grid[r][j], shift, axis)
        return self.turned[at]

    def side(self, r, j, shift, axis):
        here = self.rolled(r, j, shift, axis)
        r_from, j_from = (r, j - shift) if axis else (r - shift, j)
        edge = (0 if shift == 1 else LANES - 1) if axis else (0 if shift == 1 else DEEP - 1)
        if 0 <= r_from < len(self.grid) and 0 <= j_from < len(self.grid[0]):
            other = self.rolled(r_from, j_from, shift, axis)
        else:
            ghost = self.ghosts[(0 if shift == 1 else 1) + (0 if axis else 2)]
            if ghost is None:
                return here
            other = ghost[r if axis else j]
        return jnp.where((self.lane if axis else self.sub) == edge, other, here)

    def around(self, r, j):
        return self.side(r, j, -1, 1), self.side(r, j, 1, 1), self.side(r, j, -1, 0), self.side(r, j, 1, 0)


def tile(r, j, k, rows):
    return slice(k * rows + r * DEEP, k * rows + (r + 1) * DEEP), slice(j * LANES, (j + 1) * LANES)


def turn_column(turn_ref, rows):
    row = iota((rows, LANES), 0)
    column = jnp.zeros((rows, LANES), F32)
    for j in range(rows):
        column = jnp.where(row == j, turn_ref[j], column)
    return column


def mirrored(value, width):
    back = LANES - 1 - iota((value.shape[0], LANES), 1)
    blocks = [
        jnp.take_along_axis(value[:, begin : begin + LANES], back, axis=1)
        for begin in range(width - LANES, -1, -LANES)
    ]
    return jnp.concatenate(blocks, axis=1)


def scan_down(value):
    row = iota(value.shape, 0)
    for step in (1, 2, 4):
        value = value + jnp.where(row >= step, roll(value, step, 0), 0.0)
    return value


def scan_lanes(value):
    lane = iota(value.shape, 1) & 7
    for step in (1, 2, 4):
        value = value + jnp.where(lane >= step, roll(value, step, 1), 0.0)
    return value


def lanes_between(value, begin, end):
    lane = iota(value.shape, 1)
    return jnp.where((lane >= begin) & (lane < end), value, 0.0)


def buoyancy_sum(column):
    here = lanes_between(buoyancy_of(roll(column, -16, 1), roll(column, -24, 1)), 0, 8)
    return jnp.sum(here, axis=1, keepdims=True)


def inside_kernel(state_ref, mask_ref, prefix_ref, turn_ref, share_ref, new_ref, sums_ref):
    rows, cols = prefix_ref.shape
    n_r, n_j = rows // DEEP, cols // LANES
    turn = turn_column(turn_ref, rows)
    grid = [(r, j) for r in range(n_r) for j in range(n_j)]
    zero = jnp.zeros((DEEP, LANES), F32)
    prefix = Tiles([[prefix_ref[tile(r, j, 0, rows)] for j in range(n_j)] for r in range(n_r)])
    run = {}
    for at in grid:
        east, west, north, south = prefix.around(*at)
        run[at] = [0.5 * (east - west), 0.5 * (north - south), zero, zero]
    for k in range(DEEP):
        fields = [Tiles([[state_ref[(f, *tile(r, j, k, rows))] for j in range(n_j)] for r in range(n_r)]) for f in range(5)]
        for r, j in grid:
            at = tile(r, j, k, rows)
            above_x, above_y, total, absorbed = run[r, j]
            slopes = []

            def pressed(x, y):
                slopes.extend((x, y))
                return PRESS * (above_x + 0.5 * x), PRESS * (above_y + 0.5 * y)

            values = [field.grid[r][j] for field in fields]
            wet = mask_ref[at].astype(F32)
            new = advanced(
                values, [field.around(r, j) for field in fields], wet, turn[r * DEEP : (r + 1) * DEEP, 0:1], pressed
            )
            for f in range(5):
                new_ref[(f, *at)] = new[f]
            run[r, j] = [
                above_x + slopes[0],
                above_y + slopes[1],
                total + buoyancy_of(new[2], new[3]),
                absorbed + wet * share_ref[k],
            ]
    for r, j in grid:
        for kind in range(2):
            at = slice(kind * cols + j * LANES, kind * cols + (j + 1) * LANES)
            sums_ref[r * DEEP : (r + 1) * DEEP, at] = run[r, j][2 + kind]


def rim_kernel(
    n_lat, state_ref, mask_ref, prefix_ref, turn_ref, share_ref, partner_ref, own_west_ref, own_east_ref,
    from_west_ref, from_east_ref, pair_ref, cross_ref, first_ref, second_ref, inside_ref, ring_rows_ref, ring_cols_ref,
    edge_rows_ref, edge_cols_ref, sums_ref, south_ref, north_ref,
):
    rows, cols = prefix_ref.shape
    lat = lax.axis_index("lat")
    odd = lax.rem(lat, 2) == 1
    hinge = partner_ref[0]
    within = hinge - (hinge // cols) * cols
    at_top = lat == n_lat - 1

    @pl.when(odd)
    def _():
        south_ref[...] = pair_ref[...]

    @pl.when(jnp.logical_not(odd))
    def _():
        north_ref[...] = pair_ref[...]

    @pl.when(jnp.logical_not(odd) & (lat > 0))
    def _():
        south_ref[...] = cross_ref[...]

    @pl.when(odd & (lat < n_lat - 1))
    def _():
        north_ref[...] = cross_ref[...]

    @pl.when(lat == 0)
    def _():
        edge_rows(state_ref, mask_ref, south_ref, rows, 0, 0)
        corner_slab(south_ref, prefix_ref, turn_ref, from_west_ref, from_east_ref, 0, 0)

    sub8, lane8 = iota((DEEP, LANES), 0), iota((DEEP, LANES), 1)

    @pl.when(at_top)
    def _():
        for slab in range(SLABS + 1):
            row = jnp.concatenate([second_ref[slab], first_ref[slab]], axis=1)
            row = pltpu.roll(row, 2 * cols - 1 - within, 1)
            if slab < 4:
                row = -row
            north_ref[slab] = mirrored(row, cols)
        north_ref[CORNERS, 0:1, 0:LANES] = from_west_ref[rows : rows + 1, :]
        north_ref[CORNERS, 1:2, 0:LANES] = from_east_ref[rows : rows + 1, :]
        north_ref[CORNERS, 2:3, :] = jnp.full((1, cols), turn_ref[rows - 1], F32)

    wide = cols + LANES
    sums_ref[rows:, :] = jnp.zeros((DEEP, 2 * wide), F32)
    for kind in range(2):
        sums_ref[0:rows, kind * wide : kind * wide + cols] = inside_ref[:, kind * cols : (kind + 1) * cols]

    share_down = jnp.zeros((DEEP, LANES), F32)
    for k in range(DEEP):
        share_down = jnp.where(sub8 == k, share_ref[k], share_down)

    def down(line, f):
        return jnp.sum(jnp.where(lane8 == f * DEEP + sub8, line, 0.0), axis=1, keepdims=True)

    def row_step(near, south, north, west_line, east_line, wet, turn, above, above_south, above_north):
        col = iota((DEEP, cols), 1)
        sides = [
            (
                jnp.where(col == cols - 1, down(east_line, f), roll(near[f], -1, 1)),
                jnp.where(col == 0, down(west_line, f), roll(near[f], 1, 1)),
                north[f],
                south[f],
            )
            for f in range(5)
        ]
        east = jnp.where(col[0:1] == cols - 1, east_line[:, ABOVE : ABOVE + 1], roll(above, -1, 1))
        west = jnp.where(col[0:1] == 0, west_line[:, ABOVE : ABOVE + 1], roll(above, 1, 1))
        above_x, above_y = 0.5 * (east - west), 0.5 * (above_north - above_south)

        def pressed(x, y):
            return PRESS * (above_x + scan_down(x) - 0.5 * x), PRESS * (above_y + scan_down(y) - 0.5 * y)

        return advanced(near, sides, wet, turn, pressed)

    for side, ghost_ref, edge, inner in ((0, south_ref, 0, 1), (1, north_ref, rows - 1, rows - 2)):
        near = [ghost_ref[2 * f] for f in range(5)]
        far = [ghost_ref[2 * f + 1] for f in range(5)]
        own = [level_rows(state_ref.at[f], edge, rows) for f in range(5)]
        own_next = [level_rows(state_ref.at[f], inner, rows) for f in range(5)]
        ring_wet = ghost_ref[10]
        corners = ghost_ref[CORNERS, :, 0:LANES]
        above_near, above_far = ghost_ref[CORNERS, 3:4, :], ghost_ref[CORNERS, 4:5, :]
        above_own, above_next = prefix_ref[edge : edge + 1, :], prefix_ref[inner : inner + 1, :]
        outward, inward = (far, above_far), (own, above_own)
        (south, above_south), (north, above_north) = (outward, inward) if side == 0 else (inward, outward)
        ring = row_step(
            near, south, north, corners[0:1, :], corners[1:2, :], ring_wet, corners[2:3, 0:1], above_near, above_south, above_north
        )
        outward, inward = (near, above_near), (own_next, above_next)
        (south, above_south), (north, above_north) = (outward, inward) if side == 0 else (inward, outward)
        wet = level_rows(mask_ref, edge, rows).astype(F32)
        edge_line = slice(edge, edge + 1)
        new = row_step(
            own, south, north, from_west_ref[edge_line, :], from_east_ref[edge_line, :], wet, turn_ref[edge],
            above_own, above_south, above_north,
        )
        for f in range(5):
            edge_rows_ref[side, f] = new[f]
            ring_rows_ref[side, f] = jnp.where(lat == 0, new[f], ring[f]) if side == 0 else ring[f]
        ring_rows_ref[side, 5] = ring_wet
        at = slice(rows + side, rows + side + 1)
        here = buoyancy_of(ring_rows_ref[side, 2], ring_rows_ref[side, 3])
        sums_ref[at, 0:cols] = jnp.sum(here, axis=0, keepdims=True)
        sums_ref[at, wide : wide + cols] = jnp.sum(ring_wet * share_down[:, 0:1], axis=0, keepdims=True)

    row, lane = iota((rows, LANES), 0), iota((rows, LANES), 1)
    turn = turn_column(turn_ref, rows)
    share_lanes = jnp.zeros((rows, LANES), F32)
    for k in range(DEEP):
        share_lanes = jnp.where((lane & 7) == k, share_ref[k], share_lanes)

    def column_step(near, east, west, north, south):
        dx, dy = 0.5 * (east - west), 0.5 * (north - south)
        lap = (east + west) + (north + south) - 4.0 * near
        zonal, merid = lanes_between(near, 0, 8), lanes_between(near, 8, 16)
        wet = lanes_between(near, WET, WET + 8)
        wet_all = sum(roll(wet, -8 * n, 1) for n in range(2, 7))
        zonal_all = sum(roll(zonal, 8 * n, 1) for n in (2, 3, 4))
        merid_all = sum(roll(merid, 8 * n, 1) for n in (1, 2, 3))
        bx = lanes_between(buoyancy_of(roll(dx, -16, 1), roll(dx, -24, 1)), 0, 8)
        by = lanes_between(buoyancy_of(roll(dy, -8, 1), roll(dy, -16, 1)), 8, 16)
        press_x = lanes_between(PRESS * (dx[:, ABOVE : ABOVE + 1] + scan_lanes(bx) - 0.5 * bx), 0, 8)
        press_y = lanes_between(PRESS * (dy[:, ABOVE : ABOVE + 1] + scan_lanes(by) - 0.5 * by), 8, 16)
        trend = VISCOUS * lap - ADVECT * (zonal_all * dx + merid_all * dy) - press_x - press_y
        trend = trend + lanes_between(turn * roll(near, -8, 1), 0, 8) - lanes_between(turn * roll(near, 8, 1), 8, 16)
        return near + wet_all * trend, wet

    blocks = [jnp.zeros((rows, LANES), F32)] * 2
    sides = ((0, from_west_ref, own_west_ref), (1, from_east_ref, own_east_ref))
    for side, ghost_ref, own_ref in sides:
        near, own = ghost_ref[0:rows, :], own_ref[0:rows, :]
        far, own_next = roll(near, -FAR, 1), roll(own, -FAR, 1)
        north = jnp.where(row == rows - 1, north_ref[CORNERS, side : side + 1, 0:LANES], roll(near, -1, 0))
        south = jnp.where(row == 0, south_ref[CORNERS, side : side + 1, 0:LANES], roll(near, 1, 0))
        east, west = (own, far) if side == 0 else (far, own)
        new, wet = column_step(near, east, west, north, south)
        ring_cols_ref[side] = new
        blocks[0] = jnp.where(lane == side, buoyancy_sum(new), blocks[0])
        blocks[1] = jnp.where(lane == side, jnp.sum(wet * share_lanes, axis=1, keepdims=True), blocks[1])
        east, west = (own_next, near) if side == 0 else (near, own_next)
        new, _ = column_step(own, east, west, roll(own, -1, 0), roll(own, 1, 0))
        edge_cols_ref[side] = new
        column = 0 if side == 0 else cols - 1
        sums_ref[0:rows, column : column + 1] = buoyancy_sum(new)
    for kind in range(2):
        sums_ref[0:rows, kind * wide + cols : (kind + 1) * wide] = blocks[kind]
    for side, edge in ((0, 0), (1, rows - 1)):
        here = buoyancy_of(edge_rows_ref[side, 2], edge_rows_ref[side, 3])
        sums_ref[edge : edge + 1, 0:cols] = jnp.sum(here, axis=0, keepdims=True)


def second_kernel(
    n_lat, state_ref, mask_ref, ring_rows_ref, ring_cols_ref, edge_rows_ref, edge_cols_ref, mine_ref, theirs_ref,
    turn_ref, share_ref, partner_ref, out_hbm, flow_ref, drive_ref, tracers_ref, sem,
):
    rows, cols = mask_ref.shape[0] // DEEP, mask_ref.shape[1]
    n_r, n_j = rows // DEEP, cols // LANES
    half_cols = cols // 2
    wide = 3 * half_cols
    mine, theirs = mine_ref[...], theirs_ref[...]
    first = lax.axis_index("lev") == 0
    halves = (jnp.where(first, mine, theirs), jnp.where(first, theirs, mine))
    at_top = lax.axis_index("lat") == n_lat - 1
    hinge = partner_ref[0]
    within = hinge - (hinge // cols) * cols

    def extra(kind, c):
        found = []
        for part in halves:
            line = jnp.concatenate(
                [part[2 * kind : 2 * kind + 1, 2 * wide :], part[2 * kind + 1 : 2 * kind + 2, 2 * wide :]], axis=1
            )
            found.append(line[:, c * half_cols : (c + 1) * half_cols])
        return jnp.concatenate(found, axis=1)

    flux, flux_south, flux_north, flux_west, flux_east = [], [], [], [], []
    sub8 = iota((DEEP, LANES), 0)
    lane8 = iota((DEEP, LANES), 1)
    crossed = jnp.zeros((DEEP, 2 * cols), F32)
    for c in range(3):
        pair = jnp.concatenate([extra(2, c), extra(1, c)], axis=1)
        crossed = jnp.where(iota(crossed.shape, 0) == c, pair, crossed)
    crossed = mirrored(pltpu.roll(crossed, 2 * cols - 1 - within, 1), cols)
    row, lane = iota((rows, LANES), 0), iota((rows, LANES), 1)
    for c in range(3):
        bands = [
            jnp.concatenate([part[:, b * wide + c * half_cols : b * wide + (c + 1) * half_cols] for part in halves], axis=1)
            for b in range(2)
        ]
        flux.append(jnp.concatenate(bands, axis=0))
        flux_south.append(extra(0, c))
        flux_north.append(jnp.where(at_top, crossed[c : c + 1, :], extra(1, c)))
        here = lane == c * 16 + row
        for side, part in ((flux_west, halves[1]), (flux_east, halves[0])):
            line = part[6:7, 2 * wide : 2 * wide + LANES]
            side.append(jnp.sum(jnp.where(here, line, 0.0), axis=1, keepdims=True))

    turn = turn_column(turn_ref, rows)
    share_down = jnp.zeros((DEEP, LANES), F32)
    share_lanes = jnp.zeros((rows, LANES), F32)
    for k in range(DEEP):
        share_down = jnp.where(sub8 == k, share_ref[k], share_down)
        share_lanes = jnp.where((lane & 7) == k, share_ref[k], share_lanes)

    drive_ref[...] = jnp.zeros(drive_ref.shape, F32)
    drive_ref[0:rows, 0:cols] = buoyancy_of(flux[0], flux[1])

    ring_rows, ring_cols = [], []
    for side, source in ((0, flux_south), (1, flux_north)):
        taken = ring_rows_ref[side, 5] * share_down[:, 0:1]
        values = [ring_rows_ref[side, f] for f in range(2)]
        ring_rows.append(values + [ring_rows_ref[side, 2 + c] + taken * source[c] for c in range(3)])
        drive_ref[rows + side : rows + side + 1, 0:cols] = buoyancy_of(source[0], source[1])
    for side, source in ((0, flux_west), (1, flux_east)):
        found = ring_cols_ref[side]
        taken = lanes_between(found, WET, WET + 8) * share_lanes
        for c in range(3):
            found = found + roll(taken, 8 * (2 + c) - WET, 1) * source[c]
        ring_cols.append(found)
        drive_ref[0:rows, cols + side : cols + side + 1] = buoyancy_of(source[0], source[1])

    grid = [(r, j) for r in range(n_r) for j in range(n_j)]

    def cut(value, r, j):
        return value[r * DEEP : (r + 1) * DEEP, j * LANES : (j + 1) * LANES]

    zero = jnp.zeros((DEEP, LANES), F32)
    run = {at: (zero, zero) for at in grid}
    edge_cols = [edge_cols_ref[side] for side in range(2)]
    copies = []

    def column(value, r, n):
        return jnp.broadcast_to(value[r * DEEP : (r + 1) * DEEP, n : n + 1], (DEEP, LANES))

    for k in range(DEEP):
        wets, heats, grids = {}, {}, [[[None] * n_j for _ in range(n_r)] for _ in range(5)]
        for r, j in grid:
            at = tile(r, j, k, rows)
            wet = mask_ref[at].astype(F32)
            taken = wet * share_ref[k]
            wets[r, j] = wet
            heats[r, j] = [taken * cut(flux[c], r, j) for c in range(3)]
            for f in range(5):
                value = state_ref[(f, *at)]
                if j == 0:
                    value = jnp.where(lane8 == 0, column(edge_cols[0], r, f * DEEP + k), value)
                if j == n_j - 1:
                    value = jnp.where(lane8 == LANES - 1, column(edge_cols[1], r, f * DEEP + k), value)
                if r == 0:
                    value = jnp.where(sub8 == 0, edge_rows_ref[0, f, k : k + 1, at[1]], value)
                if r == n_r - 1:
                    value = jnp.where(sub8 == DEEP - 1, edge_rows_ref[1, f, k : k + 1, at[1]], value)
                if f >= 2:
                    value = value + heats[r, j][f - 2]
                grids[f][r][j] = value
        fields = [
            Tiles(
                grids[f],
                [column(ring_cols[0], r, f * DEEP + k) for r in range(n_r)],
                [column(ring_cols[1], r, f * DEEP + k) for r in range(n_r)],
                [ring_rows[0][f][k : k + 1, j * LANES : (j + 1) * LANES] for j in range(n_j)],
                [ring_rows[1][f][k : k + 1, j * LANES : (j + 1) * LANES] for j in range(n_j)],
            )
            for f in range(5)
        ]
        for r, j in grid:
            at = tile(r, j, k, rows)
            over_x, over_y = run[r, j]

            def pressed(x, y):
                run[r, j] = (over_x + x, over_y + y)
                return PRESS * (over_x + 0.5 * x), PRESS * (over_y + 0.5 * y)

            new = advanced(
                [field.grid[r][j] for field in fields],
                [field.around(r, j) for field in fields],
                wets[r, j],
                turn[r * DEEP : (r + 1) * DEEP, 0:1],
                pressed,
                heats[r, j],
            )
            for f in range(5):
                if f < 2:
                    flow_ref[(f, *at)] = new[f]
                else:
                    tracers_ref[(f - 2, *at)] = new[f]
        whole = pl.ds(k * rows, rows)
        copies.append(
            pltpu.make_async_copy(tracers_ref.at[:, whole, :], out_hbm.at[pl.ds(2, 3), whole, :], sem.at[k])
        )
        copies[-1].start()
    for copy in copies:
        copy.wait()


def last_kernel(out_in_hbm, flow_ref, mask_ref, sums_ref, drive_ref, out_hbm, moved_ref, sem):
    del out_in_hbm
    rows, cols = mask_ref.shape[0] // DEEP, mask_ref.shape[1]
    wide = cols + LANES
    above = sums_ref[:, 0:wide] + sums_ref[:, wide : 2 * wide] * drive_ref[...]
    east, west, north, south = around(
        above[0:rows, 0:cols],
        above[0:rows, cols : cols + 1],
        above[0:rows, cols + 1 : cols + 2],
        above[rows : rows + 1, 0:cols],
        above[rows + 1 : rows + 2, 0:cols],
    )
    push_x, push_y = (0.5 * PRESS) * (east - west), (0.5 * PRESS) * (north - south)
    copies = []
    for k in range(DEEP):
        whole = pl.ds(k * rows, rows)
        wet = mask_ref[whole, :].astype(F32)
        moved_ref[0, whole, :] = flow_ref[0, whole, :] - wet * push_x
        moved_ref[1, whole, :] = flow_ref[1, whole, :] - wet * push_y
        copies.append(pltpu.make_async_copy(moved_ref.at[:, whole, :], out_hbm.at[pl.ds(0, 2), whole, :], sem.at[k]))
        copies[-1].start()
    for copy in copies:
        copy.wait()


def body(n_lon, n_lat, state, mask, coriolis, penetration, flux_tiles, flux_owner, flux_row, fold_partner):
    fields, levels, rows, cols = state.shape
    flat_state = state.reshape(fields, levels * rows, cols)
    flat_mask = mask.reshape(levels * rows, cols)
    last = n_lat - 1

    keep, send, west, east, total = prepare(
        flat_state, flat_mask, flux_tiles, flux_owner, flux_row, fold_partner, n_lon, n_lat
    )

    stages = []
    for axis, size, least in (("lat", n_lat, 2), ("lon", n_lon, 1)):
        bit = size // 2
        while bit >= least:
            stages.append((axis, size, bit))
            bit //= 2
    got = lax.ppermute(send, "lat", [(i, i ^ 1) for i in range(n_lat)])
    prefix = lax.ppermute(total, "lev", [(0, 1)])

    def merged(keep, got):
        half = shape(keep.shape[0] // 2, keep.shape[1])
        return call(merge_kernel, (half, half), [VMEM] * 2, (keep, got), name="merge_flux")

    def passed_on(send, stage):
        axis, size, bit = stage
        return lax.ppermute(send, axis, [(i, i ^ bit) for i in range(size)])

    hinge_block = fold_partner[0] >> (cols.bit_length() - 1)
    keep = after(keep, (prefix, hinge_block))
    keep, send = merged(keep, got)
    got = passed_on(send, stages[0])

    message = shape(SLABS + 1, DEEP, cols)
    top = call(top_kernel, message, [VMEM] * 3, (flat_state, flat_mask, prefix), name="top_rows")
    top = after(top, send)

    def folded(block):
        def swap(rows_out):
            return tuple(
                lax.ppermute(
                    rows_out,
                    ("lon", "lat"),
                    [(a * n_lat + last, (block - more - a) % n_lon * n_lat + last) for a in range(n_lon)],
                )
                for more in (0, 1)
            )

        return swap

    first, second = lax.switch(hinge_block, [folded(block) for block in range(n_lon)], top)
    keep = after(keep, (first, second))
    keep, send = merged(keep, got)
    got = passed_on(send, stages[1])

    west, east = after((west, east), send)
    side = shape(rows + DEEP, LANES)
    west, east = call(
        functools.partial(columns_kernel, n_lat),
        (side, side),
        [VMEM] * 5 + [SMEM],
        (west, east, prefix, first, second, fold_partner),
        name="edge_columns",
    )
    from_west = lax.ppermute(east, "lon", [(i, (i + 1) % n_lon) for i in range(n_lon)])
    from_east = lax.ppermute(west, "lon", [((i + 1) % n_lon, i) for i in range(n_lon)])
    pair, cross = call(
        rows_kernel,
        (message, message),
        [VMEM, VMEM, VMEM, SMEM, VMEM, VMEM],
        (flat_state, flat_mask, prefix, coriolis, from_west, from_east),
        name="edge_rows",
    )
    from_pair = lax.ppermute(pair, "lat", [(i, i ^ 1) for i in range(n_lat)])
    from_cross = lax.ppermute(cross, "lat", [(i, i + 1 if i % 2 else i - 1) for i in range(1, last)])
    keep = after(keep, (pair, cross))
    for stage in stages[2:]:
        keep, send = merged(keep, got)
        got = passed_on(send, stage)

    near_state, near_mask = after((flat_state, flat_mask), send)
    new_state, inside = call(
        inside_kernel,
        (shape(fields, levels * rows, cols), shape(rows, 2 * cols)),
        [VMEM, VMEM, VMEM, SMEM, SMEM],
        (near_state, near_mask, prefix, coriolis, penetration),
        name="first_inside",
    )
    keep = after(keep, inside)
    mine = keep + got
    theirs = lax.ppermute(mine, "lev", [(0, 1), (1, 0)])

    inside = after(inside, mine)
    wide = cols + LANES
    *ring, sums = call(
        functools.partial(rim_kernel, n_lat),
        (
            shape(2, 6, DEEP, cols),
            shape(2, rows, LANES),
            shape(2, 5, DEEP, cols),
            shape(2, rows, LANES),
            shape(rows + DEEP, 2 * wide),
        ),
        [VMEM, VMEM, VMEM, SMEM, SMEM, SMEM] + [VMEM] * 9,
        (
            flat_state, flat_mask, prefix, coriolis, penetration, fold_partner, west, east, from_west, from_east, from_pair,
            from_cross, first, second, inside,
        ),
        [pltpu.VMEM((SLABS + 1, DEEP, cols), F32), pltpu.VMEM((SLABS + 1, DEEP, cols), F32)],
        name="first_rim",
    )
    sums = after(sums, theirs)
    sums = lax.ppermute(sums, "lev", [(0, 1)])

    out = jax.ShapeDtypeStruct(flat_state.shape, F32)
    result, flow, drive = call(
        functools.partial(second_kernel, n_lat),
        (out, shape(2, levels * rows, cols), shape(rows + DEEP, wide)),
        [VMEM] * 8 + [SMEM] * 3,
        (new_state, flat_mask, *ring, mine, theirs, coriolis, penetration, fold_partner),
        [pltpu.VMEM((3, levels * rows, cols), F32), pltpu.SemaphoreType.DMA((DEEP,))],
        name="second_substep",
        out_specs=(ANY, VMEM, VMEM),
    )
    result = call(
        last_kernel,
        out,
        [ANY] + [VMEM] * 4,
        (result, flow, flat_mask, sums, drive),
        [pltpu.VMEM((2, levels * rows, cols), F32), pltpu.SemaphoreType.DMA((DEEP,))],
        name="deeper_pressure",
        out_specs=ANY,
        aliases={0: 0},
    )
    return result.reshape(fields, levels, rows, cols)


def solution(mesh):
    n_lon, n_lat = mesh.shape["lon"], mesh.shape["lat"]
    assert mesh.shape["lev"] == 2 and n_lat % 2 == 0 and n_lon > 2
    return jax.shard_map(
        functools.partial(body, n_lon, n_lat),
        mesh=mesh,
        in_specs=(
            P(None, "lev", "lat", "lon"),
            P("lev", "lat", "lon"),
            P("lat"),
            P("lev"),
            P(("lon", "lat"), None, None),
            P(("lon", "lat"), None),
            P(("lon", "lat")),
            P(),
        ),
        out_specs=P(None, "lev", "lat", "lon"),
        check_vma=False,
    )
```

```python
import functools

import jax
import jax.numpy as jnp
from jax import lax
from jax.experimental import pallas as pl
from jax.experimental.pallas import tpu as pltpu
from jax.sharding import PartitionSpec as P

ALPHA = 0.2
BETA = 0.15
PRESS = 0.1
VISCOUS = 0.1
DIFFUSE = 0.1
ADVECT = 0.1

F32 = jnp.float32
I32 = jnp.int32
LANES = 128
DEEP = 8
FAR = 64
WET = 48
ABOVE = 56
SLABS = 11
CORNERS = SLABS
VMEM_BYTES = 24 * 1024 * 1024

VMEM = pl.BlockSpec(memory_space=pltpu.VMEM)
SMEM = pl.BlockSpec(memory_space=pltpu.SMEM)
ANY = pl.BlockSpec(memory_space=pl.ANY)
HBM = pl.BlockSpec(memory_space=pltpu.HBM)


def iota(shape, dim):
    return lax.broadcasted_iota(I32, shape, dim)


def roll(value, shift, axis):
    return pltpu.roll(value, shift % value.shape[axis], axis)


def call(kernel, out_shape, in_specs, args, scratch=(), name=None, out_specs=None, aliases=None):
    return pl.pallas_call(
        kernel,
        out_shape=out_shape,
        in_specs=in_specs,
        out_specs=out_specs or jax.tree.map(lambda _: VMEM, out_shape),
        input_output_aliases=aliases or {},
        scratch_shapes=list(scratch),
        compiler_params=pltpu.CompilerParams(vmem_limit_bytes=VMEM_BYTES),
        name=name,
    )(*args)


def after(values, *others):
    return lax.optimization_barrier((values, others))[0]


def shape(*dims):
    return pltpu.VMEM(dims, F32)


def in_hbm(*arrays):
    return tuple(pltpu.with_memory_space_constraint(array, pltpu.HBM) for array in arrays)


def prepare_kernel(
    n_lon, n_lat, state_hbm, mask_hbm, tiles_hbm, owner_hbm, row_hbm, partner_hbm, keep_ref, send_ref, west_ref, east_ref,
    total_ref, state_ref, mask_ref, x_ref, owners_ref, rows_ref, hinge_ref, sem,
):
    tiles, cols = tiles_hbm.shape[1], tiles_hbm.shape[2]
    half_cols = cols // 2
    rows = 2 * DEEP
    n_y = n_lat // 2
    half = lax.axis_index("lev")
    lat = lax.axis_index("lat")
    core = lax.rem(lat, 2)
    begin = pl.multiple_of(half * half_cols, LANES)
    indices = [
        pltpu.make_async_copy(owner_hbm, owners_ref, sem.at[0]),
        pltpu.make_async_copy(row_hbm, rows_ref, sem.at[1]),
        pltpu.make_async_copy(partner_hbm, hinge_ref, sem.at[2]),
    ]
    fluxes = [
        pltpu.make_async_copy(
            tiles_hbm.at[c, :, pl.ds(begin, half_cols)], x_ref.at[:, pl.ds(c * half_cols, half_cols)], sem.at[3 + c]
        )
        for c in range(3)
    ]
    fields = [
        pltpu.make_async_copy(state_hbm, state_ref, sem.at[6]),
        pltpu.make_async_copy(mask_hbm, mask_ref, sem.at[7]),
    ]
    for copy in indices + fluxes + fields:
        copy.start()
    for copy in indices:
        copy.wait()

    key = owners_ref[...] * rows + rows_ref[...]
    hinge_block = hinge_ref[0] // cols
    slots = keep_ref.shape[0]
    slot = iota((slots, tiles), 0)
    group, sub = slot >> 3, slot & 7
    at_y = (group >> (n_lon.bit_length() - 1)) ^ (lat // 2)
    at_lon = (group & (n_lon - 1)) ^ lax.axis_index("lon")

    def wrapped(lon):
        return jnp.where(lon < 0, lon + n_lon, jnp.where(lon >= n_lon, lon - n_lon, lon))

    def one_hot(hit):
        return jnp.where(hit, 1.0, 0.0).astype(jnp.bfloat16)

    def weights(to_core):
        lat = 2 * at_y + to_core
        owner = at_lon * n_lat + lat
        last = lat == n_lat - 1
        top = n_lat * rows - 1
        south = jnp.where(lat == 0, owner * rows, owner * rows - 1)
        north = jnp.where(last, wrapped(hinge_block - at_lon) * (n_lat * rows) + top, (owner + 1) * rows)
        third = jnp.where(last, wrapped(hinge_block - at_lon - 1) * (n_lat * rows) + top, -1)
        kind = sub >> 1
        extra_key = jnp.where(kind == 0, south, jnp.where(kind == 1, north, jnp.where(kind == 2, third, -1)))
        extra = key == extra_key
        beside = wrapped(at_lon + 1 - 2 * half) * n_lat + lat
        return (
            one_hot(key == owner * rows + sub),
            one_hot(key == owner * rows + DEEP + sub),
            one_hot(extra & ((sub & 1) == 0)),
            one_hot(extra & ((sub & 1) == 1)),
            one_hot(((key >> 4) == beside) & (sub == 6)),
        )

    def split(x):
        first = x.astype(jnp.bfloat16)
        rest = x - first.astype(F32)
        second = rest.astype(jnp.bfloat16)
        third = (rest - second.astype(F32)).astype(jnp.bfloat16)
        return first, second, third

    square = iota((tiles, tiles), 0) == iota((tiles, tiles), 1)
    row_of = jnp.sum(jnp.where(square, (key & (rows - 1)).astype(F32), 0.0), axis=1, keepdims=True).astype(I32)

    for copy in fluxes:
        copy.wait()
    x = x_ref[...]
    lane = iota((tiles, LANES), 1)
    edge = jnp.zeros((tiles, LANES), F32)
    for c in range(3):
        begin = c * half_cols
        value = jnp.where(half == 0, x[:, begin : begin + 1], x[:, begin + half_cols - 1 : begin + half_cols])
        edge = jnp.where(((lane >> 4) == c) & ((lane & 15) == row_of), value, edge)
    parts, edges = split(x), split(edge)
    wide = 3 * half_cols
    quarter = wide // 2

    def dot(hot, terms, begin, end):
        products = [
            jnp.dot(hot, term[:, begin:end], preferred_element_type=F32) for term in reversed(terms)
        ]
        return products[0] + products[1] + products[2]

    for out_ref, to_core in ((keep_ref, core), (send_ref, 1 - core)):
        low, high, even, odd, ring = weights(to_core)
        out_ref[:, 0:wide] = dot(low, parts, 0, wide)
        out_ref[:, wide : 2 * wide] = dot(high, parts, 0, wide)
        rest = dot(even, parts, 0, quarter) + dot(odd, parts, quarter, wide)
        beside = dot(ring, edges, 0, LANES)
        out_ref[:, 2 * wide : 2 * wide + LANES] = rest[:, 0:LANES] + beside
        out_ref[:, 2 * wide + LANES :] = rest[:, LANES:]

    for copy in fields:
        copy.wait()
    total = jnp.zeros(total_ref.shape, F32)
    for k in range(DEEP):
        at = slice(k * rows, (k + 1) * rows)
        total = total + buoyancy_of(state_ref[2, at, :], state_ref[3, at, :])
    total_ref[...] = total
    edge_columns(state_ref, mask_ref, west_ref, east_ref)


def merge_kernel(kept_ref, got_ref, keep_ref, send_ref):
    half = keep_ref.shape[0]
    send_ref[...] = kept_ref[half:, :] + got_ref[half:, :]
    keep_ref[...] = kept_ref[0:half, :] + got_ref[0:half, :]


def prepare(state, mask, flux_tiles, flux_owner, flux_row, fold_partner, n_lon, n_lat):
    tiles, _, cols = flux_tiles.shape
    wide = 3 * (cols // 2)
    slots = shape(n_lon * n_lat // 2 * DEEP, 2 * wide + wide // 2)
    side = shape(2 * DEEP, LANES)
    return call(
        functools.partial(prepare_kernel, n_lon, n_lat),
        (slots, slots, side, side, shape(2 * DEEP, cols)),
        [HBM] * 6,
        in_hbm(
            state,
            mask,
            flux_tiles.transpose(1, 0, 2),
            flux_owner.reshape(1, tiles),
            flux_row.reshape(1, tiles),
            fold_partner,
        ),
        [
            pltpu.VMEM(state.shape, F32),
            pltpu.VMEM(mask.shape, I32),
            pltpu.VMEM((tiles, wide), F32),
            pltpu.VMEM((1, tiles), I32),
            pltpu.VMEM((1, tiles), I32),
            pltpu.SMEM(fold_partner.shape, I32),
            pltpu.SemaphoreType.DMA((8,)),
        ],
        name="prepare",
    )


def level_rows(ref, row, rows):
    return jnp.concatenate([ref[k * rows + row : k * rows + row + 1, :] for k in range(DEEP)], axis=0)


def buoyancy_of(temper, saline):
    return ALPHA * temper - BETA * saline


def edge_rows(state_ref, mask_ref, out_ref, rows, near, far):
    for f in range(5):
        out_ref[2 * f] = level_rows(state_ref.at[f], near, rows)
        out_ref[2 * f + 1] = level_rows(state_ref.at[f], far, rows)
    out_ref[10] = level_rows(mask_ref, near, rows).astype(F32)


def edge_columns(state_ref, mask_ref, west_ref, east_ref):
    rows, cols = west_ref.shape[0], state_ref.shape[2]
    lane = iota((rows, LANES), 1)
    last = slice(cols - LANES, cols)
    west = jnp.zeros((rows, LANES), F32)
    east = jnp.zeros((rows, LANES), F32)
    for k in range(DEEP):
        at = slice(k * rows, (k + 1) * rows)
        for f in range(5):
            to = f * DEEP + k
            left, right = state_ref[f, at, 0:LANES], state_ref[f, at, last]
            west = jnp.where(lane == to, roll(left, to, 1), west)
            west = jnp.where(lane == FAR + to, roll(left, FAR + to - 1, 1), west)
            east = jnp.where(lane == to, roll(right, to + 1, 1), east)
            east = jnp.where(lane == FAR + to, roll(right, FAR + to + 2, 1), east)
        west = jnp.where(lane == WET + k, roll(mask_ref[at, 0:LANES].astype(F32), WET + k, 1), west)
        east = jnp.where(lane == WET + k, roll(mask_ref[at, last].astype(F32), WET + k + 1, 1), east)
    west_ref[...] = west
    east_ref[...] = east


def top_kernel(state_ref, mask_ref, prefix_ref, top_ref):
    rows, cols = prefix_ref.shape
    for slab in range(SLABS):
        if slab < 10:
            line = level_rows(state_ref.at[slab // 2], rows - 1 - slab % 2, rows)
        else:
            line = level_rows(mask_ref, rows - 1, rows).astype(F32)
        for piece in range(cols // LANES):
            top_ref[piece, slab] = line[:, piece * LANES : (piece + 1) * LANES]
    top_ref[:, CORNERS] = jnp.zeros((cols // LANES, DEEP, LANES), F32)
    for n in (1, 2):
        for piece in range(cols // LANES):
            top_ref[piece, CORNERS, 2 + n : 3 + n, :] = prefix_ref[rows - n : rows - n + 1, piece * LANES : (piece + 1) * LANES]


def columns_kernel(n_lat, west_ref, east_ref, prefix_ref, fold_ref, partner_ref, west_out_ref, east_out_ref):
    rows, cols = prefix_ref.shape
    lane = iota((rows, LANES), 1)
    for side, in_ref, out_ref in ((0, west_ref, west_out_ref), (1, east_ref, east_out_ref)):
        near, far = (0, 1) if side == 0 else (cols - 1, cols - 2)
        value = jnp.where(lane == ABOVE, prefix_ref[:, near : near + 1], in_ref[...])
        out_ref[0:rows, :] = jnp.where(lane == FAR + ABOVE, prefix_ref[:, far : far + 1], value)
        out_ref[rows:, :] = jnp.zeros((DEEP, LANES), F32)

    @pl.when(lax.axis_index("lat") == n_lat - 1)
    def _():
        within = partner_ref[0] & (LANES - 1)
        sub8, lane8 = iota((DEEP, LANES), 0), iota((DEEP, LANES), 1)
        col = iota((DEEP, cols + LANES), 1)
        for place, out_ref in ((cols + within, west_out_ref), (within + 1, east_out_ref)):
            line = jnp.zeros((DEEP, LANES), F32)
            for slab in (0, 2, 4, 6, 8, CORNERS):
                line_there = jnp.concatenate([fold_ref[piece, slab] for piece in range(fold_ref.shape[0])], axis=1)
                cell = jnp.sum(jnp.where(col == place, line_there, 0.0), axis=1, keepdims=True)
                here = (lane8 == ABOVE) & (sub8 == 3) if slab == CORNERS else lane8 == (slab // 2) * DEEP + sub8
                line = jnp.where(here, -cell if slab < 4 else cell, line)
            out_ref[rows : rows + 1, :] = jnp.sum(line, axis=0, keepdims=True)


def corner_slab(out_ref, prefix_ref, turn_ref, from_west_ref, from_east_ref, near, far):
    out_ref[CORNERS] = jnp.full(out_ref.shape[1:], turn_ref[near], F32)
    out_ref[CORNERS, 0:1, 0:LANES] = from_west_ref[near : near + 1, :]
    out_ref[CORNERS, 1:2, 0:LANES] = from_east_ref[near : near + 1, :]
    out_ref[CORNERS, 3:4, :] = prefix_ref[near : near + 1, :]
    out_ref[CORNERS, 4:5, :] = prefix_ref[far : far + 1, :]


def rows_kernel(state_ref, mask_ref, prefix_ref, turn_ref, from_west_ref, from_east_ref, pair_ref, cross_ref):
    rows = prefix_ref.shape[0]
    odd = lax.rem(lax.axis_index("lat"), 2) == 1

    def fill(out_ref, near, far):
        edge_rows(state_ref, mask_ref, out_ref, rows, near, far)
        corner_slab(out_ref, prefix_ref, turn_ref, from_west_ref, from_east_ref, near, far)

    @pl.when(odd)
    def _():
        fill(pair_ref, 0, 1)
        fill(cross_ref, rows - 1, rows - 2)

    @pl.when(jnp.logical_not(odd))
    def _():
        fill(pair_ref, rows - 1, rows - 2)
        fill(cross_ref, 0, 1)


def around(value, west, east, south, north):
    rows, cols = value.shape
    row, col = iota((rows, cols), 0), iota((rows, cols), 1)
    return (
        jnp.where(col == cols - 1, east, roll(value, -1, 1)),
        jnp.where(col == 0, west, roll(value, 1, 1)),
        jnp.where(row == rows - 1, north, roll(value, -1, 0)),
        jnp.where(row == 0, south, roll(value, 1, 0)),
    )


def advanced(values, sides, wet, turn, pressed, heat=None):
    zonal, merid = values[0], values[1]
    sums = [(e + w) + (n + s) for e, w, n, s in sides]
    across = [(e - w, n - s) for e, w, n, s in sides]
    press_x, press_y = pressed(
        0.5 * buoyancy_of(across[2][0], across[3][0]), 0.5 * buoyancy_of(across[2][1], across[3][1])
    )
    out = []
    carry_x, carry_y = (0.5 * ADVECT) * zonal, (0.5 * ADVECT) * merid
    for f in range(5):
        spread = (VISCOUS if f < 2 else DIFFUSE) * (sums[f] - 4.0 * values[f])
        if f == 0:
            trend = spread + (turn * merid - press_x)
        elif f == 1:
            trend = spread - (turn * zonal + press_y)
        else:
            trend = spread - (carry_x * across[f][0] + carry_y * across[f][1])
        new = values[f] + wet * trend
        out.append(new if heat is None or f < 2 else new + heat[f - 2])
    return out


class Tiles:
    def __init__(self, grid, west=None, east=None, south=None, north=None):
        self.grid, self.ghosts, self.turned = grid, (west, east, south, north), {}
        self.lane, self.sub = iota((DEEP, LANES), 1), iota((DEEP, LANES), 0)

    def rolled(self, r, j, shift, axis):
        at = (r, j, shift, axis)
        if at not in self.turned:
            self.turned[at] = roll(self.grid[r][j], shift, axis)
        return self.turned[at]

    def side(self, r, j, shift, axis):
        here = self.rolled(r, j, shift, axis)
        r_from, j_from = (r, j - shift) if axis else (r - shift, j)
        edge = (0 if shift == 1 else LANES - 1) if axis else (0 if shift == 1 else DEEP - 1)
        if 0 <= r_from < len(self.grid) and 0 <= j_from < len(self.grid[0]):
            other = self.rolled(r_from, j_from, shift, axis)
        else:
            ghost = self.ghosts[(0 if shift == 1 else 1) + (0 if axis else 2)]
            if ghost is None:
                return here
            other = ghost[r if axis else j]
        return jnp.where((self.lane if axis else self.sub) == edge, other, here)

    def around(self, r, j):
        return self.side(r, j, -1, 1), self.side(r, j, 1, 1), self.side(r, j, -1, 0), self.side(r, j, 1, 0)


def tile(r, j, k, rows):
    return slice(k * rows + r * DEEP, k * rows + (r + 1) * DEEP), slice(j * LANES, (j + 1) * LANES)


def turn_column(turn_ref, rows):
    row = iota((rows, LANES), 0)
    column = jnp.zeros((rows, LANES), F32)
    for j in range(rows):
        column = jnp.where(row == j, turn_ref[j], column)
    return column


def mirrored(value, width):
    back = LANES - 1 - iota((value.shape[0], LANES), 1)
    blocks = [
        jnp.take_along_axis(value[:, begin : begin + LANES], back, axis=1)
        for begin in range(width - LANES, -1, -LANES)
    ]
    return jnp.concatenate(blocks, axis=1)


def scan_down(value):
    row = iota(value.shape, 0)
    for step in (1, 2, 4):
        value = value + jnp.where(row >= step, roll(value, step, 0), 0.0)
    return value


def scan_lanes(value):
    lane = iota(value.shape, 1) & 7
    for step in (1, 2, 4):
        value = value + jnp.where(lane >= step, roll(value, step, 1), 0.0)
    return value


def lanes_between(value, begin, end):
    lane = iota(value.shape, 1)
    return jnp.where((lane >= begin) & (lane < end), value, 0.0)


def buoyancy_sum(column):
    here = lanes_between(buoyancy_of(roll(column, -16, 1), roll(column, -24, 1)), 0, 8)
    return jnp.sum(here, axis=1, keepdims=True)


def inside_kernel(state_ref, mask_ref, prefix_ref, turn_ref, share_ref, new_ref, sums_ref):
    rows, cols = prefix_ref.shape
    n_r, n_j = rows // DEEP, cols // LANES
    turn = turn_column(turn_ref, rows)
    grid = [(r, j) for r in range(n_r) for j in range(n_j)]
    zero = jnp.zeros((DEEP, LANES), F32)
    prefix = Tiles([[prefix_ref[tile(r, j, 0, rows)] for j in range(n_j)] for r in range(n_r)])
    run = {}
    for at in grid:
        east, west, north, south = prefix.around(*at)
        run[at] = [0.5 * (east - west), 0.5 * (north - south), zero, zero]
    for k in range(DEEP):
        fields = [Tiles([[state_ref[(f, *tile(r, j, k, rows))] for j in range(n_j)] for r in range(n_r)]) for f in range(5)]
        for r, j in grid:
            at = tile(r, j, k, rows)
            above_x, above_y, total, absorbed = run[r, j]
            slopes = []

            def pressed(x, y):
                slopes.extend((x, y))
                return PRESS * (above_x + 0.5 * x), PRESS * (above_y + 0.5 * y)

            values = [field.grid[r][j] for field in fields]
            wet = mask_ref[at].astype(F32)
            new = advanced(
                values, [field.around(r, j) for field in fields], wet, turn[r * DEEP : (r + 1) * DEEP, 0:1], pressed
            )
            for f in range(5):
                new_ref[(f, *at)] = new[f]
            run[r, j] = [
                above_x + slopes[0],
                above_y + slopes[1],
                total + buoyancy_of(new[2], new[3]),
                absorbed + wet * share_ref[k],
            ]
    for r, j in grid:
        for kind in range(2):
            at = slice(kind * cols + j * LANES, kind * cols + (j + 1) * LANES)
            sums_ref[r * DEEP : (r + 1) * DEEP, at] = run[r, j][2 + kind]


def rim_kernel(
    n_lat, state_ref, mask_ref, prefix_ref, turn_ref, share_ref, partner_ref, own_west_ref, own_east_ref,
    from_west_ref, from_east_ref, pair_ref, cross_ref, fold_ref, inside_ref, ring_rows_ref, ring_cols_ref,
    edge_rows_ref, edge_cols_ref, sums_ref, south_ref, north_ref,
):
    rows, cols = prefix_ref.shape
    lat = lax.axis_index("lat")
    odd = lax.rem(lat, 2) == 1
    within = partner_ref[0] & (LANES - 1)
    at_top = lat == n_lat - 1

    @pl.when(odd)
    def _():
        south_ref[...] = pair_ref[...]

    @pl.when(jnp.logical_not(odd))
    def _():
        north_ref[...] = pair_ref[...]

    @pl.when(jnp.logical_not(odd) & (lat > 0))
    def _():
        south_ref[...] = cross_ref[...]

    @pl.when(odd & (lat < n_lat - 1))
    def _():
        north_ref[...] = cross_ref[...]

    @pl.when(lat == 0)
    def _():
        edge_rows(state_ref, mask_ref, south_ref, rows, 0, 0)
        corner_slab(south_ref, prefix_ref, turn_ref, from_west_ref, from_east_ref, 0, 0)

    sub8, lane8 = iota((DEEP, LANES), 0), iota((DEEP, LANES), 1)

    @pl.when(at_top)
    def _():
        for slab in range(SLABS + 1):
            row = jnp.concatenate([fold_ref[piece, slab] for piece in range(fold_ref.shape[0])], axis=1)
            row = pltpu.roll(row, cols + LANES - 1 - within, 1)
            if slab < 4:
                row = -row
            north_ref[slab] = mirrored(row, cols)
        north_ref[CORNERS, 0:1, 0:LANES] = from_west_ref[rows : rows + 1, :]
        north_ref[CORNERS, 1:2, 0:LANES] = from_east_ref[rows : rows + 1, :]
        north_ref[CORNERS, 2:3, :] = jnp.full((1, cols), turn_ref[rows - 1], F32)

    wide = cols + LANES
    sums_ref[rows:, :] = jnp.zeros((DEEP, 2 * wide), F32)
    for kind in range(2):
        sums_ref[0:rows, kind * wide : kind * wide + cols] = inside_ref[:, kind * cols : (kind + 1) * cols]

    share_down = jnp.zeros((DEEP, LANES), F32)
    for k in range(DEEP):
        share_down = jnp.where(sub8 == k, share_ref[k], share_down)

    def down(line, f):
        return jnp.sum(jnp.where(lane8 == f * DEEP + sub8, line, 0.0), axis=1, keepdims=True)

    def row_step(near, south, north, west_line, east_line, wet, turn, above, above_south, above_north):
        col = iota((DEEP, cols), 1)
        sides = [
            (
                jnp.where(col == cols - 1, down(east_line, f), roll(near[f], -1, 1)),
                jnp.where(col == 0, down(west_line, f), roll(near[f], 1, 1)),
                north[f],
                south[f],
            )
            for f in range(5)
        ]
        east = jnp.where(col[0:1] == cols - 1, east_line[:, ABOVE : ABOVE + 1], roll(above, -1, 1))
        west = jnp.where(col[0:1] == 0, west_line[:, ABOVE : ABOVE + 1], roll(above, 1, 1))
        above_x, above_y = 0.5 * (east - west), 0.5 * (above_north - above_south)

        def pressed(x, y):
            return PRESS * (above_x + scan_down(x) - 0.5 * x), PRESS * (above_y + scan_down(y) - 0.5 * y)

        return advanced(near, sides, wet, turn, pressed)

    for side, ghost_ref, edge, inner in ((0, south_ref, 0, 1), (1, north_ref, rows - 1, rows - 2)):
        near = [ghost_ref[2 * f] for f in range(5)]
        far = [ghost_ref[2 * f + 1] for f in range(5)]
        own = [level_rows(state_ref.at[f], edge, rows) for f in range(5)]
        own_next = [level_rows(state_ref.at[f], inner, rows) for f in range(5)]
        ring_wet = ghost_ref[10]
        corners = ghost_ref[CORNERS, :, 0:LANES]
        above_near, above_far = ghost_ref[CORNERS, 3:4, :], ghost_ref[CORNERS, 4:5, :]
        above_own, above_next = prefix_ref[edge : edge + 1, :], prefix_ref[inner : inner + 1, :]
        outward, inward = (far, above_far), (own, above_own)
        (south, above_south), (north, above_north) = (outward, inward) if side == 0 else (inward, outward)
        ring = row_step(
            near, south, north, corners[0:1, :], corners[1:2, :], ring_wet, corners[2:3, 0:1], above_near, above_south, above_north
        )
        outward, inward = (near, above_near), (own_next, above_next)
        (south, above_south), (north, above_north) = (outward, inward) if side == 0 else (inward, outward)
        wet = level_rows(mask_ref, edge, rows).astype(F32)
        edge_line = slice(edge, edge + 1)
        new = row_step(
            own, south, north, from_west_ref[edge_line, :], from_east_ref[edge_line, :], wet, turn_ref[edge],
            above_own, above_south, above_north,
        )
        for f in range(5):
            edge_rows_ref[side, f] = new[f]
            ring_rows_ref[side, f] = jnp.where(lat == 0, new[f], ring[f]) if side == 0 else ring[f]
        ring_rows_ref[side, 5] = ring_wet
        at = slice(rows + side, rows + side + 1)
        here = buoyancy_of(ring_rows_ref[side, 2], ring_rows_ref[side, 3])
        sums_ref[at, 0:cols] = jnp.sum(here, axis=0, keepdims=True)
        sums_ref[at, wide : wide + cols] = jnp.sum(ring_wet * share_down[:, 0:1], axis=0, keepdims=True)

    row, lane = iota((rows, LANES), 0), iota((rows, LANES), 1)
    turn = turn_column(turn_ref, rows)
    share_lanes = jnp.zeros((rows, LANES), F32)
    for k in range(DEEP):
        share_lanes = jnp.where((lane & 7) == k, share_ref[k], share_lanes)

    def column_step(near, east, west, north, south):
        dx, dy = 0.5 * (east - west), 0.5 * (north - south)
        lap = (east + west) + (north + south) - 4.0 * near
        zonal, merid = lanes_between(near, 0, 8), lanes_between(near, 8, 16)
        wet = lanes_between(near, WET, WET + 8)
        wet_all = sum(roll(wet, -8 * n, 1) for n in range(2, 7))
        zonal_all = sum(roll(zonal, 8 * n, 1) for n in (2, 3, 4))
        merid_all = sum(roll(merid, 8 * n, 1) for n in (1, 2, 3))
        bx = lanes_between(buoyancy_of(roll(dx, -16, 1), roll(dx, -24, 1)), 0, 8)
        by = lanes_between(buoyancy_of(roll(dy, -8, 1), roll(dy, -16, 1)), 8, 16)
        press_x = lanes_between(PRESS * (dx[:, ABOVE : ABOVE + 1] + scan_lanes(bx) - 0.5 * bx), 0, 8)
        press_y = lanes_between(PRESS * (dy[:, ABOVE : ABOVE + 1] + scan_lanes(by) - 0.5 * by), 8, 16)
        trend = VISCOUS * lap - ADVECT * (zonal_all * dx + merid_all * dy) - press_x - press_y
        trend = trend + lanes_between(turn * roll(near, -8, 1), 0, 8) - lanes_between(turn * roll(near, 8, 1), 8, 16)
        return near + wet_all * trend, wet

    blocks = [jnp.zeros((rows, LANES), F32)] * 2
    sides = ((0, from_west_ref, own_west_ref), (1, from_east_ref, own_east_ref))
    for side, ghost_ref, own_ref in sides:
        near, own = ghost_ref[0:rows, :], own_ref[0:rows, :]
        far, own_next = roll(near, -FAR, 1), roll(own, -FAR, 1)
        north = jnp.where(row == rows - 1, north_ref[CORNERS, side : side + 1, 0:LANES], roll(near, -1, 0))
        south = jnp.where(row == 0, south_ref[CORNERS, side : side + 1, 0:LANES], roll(near, 1, 0))
        east, west = (own, far) if side == 0 else (far, own)
        new, wet = column_step(near, east, west, north, south)
        ring_cols_ref[side] = new
        blocks[0] = jnp.where(lane == side, buoyancy_sum(new), blocks[0])
        blocks[1] = jnp.where(lane == side, jnp.sum(wet * share_lanes, axis=1, keepdims=True), blocks[1])
        east, west = (own_next, near) if side == 0 else (near, own_next)
        new, _ = column_step(own, east, west, roll(own, -1, 0), roll(own, 1, 0))
        edge_cols_ref[side] = new
        column = 0 if side == 0 else cols - 1
        sums_ref[0:rows, column : column + 1] = buoyancy_sum(new)
    for kind in range(2):
        sums_ref[0:rows, kind * wide + cols : (kind + 1) * wide] = blocks[kind]
    for side, edge in ((0, 0), (1, rows - 1)):
        here = buoyancy_of(edge_rows_ref[side, 2], edge_rows_ref[side, 3])
        sums_ref[edge : edge + 1, 0:cols] = jnp.sum(here, axis=0, keepdims=True)


def flux_kernel(n_lat, sums_ref, mine_ref, theirs_ref, partner_ref, flux_ref, flux_rows_ref, flux_cols_ref, above_ref):
    rows, cols = flux_ref.shape[1:]
    half_cols = cols // 2
    wide = 3 * half_cols
    mine, theirs = mine_ref[...], theirs_ref[...]
    first = lax.axis_index("lev") == 0
    halves = (jnp.where(first, mine, theirs), jnp.where(first, theirs, mine))
    at_top = lax.axis_index("lat") == n_lat - 1
    hinge = partner_ref[0]
    within = hinge - (hinge // cols) * cols

    def extra(kind, c):
        found = []
        for part in halves:
            line = jnp.concatenate(
                [part[2 * kind : 2 * kind + 1, 2 * wide :], part[2 * kind + 1 : 2 * kind + 2, 2 * wide :]], axis=1
            )
            found.append(line[:, c * half_cols : (c + 1) * half_cols])
        return jnp.concatenate(found, axis=1)

    flux, flux_south, flux_north, flux_west, flux_east = [], [], [], [], []
    crossed = jnp.zeros((DEEP, 2 * cols), F32)
    for c in range(3):
        pair = jnp.concatenate([extra(2, c), extra(1, c)], axis=1)
        crossed = jnp.where(iota(crossed.shape, 0) == c, pair, crossed)
    crossed = mirrored(pltpu.roll(crossed, 2 * cols - 1 - within, 1), cols)
    row, lane = iota((rows, LANES), 0), iota((rows, LANES), 1)
    for c in range(3):
        bands = [
            jnp.concatenate([part[:, b * wide + c * half_cols : b * wide + (c + 1) * half_cols] for part in halves], axis=1)
            for b in range(2)
        ]
        flux.append(jnp.concatenate(bands, axis=0))
        flux_south.append(extra(0, c))
        flux_north.append(jnp.where(at_top, crossed[c : c + 1, :], extra(1, c)))
        here = lane == c * 16 + row
        for side, part in ((flux_west, halves[1]), (flux_east, halves[0])):
            line = part[6:7, 2 * wide : 2 * wide + LANES]
            side.append(jnp.sum(jnp.where(here, line, 0.0), axis=1, keepdims=True))

    flux_cols = jnp.zeros((rows, LANES), F32)
    for c in range(3):
        flux_ref[c] = flux[c]
        flux_rows_ref[c : c + 1, :] = flux_south[c]
        flux_rows_ref[3 + c : 4 + c, :] = flux_north[c]
        flux_cols = jnp.where(lane == c, flux_west[c], jnp.where(lane == 3 + c, flux_east[c], flux_cols))
    flux_rows_ref[6:8, :] = jnp.zeros((2, cols), F32)
    flux_cols_ref[...] = flux_cols
    reach = cols + LANES
    above_ref[rows:, :] = jnp.zeros((DEEP, reach), F32)
    above_ref[0:rows, 0:cols] = sums_ref[0:rows, 0:cols] + sums_ref[0:rows, reach : reach + cols] * buoyancy_of(flux[0], flux[1])
    ends = jnp.zeros((rows, LANES), F32)
    for side, column, line in ((0, (flux_west[0], flux_west[1]), flux_south), (1, (flux_east[0], flux_east[1]), flux_north)):
        at = slice(rows + side, rows + side + 1)
        above_ref[at, 0:cols] = sums_ref[at, 0:cols] + sums_ref[at, reach : reach + cols] * buoyancy_of(line[0], line[1])
        before, taken = sums_ref[0:rows, cols:reach], sums_ref[0:rows, reach + cols :]
        ends = jnp.where(lane == side, before + taken * buoyancy_of(*column), ends)
    above_ref[0:rows, cols:reach] = ends


def second_kernel(
    state_ref, mask_ref, ring_rows_ref, ring_cols_ref, edge_rows_ref, edge_cols_ref, flux_ref, flux_rows_ref,
    flux_cols_ref, turn_ref, share_ref, out_hbm, flow_ref, tracers_ref, sem,
):
    rows, cols = flux_ref.shape[1:]
    n_r, n_j = rows // DEEP, cols // LANES
    sub8, lane8 = iota((DEEP, LANES), 0), iota((DEEP, LANES), 1)
    lane = iota((rows, LANES), 1)
    turn = turn_column(turn_ref, rows)
    share_down = jnp.zeros((DEEP, LANES), F32)
    share_lanes = jnp.zeros((rows, LANES), F32)
    for k in range(DEEP):
        share_down = jnp.where(sub8 == k, share_ref[k], share_down)
        share_lanes = jnp.where((lane & 7) == k, share_ref[k], share_lanes)

    ring_rows, ring_cols = [], []
    for side in range(2):
        taken = ring_rows_ref[side, 5] * share_down[:, 0:1]
        values = [ring_rows_ref[side, f] for f in range(2)]
        values += [ring_rows_ref[side, 2 + c] + taken * flux_rows_ref[3 * side + c : 3 * side + c + 1, :] for c in range(3)]
        ring_rows.append(values)
        found = ring_cols_ref[side]
        taken = lanes_between(found, WET, WET + 8) * share_lanes
        for c in range(3):
            found = found + roll(taken, 8 * (2 + c) - WET, 1) * flux_cols_ref[:, 3 * side + c : 3 * side + c + 1]
        ring_cols.append(found)

    grid = [(r, j) for r in range(n_r) for j in range(n_j)]

    def cut(value, r, j):
        return value[r * DEEP : (r + 1) * DEEP, j * LANES : (j + 1) * LANES]

    zero = jnp.zeros((DEEP, LANES), F32)
    run = {at: (zero, zero) for at in grid}
    edge_cols = [edge_cols_ref[side] for side in range(2)]
    copies = []

    def column(value, r, n):
        return jnp.broadcast_to(value[r * DEEP : (r + 1) * DEEP, n : n + 1], (DEEP, LANES))

    for k in range(DEEP):
        wets, heats, grids = {}, {}, [[[None] * n_j for _ in range(n_r)] for _ in range(5)]
        for r, j in grid:
            at = tile(r, j, k, rows)
            wet = mask_ref[at].astype(F32)
            taken = wet * share_ref[k]
            wets[r, j] = wet
            heats[r, j] = [taken * cut(flux_ref[c], r, j) for c in range(3)]
            for f in range(5):
                value = state_ref[(f, *at)]
                if j == 0:
                    value = jnp.where(lane8 == 0, column(edge_cols[0], r, f * DEEP + k), value)
                if j == n_j - 1:
                    value = jnp.where(lane8 == LANES - 1, column(edge_cols[1], r, f * DEEP + k), value)
                if r == 0:
                    value = jnp.where(sub8 == 0, edge_rows_ref[0, f, k : k + 1, at[1]], value)
                if r == n_r - 1:
                    value = jnp.where(sub8 == DEEP - 1, edge_rows_ref[1, f, k : k + 1, at[1]], value)
                if f >= 2:
                    value = value + heats[r, j][f - 2]
                grids[f][r][j] = value
        fields = [
            Tiles(
                grids[f],
                [column(ring_cols[0], r, f * DEEP + k) for r in range(n_r)],
                [column(ring_cols[1], r, f * DEEP + k) for r in range(n_r)],
                [ring_rows[0][f][k : k + 1, j * LANES : (j + 1) * LANES] for j in range(n_j)],
                [ring_rows[1][f][k : k + 1, j * LANES : (j + 1) * LANES] for j in range(n_j)],
            )
            for f in range(5)
        ]
        for r, j in grid:
            at = tile(r, j, k, rows)
            over_x, over_y = run[r, j]

            def pressed(x, y):
                run[r, j] = (over_x + x, over_y + y)
                return PRESS * (over_x + 0.5 * x), PRESS * (over_y + 0.5 * y)

            new = advanced(
                [field.grid[r][j] for field in fields],
                [field.around(r, j) for field in fields],
                wets[r, j],
                turn[r * DEEP : (r + 1) * DEEP, 0:1],
                pressed,
                heats[r, j],
            )
            for f in range(5):
                if f < 2:
                    flow_ref[(f, *at)] = new[f]
                else:
                    tracers_ref[(f - 2, *at)] = new[f]
        whole = pl.ds(k * rows, rows)
        copies.append(
            pltpu.make_async_copy(tracers_ref.at[:, whole, :], out_hbm.at[pl.ds(2, 3), whole, :], sem.at[k])
        )
        copies[-1].start()
    for copy in copies:
        copy.wait()


def last_kernel(out_in_hbm, flow_ref, mask_ref, above_ref, out_hbm, moved_ref, sem):
    del out_in_hbm
    rows, cols = mask_ref.shape[0] // DEEP, mask_ref.shape[1]
    above = above_ref[...]
    east, west, north, south = around(
        above[0:rows, 0:cols],
        above[0:rows, cols : cols + 1],
        above[0:rows, cols + 1 : cols + 2],
        above[rows : rows + 1, 0:cols],
        above[rows + 1 : rows + 2, 0:cols],
    )
    push_x, push_y = (0.5 * PRESS) * (east - west), (0.5 * PRESS) * (north - south)
    copies = []
    for k in range(DEEP):
        whole = pl.ds(k * rows, rows)
        wet = mask_ref[whole, :].astype(F32)
        moved_ref[0, whole, :] = flow_ref[0, whole, :] - wet * push_x
        moved_ref[1, whole, :] = flow_ref[1, whole, :] - wet * push_y
        copies.append(pltpu.make_async_copy(moved_ref.at[:, whole, :], out_hbm.at[pl.ds(0, 2), whole, :], sem.at[k]))
        copies[-1].start()
    for copy in copies:
        copy.wait()


def body(n_lon, n_lat, state, mask, coriolis, penetration, flux_tiles, flux_owner, flux_row, fold_partner):
    fields, levels, rows, cols = state.shape
    flat_state = state.reshape(fields, levels * rows, cols)
    flat_mask = mask.reshape(levels * rows, cols)
    last = n_lat - 1

    keep, send, west, east, total = prepare(
        flat_state, flat_mask, flux_tiles, flux_owner, flux_row, fold_partner, n_lon, n_lat
    )

    stages = []
    for axis, size, least in (("lat", n_lat, 2), ("lon", n_lon, 1)):
        bit = size // 2
        while bit >= least:
            stages.append((axis, size, bit))
            bit //= 2
    got = lax.ppermute(send, "lat", [(i, i ^ 1) for i in range(n_lat)])
    prefix = lax.ppermute(total, "lev", [(0, 1)])

    def merged(keep, got):
        half = shape(keep.shape[0] // 2, keep.shape[1])
        return call(merge_kernel, (half, half), [VMEM] * 2, (keep, got), name="merge_flux")

    def passed_on(send, stage):
        axis, size, bit = stage
        return lax.ppermute(send, axis, [(i, i ^ bit) for i in range(size)])

    pieces = cols // LANES
    hinge_piece = fold_partner[0] >> (LANES.bit_length() - 1)
    keep = after(keep, (prefix, hinge_piece))
    keep, send = merged(keep, got)
    got = passed_on(send, stages[0])

    message = shape(SLABS + 1, DEEP, cols)
    top_shape = shape(pieces, SLABS + 1, DEEP, LANES)
    top = call(top_kernel, top_shape, [VMEM] * 3, (flat_state, flat_mask, prefix), name="top_rows")
    top = after(top, send)

    def folded(hinge_piece):
        block, piece = divmod(hinge_piece, pieces)

        def swap(rows_out):
            def across(part, other):
                pairs = [(a * n_lat + last, (other - a) % n_lon * n_lat + last) for a in range(n_lon)]
                return lax.ppermute(part, ("lon", "lat"), pairs)

            return jnp.concatenate([across(rows_out[piece:], block - 1), across(rows_out[: piece + 1], block)], axis=0)

        return swap

    fold = lax.switch(hinge_piece, [folded(n) for n in range(n_lon * pieces)], top)
    keep = after(keep, fold)
    keep, send = merged(keep, got)
    got = passed_on(send, stages[1])

    west, east = after((west, east), send)
    side = shape(rows + DEEP, LANES)
    west, east = call(
        functools.partial(columns_kernel, n_lat),
        (side, side),
        [VMEM] * 4 + [SMEM],
        (west, east, prefix, fold, fold_partner),
        name="edge_columns",
    )
    from_west = lax.ppermute(east, "lon", [(i, (i + 1) % n_lon) for i in range(n_lon)])
    from_east = lax.ppermute(west, "lon", [((i + 1) % n_lon, i) for i in range(n_lon)])
    pair, cross = call(
        rows_kernel,
        (message, message),
        [VMEM, VMEM, VMEM, SMEM, VMEM, VMEM],
        (flat_state, flat_mask, prefix, coriolis, from_west, from_east),
        name="edge_rows",
    )
    from_pair = lax.ppermute(pair, "lat", [(i, i ^ 1) for i in range(n_lat)])
    from_cross = lax.ppermute(cross, "lat", [(i, i + 1 if i % 2 else i - 1) for i in range(1, last)])
    keep = after(keep, (pair, cross))
    for stage in stages[2:]:
        keep, send = merged(keep, got)
        got = passed_on(send, stage)

    near_state, near_mask = after((flat_state, flat_mask), send)
    new_state, inside = call(
        inside_kernel,
        (shape(fields, levels * rows, cols), shape(rows, 2 * cols)),
        [VMEM, VMEM, VMEM, SMEM, SMEM],
        (near_state, near_mask, prefix, coriolis, penetration),
        name="first_inside",
    )
    keep = after(keep, inside)
    mine = keep + got
    theirs = lax.ppermute(mine, "lev", [(0, 1), (1, 0)])

    inside = after(inside, mine)
    wide = cols + LANES
    *ring, sums = call(
        functools.partial(rim_kernel, n_lat),
        (
            shape(2, 6, DEEP, cols),
            shape(2, rows, LANES),
            shape(2, 5, DEEP, cols),
            shape(2, rows, LANES),
            shape(rows + DEEP, 2 * wide),
        ),
        [VMEM, VMEM, VMEM, SMEM, SMEM, SMEM] + [VMEM] * 8,
        (
            flat_state, flat_mask, prefix, coriolis, penetration, fold_partner, west, east, from_west, from_east, from_pair,
            from_cross, fold, inside,
        ),
        [pltpu.VMEM((SLABS + 1, DEEP, cols), F32), pltpu.VMEM((SLABS + 1, DEEP, cols), F32)],
        name="first_rim",
    )
    *flux, above = call(
        functools.partial(flux_kernel, n_lat),
        (shape(3, rows, cols), shape(DEEP, cols), shape(rows, LANES), shape(rows + DEEP, wide)),
        [VMEM] * 3 + [SMEM],
        (sums, mine, theirs, fold_partner),
        name="flux_parts",
    )
    above = lax.ppermute(above, "lev", [(0, 1)])

    out = jax.ShapeDtypeStruct(flat_state.shape, F32)
    result, flow = call(
        second_kernel,
        (out, shape(2, levels * rows, cols)),
        [VMEM] * 9 + [SMEM] * 2,
        (new_state, flat_mask, *ring, *flux, coriolis, penetration),
        [pltpu.VMEM((3, levels * rows, cols), F32), pltpu.SemaphoreType.DMA((DEEP,))],
        name="second_substep",
        out_specs=(ANY, VMEM),
    )
    result = call(
        last_kernel,
        out,
        [ANY] + [VMEM] * 3,
        (result, flow, flat_mask, above),
        [pltpu.VMEM((2, levels * rows, cols), F32), pltpu.SemaphoreType.DMA((DEEP,))],
        name="deeper_pressure",
        out_specs=ANY,
        aliases={0: 0},
    )
    return result.reshape(fields, levels, rows, cols)


def solution(mesh):
    n_lon, n_lat = mesh.shape["lon"], mesh.shape["lat"]
    assert mesh.shape["lev"] == 2 and n_lat % 2 == 0 and n_lon > 2
    return jax.shard_map(
        functools.partial(body, n_lon, n_lat),
        mesh=mesh,
        in_specs=(
            P(None, "lev", "lat", "lon"),
            P("lev", "lat", "lon"),
            P("lat"),
            P("lev"),
            P(("lon", "lat"), None, None),
            P(("lon", "lat"), None),
            P(("lon", "lat")),
            P(),
        ),
        out_specs=P(None, "lev", "lat", "lon"),
        check_vma=False,
    )
```

```python
import functools

import jax
import jax.numpy as jnp
from jax import lax
from jax.experimental import pallas as pl
from jax.experimental.pallas import tpu as pltpu
from jax.sharding import PartitionSpec as P

ALPHA = 0.2
BETA = 0.15
PRESS = 0.1
VISCOUS = 0.1
DIFFUSE = 0.1
ADVECT = 0.1

F32 = jnp.float32
I32 = jnp.int32
LANES = 128
DEEP = 8
FAR = 64
WET = 48
ABOVE = 56
SLABS = 11
CORNERS = SLABS
VMEM_BYTES = 24 * 1024 * 1024

VMEM = pl.BlockSpec(memory_space=pltpu.VMEM)
SMEM = pl.BlockSpec(memory_space=pltpu.SMEM)
ANY = pl.BlockSpec(memory_space=pl.ANY)
HBM = pl.BlockSpec(memory_space=pltpu.HBM)


def iota(shape, dim):
    return lax.broadcasted_iota(I32, shape, dim)


def roll(value, shift, axis):
    return pltpu.roll(value, shift % value.shape[axis], axis)


def call(kernel, out_shape, in_specs, args, scratch=(), name=None, out_specs=None, aliases=None):
    return pl.pallas_call(
        kernel,
        out_shape=out_shape,
        in_specs=in_specs,
        out_specs=out_specs or jax.tree.map(lambda _: VMEM, out_shape),
        input_output_aliases=aliases or {},
        scratch_shapes=list(scratch),
        compiler_params=pltpu.CompilerParams(vmem_limit_bytes=VMEM_BYTES),
        name=name,
    )(*args)


def after(values, *others):
    return lax.optimization_barrier((values, others))[0]


def shape(*dims):
    return pltpu.VMEM(dims, F32)


def in_hbm(*arrays):
    return tuple(pltpu.with_memory_space_constraint(array, pltpu.HBM) for array in arrays)


def prepare_kernel(
    n_lon, n_lat, state_hbm, mask_hbm, tiles_hbm, owner_hbm, row_hbm, partner_hbm, keep_ref, send_ref, west_ref, east_ref,
    total_ref, state_ref, mask_ref, x_ref, owners_ref, rows_ref, hinge_ref, sem,
):
    tiles, cols = tiles_hbm.shape[1], tiles_hbm.shape[2]
    half_cols = cols // 2
    rows = 2 * DEEP
    n_y = n_lat // 2
    half = lax.axis_index("lev")
    lat = lax.axis_index("lat")
    core = lax.rem(lat, 2)
    begin = pl.multiple_of(half * half_cols, LANES)
    indices = [
        pltpu.make_async_copy(owner_hbm, owners_ref, sem.at[0]),
        pltpu.make_async_copy(row_hbm, rows_ref, sem.at[1]),
        pltpu.make_async_copy(partner_hbm, hinge_ref, sem.at[2]),
    ]
    fluxes = [
        pltpu.make_async_copy(
            tiles_hbm.at[c, :, pl.ds(begin, half_cols)], x_ref.at[:, pl.ds(c * half_cols, half_cols)], sem.at[3 + c]
        )
        for c in range(3)
    ]
    fields = [
        pltpu.make_async_copy(state_hbm, state_ref, sem.at[6]),
        pltpu.make_async_copy(mask_hbm, mask_ref, sem.at[7]),
    ]
    for copy in indices + fluxes + fields:
        copy.start()
    for copy in indices:
        copy.wait()

    key = owners_ref[...] * rows + rows_ref[...]
    hinge_block = hinge_ref[0] // cols
    slots = keep_ref.shape[0]
    slot = iota((slots, tiles), 0)
    group, sub = slot >> 3, slot & 7
    at_y = (group >> (n_lon.bit_length() - 1)) ^ (lat // 2)
    at_lon = (group & (n_lon - 1)) ^ lax.axis_index("lon")

    def wrapped(lon):
        return jnp.where(lon < 0, lon + n_lon, jnp.where(lon >= n_lon, lon - n_lon, lon))

    def one_hot(hit):
        return jnp.where(hit, 1.0, 0.0).astype(jnp.bfloat16)

    def weights(to_core):
        lat = 2 * at_y + to_core
        owner = at_lon * n_lat + lat
        last = lat == n_lat - 1
        top = n_lat * rows - 1
        south = jnp.where(lat == 0, owner * rows, owner * rows - 1)
        north = jnp.where(last, wrapped(hinge_block - at_lon) * (n_lat * rows) + top, (owner + 1) * rows)
        third = jnp.where(last, wrapped(hinge_block - at_lon - 1) * (n_lat * rows) + top, -1)
        kind = sub >> 1
        extra_key = jnp.where(kind == 0, south, jnp.where(kind == 1, north, jnp.where(kind == 2, third, -1)))
        extra = key == extra_key
        beside = wrapped(at_lon + 1 - 2 * half) * n_lat + lat
        return (
            one_hot(key == owner * rows + sub),
            one_hot(key == owner * rows + DEEP + sub),
            one_hot(extra & ((sub & 1) == 0)),
            one_hot(extra & ((sub & 1) == 1)),
            one_hot(((key >> 4) == beside) & (sub == 6)),
        )

    def split(x):
        first = x.astype(jnp.bfloat16)
        rest = x - first.astype(F32)
        second = rest.astype(jnp.bfloat16)
        third = (rest - second.astype(F32)).astype(jnp.bfloat16)
        return first, second, third

    square = iota((tiles, tiles), 0) == iota((tiles, tiles), 1)
    row_of = jnp.sum(jnp.where(square, (key & (rows - 1)).astype(F32), 0.0), axis=1, keepdims=True).astype(I32)

    for copy in fluxes:
        copy.wait()
    x = x_ref[...]
    lane = iota((tiles, LANES), 1)
    edge = jnp.zeros((tiles, LANES), F32)
    for c in range(3):
        begin = c * half_cols
        value = jnp.where(half == 0, x[:, begin : begin + 1], x[:, begin + half_cols - 1 : begin + half_cols])
        edge = jnp.where(((lane >> 4) == c) & ((lane & 15) == row_of), value, edge)
    parts, edges = split(x), split(edge)
    wide = 3 * half_cols
    quarter = wide // 2

    def dot(hot, terms, begin, end):
        products = [
            jnp.dot(hot, term[:, begin:end], preferred_element_type=F32) for term in reversed(terms)
        ]
        return products[0] + products[1] + products[2]

    for out_ref, to_core in ((keep_ref, core), (send_ref, 1 - core)):
        low, high, even, odd, ring = weights(to_core)
        out_ref[:, 0:wide] = dot(low, parts, 0, wide)
        out_ref[:, wide : 2 * wide] = dot(high, parts, 0, wide)
        rest = dot(even, parts, 0, quarter) + dot(odd, parts, quarter, wide)
        beside = dot(ring, edges, 0, LANES)
        out_ref[:, 2 * wide : 2 * wide + LANES] = rest[:, 0:LANES] + beside
        out_ref[:, 2 * wide + LANES :] = rest[:, LANES:]

    for copy in fields:
        copy.wait()
    total = jnp.zeros(total_ref.shape, F32)
    for k in range(DEEP):
        at = slice(k * rows, (k + 1) * rows)
        total = total + buoyancy_of(state_ref[2, at, :], state_ref[3, at, :])
    total_ref[...] = total
    edge_columns(state_ref, mask_ref, west_ref, east_ref)


def merge_kernel(kept_ref, got_ref, keep_ref, send_ref):
    half = keep_ref.shape[0]
    send_ref[...] = kept_ref[half:, :] + got_ref[half:, :]
    keep_ref[...] = kept_ref[0:half, :] + got_ref[0:half, :]


def prepare(state, mask, flux_tiles, flux_owner, flux_row, fold_partner, n_lon, n_lat):
    tiles, _, cols = flux_tiles.shape
    wide = 3 * (cols // 2)
    slots = shape(n_lon * n_lat // 2 * DEEP, 2 * wide + wide // 2)
    side = shape(2 * DEEP, LANES)
    return call(
        functools.partial(prepare_kernel, n_lon, n_lat),
        (slots, slots, side, side, shape(2 * DEEP, cols)),
        [HBM] * 6,
        in_hbm(
            state,
            mask,
            flux_tiles.transpose(1, 0, 2),
            flux_owner.reshape(1, tiles),
            flux_row.reshape(1, tiles),
            fold_partner,
        ),
        [
            pltpu.VMEM(state.shape, F32),
            pltpu.VMEM(mask.shape, I32),
            pltpu.VMEM((tiles, wide), F32),
            pltpu.VMEM((1, tiles), I32),
            pltpu.VMEM((1, tiles), I32),
            pltpu.SMEM(fold_partner.shape, I32),
            pltpu.SemaphoreType.DMA((8,)),
        ],
        name="prepare",
    )


def level_rows(ref, row, rows):
    return jnp.concatenate([ref[k * rows + row : k * rows + row + 1, :] for k in range(DEEP)], axis=0)


def buoyancy_of(temper, saline):
    return ALPHA * temper - BETA * saline


def edge_rows(state_ref, mask_ref, out_ref, rows, near, far):
    for f in range(5):
        out_ref[2 * f] = level_rows(state_ref.at[f], near, rows)
        out_ref[2 * f + 1] = level_rows(state_ref.at[f], far, rows)
    out_ref[10] = level_rows(mask_ref, near, rows).astype(F32)


def edge_columns(state_ref, mask_ref, west_ref, east_ref):
    rows, cols = west_ref.shape[0], state_ref.shape[2]
    lane = iota((rows, LANES), 1)
    last = slice(cols - LANES, cols)
    west = jnp.zeros((rows, LANES), F32)
    east = jnp.zeros((rows, LANES), F32)
    for k in range(DEEP):
        at = slice(k * rows, (k + 1) * rows)
        for f in range(5):
            to = f * DEEP + k
            left, right = state_ref[f, at, 0:LANES], state_ref[f, at, last]
            west = jnp.where(lane == to, roll(left, to, 1), west)
            west = jnp.where(lane == FAR + to, roll(left, FAR + to - 1, 1), west)
            east = jnp.where(lane == to, roll(right, to + 1, 1), east)
            east = jnp.where(lane == FAR + to, roll(right, FAR + to + 2, 1), east)
        west = jnp.where(lane == WET + k, roll(mask_ref[at, 0:LANES].astype(F32), WET + k, 1), west)
        east = jnp.where(lane == WET + k, roll(mask_ref[at, last].astype(F32), WET + k + 1, 1), east)
    west_ref[...] = west
    east_ref[...] = east


def columns_kernel(west_ref, east_ref, prefix_ref, west_out_ref, east_out_ref):
    rows, cols = prefix_ref.shape
    lane = iota((rows, LANES), 1)
    for side, in_ref, out_ref in ((0, west_ref, west_out_ref), (1, east_ref, east_out_ref)):
        near, far = (0, 1) if side == 0 else (cols - 1, cols - 2)
        value = jnp.where(lane == ABOVE, prefix_ref[:, near : near + 1], in_ref[...])
        out_ref[...] = jnp.where(lane == FAR + ABOVE, prefix_ref[:, far : far + 1], value)


def corner_slab(out_ref, prefix_ref, turn_ref, from_west_ref, from_east_ref, near, far):
    out_ref[CORNERS] = jnp.full(out_ref.shape[1:], turn_ref[near], F32)
    out_ref[CORNERS, 0:1, 0:LANES] = from_west_ref[near : near + 1, :]
    out_ref[CORNERS, 1:2, 0:LANES] = from_east_ref[near : near + 1, :]
    out_ref[CORNERS, 3:4, :] = prefix_ref[near : near + 1, :]
    out_ref[CORNERS, 4:5, :] = prefix_ref[far : far + 1, :]


def rows_kernel(
    state_ref, mask_ref, prefix_ref, turn_ref, from_west_ref, from_east_ref, pair_ref, cross_ref, top_ref
):
    rows, cols = prefix_ref.shape
    odd = lax.rem(lax.axis_index("lat"), 2) == 1

    def fill(out_ref, near, far):
        edge_rows(state_ref, mask_ref, out_ref, rows, near, far)
        corner_slab(out_ref, prefix_ref, turn_ref, from_west_ref, from_east_ref, near, far)

    @pl.when(odd)
    def _():
        fill(pair_ref, 0, 1)
        fill(cross_ref, rows - 1, rows - 2)
        sub, lane = iota((DEEP, LANES), 0), iota((DEEP, LANES), 1)
        pieces = cols // LANES
        for piece in range(pieces):
            top_ref[piece] = cross_ref[:, :, piece * LANES : (piece + 1) * LANES]
            if piece < pieces - 1:
                beyond = (piece + 1) * LANES
                line = jnp.zeros((DEEP, LANES), F32)
                for f in range(5):
                    line = jnp.where(lane == f * DEEP + sub, cross_ref[2 * f, :, beyond : beyond + 1], line)
                line = jnp.where((lane == ABOVE) & (sub == 3), cross_ref[CORNERS, :, beyond : beyond + 1], line)
                top_ref[piece, CORNERS, 1:2, :] = jnp.sum(line, axis=0, keepdims=True)
            else:
                top_ref[piece, CORNERS, 1:2, :] = from_east_ref[rows - 1 : rows, :]

    @pl.when(jnp.logical_not(odd))
    def _():
        fill(pair_ref, rows - 1, rows - 2)
        fill(cross_ref, 0, 1)
        top_ref[...] = jnp.zeros(top_ref.shape, F32)


def around(value, west, east, south, north):
    rows, cols = value.shape
    row, col = iota((rows, cols), 0), iota((rows, cols), 1)
    return (
        jnp.where(col == cols - 1, east, roll(value, -1, 1)),
        jnp.where(col == 0, west, roll(value, 1, 1)),
        jnp.where(row == rows - 1, north, roll(value, -1, 0)),
        jnp.where(row == 0, south, roll(value, 1, 0)),
    )


def advanced(values, sides, wet, turn, pressed, heat=None):
    zonal, merid = values[0], values[1]
    sums = [(e + w) + (n + s) for e, w, n, s in sides]
    across = [(e - w, n - s) for e, w, n, s in sides]
    press_x, press_y = pressed(
        0.5 * buoyancy_of(across[2][0], across[3][0]), 0.5 * buoyancy_of(across[2][1], across[3][1])
    )
    out = []
    carry_x, carry_y = (0.5 * ADVECT) * zonal, (0.5 * ADVECT) * merid
    for f in range(5):
        spread = (VISCOUS if f < 2 else DIFFUSE) * (sums[f] - 4.0 * values[f])
        if f == 0:
            trend = spread + (turn * merid - press_x)
        elif f == 1:
            trend = spread - (turn * zonal + press_y)
        else:
            trend = spread - (carry_x * across[f][0] + carry_y * across[f][1])
        new = values[f] + wet * trend
        out.append(new if heat is None or f < 2 else new + heat[f - 2])
    return out


class Tiles:
    def __init__(self, grid, west=None, east=None, south=None, north=None):
        self.grid, self.ghosts, self.turned = grid, (west, east, south, north), {}
        self.lane, self.sub = iota((DEEP, LANES), 1), iota((DEEP, LANES), 0)

    def rolled(self, r, j, shift, axis):
        at = (r, j, shift, axis)
        if at not in self.turned:
            self.turned[at] = roll(self.grid[r][j], shift, axis)
        return self.turned[at]

    def side(self, r, j, shift, axis):
        here = self.rolled(r, j, shift, axis)
        r_from, j_from = (r, j - shift) if axis else (r - shift, j)
        edge = (0 if shift == 1 else LANES - 1) if axis else (0 if shift == 1 else DEEP - 1)
        if 0 <= r_from < len(self.grid) and 0 <= j_from < len(self.grid[0]):
            other = self.rolled(r_from, j_from, shift, axis)
        else:
            ghost = self.ghosts[(0 if shift == 1 else 1) + (0 if axis else 2)]
            if ghost is None:
                return here
            other = ghost[r if axis else j]
        return jnp.where((self.lane if axis else self.sub) == edge, other, here)

    def around(self, r, j):
        return self.side(r, j, -1, 1), self.side(r, j, 1, 1), self.side(r, j, -1, 0), self.side(r, j, 1, 0)


def tile(r, j, k, rows):
    return slice(k * rows + r * DEEP, k * rows + (r + 1) * DEEP), slice(j * LANES, (j + 1) * LANES)


def turn_column(turn_ref, rows):
    row = iota((rows, LANES), 0)
    column = jnp.zeros((rows, LANES), F32)
    for j in range(rows):
        column = jnp.where(row == j, turn_ref[j], column)
    return column


def mirrored(value, width):
    back = LANES - 1 - iota((value.shape[0], LANES), 1)
    blocks = [
        jnp.take_along_axis(value[:, begin : begin + LANES], back, axis=1)
        for begin in range(width - LANES, -1, -LANES)
    ]
    return jnp.concatenate(blocks, axis=1)


def scan_down(value):
    row = iota(value.shape, 0)
    for step in (1, 2, 4):
        value = value + jnp.where(row >= step, roll(value, step, 0), 0.0)
    return value


def scan_lanes(value):
    lane = iota(value.shape, 1) & 7
    for step in (1, 2, 4):
        value = value + jnp.where(lane >= step, roll(value, step, 1), 0.0)
    return value


def lanes_between(value, begin, end):
    lane = iota(value.shape, 1)
    return jnp.where((lane >= begin) & (lane < end), value, 0.0)


def buoyancy_sum(column):
    here = lanes_between(buoyancy_of(roll(column, -16, 1), roll(column, -24, 1)), 0, 8)
    return jnp.sum(here, axis=1, keepdims=True)


def inside_kernel(state_ref, mask_ref, turn_ref, share_ref, new_ref, sums_ref):
    rows, cols = sums_ref.shape[0], state_ref.shape[2]
    n_r, n_j = rows // DEEP, cols // LANES
    turn = turn_column(turn_ref, rows)
    grid = [(r, j) for r in range(n_r) for j in range(n_j)]
    zero = jnp.zeros((DEEP, LANES), F32)
    run = {at: [zero] * 4 for at in grid}
    for k in range(DEEP):
        fields = [Tiles([[state_ref[(f, *tile(r, j, k, rows))] for j in range(n_j)] for r in range(n_r)]) for f in range(5)]
        for r, j in grid:
            at = tile(r, j, k, rows)
            above_x, above_y, total, absorbed = run[r, j]
            slopes = []

            def pressed(x, y):
                slopes.extend((x, y))
                return PRESS * (above_x + 0.5 * x), PRESS * (above_y + 0.5 * y)

            values = [field.grid[r][j] for field in fields]
            wet = mask_ref[at].astype(F32)
            new = advanced(
                values, [field.around(r, j) for field in fields], wet, turn[r * DEEP : (r + 1) * DEEP, 0:1], pressed
            )
            for f in range(5):
                new_ref[(f, *at)] = new[f]
            run[r, j] = [
                above_x + slopes[0],
                above_y + slopes[1],
                total + buoyancy_of(new[2], new[3]),
                absorbed + wet * share_ref[k],
            ]
    for r, j in grid:
        for kind in range(2):
            at = slice(kind * cols + j * LANES, kind * cols + (j + 1) * LANES)
            sums_ref[r * DEEP : (r + 1) * DEEP, at] = run[r, j][2 + kind]


def rim_kernel(
    n_lat, state_ref, mask_ref, prefix_ref, turn_ref, share_ref, partner_ref, own_west_ref, own_east_ref,
    from_west_ref, from_east_ref, pair_ref, cross_ref, fold_ref, inside_ref, ring_rows_ref, ring_cols_ref,
    edge_rows_ref, edge_cols_ref, sums_ref, south_ref, north_ref,
):
    rows, cols = prefix_ref.shape
    lat = lax.axis_index("lat")
    odd = lax.rem(lat, 2) == 1
    within = partner_ref[0] & (LANES - 1)
    at_top = lat == n_lat - 1

    @pl.when(odd)
    def _():
        south_ref[...] = pair_ref[...]

    @pl.when(jnp.logical_not(odd))
    def _():
        north_ref[...] = pair_ref[...]

    @pl.when(jnp.logical_not(odd) & (lat > 0))
    def _():
        south_ref[...] = cross_ref[...]

    @pl.when(odd & (lat < n_lat - 1))
    def _():
        north_ref[...] = cross_ref[...]

    @pl.when(lat == 0)
    def _():
        edge_rows(state_ref, mask_ref, south_ref, rows, 0, 0)
        corner_slab(south_ref, prefix_ref, turn_ref, from_west_ref, from_east_ref, 0, 0)

    sub8, lane8 = iota((DEEP, LANES), 0), iota((DEEP, LANES), 1)

    @pl.when(at_top)
    def _():
        west = jnp.zeros((DEEP, LANES), F32)
        east = jnp.zeros((DEEP, LANES), F32)
        for slab in range(SLABS + 1):
            row = jnp.concatenate([fold_ref[piece, slab] for piece in range(fold_ref.shape[0])], axis=1)
            row = pltpu.roll(row, cols + LANES - 1 - within, 1)
            if slab < 4:
                row = -row
            north_ref[slab] = mirrored(row, cols)
            if slab < 10 and slab % 2 == 0:
                here = lane8 == (slab // 2) * DEEP + sub8
            elif slab == CORNERS:
                here = (lane8 == ABOVE) & (sub8 == 3)
            else:
                continue
            west = jnp.where(here, row[:, cols : cols + 1], west)
            east = jnp.where(here, row[:, cols + LANES - 1 :], east)
        beyond = fold_ref[fold_ref.shape[0] - 1, CORNERS, 1:2, :]
        beyond = jnp.where(iota((1, LANES), 1) < 16, -beyond, beyond)
        west = jnp.where(within == LANES - 1, beyond, jnp.sum(west, axis=0, keepdims=True))
        north_ref[CORNERS, 0:1, 0:LANES] = west
        north_ref[CORNERS, 1:2, 0:LANES] = jnp.sum(east, axis=0, keepdims=True)
        north_ref[CORNERS, 2:3, :] = jnp.full((1, cols), turn_ref[rows - 1], F32)

    wide = cols + LANES
    sums_ref[rows:, :] = jnp.zeros((DEEP, 2 * wide), F32)
    for kind in range(2):
        sums_ref[0:rows, kind * wide : kind * wide + cols] = inside_ref[:, kind * cols : (kind + 1) * cols]

    share_down = jnp.zeros((DEEP, LANES), F32)
    for k in range(DEEP):
        share_down = jnp.where(sub8 == k, share_ref[k], share_down)

    def down(line, f):
        return jnp.sum(jnp.where(lane8 == f * DEEP + sub8, line, 0.0), axis=1, keepdims=True)

    def row_step(near, south, north, west_line, east_line, wet, turn, above, above_south, above_north):
        col = iota((DEEP, cols), 1)
        sides = [
            (
                jnp.where(col == cols - 1, down(east_line, f), roll(near[f], -1, 1)),
                jnp.where(col == 0, down(west_line, f), roll(near[f], 1, 1)),
                north[f],
                south[f],
            )
            for f in range(5)
        ]
        east = jnp.where(col[0:1] == cols - 1, east_line[:, ABOVE : ABOVE + 1], roll(above, -1, 1))
        west = jnp.where(col[0:1] == 0, west_line[:, ABOVE : ABOVE + 1], roll(above, 1, 1))
        above_x, above_y = 0.5 * (east - west), 0.5 * (above_north - above_south)

        def pressed(x, y):
            return PRESS * (above_x + scan_down(x) - 0.5 * x), PRESS * (above_y + scan_down(y) - 0.5 * y)

        return advanced(near, sides, wet, turn, pressed)

    for side, ghost_ref, edge, inner in ((0, south_ref, 0, 1), (1, north_ref, rows - 1, rows - 2)):
        near = [ghost_ref[2 * f] for f in range(5)]
        far = [ghost_ref[2 * f + 1] for f in range(5)]
        own = [level_rows(state_ref.at[f], edge, rows) for f in range(5)]
        own_next = [level_rows(state_ref.at[f], inner, rows) for f in range(5)]
        ring_wet = ghost_ref[10]
        corners = ghost_ref[CORNERS, :, 0:LANES]
        above_near, above_far = ghost_ref[CORNERS, 3:4, :], ghost_ref[CORNERS, 4:5, :]
        above_own, above_next = prefix_ref[edge : edge + 1, :], prefix_ref[inner : inner + 1, :]
        outward, inward = (far, above_far), (own, above_own)
        (south, above_south), (north, above_north) = (outward, inward) if side == 0 else (inward, outward)
        ring = row_step(
            near, south, north, corners[0:1, :], corners[1:2, :], ring_wet, corners[2:3, 0:1], above_near, above_south, above_north
        )
        outward, inward = (near, above_near), (own_next, above_next)
        (south, above_south), (north, above_north) = (outward, inward) if side == 0 else (inward, outward)
        wet = level_rows(mask_ref, edge, rows).astype(F32)
        edge_line = slice(edge, edge + 1)
        new = row_step(
            own, south, north, from_west_ref[edge_line, :], from_east_ref[edge_line, :], wet, turn_ref[edge],
            above_own, above_south, above_north,
        )
        for f in range(5):
            edge_rows_ref[side, f] = new[f]
            ring_rows_ref[side, f] = jnp.where(lat == 0, new[f], ring[f]) if side == 0 else ring[f]
        ring_rows_ref[side, 5] = ring_wet
        at = slice(rows + side, rows + side + 1)
        here = buoyancy_of(ring_rows_ref[side, 2], ring_rows_ref[side, 3])
        sums_ref[at, 0:cols] = jnp.sum(here, axis=0, keepdims=True)
        sums_ref[at, wide : wide + cols] = jnp.sum(ring_wet * share_down[:, 0:1], axis=0, keepdims=True)

    row, lane = iota((rows, LANES), 0), iota((rows, LANES), 1)
    turn = turn_column(turn_ref, rows)
    share_lanes = jnp.zeros((rows, LANES), F32)
    for k in range(DEEP):
        share_lanes = jnp.where((lane & 7) == k, share_ref[k], share_lanes)

    def column_step(near, east, west, north, south):
        dx, dy = 0.5 * (east - west), 0.5 * (north - south)
        lap = (east + west) + (north + south) - 4.0 * near
        zonal, merid = lanes_between(near, 0, 8), lanes_between(near, 8, 16)
        wet = lanes_between(near, WET, WET + 8)
        wet_all = sum(roll(wet, -8 * n, 1) for n in range(2, 7))
        zonal_all = sum(roll(zonal, 8 * n, 1) for n in (2, 3, 4))
        merid_all = sum(roll(merid, 8 * n, 1) for n in (1, 2, 3))
        bx = lanes_between(buoyancy_of(roll(dx, -16, 1), roll(dx, -24, 1)), 0, 8)
        by = lanes_between(buoyancy_of(roll(dy, -8, 1), roll(dy, -16, 1)), 8, 16)
        press_x = lanes_between(PRESS * (dx[:, ABOVE : ABOVE + 1] + scan_lanes(bx) - 0.5 * bx), 0, 8)
        press_y = lanes_between(PRESS * (dy[:, ABOVE : ABOVE + 1] + scan_lanes(by) - 0.5 * by), 8, 16)
        trend = VISCOUS * lap - ADVECT * (zonal_all * dx + merid_all * dy) - press_x - press_y
        trend = trend + lanes_between(turn * roll(near, -8, 1), 0, 8) - lanes_between(turn * roll(near, 8, 1), 8, 16)
        return near + wet_all * trend, wet

    blocks = [jnp.zeros((rows, LANES), F32)] * 2
    sides = ((0, from_west_ref, own_west_ref), (1, from_east_ref, own_east_ref))
    for side, ghost_ref, own_ref in sides:
        near, own = ghost_ref[0:rows, :], own_ref[0:rows, :]
        far, own_next = roll(near, -FAR, 1), roll(own, -FAR, 1)
        north = jnp.where(row == rows - 1, north_ref[CORNERS, side : side + 1, 0:LANES], roll(near, -1, 0))
        south = jnp.where(row == 0, south_ref[CORNERS, side : side + 1, 0:LANES], roll(near, 1, 0))
        east, west = (own, far) if side == 0 else (far, own)
        new, wet = column_step(near, east, west, north, south)
        ring_cols_ref[side] = new
        blocks[0] = jnp.where(lane == side, buoyancy_sum(new), blocks[0])
        blocks[1] = jnp.where(lane == side, jnp.sum(wet * share_lanes, axis=1, keepdims=True), blocks[1])
        east, west = (own_next, near) if side == 0 else (near, own_next)
        new, _ = column_step(own, east, west, roll(own, -1, 0), roll(own, 1, 0))
        edge_cols_ref[side] = new
        column = 0 if side == 0 else cols - 1
        sums_ref[0:rows, column : column + 1] = buoyancy_sum(new)
    for kind in range(2):
        sums_ref[0:rows, kind * wide + cols : (kind + 1) * wide] = blocks[kind]
    for side, edge in ((0, 0), (1, rows - 1)):
        here = buoyancy_of(edge_rows_ref[side, 2], edge_rows_ref[side, 3])
        sums_ref[edge : edge + 1, 0:cols] = jnp.sum(here, axis=0, keepdims=True)


def flux_kernel(n_lat, mine_ref, theirs_ref, partner_ref, flux_ref, flux_rows_ref, flux_cols_ref, drive_ref):
    rows, cols = flux_ref.shape[1:]
    half_cols = cols // 2
    wide = 3 * half_cols
    mine, theirs = mine_ref[...], theirs_ref[...]
    first = lax.axis_index("lev") == 0
    halves = (jnp.where(first, mine, theirs), jnp.where(first, theirs, mine))
    at_top = lax.axis_index("lat") == n_lat - 1
    hinge = partner_ref[0]
    within = hinge - (hinge // cols) * cols

    def extra(kind, c):
        found = []
        for part in halves:
            line = jnp.concatenate(
                [part[2 * kind : 2 * kind + 1, 2 * wide :], part[2 * kind + 1 : 2 * kind + 2, 2 * wide :]], axis=1
            )
            found.append(line[:, c * half_cols : (c + 1) * half_cols])
        return jnp.concatenate(found, axis=1)

    flux, flux_south, flux_north, flux_west, flux_east = [], [], [], [], []
    crossed = jnp.zeros((DEEP, 2 * cols), F32)
    for c in range(3):
        pair = jnp.concatenate([extra(2, c), extra(1, c)], axis=1)
        crossed = jnp.where(iota(crossed.shape, 0) == c, pair, crossed)
    crossed = mirrored(pltpu.roll(crossed, 2 * cols - 1 - within, 1), cols)
    row, lane = iota((rows, LANES), 0), iota((rows, LANES), 1)
    for c in range(3):
        bands = [
            jnp.concatenate([part[:, b * wide + c * half_cols : b * wide + (c + 1) * half_cols] for part in halves], axis=1)
            for b in range(2)
        ]
        flux.append(jnp.concatenate(bands, axis=0))
        flux_south.append(extra(0, c))
        flux_north.append(jnp.where(at_top, crossed[c : c + 1, :], extra(1, c)))
        here = lane == c * 16 + row
        for side, part in ((flux_west, halves[1]), (flux_east, halves[0])):
            line = part[6:7, 2 * wide : 2 * wide + LANES]
            side.append(jnp.sum(jnp.where(here, line, 0.0), axis=1, keepdims=True))

    flux_cols = jnp.zeros((rows, LANES), F32)
    for c in range(3):
        flux_ref[c] = flux[c]
        flux_rows_ref[c : c + 1, :] = flux_south[c]
        flux_rows_ref[3 + c : 4 + c, :] = flux_north[c]
        flux_cols = jnp.where(lane == c, flux_west[c], jnp.where(lane == 3 + c, flux_east[c], flux_cols))
    flux_rows_ref[6:8, :] = jnp.zeros((2, cols), F32)
    flux_cols_ref[...] = flux_cols
    drive_ref[rows:, :] = jnp.zeros((DEEP, cols + LANES), F32)
    drive_ref[0:rows, 0:cols] = buoyancy_of(flux[0], flux[1])
    ends = jnp.zeros((rows, LANES), F32)
    for side, column, line in ((0, flux_west, flux_south), (1, flux_east, flux_north)):
        drive_ref[rows + side : rows + side + 1, 0:cols] = buoyancy_of(line[0], line[1])
        ends = jnp.where(lane == side, buoyancy_of(column[0], column[1]), ends)
    drive_ref[0:rows, cols:] = ends


def second_kernel(
    state_ref, mask_ref, prefix_ref, ring_rows_ref, ring_cols_ref, edge_rows_ref, edge_cols_ref, flux_ref, flux_rows_ref,
    flux_cols_ref, turn_ref, share_ref, out_hbm, flow_ref, tracers_ref, sem,
):
    rows, cols = flux_ref.shape[1:]
    n_r, n_j = rows // DEEP, cols // LANES
    sub8, lane8 = iota((DEEP, LANES), 0), iota((DEEP, LANES), 1)
    lane = iota((rows, LANES), 1)
    turn = turn_column(turn_ref, rows)
    share_down = jnp.zeros((DEEP, LANES), F32)
    share_lanes = jnp.zeros((rows, LANES), F32)
    for k in range(DEEP):
        share_down = jnp.where(sub8 == k, share_ref[k], share_down)
        share_lanes = jnp.where((lane & 7) == k, share_ref[k], share_lanes)

    ring_rows, ring_cols = [], []
    for side in range(2):
        taken = ring_rows_ref[side, 5] * share_down[:, 0:1]
        values = [ring_rows_ref[side, f] for f in range(2)]
        values += [ring_rows_ref[side, 2 + c] + taken * flux_rows_ref[3 * side + c : 3 * side + c + 1, :] for c in range(3)]
        ring_rows.append(values)
        found = ring_cols_ref[side]
        taken = lanes_between(found, WET, WET + 8) * share_lanes
        for c in range(3):
            found = found + roll(taken, 8 * (2 + c) - WET, 1) * flux_cols_ref[:, 3 * side + c : 3 * side + c + 1]
        ring_cols.append(found)

    grid = [(r, j) for r in range(n_r) for j in range(n_j)]

    def cut(value, r, j):
        return value[r * DEEP : (r + 1) * DEEP, j * LANES : (j + 1) * LANES]

    zero = jnp.zeros((DEEP, LANES), F32)
    run = {at: (zero, zero) for at in grid}
    prefix = Tiles([[prefix_ref[tile(r, j, 0, rows)] for j in range(n_j)] for r in range(n_r)])
    push = {}
    for at in grid:
        east, west, north, south = prefix.around(*at)
        push[at] = (0.5 * PRESS) * (east - west), (0.5 * PRESS) * (north - south)
    edge_cols = [edge_cols_ref[side] for side in range(2)]
    copies = []

    def column(value, r, n):
        return jnp.broadcast_to(value[r * DEEP : (r + 1) * DEEP, n : n + 1], (DEEP, LANES))

    for k in range(DEEP):
        wets, heats, grids = {}, {}, [[[None] * n_j for _ in range(n_r)] for _ in range(5)]
        for r, j in grid:
            at = tile(r, j, k, rows)
            wet = mask_ref[at].astype(F32)
            taken = wet * share_ref[k]
            wets[r, j] = wet
            heats[r, j] = [taken * cut(flux_ref[c], r, j) for c in range(3)]
            for f in range(5):
                value = state_ref[(f, *at)]
                if f < 2:
                    value = value - wet * push[r, j][f]
                if j == 0:
                    value = jnp.where(lane8 == 0, column(edge_cols[0], r, f * DEEP + k), value)
                if j == n_j - 1:
                    value = jnp.where(lane8 == LANES - 1, column(edge_cols[1], r, f * DEEP + k), value)
                if r == 0:
                    value = jnp.where(sub8 == 0, edge_rows_ref[0, f, k : k + 1, at[1]], value)
                if r == n_r - 1:
                    value = jnp.where(sub8 == DEEP - 1, edge_rows_ref[1, f, k : k + 1, at[1]], value)
                if f >= 2:
                    value = value + heats[r, j][f - 2]
                grids[f][r][j] = value
        fields = [
            Tiles(
                grids[f],
                [column(ring_cols[0], r, f * DEEP + k) for r in range(n_r)],
                [column(ring_cols[1], r, f * DEEP + k) for r in range(n_r)],
                [ring_rows[0][f][k : k + 1, j * LANES : (j + 1) * LANES] for j in range(n_j)],
                [ring_rows[1][f][k : k + 1, j * LANES : (j + 1) * LANES] for j in range(n_j)],
            )
            for f in range(5)
        ]
        for r, j in grid:
            at = tile(r, j, k, rows)
            over_x, over_y = run[r, j]

            def pressed(x, y):
                run[r, j] = (over_x + x, over_y + y)
                return PRESS * (over_x + 0.5 * x), PRESS * (over_y + 0.5 * y)

            new = advanced(
                [field.grid[r][j] for field in fields],
                [field.around(r, j) for field in fields],
                wets[r, j],
                turn[r * DEEP : (r + 1) * DEEP, 0:1],
                pressed,
                heats[r, j],
            )
            for f in range(5):
                if f < 2:
                    flow_ref[(f, *at)] = new[f]
                else:
                    tracers_ref[(f - 2, *at)] = new[f]
        whole = pl.ds(k * rows, rows)
        copies.append(
            pltpu.make_async_copy(tracers_ref.at[:, whole, :], out_hbm.at[pl.ds(2, 3), whole, :], sem.at[k])
        )
        copies[-1].start()
    for copy in copies:
        copy.wait()


def last_kernel(out_in_hbm, flow_ref, mask_ref, sums_ref, drive_ref, out_hbm, moved_ref, sem):
    del out_in_hbm
    rows, cols = mask_ref.shape[0] // DEEP, mask_ref.shape[1]
    wide = cols + LANES
    above = sums_ref[:, 0:wide] + sums_ref[:, wide : 2 * wide] * drive_ref[...]
    east, west, north, south = around(
        above[0:rows, 0:cols],
        above[0:rows, cols : cols + 1],
        above[0:rows, cols + 1 : cols + 2],
        above[rows : rows + 1, 0:cols],
        above[rows + 1 : rows + 2, 0:cols],
    )
    push_x, push_y = (0.5 * PRESS) * (east - west), (0.5 * PRESS) * (north - south)
    copies = []
    for k in range(DEEP):
        whole = pl.ds(k * rows, rows)
        wet = mask_ref[whole, :].astype(F32)
        moved_ref[0, whole, :] = flow_ref[0, whole, :] - wet * push_x
        moved_ref[1, whole, :] = flow_ref[1, whole, :] - wet * push_y
        copies.append(pltpu.make_async_copy(moved_ref.at[:, whole, :], out_hbm.at[pl.ds(0, 2), whole, :], sem.at[k]))
        copies[-1].start()
    for copy in copies:
        copy.wait()


def body(n_lon, n_lat, state, mask, coriolis, penetration, flux_tiles, flux_owner, flux_row, fold_partner):
    fields, levels, rows, cols = state.shape
    flat_state = state.reshape(fields, levels * rows, cols)
    flat_mask = mask.reshape(levels * rows, cols)
    last = n_lat - 1

    keep, send, west, east, total = prepare(
        flat_state, flat_mask, flux_tiles, flux_owner, flux_row, fold_partner, n_lon, n_lat
    )

    stages = []
    for axis, size, least in (("lat", n_lat, 2), ("lon", n_lon, 1)):
        bit = size // 2
        while bit >= least:
            stages.append((axis, size, bit))
            bit //= 2
    got = lax.ppermute(send, "lat", [(i, i ^ 1) for i in range(n_lat)])
    prefix = lax.ppermute(total, "lev", [(0, 1)])

    def merged(keep, got):
        half = shape(keep.shape[0] // 2, keep.shape[1])
        return call(merge_kernel, (half, half), [VMEM] * 2, (keep, got), name="merge_flux")

    def passed_on(send, stage):
        axis, size, bit = stage
        return lax.ppermute(send, axis, [(i, i ^ bit) for i in range(size)])

    near_state, near_mask = after((flat_state, flat_mask), send)
    new_state, inside = call(
        inside_kernel,
        (shape(fields, levels * rows, cols), shape(rows, 2 * cols)),
        [VMEM, VMEM, SMEM, SMEM],
        (near_state, near_mask, coriolis, penetration),
        name="first_inside",
    )
    pieces = cols // LANES
    hinge_piece = fold_partner[0] >> (LANES.bit_length() - 1)
    keep = after(keep, (prefix, hinge_piece, inside))
    keep, send = merged(keep, got)
    got = passed_on(send, stages[0])

    prefix = after(prefix, send)
    side = shape(rows, LANES)
    west, east = call(columns_kernel, (side, side), [VMEM] * 3, (west, east, prefix), name="edge_columns")
    from_west = lax.ppermute(east, "lon", [(i, (i + 1) % n_lon) for i in range(n_lon)])
    from_east = lax.ppermute(west, "lon", [((i + 1) % n_lon, i) for i in range(n_lon)])
    message = shape(SLABS + 1, DEEP, cols)
    pair, cross, top = call(
        rows_kernel,
        (message, message, shape(pieces, SLABS + 1, DEEP, LANES)),
        [VMEM, VMEM, VMEM, SMEM, VMEM, VMEM],
        (flat_state, flat_mask, prefix, coriolis, from_west, from_east),
        name="edge_rows",
    )
    from_pair = lax.ppermute(pair, "lat", [(i, i ^ 1) for i in range(n_lat)])
    from_cross = lax.ppermute(cross, "lat", [(i, i + 1 if i % 2 else i - 1) for i in range(1, last)])
    keep = after(keep, (pair, cross, top))
    keep, send = merged(keep, got)
    got = passed_on(send, stages[1])

    top = after(top, send)

    def folded(hinge_piece):
        block, piece = divmod(hinge_piece, pieces)

        def swap(rows_out):
            def across(part, other):
                pairs = [(a * n_lat + last, (other - a) % n_lon * n_lat + last) for a in range(n_lon)]
                return lax.ppermute(part, ("lon", "lat"), pairs)

            return jnp.concatenate([across(rows_out[piece:], block - 1), across(rows_out[: piece + 1], block)], axis=0)

        return swap

    fold = lax.switch(hinge_piece, [folded(n) for n in range(n_lon * pieces)], top)
    keep = after(keep, (fold, from_pair, from_cross))
    for stage in stages[2:]:
        keep, send = merged(keep, got)
        got = passed_on(send, stage)

    inside = after(inside, send)
    wide = cols + LANES
    *ring, sums = call(
        functools.partial(rim_kernel, n_lat),
        (
            shape(2, 6, DEEP, cols),
            shape(2, rows, LANES),
            shape(2, 5, DEEP, cols),
            shape(2, rows, LANES),
            shape(rows + DEEP, 2 * wide),
        ),
        [VMEM, VMEM, VMEM, SMEM, SMEM, SMEM] + [VMEM] * 8,
        (
            flat_state, flat_mask, prefix, coriolis, penetration, fold_partner, west, east, from_west, from_east, from_pair,
            from_cross, fold, inside,
        ),
        [pltpu.VMEM((SLABS + 1, DEEP, cols), F32), pltpu.VMEM((SLABS + 1, DEEP, cols), F32)],
        name="first_rim",
    )
    keep = after(keep, sums)
    mine = keep + got
    theirs = lax.ppermute(mine, "lev", [(0, 1), (1, 0)])
    sums = lax.ppermute(after(sums, mine), "lev", [(0, 1)])
    *flux, drive = call(
        functools.partial(flux_kernel, n_lat),
        (shape(3, rows, cols), shape(DEEP, cols), shape(rows, LANES), shape(rows + DEEP, wide)),
        [VMEM] * 2 + [SMEM],
        (mine, theirs, fold_partner),
        name="flux_parts",
    )

    out = jax.ShapeDtypeStruct(flat_state.shape, F32)
    result, flow = call(
        second_kernel,
        (out, shape(2, levels * rows, cols)),
        [VMEM] * 10 + [SMEM] * 2,
        (new_state, flat_mask, prefix, *ring, *flux, coriolis, penetration),
        [pltpu.VMEM((3, levels * rows, cols), F32), pltpu.SemaphoreType.DMA((DEEP,))],
        name="second_substep",
        out_specs=(ANY, VMEM),
    )
    result = call(
        last_kernel,
        out,
        [ANY] + [VMEM] * 4,
        (result, flow, flat_mask, sums, drive),
        [pltpu.VMEM((2, levels * rows, cols), F32), pltpu.SemaphoreType.DMA((DEEP,))],
        name="deeper_pressure",
        out_specs=ANY,
        aliases={0: 0},
    )
    return result.reshape(fields, levels, rows, cols)


def solution(mesh):
    n_lon, n_lat = mesh.shape["lon"], mesh.shape["lat"]
    assert mesh.shape["lev"] == 2 and n_lat % 2 == 0 and n_lon > 2
    return jax.shard_map(
        functools.partial(body, n_lon, n_lat),
        mesh=mesh,
        in_specs=(
            P(None, "lev", "lat", "lon"),
            P("lev", "lat", "lon"),
            P("lat"),
            P("lev"),
            P(("lon", "lat"), None, None),
            P(("lon", "lat"), None),
            P(("lon", "lat")),
            P(),
        ),
        out_specs=P(None, "lev", "lat", "lon"),
        check_vma=False,
    )
```

```python
import functools

import jax
import jax.numpy as jnp
from jax import lax
from jax.experimental import pallas as pl
from jax.experimental.pallas import tpu as pltpu
from jax.sharding import PartitionSpec as P

ALPHA = 0.2
BETA = 0.15
PRESS = 0.1
VISCOUS = 0.1
DIFFUSE = 0.1
ADVECT = 0.1

F32 = jnp.float32
I32 = jnp.int32
LANES = 128
DEEP = 8
FAR = 64
WET = 48
ABOVE = 56
SLABS = 11
CORNERS = SLABS
VMEM_BYTES = 24 * 1024 * 1024

VMEM = pl.BlockSpec(memory_space=pltpu.VMEM)
SMEM = pl.BlockSpec(memory_space=pltpu.SMEM)
ANY = pl.BlockSpec(memory_space=pl.ANY)
HBM = pl.BlockSpec(memory_space=pltpu.HBM)


def iota(shape, dim):
    return lax.broadcasted_iota(I32, shape, dim)


def roll(value, shift, axis):
    return pltpu.roll(value, shift % value.shape[axis], axis)


def call(kernel, out_shape, in_specs, args, scratch=(), name=None, out_specs=None, aliases=None):
    return pl.pallas_call(
        kernel,
        out_shape=out_shape,
        in_specs=in_specs,
        out_specs=out_specs or jax.tree.map(lambda _: VMEM, out_shape),
        input_output_aliases=aliases or {},
        scratch_shapes=list(scratch),
        compiler_params=pltpu.CompilerParams(vmem_limit_bytes=VMEM_BYTES),
        name=name,
    )(*args)


def after(values, *others):
    return lax.optimization_barrier((values, others))[0]


def shape(*dims):
    return pltpu.VMEM(dims, F32)


def in_hbm(*arrays):
    return tuple(pltpu.with_memory_space_constraint(array, pltpu.HBM) for array in arrays)


def prepare_kernel(
    n_lon, n_lat, state_hbm, mask_hbm, tiles_hbm, owner_hbm, row_hbm, partner_hbm, keep_ref, send_ref, west_ref, east_ref,
    total_ref, state_ref, mask_ref, x_ref, owners_ref, rows_ref, hinge_ref, sem,
):
    tiles, cols = tiles_hbm.shape[1], tiles_hbm.shape[2]
    half_cols = cols // 2
    rows = 2 * DEEP
    n_y = n_lat // 2
    half = lax.axis_index("lev")
    lat = lax.axis_index("lat")
    core = lax.rem(lat, 2)
    begin = pl.multiple_of(half * half_cols, LANES)
    indices = [
        pltpu.make_async_copy(owner_hbm, owners_ref, sem.at[0]),
        pltpu.make_async_copy(row_hbm, rows_ref, sem.at[1]),
        pltpu.make_async_copy(partner_hbm, hinge_ref, sem.at[2]),
    ]
    fluxes = [
        pltpu.make_async_copy(
            tiles_hbm.at[c, :, pl.ds(begin, half_cols)], x_ref.at[:, pl.ds(c * half_cols, half_cols)], sem.at[3 + c]
        )
        for c in range(3)
    ]
    fields = [
        pltpu.make_async_copy(state_hbm, state_ref, sem.at[6]),
        pltpu.make_async_copy(mask_hbm, mask_ref, sem.at[7]),
    ]
    for copy in indices + fluxes + fields:
        copy.start()
    for copy in indices:
        copy.wait()

    key = owners_ref[...] * rows + rows_ref[...]
    hinge_block = hinge_ref[0] // cols
    slots = keep_ref.shape[0]
    slot = iota((slots, tiles), 0)
    group, sub = slot >> 3, slot & 7
    at_y = (group >> (n_lon.bit_length() - 1)) ^ (lat // 2)
    at_lon = (group & (n_lon - 1)) ^ lax.axis_index("lon")

    def wrapped(lon):
        return jnp.where(lon < 0, lon + n_lon, jnp.where(lon >= n_lon, lon - n_lon, lon))

    def one_hot(hit):
        return jnp.where(hit, 1.0, 0.0).astype(jnp.bfloat16)

    def weights(to_core):
        lat = 2 * at_y + to_core
        owner = at_lon * n_lat + lat
        last = lat == n_lat - 1
        top = n_lat * rows - 1
        south = jnp.where(lat == 0, owner * rows, owner * rows - 1)
        north = jnp.where(last, wrapped(hinge_block - at_lon) * (n_lat * rows) + top, (owner + 1) * rows)
        third = jnp.where(last, wrapped(hinge_block - at_lon - 1) * (n_lat * rows) + top, -1)
        kind = sub >> 1
        extra_key = jnp.where(kind == 0, south, jnp.where(kind == 1, north, jnp.where(kind == 2, third, -1)))
        extra = key == extra_key
        beside = wrapped(at_lon + 1 - 2 * half) * n_lat + lat
        return (
            one_hot(key == owner * rows + sub),
            one_hot(key == owner * rows + DEEP + sub),
            one_hot(extra & ((sub & 1) == 0)),
            one_hot(extra & ((sub & 1) == 1)),
            one_hot(((key >> 4) == beside) & (sub == 6)),
        )

    def split(x):
        first = x.astype(jnp.bfloat16)
        rest = x - first.astype(F32)
        second = rest.astype(jnp.bfloat16)
        third = (rest - second.astype(F32)).astype(jnp.bfloat16)
        return first, second, third

    square = iota((tiles, tiles), 0) == iota((tiles, tiles), 1)
    row_of = jnp.sum(jnp.where(square, (key & (rows - 1)).astype(F32), 0.0), axis=1, keepdims=True).astype(I32)

    for copy in fluxes:
        copy.wait()
    x = x_ref[...]
    lane = iota((tiles, LANES), 1)
    edge = jnp.zeros((tiles, LANES), F32)
    for c in range(3):
        begin = c * half_cols
        value = jnp.where(half == 0, x[:, begin : begin + 1], x[:, begin + half_cols - 1 : begin + half_cols])
        edge = jnp.where(((lane >> 4) == c) & ((lane & 15) == row_of), value, edge)
    parts, edges = split(x), split(edge)
    wide = 3 * half_cols
    quarter = wide // 2

    def dot(hot, terms, begin, end):
        products = [
            jnp.dot(hot, term[:, begin:end], preferred_element_type=F32) for term in reversed(terms)
        ]
        return products[0] + products[1] + products[2]

    for out_ref, to_core in ((keep_ref, core), (send_ref, 1 - core)):
        low, high, even, odd, ring = weights(to_core)
        out_ref[:, 0:wide] = dot(low, parts, 0, wide)
        out_ref[:, wide : 2 * wide] = dot(high, parts, 0, wide)
        rest = dot(even, parts, 0, quarter) + dot(odd, parts, quarter, wide)
        beside = dot(ring, edges, 0, LANES)
        out_ref[:, 2 * wide : 2 * wide + LANES] = rest[:, 0:LANES] + beside
        out_ref[:, 2 * wide + LANES :] = rest[:, LANES:]

    for copy in fields:
        copy.wait()
    total = jnp.zeros(total_ref.shape, F32)
    for k in range(DEEP):
        at = slice(k * rows, (k + 1) * rows)
        total = total + buoyancy_of(state_ref[2, at, :], state_ref[3, at, :])
    total_ref[...] = total
    edge_columns(state_ref, mask_ref, west_ref, east_ref)


def merge_kernel(kept_ref, got_ref, keep_ref, send_ref):
    half = keep_ref.shape[0]
    send_ref[...] = kept_ref[half:, :] + got_ref[half:, :]
    keep_ref[...] = kept_ref[0:half, :] + got_ref[0:half, :]


def prepare(state, mask, flux_tiles, flux_owner, flux_row, fold_partner, n_lon, n_lat):
    tiles, _, cols = flux_tiles.shape
    wide = 3 * (cols // 2)
    slots = shape(n_lon * n_lat // 2 * DEEP, 2 * wide + wide // 2)
    side = shape(2 * DEEP, LANES)
    return call(
        functools.partial(prepare_kernel, n_lon, n_lat),
        (slots, slots, side, side, shape(2 * DEEP, cols)),
        [HBM] * 6,
        in_hbm(
            state,
            mask,
            flux_tiles.transpose(1, 0, 2),
            flux_owner.reshape(1, tiles),
            flux_row.reshape(1, tiles),
            fold_partner,
        ),
        [
            pltpu.VMEM(state.shape, F32),
            pltpu.VMEM(mask.shape, I32),
            pltpu.VMEM((tiles, wide), F32),
            pltpu.VMEM((1, tiles), I32),
            pltpu.VMEM((1, tiles), I32),
            pltpu.SMEM(fold_partner.shape, I32),
            pltpu.SemaphoreType.DMA((8,)),
        ],
        name="prepare",
    )


def level_rows(ref, row, rows):
    return jnp.concatenate([ref[k * rows + row : k * rows + row + 1, :] for k in range(DEEP)], axis=0)


def buoyancy_of(temper, saline):
    return ALPHA * temper - BETA * saline


def edge_rows(state_ref, mask_ref, out_ref, rows, near, far):
    for f in range(5):
        out_ref[2 * f] = level_rows(state_ref.at[f], near, rows)
        out_ref[2 * f + 1] = level_rows(state_ref.at[f], far, rows)
    out_ref[10] = level_rows(mask_ref, near, rows).astype(F32)


def edge_columns(state_ref, mask_ref, west_ref, east_ref):
    rows, cols = west_ref.shape[0], state_ref.shape[2]
    lane = iota((rows, LANES), 1)
    last = slice(cols - LANES, cols)
    west = jnp.zeros((rows, LANES), F32)
    east = jnp.zeros((rows, LANES), F32)
    for k in range(DEEP):
        at = slice(k * rows, (k + 1) * rows)
        for f in range(5):
            to = f * DEEP + k
            left, right = state_ref[f, at, 0:LANES], state_ref[f, at, last]
            west = jnp.where(lane == to, roll(left, to, 1), west)
            west = jnp.where(lane == FAR + to, roll(left, FAR + to - 1, 1), west)
            east = jnp.where(lane == to, roll(right, to + 1, 1), east)
            east = jnp.where(lane == FAR + to, roll(right, FAR + to + 2, 1), east)
        west = jnp.where(lane == WET + k, roll(mask_ref[at, 0:LANES].astype(F32), WET + k, 1), west)
        east = jnp.where(lane == WET + k, roll(mask_ref[at, last].astype(F32), WET + k + 1, 1), east)
    west_ref[...] = west
    east_ref[...] = east


def top_kernel(state_ref, mask_ref, prefix_ref, top_ref):
    rows, cols = prefix_ref.shape
    for slab in range(SLABS):
        if slab < 10:
            line = level_rows(state_ref.at[slab // 2], rows - 1 - slab % 2, rows)
        else:
            line = level_rows(mask_ref, rows - 1, rows).astype(F32)
        for piece in range(cols // LANES):
            top_ref[piece, slab] = line[:, piece * LANES : (piece + 1) * LANES]
    top_ref[:, CORNERS] = jnp.zeros((cols // LANES, DEEP, LANES), F32)
    for n in (1, 2):
        for piece in range(cols // LANES):
            top_ref[piece, CORNERS, 2 + n : 3 + n, :] = prefix_ref[rows - n : rows - n + 1, piece * LANES : (piece + 1) * LANES]


def columns_kernel(n_lat, west_ref, east_ref, prefix_ref, fold_ref, partner_ref, west_out_ref, east_out_ref):
    rows, cols = prefix_ref.shape
    lane = iota((rows, LANES), 1)
    for side, in_ref, out_ref in ((0, west_ref, west_out_ref), (1, east_ref, east_out_ref)):
        near, far = (0, 1) if side == 0 else (cols - 1, cols - 2)
        value = jnp.where(lane == ABOVE, prefix_ref[:, near : near + 1], in_ref[...])
        out_ref[0:rows, :] = jnp.where(lane == FAR + ABOVE, prefix_ref[:, far : far + 1], value)
        out_ref[rows:, :] = jnp.zeros((DEEP, LANES), F32)

    @pl.when(lax.axis_index("lat") == n_lat - 1)
    def _():
        within = partner_ref[0] & (LANES - 1)
        sub8, lane8 = iota((DEEP, LANES), 0), iota((DEEP, LANES), 1)
        col = iota((DEEP, cols + LANES), 1)
        for place, out_ref in ((cols + within, west_out_ref), (within + 1, east_out_ref)):
            line = jnp.zeros((DEEP, LANES), F32)
            for slab in (0, 2, 4, 6, 8, CORNERS):
                line_there = jnp.concatenate([fold_ref[piece, slab] for piece in range(fold_ref.shape[0])], axis=1)
                cell = jnp.sum(jnp.where(col == place, line_there, 0.0), axis=1, keepdims=True)
                here = (lane8 == ABOVE) & (sub8 == 3) if slab == CORNERS else lane8 == (slab // 2) * DEEP + sub8
                line = jnp.where(here, -cell if slab < 4 else cell, line)
            out_ref[rows : rows + 1, :] = jnp.sum(line, axis=0, keepdims=True)


def corner_slab(out_ref, prefix_ref, turn_ref, from_west_ref, from_east_ref, near, far):
    out_ref[CORNERS] = jnp.full(out_ref.shape[1:], turn_ref[near], F32)
    out_ref[CORNERS, 0:1, 0:LANES] = from_west_ref[near : near + 1, :]
    out_ref[CORNERS, 1:2, 0:LANES] = from_east_ref[near : near + 1, :]
    out_ref[CORNERS, 3:4, :] = prefix_ref[near : near + 1, :]
    out_ref[CORNERS, 4:5, :] = prefix_ref[far : far + 1, :]


def rows_kernel(state_ref, mask_ref, prefix_ref, turn_ref, from_west_ref, from_east_ref, pair_ref, cross_ref):
    rows = prefix_ref.shape[0]
    odd = lax.rem(lax.axis_index("lat"), 2) == 1

    def fill(out_ref, near, far):
        edge_rows(state_ref, mask_ref, out_ref, rows, near, far)
        corner_slab(out_ref, prefix_ref, turn_ref, from_west_ref, from_east_ref, near, far)

    @pl.when(odd)
    def _():
        fill(pair_ref, 0, 1)
        fill(cross_ref, rows - 1, rows - 2)

    @pl.when(jnp.logical_not(odd))
    def _():
        fill(pair_ref, rows - 1, rows - 2)
        fill(cross_ref, 0, 1)


def around(value, west, east, south, north):
    rows, cols = value.shape
    row, col = iota((rows, cols), 0), iota((rows, cols), 1)
    return (
        jnp.where(col == cols - 1, east, roll(value, -1, 1)),
        jnp.where(col == 0, west, roll(value, 1, 1)),
        jnp.where(row == rows - 1, north, roll(value, -1, 0)),
        jnp.where(row == 0, south, roll(value, 1, 0)),
    )


def advanced(values, sides, wet, turn, pressed, heat=None):
    zonal, merid = values[0], values[1]
    sums = [(e + w) + (n + s) for e, w, n, s in sides]
    across = [(e - w, n - s) for e, w, n, s in sides]
    press_x, press_y = pressed(
        0.5 * buoyancy_of(across[2][0], across[3][0]), 0.5 * buoyancy_of(across[2][1], across[3][1])
    )
    out = []
    carry_x, carry_y = (0.5 * ADVECT) * zonal, (0.5 * ADVECT) * merid
    for f in range(5):
        spread = (VISCOUS if f < 2 else DIFFUSE) * (sums[f] - 4.0 * values[f])
        if f == 0:
            trend = spread + (turn * merid - press_x)
        elif f == 1:
            trend = spread - (turn * zonal + press_y)
        else:
            trend = spread - (carry_x * across[f][0] + carry_y * across[f][1])
        new = values[f] + wet * trend
        out.append(new if heat is None or f < 2 else new + heat[f - 2])
    return out


class Tiles:
    def __init__(self, grid, west=None, east=None, south=None, north=None):
        self.grid, self.ghosts, self.turned = grid, (west, east, south, north), {}
        self.lane, self.sub = iota((DEEP, LANES), 1), iota((DEEP, LANES), 0)

    def rolled(self, r, j, shift, axis):
        at = (r, j, shift, axis)
        if at not in self.turned:
            self.turned[at] = roll(self.grid[r][j], shift, axis)
        return self.turned[at]

    def side(self, r, j, shift, axis):
        here = self.rolled(r, j, shift, axis)
        r_from, j_from = (r, j - shift) if axis else (r - shift, j)
        edge = (0 if shift == 1 else LANES - 1) if axis else (0 if shift == 1 else DEEP - 1)
        if 0 <= r_from < len(self.grid) and 0 <= j_from < len(self.grid[0]):
            other = self.rolled(r_from, j_from, shift, axis)
        else:
            ghost = self.ghosts[(0 if shift == 1 else 1) + (0 if axis else 2)]
            if ghost is None:
                return here
            other = ghost[r if axis else j]
        return jnp.where((self.lane if axis else self.sub) == edge, other, here)

    def around(self, r, j):
        return self.side(r, j, -1, 1), self.side(r, j, 1, 1), self.side(r, j, -1, 0), self.side(r, j, 1, 0)


def tile(r, j, k, rows):
    return slice(k * rows + r * DEEP, k * rows + (r + 1) * DEEP), slice(j * LANES, (j + 1) * LANES)


def turn_column(turn_ref, rows):
    row = iota((rows, LANES), 0)
    column = jnp.zeros((rows, LANES), F32)
    for j in range(rows):
        column = jnp.where(row == j, turn_ref[j], column)
    return column


def mirrored(value, width):
    back = LANES - 1 - iota((value.shape[0], LANES), 1)
    blocks = [
        jnp.take_along_axis(value[:, begin : begin + LANES], back, axis=1)
        for begin in range(width - LANES, -1, -LANES)
    ]
    return jnp.concatenate(blocks, axis=1)


def scan_down(value):
    row = iota(value.shape, 0)
    for step in (1, 2, 4):
        value = value + jnp.where(row >= step, roll(value, step, 0), 0.0)
    return value


def scan_lanes(value):
    lane = iota(value.shape, 1) & 7
    for step in (1, 2, 4):
        value = value + jnp.where(lane >= step, roll(value, step, 1), 0.0)
    return value


def lanes_between(value, begin, end):
    lane = iota(value.shape, 1)
    return jnp.where((lane >= begin) & (lane < end), value, 0.0)


def buoyancy_sum(column):
    here = lanes_between(buoyancy_of(roll(column, -16, 1), roll(column, -24, 1)), 0, 8)
    return jnp.sum(here, axis=1, keepdims=True)


def inside_kernel(state_ref, mask_ref, turn_ref, share_ref, new_ref, sums_ref):
    rows, cols = sums_ref.shape[0], state_ref.shape[2]
    n_r, n_j = rows // DEEP, cols // LANES
    turn = turn_column(turn_ref, rows)
    grid = [(r, j) for r in range(n_r) for j in range(n_j)]
    zero = jnp.zeros((DEEP, LANES), F32)
    run = {at: [zero] * 4 for at in grid}
    for k in range(DEEP):
        fields = [Tiles([[state_ref[(f, *tile(r, j, k, rows))] for j in range(n_j)] for r in range(n_r)]) for f in range(5)]
        for r, j in grid:
            at = tile(r, j, k, rows)
            above_x, above_y, total, absorbed = run[r, j]
            slopes = []

            def pressed(x, y):
                slopes.extend((x, y))
                return PRESS * (above_x + 0.5 * x), PRESS * (above_y + 0.5 * y)

            values = [field.grid[r][j] for field in fields]
            wet = mask_ref[at].astype(F32)
            new = advanced(
                values, [field.around(r, j) for field in fields], wet, turn[r * DEEP : (r + 1) * DEEP, 0:1], pressed
            )
            for f in range(5):
                new_ref[(f, *at)] = new[f]
            run[r, j] = [
                above_x + slopes[0],
                above_y + slopes[1],
                total + buoyancy_of(new[2], new[3]),
                absorbed + wet * share_ref[k],
            ]
    for r, j in grid:
        for kind in range(2):
            at = slice(kind * cols + j * LANES, kind * cols + (j + 1) * LANES)
            sums_ref[r * DEEP : (r + 1) * DEEP, at] = run[r, j][2 + kind]


def rim_kernel(
    n_lat, state_ref, mask_ref, prefix_ref, turn_ref, share_ref, partner_ref, own_west_ref, own_east_ref,
    from_west_ref, from_east_ref, pair_ref, cross_ref, fold_ref, inside_ref, ring_rows_ref, ring_cols_ref,
    edge_rows_ref, edge_cols_ref, sums_ref, south_ref, north_ref,
):
    rows, cols = prefix_ref.shape
    lat = lax.axis_index("lat")
    odd = lax.rem(lat, 2) == 1
    within = partner_ref[0] & (LANES - 1)
    at_top = lat == n_lat - 1

    @pl.when(odd)
    def _():
        south_ref[...] = pair_ref[...]

    @pl.when(jnp.logical_not(odd))
    def _():
        north_ref[...] = pair_ref[...]

    @pl.when(jnp.logical_not(odd) & (lat > 0))
    def _():
        south_ref[...] = cross_ref[...]

    @pl.when(odd & (lat < n_lat - 1))
    def _():
        north_ref[...] = cross_ref[...]

    @pl.when(lat == 0)
    def _():
        edge_rows(state_ref, mask_ref, south_ref, rows, 0, 0)
        corner_slab(south_ref, prefix_ref, turn_ref, from_west_ref, from_east_ref, 0, 0)

    sub8, lane8 = iota((DEEP, LANES), 0), iota((DEEP, LANES), 1)

    @pl.when(at_top)
    def _():
        for slab in range(SLABS + 1):
            row = jnp.concatenate([fold_ref[piece, slab] for piece in range(fold_ref.shape[0])], axis=1)
            row = pltpu.roll(row, cols + LANES - 1 - within, 1)
            if slab < 4:
                row = -row
            north_ref[slab] = mirrored(row, cols)
        north_ref[CORNERS, 0:1, 0:LANES] = from_west_ref[rows : rows + 1, :]
        north_ref[CORNERS, 1:2, 0:LANES] = from_east_ref[rows : rows + 1, :]
        north_ref[CORNERS, 2:3, :] = jnp.full((1, cols), turn_ref[rows - 1], F32)

    wide = cols + LANES
    sums_ref[rows:, :] = jnp.zeros((DEEP, 2 * wide), F32)
    for kind in range(2):
        sums_ref[0:rows, kind * wide : kind * wide + cols] = inside_ref[:, kind * cols : (kind + 1) * cols]

    share_down = jnp.zeros((DEEP, LANES), F32)
    for k in range(DEEP):
        share_down = jnp.where(sub8 == k, share_ref[k], share_down)

    def down(line, f):
        return jnp.sum(jnp.where(lane8 == f * DEEP + sub8, line, 0.0), axis=1, keepdims=True)

    def row_step(near, south, north, west_line, east_line, wet, turn, above, above_south, above_north):
        col = iota((DEEP, cols), 1)
        sides = [
            (
                jnp.where(col == cols - 1, down(east_line, f), roll(near[f], -1, 1)),
                jnp.where(col == 0, down(west_line, f), roll(near[f], 1, 1)),
                north[f],
                south[f],
            )
            for f in range(5)
        ]
        east = jnp.where(col[0:1] == cols - 1, east_line[:, ABOVE : ABOVE + 1], roll(above, -1, 1))
        west = jnp.where(col[0:1] == 0, west_line[:, ABOVE : ABOVE + 1], roll(above, 1, 1))
        above_x, above_y = 0.5 * (east - west), 0.5 * (above_north - above_south)

        def pressed(x, y):
            return PRESS * (above_x + scan_down(x) - 0.5 * x), PRESS * (above_y + scan_down(y) - 0.5 * y)

        return advanced(near, sides, wet, turn, pressed)

    for side, ghost_ref, edge, inner in ((0, south_ref, 0, 1), (1, north_ref, rows - 1, rows - 2)):
        near = [ghost_ref[2 * f] for f in range(5)]
        far = [ghost_ref[2 * f + 1] for f in range(5)]
        own = [level_rows(state_ref.at[f], edge, rows) for f in range(5)]
        own_next = [level_rows(state_ref.at[f], inner, rows) for f in range(5)]
        ring_wet = ghost_ref[10]
        corners = ghost_ref[CORNERS, :, 0:LANES]
        above_near, above_far = ghost_ref[CORNERS, 3:4, :], ghost_ref[CORNERS, 4:5, :]
        above_own, above_next = prefix_ref[edge : edge + 1, :], prefix_ref[inner : inner + 1, :]
        outward, inward = (far, above_far), (own, above_own)
        (south, above_south), (north, above_north) = (outward, inward) if side == 0 else (inward, outward)
        ring = row_step(
            near, south, north, corners[0:1, :], corners[1:2, :], ring_wet, corners[2:3, 0:1], above_near, above_south, above_north
        )
        outward, inward = (near, above_near), (own_next, above_next)
        (south, above_south), (north, above_north) = (outward, inward) if side == 0 else (inward, outward)
        wet = level_rows(mask_ref, edge, rows).astype(F32)
        edge_line = slice(edge, edge + 1)
        new = row_step(
            own, south, north, from_west_ref[edge_line, :], from_east_ref[edge_line, :], wet, turn_ref[edge],
            above_own, above_south, above_north,
        )
        for f in range(5):
            edge_rows_ref[side, f] = new[f]
            ring_rows_ref[side, f] = jnp.where(lat == 0, new[f], ring[f]) if side == 0 else ring[f]
        ring_rows_ref[side, 5] = ring_wet
        at = slice(rows + side, rows + side + 1)
        here = buoyancy_of(ring_rows_ref[side, 2], ring_rows_ref[side, 3])
        sums_ref[at, 0:cols] = jnp.sum(here, axis=0, keepdims=True)
        sums_ref[at, wide : wide + cols] = jnp.sum(ring_wet * share_down[:, 0:1], axis=0, keepdims=True)

    row, lane = iota((rows, LANES), 0), iota((rows, LANES), 1)
    turn = turn_column(turn_ref, rows)
    share_lanes = jnp.zeros((rows, LANES), F32)
    for k in range(DEEP):
        share_lanes = jnp.where((lane & 7) == k, share_ref[k], share_lanes)

    def column_step(near, east, west, north, south):
        dx, dy = 0.5 * (east - west), 0.5 * (north - south)
        lap = (east + west) + (north + south) - 4.0 * near
        zonal, merid = lanes_between(near, 0, 8), lanes_between(near, 8, 16)
        wet = lanes_between(near, WET, WET + 8)
        wet_all = sum(roll(wet, -8 * n, 1) for n in range(2, 7))
        zonal_all = sum(roll(zonal, 8 * n, 1) for n in (2, 3, 4))
        merid_all = sum(roll(merid, 8 * n, 1) for n in (1, 2, 3))
        bx = lanes_between(buoyancy_of(roll(dx, -16, 1), roll(dx, -24, 1)), 0, 8)
        by = lanes_between(buoyancy_of(roll(dy, -8, 1), roll(dy, -16, 1)), 8, 16)
        press_x = lanes_between(PRESS * (dx[:, ABOVE : ABOVE + 1] + scan_lanes(bx) - 0.5 * bx), 0, 8)
        press_y = lanes_between(PRESS * (dy[:, ABOVE : ABOVE + 1] + scan_lanes(by) - 0.5 * by), 8, 16)
        trend = VISCOUS * lap - ADVECT * (zonal_all * dx + merid_all * dy) - press_x - press_y
        trend = trend + lanes_between(turn * roll(near, -8, 1), 0, 8) - lanes_between(turn * roll(near, 8, 1), 8, 16)
        return near + wet_all * trend, wet

    blocks = [jnp.zeros((rows, LANES), F32)] * 2
    sides = ((0, from_west_ref, own_west_ref), (1, from_east_ref, own_east_ref))
    for side, ghost_ref, own_ref in sides:
        near, own = ghost_ref[0:rows, :], own_ref[0:rows, :]
        far, own_next = roll(near, -FAR, 1), roll(own, -FAR, 1)
        north = jnp.where(row == rows - 1, north_ref[CORNERS, side : side + 1, 0:LANES], roll(near, -1, 0))
        south = jnp.where(row == 0, south_ref[CORNERS, side : side + 1, 0:LANES], roll(near, 1, 0))
        east, west = (own, far) if side == 0 else (far, own)
        new, wet = column_step(near, east, west, north, south)
        ring_cols_ref[side] = new
        blocks[0] = jnp.where(lane == side, buoyancy_sum(new), blocks[0])
        blocks[1] = jnp.where(lane == side, jnp.sum(wet * share_lanes, axis=1, keepdims=True), blocks[1])
        east, west = (own_next, near) if side == 0 else (near, own_next)
        new, _ = column_step(own, east, west, roll(own, -1, 0), roll(own, 1, 0))
        edge_cols_ref[side] = new
        column = 0 if side == 0 else cols - 1
        sums_ref[0:rows, column : column + 1] = buoyancy_sum(new)
    for kind in range(2):
        sums_ref[0:rows, kind * wide + cols : (kind + 1) * wide] = blocks[kind]
    for side, edge in ((0, 0), (1, rows - 1)):
        here = buoyancy_of(edge_rows_ref[side, 2], edge_rows_ref[side, 3])
        sums_ref[edge : edge + 1, 0:cols] = jnp.sum(here, axis=0, keepdims=True)


def flux_kernel(n_lat, mine_ref, theirs_ref, partner_ref, flux_ref, flux_rows_ref, flux_cols_ref, drive_ref):
    rows, cols = flux_ref.shape[1:]
    half_cols = cols // 2
    wide = 3 * half_cols
    mine, theirs = mine_ref[...], theirs_ref[...]
    first = lax.axis_index("lev") == 0
    halves = (jnp.where(first, mine, theirs), jnp.where(first, theirs, mine))
    at_top = lax.axis_index("lat") == n_lat - 1
    hinge = partner_ref[0]
    within = hinge - (hinge // cols) * cols

    def extra(kind, c):
        found = []
        for part in halves:
            line = jnp.concatenate(
                [part[2 * kind : 2 * kind + 1, 2 * wide :], part[2 * kind + 1 : 2 * kind + 2, 2 * wide :]], axis=1
            )
            found.append(line[:, c * half_cols : (c + 1) * half_cols])
        return jnp.concatenate(found, axis=1)

    flux, flux_south, flux_north, flux_west, flux_east = [], [], [], [], []
    crossed = jnp.zeros((DEEP, 2 * cols), F32)
    for c in range(3):
        pair = jnp.concatenate([extra(2, c), extra(1, c)], axis=1)
        crossed = jnp.where(iota(crossed.shape, 0) == c, pair, crossed)
    crossed = mirrored(pltpu.roll(crossed, 2 * cols - 1 - within, 1), cols)
    row, lane = iota((rows, LANES), 0), iota((rows, LANES), 1)
    for c in range(3):
        bands = [
            jnp.concatenate([part[:, b * wide + c * half_cols : b * wide + (c + 1) * half_cols] for part in halves], axis=1)
            for b in range(2)
        ]
        flux.append(jnp.concatenate(bands, axis=0))
        flux_south.append(extra(0, c))
        flux_north.append(jnp.where(at_top, crossed[c : c + 1, :], extra(1, c)))
        here = lane == c * 16 + row
        for side, part in ((flux_west, halves[1]), (flux_east, halves[0])):
            line = part[6:7, 2 * wide : 2 * wide + LANES]
            side.append(jnp.sum(jnp.where(here, line, 0.0), axis=1, keepdims=True))

    flux_cols = jnp.zeros((rows, LANES), F32)
    for c in range(3):
        flux_ref[c] = flux[c]
        flux_rows_ref[c : c + 1, :] = flux_south[c]
        flux_rows_ref[3 + c : 4 + c, :] = flux_north[c]
        flux_cols = jnp.where(lane == c, flux_west[c], jnp.where(lane == 3 + c, flux_east[c], flux_cols))
    flux_rows_ref[6:8, :] = jnp.zeros((2, cols), F32)
    flux_cols_ref[...] = flux_cols
    drive_ref[rows:, :] = jnp.zeros((DEEP, cols + LANES), F32)
    drive_ref[0:rows, 0:cols] = buoyancy_of(flux[0], flux[1])
    ends = jnp.zeros((rows, LANES), F32)
    for side, column, line in ((0, flux_west, flux_south), (1, flux_east, flux_north)):
        drive_ref[rows + side : rows + side + 1, 0:cols] = buoyancy_of(line[0], line[1])
        ends = jnp.where(lane == side, buoyancy_of(column[0], column[1]), ends)
    drive_ref[0:rows, cols:] = ends


def second_kernel(
    state_ref, mask_ref, prefix_ref, ring_rows_ref, ring_cols_ref, edge_rows_ref, edge_cols_ref, flux_ref, flux_rows_ref,
    flux_cols_ref, turn_ref, share_ref, out_hbm, flow_ref, tracers_ref, sem,
):
    rows, cols = flux_ref.shape[1:]
    n_r, n_j = rows // DEEP, cols // LANES
    sub8, lane8 = iota((DEEP, LANES), 0), iota((DEEP, LANES), 1)
    lane = iota((rows, LANES), 1)
    turn = turn_column(turn_ref, rows)
    share_down = jnp.zeros((DEEP, LANES), F32)
    share_lanes = jnp.zeros((rows, LANES), F32)
    for k in range(DEEP):
        share_down = jnp.where(sub8 == k, share_ref[k], share_down)
        share_lanes = jnp.where((lane & 7) == k, share_ref[k], share_lanes)

    ring_rows, ring_cols = [], []
    for side in range(2):
        taken = ring_rows_ref[side, 5] * share_down[:, 0:1]
        values = [ring_rows_ref[side, f] for f in range(2)]
        values += [ring_rows_ref[side, 2 + c] + taken * flux_rows_ref[3 * side + c : 3 * side + c + 1, :] for c in range(3)]
        ring_rows.append(values)
        found = ring_cols_ref[side]
        taken = lanes_between(found, WET, WET + 8) * share_lanes
        for c in range(3):
            found = found + roll(taken, 8 * (2 + c) - WET, 1) * flux_cols_ref[:, 3 * side + c : 3 * side + c + 1]
        ring_cols.append(found)

    grid = [(r, j) for r in range(n_r) for j in range(n_j)]

    def cut(value, r, j):
        return value[r * DEEP : (r + 1) * DEEP, j * LANES : (j + 1) * LANES]

    zero = jnp.zeros((DEEP, LANES), F32)
    run = {at: (zero, zero) for at in grid}
    prefix = Tiles([[prefix_ref[tile(r, j, 0, rows)] for j in range(n_j)] for r in range(n_r)])
    push = {}
    for at in grid:
        east, west, north, south = prefix.around(*at)
        push[at] = (0.5 * PRESS) * (east - west), (0.5 * PRESS) * (north - south)
    edge_cols = [edge_cols_ref[side] for side in range(2)]
    copies = []

    def column(value, r, n):
        return jnp.broadcast_to(value[r * DEEP : (r + 1) * DEEP, n : n + 1], (DEEP, LANES))

    for k in range(DEEP):
        wets, heats, grids = {}, {}, [[[None] * n_j for _ in range(n_r)] for _ in range(5)]
        for r, j in grid:
            at = tile(r, j, k, rows)
            wet = mask_ref[at].astype(F32)
            taken = wet * share_ref[k]
            wets[r, j] = wet
            heats[r, j] = [taken * cut(flux_ref[c], r, j) for c in range(3)]
            for f in range(5):
                value = state_ref[(f, *at)]
                if f < 2:
                    value = value - wet * push[r, j][f]
                if j == 0:
                    value = jnp.where(lane8 == 0, column(edge_cols[0], r, f * DEEP + k), value)
                if j == n_j - 1:
                    value = jnp.where(lane8 == LANES - 1, column(edge_cols[1], r, f * DEEP + k), value)
                if r == 0:
                    value = jnp.where(sub8 == 0, edge_rows_ref[0, f, k : k + 1, at[1]], value)
                if r == n_r - 1:
                    value = jnp.where(sub8 == DEEP - 1, edge_rows_ref[1, f, k : k + 1, at[1]], value)
                if f >= 2:
                    value = value + heats[r, j][f - 2]
                grids[f][r][j] = value
        fields = [
            Tiles(
                grids[f],
                [column(ring_cols[0], r, f * DEEP + k) for r in range(n_r)],
                [column(ring_cols[1], r, f * DEEP + k) for r in range(n_r)],
                [ring_rows[0][f][k : k + 1, j * LANES : (j + 1) * LANES] for j in range(n_j)],
                [ring_rows[1][f][k : k + 1, j * LANES : (j + 1) * LANES] for j in range(n_j)],
            )
            for f in range(5)
        ]
        for r, j in grid:
            at = tile(r, j, k, rows)
            over_x, over_y = run[r, j]

            def pressed(x, y):
                run[r, j] = (over_x + x, over_y + y)
                return PRESS * (over_x + 0.5 * x), PRESS * (over_y + 0.5 * y)

            new = advanced(
                [field.grid[r][j] for field in fields],
                [field.around(r, j) for field in fields],
                wets[r, j],
                turn[r * DEEP : (r + 1) * DEEP, 0:1],
                pressed,
                heats[r, j],
            )
            for f in range(5):
                if f < 2:
                    flow_ref[(f, *at)] = new[f]
                else:
                    tracers_ref[(f - 2, *at)] = new[f]
        whole = pl.ds(k * rows, rows)
        copies.append(
            pltpu.make_async_copy(tracers_ref.at[:, whole, :], out_hbm.at[pl.ds(2, 3), whole, :], sem.at[k])
        )
        copies[-1].start()
    for copy in copies:
        copy.wait()


def last_kernel(out_in_hbm, flow_ref, mask_ref, sums_ref, drive_ref, out_hbm, moved_ref, sem):
    del out_in_hbm
    rows, cols = mask_ref.shape[0] // DEEP, mask_ref.shape[1]
    wide = cols + LANES
    above = sums_ref[:, 0:wide] + sums_ref[:, wide : 2 * wide] * drive_ref[...]
    east, west, north, south = around(
        above[0:rows, 0:cols],
        above[0:rows, cols : cols + 1],
        above[0:rows, cols + 1 : cols + 2],
        above[rows : rows + 1, 0:cols],
        above[rows + 1 : rows + 2, 0:cols],
    )
    push_x, push_y = (0.5 * PRESS) * (east - west), (0.5 * PRESS) * (north - south)
    copies = []
    for k in range(DEEP):
        whole = pl.ds(k * rows, rows)
        wet = mask_ref[whole, :].astype(F32)
        moved_ref[0, whole, :] = flow_ref[0, whole, :] - wet * push_x
        moved_ref[1, whole, :] = flow_ref[1, whole, :] - wet * push_y
        copies.append(pltpu.make_async_copy(moved_ref.at[:, whole, :], out_hbm.at[pl.ds(0, 2), whole, :], sem.at[k]))
        copies[-1].start()
    for copy in copies:
        copy.wait()


def body(n_lon, n_lat, state, mask, coriolis, penetration, flux_tiles, flux_owner, flux_row, fold_partner):
    fields, levels, rows, cols = state.shape
    flat_state = state.reshape(fields, levels * rows, cols)
    flat_mask = mask.reshape(levels * rows, cols)
    last = n_lat - 1

    keep, send, west, east, total = prepare(
        flat_state, flat_mask, flux_tiles, flux_owner, flux_row, fold_partner, n_lon, n_lat
    )

    stages = []
    for axis, size, least in (("lat", n_lat, 2), ("lon", n_lon, 1)):
        bit = size // 2
        while bit >= least:
            stages.append((axis, size, bit))
            bit //= 2
    got = lax.ppermute(send, "lat", [(i, i ^ 1) for i in range(n_lat)])
    prefix = lax.ppermute(total, "lev", [(0, 1)])

    def merged(keep, got):
        half = shape(keep.shape[0] // 2, keep.shape[1])
        return call(merge_kernel, (half, half), [VMEM] * 2, (keep, got), name="merge_flux")

    def passed_on(send, stage):
        axis, size, bit = stage
        return lax.ppermute(send, axis, [(i, i ^ bit) for i in range(size)])

    near_state, near_mask = after((flat_state, flat_mask), send)
    new_state, inside = call(
        inside_kernel,
        (shape(fields, levels * rows, cols), shape(rows, 2 * cols)),
        [VMEM, VMEM, SMEM, SMEM],
        (near_state, near_mask, coriolis, penetration),
        name="first_inside",
    )
    pieces = cols // LANES
    hinge_piece = fold_partner[0] >> (LANES.bit_length() - 1)
    keep = after(keep, (prefix, hinge_piece, inside))
    keep, send = merged(keep, got)
    got = passed_on(send, stages[0])

    top_shape = shape(pieces, SLABS + 1, DEEP, LANES)
    top = call(top_kernel, top_shape, [VMEM] * 3, (flat_state, flat_mask, prefix), name="top_rows")
    top = after(top, send)

    def folded(hinge_piece):
        block, piece = divmod(hinge_piece, pieces)

        def swap(rows_out):
            def across(part, other):
                pairs = [(a * n_lat + last, (other - a) % n_lon * n_lat + last) for a in range(n_lon)]
                return lax.ppermute(part, ("lon", "lat"), pairs)

            return jnp.concatenate([across(rows_out[piece:], block - 1), across(rows_out[: piece + 1], block)], axis=0)

        return swap

    fold = lax.switch(hinge_piece, [folded(n) for n in range(n_lon * pieces)], top)
    keep = after(keep, fold)
    keep, send = merged(keep, got)
    got = passed_on(send, stages[1])

    west, east = after((west, east), send)
    side = shape(rows + DEEP, LANES)
    west, east = call(
        functools.partial(columns_kernel, n_lat),
        (side, side),
        [VMEM] * 4 + [SMEM],
        (west, east, prefix, fold, fold_partner),
        name="edge_columns",
    )
    from_west = lax.ppermute(east, "lon", [(i, (i + 1) % n_lon) for i in range(n_lon)])
    from_east = lax.ppermute(west, "lon", [((i + 1) % n_lon, i) for i in range(n_lon)])
    keep = after(keep, (from_west, from_east))
    for stage in stages[2:]:
        keep, send = merged(keep, got)
        got = passed_on(send, stage)

    message = shape(SLABS + 1, DEEP, cols)
    from_west, from_east = after((from_west, from_east), send)
    pair, cross = call(
        rows_kernel,
        (message, message),
        [VMEM, VMEM, VMEM, SMEM, VMEM, VMEM],
        (flat_state, flat_mask, prefix, coriolis, from_west, from_east),
        name="edge_rows",
    )
    from_pair = lax.ppermute(pair, "lat", [(i, i ^ 1) for i in range(n_lat)])
    from_cross = lax.ppermute(cross, "lat", [(i, i + 1 if i % 2 else i - 1) for i in range(1, last)])
    keep = after(keep, (from_pair, from_cross))
    mine = keep + got
    theirs = lax.ppermute(mine, "lev", [(0, 1), (1, 0)])

    inside = after(inside, mine)
    wide = cols + LANES
    *ring, sums = call(
        functools.partial(rim_kernel, n_lat),
        (
            shape(2, 6, DEEP, cols),
            shape(2, rows, LANES),
            shape(2, 5, DEEP, cols),
            shape(2, rows, LANES),
            shape(rows + DEEP, 2 * wide),
        ),
        [VMEM, VMEM, VMEM, SMEM, SMEM, SMEM] + [VMEM] * 8,
        (
            flat_state, flat_mask, prefix, coriolis, penetration, fold_partner, west, east, from_west, from_east, from_pair,
            from_cross, fold, inside,
        ),
        [pltpu.VMEM((SLABS + 1, DEEP, cols), F32), pltpu.VMEM((SLABS + 1, DEEP, cols), F32)],
        name="first_rim",
    )
    sums = lax.ppermute(after(sums, theirs), "lev", [(0, 1)])
    *flux, drive = call(
        functools.partial(flux_kernel, n_lat),
        (shape(3, rows, cols), shape(DEEP, cols), shape(rows, LANES), shape(rows + DEEP, wide)),
        [VMEM] * 2 + [SMEM],
        (mine, theirs, fold_partner),
        name="flux_parts",
    )

    out = jax.ShapeDtypeStruct(flat_state.shape, F32)
    result, flow = call(
        second_kernel,
        (out, shape(2, levels * rows, cols)),
        [VMEM] * 10 + [SMEM] * 2,
        (new_state, flat_mask, prefix, *ring, *flux, coriolis, penetration),
        [pltpu.VMEM((3, levels * rows, cols), F32), pltpu.SemaphoreType.DMA((DEEP,))],
        name="second_substep",
        out_specs=(ANY, VMEM),
    )
    result = call(
        last_kernel,
        out,
        [ANY] + [VMEM] * 4,
        (result, flow, flat_mask, sums, drive),
        [pltpu.VMEM((2, levels * rows, cols), F32), pltpu.SemaphoreType.DMA((DEEP,))],
        name="deeper_pressure",
        out_specs=ANY,
        aliases={0: 0},
    )
    return result.reshape(fields, levels, rows, cols)


def solution(mesh):
    n_lon, n_lat = mesh.shape["lon"], mesh.shape["lat"]
    assert mesh.shape["lev"] == 2 and n_lat % 2 == 0 and n_lon > 2
    return jax.shard_map(
        functools.partial(body, n_lon, n_lat),
        mesh=mesh,
        in_specs=(
            P(None, "lev", "lat", "lon"),
            P("lev", "lat", "lon"),
            P("lat"),
            P("lev"),
            P(("lon", "lat"), None, None),
            P(("lon", "lat"), None),
            P(("lon", "lat")),
            P(),
        ),
        out_specs=P(None, "lev", "lat", "lon"),
        check_vma=False,
    )
```

```python
import functools

import jax
import jax.numpy as jnp
from jax import lax
from jax.experimental import pallas as pl
from jax.experimental.pallas import tpu as pltpu
from jax.sharding import PartitionSpec as P

ALPHA = 0.2
BETA = 0.15
PRESS = 0.1
VISCOUS = 0.1
DIFFUSE = 0.1
ADVECT = 0.1

F32 = jnp.float32
I32 = jnp.int32
LANES = 128
DEEP = 8
FAR = 64
WET = 48
ABOVE = 56
SLABS = 11
CORNERS = SLABS
VMEM_BYTES = 16 * 1024 * 1024

VMEM = pl.BlockSpec(memory_space=pltpu.VMEM)
SMEM = pl.BlockSpec(memory_space=pltpu.SMEM)
ANY = pl.BlockSpec(memory_space=pl.ANY)
HBM = pl.BlockSpec(memory_space=pltpu.HBM)


def iota(shape, dim):
    return lax.broadcasted_iota(I32, shape, dim)


def roll(value, shift, axis):
    return pltpu.roll(value, shift % value.shape[axis], axis)


def call(kernel, out_shape, in_specs, args, scratch=(), name=None, out_specs=None, aliases=None):
    return pl.pallas_call(
        kernel,
        out_shape=out_shape,
        in_specs=in_specs,
        out_specs=out_specs or jax.tree.map(lambda _: VMEM, out_shape),
        input_output_aliases=aliases or {},
        scratch_shapes=list(scratch),
        compiler_params=pltpu.CompilerParams(vmem_limit_bytes=VMEM_BYTES),
        name=name,
    )(*args)


def after(values, *others):
    return lax.optimization_barrier((values, others))[0]


def shape(*dims):
    return pltpu.VMEM(dims, F32)


def in_hbm(*arrays):
    return tuple(pltpu.with_memory_space_constraint(array, pltpu.HBM) for array in arrays)


def prepare_kernel(
    n_lon, n_lat, state_hbm, mask_hbm, tiles_hbm, owner_hbm, row_hbm, partner_hbm, keep_ref, send_ref, west_ref, east_ref,
    total_ref, state_ref, mask_ref, x_ref, owners_ref, rows_ref, hinge_ref, sem,
):
    tiles, cols = tiles_hbm.shape[1], tiles_hbm.shape[2]
    half_cols = cols // 2
    rows = 2 * DEEP
    n_y = n_lat // 2
    half = lax.axis_index("lev")
    lat = lax.axis_index("lat")
    core = lax.rem(lat, 2)
    begin = pl.multiple_of(half * half_cols, LANES)
    indices = [
        pltpu.make_async_copy(owner_hbm, owners_ref, sem.at[0]),
        pltpu.make_async_copy(row_hbm, rows_ref, sem.at[1]),
        pltpu.make_async_copy(partner_hbm, hinge_ref, sem.at[2]),
    ]
    fluxes = [
        pltpu.make_async_copy(
            tiles_hbm.at[c, :, pl.ds(begin, half_cols)], x_ref.at[:, pl.ds(c * half_cols, half_cols)], sem.at[3 + c]
        )
        for c in range(3)
    ]
    fields = [
        pltpu.make_async_copy(state_hbm, state_ref, sem.at[6]),
        pltpu.make_async_copy(mask_hbm, mask_ref, sem.at[7]),
    ]
    for copy in indices + fluxes + fields:
        copy.start()
    for copy in indices:
        copy.wait()

    key = owners_ref[...] * rows + rows_ref[...]
    hinge_block = hinge_ref[0] // cols
    slots = keep_ref.shape[0]
    slot = iota((slots, tiles), 0)
    group, sub = slot >> 3, slot & 7
    at_y = (group >> (n_lon.bit_length() - 1)) ^ (lat // 2)
    at_lon = (group & (n_lon - 1)) ^ lax.axis_index("lon")

    def wrapped(lon):
        return jnp.where(lon < 0, lon + n_lon, jnp.where(lon >= n_lon, lon - n_lon, lon))

    def one_hot(hit):
        return jnp.where(hit, 1.0, 0.0).astype(jnp.bfloat16)

    def weights(to_core):
        lat = 2 * at_y + to_core
        owner = at_lon * n_lat + lat
        last = lat == n_lat - 1
        top = n_lat * rows - 1
        south = jnp.where(lat == 0, owner * rows, owner * rows - 1)
        north = jnp.where(last, wrapped(hinge_block - at_lon) * (n_lat * rows) + top, (owner + 1) * rows)
        third = jnp.where(last, wrapped(hinge_block - at_lon - 1) * (n_lat * rows) + top, -1)
        kind = sub >> 1
        extra_key = jnp.where(kind == 0, south, jnp.where(kind == 1, north, jnp.where(kind == 2, third, -1)))
        extra = key == extra_key
        beside = wrapped(at_lon + 1 - 2 * half) * n_lat + lat
        return (
            one_hot(key == owner * rows + sub),
            one_hot(key == owner * rows + DEEP + sub),
            one_hot(extra & ((sub & 1) == 0)),
            one_hot(extra & ((sub & 1) == 1)),
            one_hot(((key >> 4) == beside) & (sub == 6)),
        )

    def split(x):
        first = x.astype(jnp.bfloat16)
        rest = x - first.astype(F32)
        second = rest.astype(jnp.bfloat16)
        third = (rest - second.astype(F32)).astype(jnp.bfloat16)
        return first, second, third

    square = iota((tiles, tiles), 0) == iota((tiles, tiles), 1)
    row_of = jnp.sum(jnp.where(square, (key & (rows - 1)).astype(F32), 0.0), axis=1, keepdims=True).astype(I32)

    for copy in fluxes:
        copy.wait()
    x = x_ref[...]
    lane = iota((tiles, LANES), 1)
    edge = jnp.zeros((tiles, LANES), F32)
    for c in range(3):
        begin = c * half_cols
        value = jnp.where(half == 0, x[:, begin : begin + 1], x[:, begin + half_cols - 1 : begin + half_cols])
        edge = jnp.where(((lane >> 4) == c) & ((lane & 15) == row_of), value, edge)
    parts, edges = split(x), split(edge)
    wide = 3 * half_cols
    quarter = wide // 2

    def dot(hot, terms, begin, end):
        products = [
            jnp.dot(hot, term[:, begin:end], preferred_element_type=F32) for term in reversed(terms)
        ]
        return products[0] + products[1] + products[2]

    for out_ref, to_core in ((keep_ref, core), (send_ref, 1 - core)):
        low, high, even, odd, ring = weights(to_core)
        out_ref[:, 0:wide] = dot(low, parts, 0, wide)
        out_ref[:, wide : 2 * wide] = dot(high, parts, 0, wide)
        rest = dot(even, parts, 0, quarter) + dot(odd, parts, quarter, wide)
        beside = dot(ring, edges, 0, LANES)
        out_ref[:, 2 * wide : 2 * wide + LANES] = rest[:, 0:LANES] + beside
        out_ref[:, 2 * wide + LANES :] = rest[:, LANES:]

    for copy in fields:
        copy.wait()
    total = jnp.zeros(total_ref.shape, F32)
    for k in range(DEEP):
        at = slice(k * rows, (k + 1) * rows)
        total = total + buoyancy_of(state_ref[2, at, :], state_ref[3, at, :])
    total_ref[...] = total
    edge_columns(state_ref, mask_ref, west_ref, east_ref)


def merge_kernel(kept_ref, got_ref, keep_ref, send_ref):
    half = keep_ref.shape[0]
    send_ref[...] = kept_ref[half:, :] + got_ref[half:, :]
    keep_ref[...] = kept_ref[0:half, :] + got_ref[0:half, :]


def prepare(state, mask, flux_tiles, flux_owner, flux_row, fold_partner, n_lon, n_lat):
    tiles, _, cols = flux_tiles.shape
    wide = 3 * (cols // 2)
    slots = shape(n_lon * n_lat // 2 * DEEP, 2 * wide + wide // 2)
    side = shape(2 * DEEP, LANES)
    return call(
        functools.partial(prepare_kernel, n_lon, n_lat),
        (slots, slots, side, side, shape(2 * DEEP, cols)),
        [HBM] * 6,
        in_hbm(
            state,
            mask,
            flux_tiles.transpose(1, 0, 2),
            flux_owner.reshape(1, tiles),
            flux_row.reshape(1, tiles),
            fold_partner,
        ),
        [
            pltpu.VMEM(state.shape, F32),
            pltpu.VMEM(mask.shape, I32),
            pltpu.VMEM((tiles, wide), F32),
            pltpu.VMEM((1, tiles), I32),
            pltpu.VMEM((1, tiles), I32),
            pltpu.SMEM(fold_partner.shape, I32),
            pltpu.SemaphoreType.DMA((8,)),
        ],
        name="prepare",
    )


def level_rows(ref, row, rows):
    return jnp.concatenate([ref[k * rows + row : k * rows + row + 1, :] for k in range(DEEP)], axis=0)


def buoyancy_of(temper, saline):
    return ALPHA * temper - BETA * saline


def edge_rows(state_ref, mask_ref, out_ref, rows, near, far):
    for f in range(5):
        out_ref[2 * f] = level_rows(state_ref.at[f], near, rows)
        out_ref[2 * f + 1] = level_rows(state_ref.at[f], far, rows)
    out_ref[10] = level_rows(mask_ref, near, rows).astype(F32)


def edge_columns(state_ref, mask_ref, west_ref, east_ref):
    rows, cols = west_ref.shape[0], state_ref.shape[2]
    lane = iota((rows, LANES), 1)
    last = slice(cols - LANES, cols)
    west = jnp.zeros((rows, LANES), F32)
    east = jnp.zeros((rows, LANES), F32)
    for k in range(DEEP):
        at = slice(k * rows, (k + 1) * rows)
        for f in range(5):
            to = f * DEEP + k
            left, right = state_ref[f, at, 0:LANES], state_ref[f, at, last]
            west = jnp.where(lane == to, roll(left, to, 1), west)
            west = jnp.where(lane == FAR + to, roll(left, FAR + to - 1, 1), west)
            east = jnp.where(lane == to, roll(right, to + 1, 1), east)
            east = jnp.where(lane == FAR + to, roll(right, FAR + to + 2, 1), east)
        west = jnp.where(lane == WET + k, roll(mask_ref[at, 0:LANES].astype(F32), WET + k, 1), west)
        east = jnp.where(lane == WET + k, roll(mask_ref[at, last].astype(F32), WET + k + 1, 1), east)
    west_ref[...] = west
    east_ref[...] = east


def top_kernel(own_north_ref, prefix_ref, top_ref):
    rows, cols = prefix_ref.shape
    for piece in range(cols // LANES):
        top_ref[piece, 0:SLABS] = own_north_ref[:, :, piece * LANES : (piece + 1) * LANES]
    top_ref[:, CORNERS] = jnp.zeros((cols // LANES, DEEP, LANES), F32)
    for n in (1, 2):
        for piece in range(cols // LANES):
            top_ref[piece, CORNERS, 2 + n : 3 + n, :] = prefix_ref[rows - n : rows - n + 1, piece * LANES : (piece + 1) * LANES]


def columns_kernel(n_lat, west_ref, east_ref, prefix_ref, fold_ref, partner_ref, west_out_ref, east_out_ref):
    rows, cols = prefix_ref.shape
    lane = iota((rows, LANES), 1)
    for side, in_ref, out_ref in ((0, west_ref, west_out_ref), (1, east_ref, east_out_ref)):
        near, far = (0, 1) if side == 0 else (cols - 1, cols - 2)
        value = jnp.where(lane == ABOVE, prefix_ref[:, near : near + 1], in_ref[...])
        out_ref[0:rows, :] = jnp.where(lane == FAR + ABOVE, prefix_ref[:, far : far + 1], value)
        out_ref[rows:, :] = jnp.zeros((DEEP, LANES), F32)

    @pl.when(lax.axis_index("lat") == n_lat - 1)
    def _():
        within = partner_ref[0] & (LANES - 1)
        sub8, lane8 = iota((DEEP, LANES), 0), iota((DEEP, LANES), 1)
        col = iota((DEEP, cols + LANES), 1)
        for place, out_ref in ((cols + within, west_out_ref), (within + 1, east_out_ref)):
            line = jnp.zeros((DEEP, LANES), F32)
            for slab in (0, 2, 4, 6, 8, CORNERS):
                line_there = jnp.concatenate([fold_ref[piece, slab] for piece in range(fold_ref.shape[0])], axis=1)
                cell = jnp.sum(jnp.where(col == place, line_there, 0.0), axis=1, keepdims=True)
                here = (lane8 == ABOVE) & (sub8 == 3) if slab == CORNERS else lane8 == (slab // 2) * DEEP + sub8
                line = jnp.where(here, -cell if slab < 4 else cell, line)
            out_ref[rows : rows + 1, :] = jnp.sum(line, axis=0, keepdims=True)


def corner_slab(out_ref, prefix_ref, turn_ref, from_west_ref, from_east_ref, near, far):
    out_ref[CORNERS] = jnp.full(out_ref.shape[1:], turn_ref[near], F32)
    out_ref[CORNERS, 0:1, 0:LANES] = from_west_ref[near : near + 1, :]
    out_ref[CORNERS, 1:2, 0:LANES] = from_east_ref[near : near + 1, :]
    out_ref[CORNERS, 3:4, :] = prefix_ref[near : near + 1, :]
    out_ref[CORNERS, 4:5, :] = prefix_ref[far : far + 1, :]


def rows_kernel(own_south_ref, own_north_ref, prefix_ref, turn_ref, from_west_ref, from_east_ref, pair_ref, cross_ref):
    rows = prefix_ref.shape[0]
    odd = lax.rem(lax.axis_index("lat"), 2) == 1

    def fill(out_ref, near, far):
        out_ref[0:SLABS] = (own_south_ref if near == 0 else own_north_ref)[...]
        corner_slab(out_ref, prefix_ref, turn_ref, from_west_ref, from_east_ref, near, far)

    @pl.when(odd)
    def _():
        fill(pair_ref, 0, 1)
        fill(cross_ref, rows - 1, rows - 2)

    @pl.when(jnp.logical_not(odd))
    def _():
        fill(pair_ref, rows - 1, rows - 2)
        fill(cross_ref, 0, 1)


def around(value, west, east, south, north):
    rows, cols = value.shape
    row, col = iota((rows, cols), 0), iota((rows, cols), 1)
    return (
        jnp.where(col == cols - 1, east, roll(value, -1, 1)),
        jnp.where(col == 0, west, roll(value, 1, 1)),
        jnp.where(row == rows - 1, north, roll(value, -1, 0)),
        jnp.where(row == 0, south, roll(value, 1, 0)),
    )


def advanced(values, sides, wet, turn, pressed, heat=None):
    zonal, merid = values[0], values[1]
    sums = [(e + w) + (n + s) for e, w, n, s in sides]
    across = [(e - w, n - s) for e, w, n, s in sides]
    press_x, press_y = pressed(
        0.5 * buoyancy_of(across[2][0], across[3][0]), 0.5 * buoyancy_of(across[2][1], across[3][1])
    )
    out = []
    carry_x, carry_y = (0.5 * ADVECT) * zonal, (0.5 * ADVECT) * merid
    for f in range(5):
        spread = (VISCOUS if f < 2 else DIFFUSE) * (sums[f] - 4.0 * values[f])
        if f == 0:
            trend = spread + (turn * merid - press_x)
        elif f == 1:
            trend = spread - (turn * zonal + press_y)
        else:
            trend = spread - (carry_x * across[f][0] + carry_y * across[f][1])
        new = values[f] + wet * trend
        out.append(new if heat is None or f < 2 else new + heat[f - 2])
    return out


class Tiles:
    def __init__(self, grid, west=None, east=None, south=None, north=None):
        self.grid, self.ghosts, self.turned = grid, (west, east, south, north), {}
        self.lane, self.sub = iota((DEEP, LANES), 1), iota((DEEP, LANES), 0)

    def rolled(self, r, j, shift, axis):
        at = (r, j, shift, axis)
        if at not in self.turned:
            self.turned[at] = roll(self.grid[r][j], shift, axis)
        return self.turned[at]

    def side(self, r, j, shift, axis):
        here = self.rolled(r, j, shift, axis)
        r_from, j_from = (r, j - shift) if axis else (r - shift, j)
        edge = (0 if shift == 1 else LANES - 1) if axis else (0 if shift == 1 else DEEP - 1)
        if 0 <= r_from < len(self.grid) and 0 <= j_from < len(self.grid[0]):
            other = self.rolled(r_from, j_from, shift, axis)
        else:
            ghost = self.ghosts[(0 if shift == 1 else 1) + (0 if axis else 2)]
            if ghost is None:
                return here
            other = ghost[r if axis else j]
        return jnp.where((self.lane if axis else self.sub) == edge, other, here)

    def around(self, r, j):
        return self.side(r, j, -1, 1), self.side(r, j, 1, 1), self.side(r, j, -1, 0), self.side(r, j, 1, 0)


def tile(r, j, k, rows):
    return slice(k * rows + r * DEEP, k * rows + (r + 1) * DEEP), slice(j * LANES, (j + 1) * LANES)


def turn_column(turn_ref, rows):
    row = iota((rows, LANES), 0)
    column = jnp.zeros((rows, LANES), F32)
    for j in range(rows):
        column = jnp.where(row == j, turn_ref[j], column)
    return column


def mirrored(value, width):
    back = LANES - 1 - iota((value.shape[0], LANES), 1)
    blocks = [
        jnp.take_along_axis(value[:, begin : begin + LANES], back, axis=1)
        for begin in range(width - LANES, -1, -LANES)
    ]
    return jnp.concatenate(blocks, axis=1)


def scan_down(value):
    row = iota(value.shape, 0)
    for step in (1, 2, 4):
        value = value + jnp.where(row >= step, roll(value, step, 0), 0.0)
    return value


def scan_lanes(value):
    lane = iota(value.shape, 1) & 7
    for step in (1, 2, 4):
        value = value + jnp.where(lane >= step, roll(value, step, 1), 0.0)
    return value


def lanes_between(value, begin, end):
    lane = iota(value.shape, 1)
    return jnp.where((lane >= begin) & (lane < end), value, 0.0)


def buoyancy_sum(column):
    here = lanes_between(buoyancy_of(roll(column, -16, 1), roll(column, -24, 1)), 0, 8)
    return jnp.sum(here, axis=1, keepdims=True)


def inside_kernel(state_ref, mask_ref, turn_ref, share_ref, new_ref, sums_ref, south_ref, north_ref):
    rows, cols = sums_ref.shape[0], state_ref.shape[2]
    n_r, n_j = rows // DEEP, cols // LANES
    edge_rows(state_ref, mask_ref, south_ref, rows, 0, 1)
    edge_rows(state_ref, mask_ref, north_ref, rows, rows - 1, rows - 2)
    turn = turn_column(turn_ref, rows)
    grid = [(r, j) for r in range(n_r) for j in range(n_j)]
    zero = jnp.zeros((DEEP, LANES), F32)
    run = {at: [zero] * 4 for at in grid}
    for k in range(DEEP):
        fields = [Tiles([[state_ref[(f, *tile(r, j, k, rows))] for j in range(n_j)] for r in range(n_r)]) for f in range(5)]
        for r, j in grid:
            at = tile(r, j, k, rows)
            above_x, above_y, total, absorbed = run[r, j]
            slopes = []

            def pressed(x, y):
                slopes.extend((x, y))
                return PRESS * (above_x + 0.5 * x), PRESS * (above_y + 0.5 * y)

            values = [field.grid[r][j] for field in fields]
            wet = mask_ref[at].astype(F32)
            new = advanced(
                values, [field.around(r, j) for field in fields], wet, turn[r * DEEP : (r + 1) * DEEP, 0:1], pressed
            )
            for f in range(5):
                new_ref[(f, *at)] = new[f]
            run[r, j] = [
                above_x + slopes[0],
                above_y + slopes[1],
                total + buoyancy_of(new[2], new[3]),
                absorbed + wet * share_ref[k],
            ]
    for r, j in grid:
        for kind in range(2):
            at = slice(kind * cols + j * LANES, kind * cols + (j + 1) * LANES)
            sums_ref[r * DEEP : (r + 1) * DEEP, at] = run[r, j][2 + kind]


def rim_kernel(
    n_lat, own_south_ref, own_north_ref, prefix_ref, turn_ref, share_ref, partner_ref, own_west_ref, own_east_ref,
    from_west_ref, from_east_ref, pair_ref, cross_ref, fold_ref, inside_ref, ring_rows_ref, ring_cols_ref,
    edge_rows_ref, edge_cols_ref, sums_ref, south_ref, north_ref,
):
    rows, cols = prefix_ref.shape
    lat = lax.axis_index("lat")
    odd = lax.rem(lat, 2) == 1
    within = partner_ref[0] & (LANES - 1)
    at_top = lat == n_lat - 1

    @pl.when(odd)
    def _():
        south_ref[...] = pair_ref[...]

    @pl.when(jnp.logical_not(odd))
    def _():
        north_ref[...] = pair_ref[...]

    @pl.when(jnp.logical_not(odd) & (lat > 0))
    def _():
        south_ref[...] = cross_ref[...]

    @pl.when(odd & (lat < n_lat - 1))
    def _():
        north_ref[...] = cross_ref[...]

    @pl.when(lat == 0)
    def _():
        for slab in range(SLABS):
            south_ref[slab] = own_south_ref[slab if slab == 10 else slab - slab % 2]
        corner_slab(south_ref, prefix_ref, turn_ref, from_west_ref, from_east_ref, 0, 0)

    sub8, lane8 = iota((DEEP, LANES), 0), iota((DEEP, LANES), 1)

    @pl.when(at_top)
    def _():
        for slab in range(SLABS + 1):
            row = jnp.concatenate([fold_ref[piece, slab] for piece in range(fold_ref.shape[0])], axis=1)
            row = pltpu.roll(row, cols + LANES - 1 - within, 1)
            if slab < 4:
                row = -row
            north_ref[slab] = mirrored(row, cols)
        north_ref[CORNERS, 0:1, 0:LANES] = from_west_ref[rows : rows + 1, :]
        north_ref[CORNERS, 1:2, 0:LANES] = from_east_ref[rows : rows + 1, :]
        north_ref[CORNERS, 2:3, :] = jnp.full((1, cols), turn_ref[rows - 1], F32)

    wide = cols + LANES
    sums_ref[rows:, :] = jnp.zeros((DEEP, 2 * wide), F32)
    for kind in range(2):
        sums_ref[0:rows, kind * wide : kind * wide + cols] = inside_ref[:, kind * cols : (kind + 1) * cols]

    share_down = jnp.zeros((DEEP, LANES), F32)
    for k in range(DEEP):
        share_down = jnp.where(sub8 == k, share_ref[k], share_down)

    def down(line, f):
        return jnp.sum(jnp.where(lane8 == f * DEEP + sub8, line, 0.0), axis=1, keepdims=True)

    def row_step(near, south, north, west_line, east_line, wet, turn, above, above_south, above_north):
        col = iota((DEEP, cols), 1)
        sides = [
            (
                jnp.where(col == cols - 1, down(east_line, f), roll(near[f], -1, 1)),
                jnp.where(col == 0, down(west_line, f), roll(near[f], 1, 1)),
                north[f],
                south[f],
            )
            for f in range(5)
        ]
        east = jnp.where(col[0:1] == cols - 1, east_line[:, ABOVE : ABOVE + 1], roll(above, -1, 1))
        west = jnp.where(col[0:1] == 0, west_line[:, ABOVE : ABOVE + 1], roll(above, 1, 1))
        above_x, above_y = 0.5 * (east - west), 0.5 * (above_north - above_south)

        def pressed(x, y):
            return PRESS * (above_x + scan_down(x) - 0.5 * x), PRESS * (above_y + scan_down(y) - 0.5 * y)

        return advanced(near, sides, wet, turn, pressed)

    for side, ghost_ref, own_ref in ((0, south_ref, own_south_ref), (1, north_ref, own_north_ref)):
        edge, inner = (0, 1) if side == 0 else (rows - 1, rows - 2)
        near = [ghost_ref[2 * f] for f in range(5)]
        far = [ghost_ref[2 * f + 1] for f in range(5)]
        own = [own_ref[2 * f] for f in range(5)]
        own_next = [own_ref[2 * f + 1] for f in range(5)]
        ring_wet = ghost_ref[10]
        corners = ghost_ref[CORNERS, :, 0:LANES]
        above_near, above_far = ghost_ref[CORNERS, 3:4, :], ghost_ref[CORNERS, 4:5, :]
        above_own, above_next = prefix_ref[edge : edge + 1, :], prefix_ref[inner : inner + 1, :]
        outward, inward = (far, above_far), (own, above_own)
        (south, above_south), (north, above_north) = (outward, inward) if side == 0 else (inward, outward)
        ring = row_step(
            near, south, north, corners[0:1, :], corners[1:2, :], ring_wet, corners[2:3, 0:1], above_near, above_south, above_north
        )
        outward, inward = (near, above_near), (own_next, above_next)
        (south, above_south), (north, above_north) = (outward, inward) if side == 0 else (inward, outward)
        wet = own_ref[10]
        edge_line = slice(edge, edge + 1)
        new = row_step(
            own, south, north, from_west_ref[edge_line, :], from_east_ref[edge_line, :], wet, turn_ref[edge],
            above_own, above_south, above_north,
        )
        for f in range(5):
            edge_rows_ref[side, f] = new[f]
            ring_rows_ref[side, f] = jnp.where(lat == 0, new[f], ring[f]) if side == 0 else ring[f]
        ring_rows_ref[side, 5] = ring_wet
        at = slice(rows + side, rows + side + 1)
        here = buoyancy_of(ring_rows_ref[side, 2], ring_rows_ref[side, 3])
        sums_ref[at, 0:cols] = jnp.sum(here, axis=0, keepdims=True)
        sums_ref[at, wide : wide + cols] = jnp.sum(ring_wet * share_down[:, 0:1], axis=0, keepdims=True)

    row, lane = iota((rows, LANES), 0), iota((rows, LANES), 1)
    turn = turn_column(turn_ref, rows)
    share_lanes = jnp.zeros((rows, LANES), F32)
    for k in range(DEEP):
        share_lanes = jnp.where((lane & 7) == k, share_ref[k], share_lanes)

    def column_step(near, east, west, north, south):
        dx, dy = 0.5 * (east - west), 0.5 * (north - south)
        lap = (east + west) + (north + south) - 4.0 * near
        zonal, merid = lanes_between(near, 0, 8), lanes_between(near, 8, 16)
        wet = lanes_between(near, WET, WET + 8)
        wet_all = sum(roll(wet, -8 * n, 1) for n in range(2, 7))
        zonal_all = sum(roll(zonal, 8 * n, 1) for n in (2, 3, 4))
        merid_all = sum(roll(merid, 8 * n, 1) for n in (1, 2, 3))
        bx = lanes_between(buoyancy_of(roll(dx, -16, 1), roll(dx, -24, 1)), 0, 8)
        by = lanes_between(buoyancy_of(roll(dy, -8, 1), roll(dy, -16, 1)), 8, 16)
        press_x = lanes_between(PRESS * (dx[:, ABOVE : ABOVE + 1] + scan_lanes(bx) - 0.5 * bx), 0, 8)
        press_y = lanes_between(PRESS * (dy[:, ABOVE : ABOVE + 1] + scan_lanes(by) - 0.5 * by), 8, 16)
        trend = VISCOUS * lap - ADVECT * (zonal_all * dx + merid_all * dy) - press_x - press_y
        trend = trend + lanes_between(turn * roll(near, -8, 1), 0, 8) - lanes_between(turn * roll(near, 8, 1), 8, 16)
        return near + wet_all * trend, wet

    blocks = [jnp.zeros((rows, LANES), F32)] * 2
    sides = ((0, from_west_ref, own_west_ref), (1, from_east_ref, own_east_ref))
    for side, ghost_ref, own_ref in sides:
        near, own = ghost_ref[0:rows, :], own_ref[0:rows, :]
        far, own_next = roll(near, -FAR, 1), roll(own, -FAR, 1)
        north = jnp.where(row == rows - 1, north_ref[CORNERS, side : side + 1, 0:LANES], roll(near, -1, 0))
        south = jnp.where(row == 0, south_ref[CORNERS, side : side + 1, 0:LANES], roll(near, 1, 0))
        east, west = (own, far) if side == 0 else (far, own)
        new, wet = column_step(near, east, west, north, south)
        ring_cols_ref[side] = new
        blocks[0] = jnp.where(lane == side, buoyancy_sum(new), blocks[0])
        blocks[1] = jnp.where(lane == side, jnp.sum(wet * share_lanes, axis=1, keepdims=True), blocks[1])
        east, west = (own_next, near) if side == 0 else (near, own_next)
        new, _ = column_step(own, east, west, roll(own, -1, 0), roll(own, 1, 0))
        edge_cols_ref[side] = new
        column = 0 if side == 0 else cols - 1
        sums_ref[0:rows, column : column + 1] = buoyancy_sum(new)
    for kind in range(2):
        sums_ref[0:rows, kind * wide + cols : (kind + 1) * wide] = blocks[kind]
    for side, edge in ((0, 0), (1, rows - 1)):
        here = buoyancy_of(edge_rows_ref[side, 2], edge_rows_ref[side, 3])
        sums_ref[edge : edge + 1, 0:cols] = jnp.sum(here, axis=0, keepdims=True)


def flux_kernel(n_lat, mine_ref, theirs_ref, partner_ref, flux_ref, flux_rows_ref, flux_cols_ref, drive_ref):
    rows, cols = flux_ref.shape[1:]
    half_cols = cols // 2
    wide = 3 * half_cols
    mine, theirs = mine_ref[...], theirs_ref[...]
    first = lax.axis_index("lev") == 0
    halves = (jnp.where(first, mine, theirs), jnp.where(first, theirs, mine))
    at_top = lax.axis_index("lat") == n_lat - 1
    hinge = partner_ref[0]
    within = hinge - (hinge // cols) * cols

    def extra(kind, c):
        found = []
        for part in halves:
            line = jnp.concatenate(
                [part[2 * kind : 2 * kind + 1, 2 * wide :], part[2 * kind + 1 : 2 * kind + 2, 2 * wide :]], axis=1
            )
            found.append(line[:, c * half_cols : (c + 1) * half_cols])
        return jnp.concatenate(found, axis=1)

    flux, flux_south, flux_north, flux_west, flux_east = [], [], [], [], []
    crossed = jnp.zeros((DEEP, 2 * cols), F32)
    for c in range(3):
        pair = jnp.concatenate([extra(2, c), extra(1, c)], axis=1)
        crossed = jnp.where(iota(crossed.shape, 0) == c, pair, crossed)
    crossed = mirrored(pltpu.roll(crossed, 2 * cols - 1 - within, 1), cols)
    row, lane = iota((rows, LANES), 0), iota((rows, LANES), 1)
    for c in range(3):
        bands = [
            jnp.concatenate([part[:, b * wide + c * half_cols : b * wide + (c + 1) * half_cols] for part in halves], axis=1)
            for b in range(2)
        ]
        flux.append(jnp.concatenate(bands, axis=0))
        flux_south.append(extra(0, c))
        flux_north.append(jnp.where(at_top, crossed[c : c + 1, :], extra(1, c)))
        here = lane == c * 16 + row
        for side, part in ((flux_west, halves[1]), (flux_east, halves[0])):
            line = part[6:7, 2 * wide : 2 * wide + LANES]
            side.append(jnp.sum(jnp.where(here, line, 0.0), axis=1, keepdims=True))

    flux_cols = jnp.zeros((rows, LANES), F32)
    for c in range(3):
        flux_ref[c] = flux[c]
        flux_rows_ref[c : c + 1, :] = flux_south[c]
        flux_rows_ref[3 + c : 4 + c, :] = flux_north[c]
        flux_cols = jnp.where(lane == c, flux_west[c], jnp.where(lane == 3 + c, flux_east[c], flux_cols))
    flux_rows_ref[6:8, :] = jnp.zeros((2, cols), F32)
    flux_cols_ref[...] = flux_cols
    drive_ref[rows:, :] = jnp.zeros((DEEP, cols + LANES), F32)
    drive_ref[0:rows, 0:cols] = buoyancy_of(flux[0], flux[1])
    ends = jnp.zeros((rows, LANES), F32)
    for side, column, line in ((0, flux_west, flux_south), (1, flux_east, flux_north)):
        drive_ref[rows + side : rows + side + 1, 0:cols] = buoyancy_of(line[0], line[1])
        ends = jnp.where(lane == side, buoyancy_of(column[0], column[1]), ends)
    drive_ref[0:rows, cols:] = ends


def second_kernel(
    state_ref, mask_ref, prefix_ref, ring_rows_ref, ring_cols_ref, edge_rows_ref, edge_cols_ref, flux_ref, flux_rows_ref,
    flux_cols_ref, turn_ref, share_ref, out_hbm, flow_ref, tracers_ref, sem,
):
    rows, cols = flux_ref.shape[1:]
    n_r, n_j = rows // DEEP, cols // LANES
    sub8, lane8 = iota((DEEP, LANES), 0), iota((DEEP, LANES), 1)
    lane = iota((rows, LANES), 1)
    turn = turn_column(turn_ref, rows)
    share_down = jnp.zeros((DEEP, LANES), F32)
    share_lanes = jnp.zeros((rows, LANES), F32)
    for k in range(DEEP):
        share_down = jnp.where(sub8 == k, share_ref[k], share_down)
        share_lanes = jnp.where((lane & 7) == k, share_ref[k], share_lanes)

    ring_rows, ring_cols = [], []
    for side in range(2):
        taken = ring_rows_ref[side, 5] * share_down[:, 0:1]
        values = [ring_rows_ref[side, f] for f in range(2)]
        values += [ring_rows_ref[side, 2 + c] + taken * flux_rows_ref[3 * side + c : 3 * side + c + 1, :] for c in range(3)]
        ring_rows.append(values)
        found = ring_cols_ref[side]
        taken = lanes_between(found, WET, WET + 8) * share_lanes
        for c in range(3):
            found = found + roll(taken, 8 * (2 + c) - WET, 1) * flux_cols_ref[:, 3 * side + c : 3 * side + c + 1]
        ring_cols.append(found)

    grid = [(r, j) for r in range(n_r) for j in range(n_j)]

    def cut(value, r, j):
        return value[r * DEEP : (r + 1) * DEEP, j * LANES : (j + 1) * LANES]

    zero = jnp.zeros((DEEP, LANES), F32)
    run = {at: (zero, zero) for at in grid}
    prefix = Tiles([[prefix_ref[tile(r, j, 0, rows)] for j in range(n_j)] for r in range(n_r)])
    push = {}
    for at in grid:
        east, west, north, south = prefix.around(*at)
        push[at] = (0.5 * PRESS) * (east - west), (0.5 * PRESS) * (north - south)
    edge_cols = [edge_cols_ref[side] for side in range(2)]
    copies = []

    def column(value, r, n):
        return jnp.broadcast_to(value[r * DEEP : (r + 1) * DEEP, n : n + 1], (DEEP, LANES))

    for k in range(DEEP):
        wets, heats, grids = {}, {}, [[[None] * n_j for _ in range(n_r)] for _ in range(5)]
        for r, j in grid:
            at = tile(r, j, k, rows)
            wet = mask_ref[at].astype(F32)
            taken = wet * share_ref[k]
            wets[r, j] = wet
            heats[r, j] = [taken * cut(flux_ref[c], r, j) for c in range(3)]
            for f in range(5):
                value = state_ref[(f, *at)]
                if f < 2:
                    value = value - wet * push[r, j][f]
                if j == 0:
                    value = jnp.where(lane8 == 0, column(edge_cols[0], r, f * DEEP + k), value)
                if j == n_j - 1:
                    value = jnp.where(lane8 == LANES - 1, column(edge_cols[1], r, f * DEEP + k), value)
                if r == 0:
                    value = jnp.where(sub8 == 0, edge_rows_ref[0, f, k : k + 1, at[1]], value)
                if r == n_r - 1:
                    value = jnp.where(sub8 == DEEP - 1, edge_rows_ref[1, f, k : k + 1, at[1]], value)
                if f >= 2:
                    value = value + heats[r, j][f - 2]
                grids[f][r][j] = value
        fields = [
            Tiles(
                grids[f],
                [column(ring_cols[0], r, f * DEEP + k) for r in range(n_r)],
                [column(ring_cols[1], r, f * DEEP + k) for r in range(n_r)],
                [ring_rows[0][f][k : k + 1, j * LANES : (j + 1) * LANES] for j in range(n_j)],
                [ring_rows[1][f][k : k + 1, j * LANES : (j + 1) * LANES] for j in range(n_j)],
            )
            for f in range(5)
        ]
        for r, j in grid:
            at = tile(r, j, k, rows)
            over_x, over_y = run[r, j]

            def pressed(x, y):
                run[r, j] = (over_x + x, over_y + y)
                return PRESS * (over_x + 0.5 * x), PRESS * (over_y + 0.5 * y)

            new = advanced(
                [field.grid[r][j] for field in fields],
                [field.around(r, j) for field in fields],
                wets[r, j],
                turn[r * DEEP : (r + 1) * DEEP, 0:1],
                pressed,
                heats[r, j],
            )
            for f in range(5):
                if f < 2:
                    flow_ref[(f, *at)] = new[f]
                else:
                    tracers_ref[(f - 2, *at)] = new[f]
        whole = pl.ds(k * rows, rows)
        copies.append(
            pltpu.make_async_copy(tracers_ref.at[:, whole, :], out_hbm.at[pl.ds(2, 3), whole, :], sem.at[k])
        )
        copies[-1].start()
    for copy in copies:
        copy.wait()


def last_kernel(out_in_hbm, flow_ref, mask_ref, sums_ref, drive_ref, out_hbm, moved_ref, sem):
    del out_in_hbm
    rows, cols = mask_ref.shape[0] // DEEP, mask_ref.shape[1]
    wide = cols + LANES
    above = sums_ref[:, 0:wide] + sums_ref[:, wide : 2 * wide] * drive_ref[...]
    east, west, north, south = around(
        above[0:rows, 0:cols],
        above[0:rows, cols : cols + 1],
        above[0:rows, cols + 1 : cols + 2],
        above[rows : rows + 1, 0:cols],
        above[rows + 1 : rows + 2, 0:cols],
    )
    push_x, push_y = (0.5 * PRESS) * (east - west), (0.5 * PRESS) * (north - south)
    copies = []
    for k in range(DEEP):
        whole = pl.ds(k * rows, rows)
        wet = mask_ref[whole, :].astype(F32)
        moved_ref[0, whole, :] = flow_ref[0, whole, :] - wet * push_x
        moved_ref[1, whole, :] = flow_ref[1, whole, :] - wet * push_y
        copies.append(pltpu.make_async_copy(moved_ref.at[:, whole, :], out_hbm.at[pl.ds(0, 2), whole, :], sem.at[k]))
        copies[-1].start()
    for copy in copies:
        copy.wait()


def body(n_lon, n_lat, state, mask, coriolis, penetration, flux_tiles, flux_owner, flux_row, fold_partner):
    fields, levels, rows, cols = state.shape
    flat_state = state.reshape(fields, levels * rows, cols)
    flat_mask = mask.reshape(levels * rows, cols)
    last = n_lat - 1

    keep, send, west, east, total = prepare(
        flat_state, flat_mask, flux_tiles, flux_owner, flux_row, fold_partner, n_lon, n_lat
    )

    stages = []
    for axis, size, least in (("lat", n_lat, 2), ("lon", n_lon, 1)):
        bit = size // 2
        while bit >= least:
            stages.append((axis, size, bit))
            bit //= 2
    got = lax.ppermute(send, "lat", [(i, i ^ 1) for i in range(n_lat)])
    prefix = lax.ppermute(total, "lev", [(0, 1)])

    def merged(keep, got):
        half = shape(keep.shape[0] // 2, keep.shape[1])
        return call(merge_kernel, (half, half), [VMEM] * 2, (keep, got), name="merge_flux")

    def passed_on(send, stage):
        axis, size, bit = stage
        return lax.ppermute(send, axis, [(i, i ^ bit) for i in range(size)])

    near_state, near_mask = after((flat_state, flat_mask), send)
    own_rows = shape(SLABS, DEEP, cols)
    new_state, inside, own_south, own_north = call(
        inside_kernel,
        (shape(fields, levels * rows, cols), shape(rows, 2 * cols), own_rows, own_rows),
        [VMEM, VMEM, SMEM, SMEM],
        (near_state, near_mask, coriolis, penetration),
        name="first_inside",
    )
    pieces = cols // LANES
    hinge_piece = fold_partner[0] >> (LANES.bit_length() - 1)
    keep = after(keep, (prefix, hinge_piece, inside))
    keep, send = merged(keep, got)
    got = passed_on(send, stages[0])

    top_shape = shape(pieces, SLABS + 1, DEEP, LANES)
    top = call(top_kernel, top_shape, [VMEM] * 2, (own_north, prefix), name="top_rows")
    top = after(top, send)

    def folded(hinge_piece):
        block, piece = divmod(hinge_piece, pieces)

        def swap(rows_out):
            def across(part, other):
                pairs = [(a * n_lat + last, (other - a) % n_lon * n_lat + last) for a in range(n_lon)]
                return lax.ppermute(part, ("lon", "lat"), pairs)

            return jnp.concatenate([across(rows_out[piece:], block - 1), across(rows_out[: piece + 1], block)], axis=0)

        return swap

    fold = lax.switch(hinge_piece, [folded(n) for n in range(n_lon * pieces)], top)
    keep = after(keep, fold)
    keep, send = merged(keep, got)
    got = passed_on(send, stages[1])

    west, east = after((west, east), send)
    side = shape(rows + DEEP, LANES)
    west, east = call(
        functools.partial(columns_kernel, n_lat),
        (side, side),
        [VMEM] * 4 + [SMEM],
        (west, east, prefix, fold, fold_partner),
        name="edge_columns",
    )
    from_west = lax.ppermute(east, "lon", [(i, (i + 1) % n_lon) for i in range(n_lon)])
    from_east = lax.ppermute(west, "lon", [((i + 1) % n_lon, i) for i in range(n_lon)])
    keep = after(keep, (from_west, from_east))
    for stage in stages[2:]:
        keep, send = merged(keep, got)
        got = passed_on(send, stage)

    from_west, from_east = after((from_west, from_east), send)
    message = shape(SLABS + 1, DEEP, cols)
    pair, cross = call(
        rows_kernel,
        (message, message),
        [VMEM, VMEM, VMEM, SMEM, VMEM, VMEM],
        (own_south, own_north, prefix, coriolis, from_west, from_east),
        name="edge_rows",
    )
    from_pair = lax.ppermute(pair, "lat", [(i, i ^ 1) for i in range(n_lat)])
    from_cross = lax.ppermute(cross, "lat", [(i, i + 1 if i % 2 else i - 1) for i in range(1, last)])
    inside = after(inside, send)
    wide = cols + LANES
    *ring, sums = call(
        functools.partial(rim_kernel, n_lat),
        (
            shape(2, 6, DEEP, cols),
            shape(2, rows, LANES),
            shape(2, 5, DEEP, cols),
            shape(2, rows, LANES),
            shape(rows + DEEP, 2 * wide),
        ),
        [VMEM, VMEM, VMEM, SMEM, SMEM, SMEM] + [VMEM] * 8,
        (
            own_south, own_north, prefix, coriolis, penetration, fold_partner, west, east, from_west, from_east, from_pair,
            from_cross, fold, inside,
        ),
        [pltpu.VMEM((SLABS + 1, DEEP, cols), F32), pltpu.VMEM((SLABS + 1, DEEP, cols), F32)],
        name="first_rim",
    )
    keep = after(keep, sums)
    mine = keep + got
    theirs = lax.ppermute(mine, "lev", [(0, 1), (1, 0)])
    sums = lax.ppermute(after(sums, theirs), "lev", [(0, 1)])
    *flux, drive = call(
        functools.partial(flux_kernel, n_lat),
        (shape(3, rows, cols), shape(DEEP, cols), shape(rows, LANES), shape(rows + DEEP, wide)),
        [VMEM] * 2 + [SMEM],
        (mine, theirs, fold_partner),
        name="flux_parts",
    )

    out = jax.ShapeDtypeStruct(flat_state.shape, F32)
    result, flow = call(
        second_kernel,
        (out, shape(2, levels * rows, cols)),
        [VMEM] * 10 + [SMEM] * 2,
        (new_state, flat_mask, prefix, *ring, *flux, coriolis, penetration),
        [pltpu.VMEM((3, levels * rows, cols), F32), pltpu.SemaphoreType.DMA((DEEP,))],
        name="second_substep",
        out_specs=(ANY, VMEM),
    )
    result = call(
        last_kernel,
        out,
        [ANY] + [VMEM] * 4,
        (result, flow, flat_mask, sums, drive),
        [pltpu.VMEM((2, levels * rows, cols), F32), pltpu.SemaphoreType.DMA((DEEP,))],
        name="deeper_pressure",
        out_specs=ANY,
        aliases={0: 0},
    )
    return result.reshape(fields, levels, rows, cols)


def solution(mesh):
    n_lon, n_lat = mesh.shape["lon"], mesh.shape["lat"]
    assert mesh.shape["lev"] == 2 and n_lat % 2 == 0 and n_lon > 2
    return jax.shard_map(
        functools.partial(body, n_lon, n_lat),
        mesh=mesh,
        in_specs=(
            P(None, "lev", "lat", "lon"),
            P("lev", "lat", "lon"),
            P("lat"),
            P("lev"),
            P(("lon", "lat"), None, None),
            P(("lon", "lat"), None),
            P(("lon", "lat")),
            P(),
        ),
        out_specs=P(None, "lev", "lat", "lon"),
        check_vma=False,
    )
```

```python
import functools

import jax
import jax.numpy as jnp
from jax import lax
from jax.experimental import pallas as pl
from jax.experimental.pallas import tpu as pltpu
from jax.sharding import PartitionSpec as P

ALPHA = 0.2
BETA = 0.15
PRESS = 0.1
VISCOUS = 0.1
DIFFUSE = 0.1
ADVECT = 0.1

F32 = jnp.float32
I32 = jnp.int32
LANES = 128
DEEP = 8
FAR = 64
WET = 48
ABOVE = 56
SLABS = 11
CORNERS = SLABS
VMEM_BYTES = 16 * 1024 * 1024

VMEM = pl.BlockSpec(memory_space=pltpu.VMEM)
SMEM = pl.BlockSpec(memory_space=pltpu.SMEM)
ANY = pl.BlockSpec(memory_space=pl.ANY)
HBM = pl.BlockSpec(memory_space=pltpu.HBM)


def iota(shape, dim):
    return lax.broadcasted_iota(I32, shape, dim)


def roll(value, shift, axis):
    return pltpu.roll(value, shift % value.shape[axis], axis)


def call(kernel, out_shape, in_specs, args, scratch=(), name=None, out_specs=None, aliases=None):
    return pl.pallas_call(
        kernel,
        out_shape=out_shape,
        in_specs=in_specs,
        out_specs=out_specs or jax.tree.map(lambda _: VMEM, out_shape),
        input_output_aliases=aliases or {},
        scratch_shapes=list(scratch),
        compiler_params=pltpu.CompilerParams(vmem_limit_bytes=VMEM_BYTES),
        name=name,
    )(*args)


def after(values, *others):
    return lax.optimization_barrier((values, others))[0]


def shape(*dims):
    return pltpu.VMEM(dims, F32)


def in_hbm(*arrays):
    return tuple(pltpu.with_memory_space_constraint(array, pltpu.HBM) for array in arrays)


def prepare_kernel(
    n_lon, n_lat, state_hbm, mask_hbm, tiles_hbm, owner_hbm, row_hbm, partner_hbm, keep_ref, send_ref, west_ref, east_ref,
    total_ref, state_ref, mask_ref, x_ref, owners_ref, rows_ref, hinge_ref, sem,
):
    tiles, cols = tiles_hbm.shape[1], tiles_hbm.shape[2]
    half_cols = cols // 2
    rows = 2 * DEEP
    n_y = n_lat // 2
    half = lax.axis_index("lev")
    lat = lax.axis_index("lat")
    core = lax.rem(lat, 2)
    begin = pl.multiple_of(half * half_cols, LANES)
    indices = [
        pltpu.make_async_copy(owner_hbm, owners_ref, sem.at[0]),
        pltpu.make_async_copy(row_hbm, rows_ref, sem.at[1]),
        pltpu.make_async_copy(partner_hbm, hinge_ref, sem.at[2]),
    ]
    fluxes = [
        pltpu.make_async_copy(
            tiles_hbm.at[c, :, pl.ds(begin, half_cols)], x_ref.at[:, pl.ds(c * half_cols, half_cols)], sem.at[3 + c]
        )
        for c in range(3)
    ]
    fields = [
        pltpu.make_async_copy(state_hbm, state_ref, sem.at[6]),
        pltpu.make_async_copy(mask_hbm, mask_ref, sem.at[7]),
    ]
    for copy in indices + fluxes + fields:
        copy.start()
    for copy in indices:
        copy.wait()

    key = owners_ref[...] * rows + rows_ref[...]
    hinge_block = hinge_ref[0] // cols
    slots = keep_ref.shape[0]
    slot = iota((slots, tiles), 0)
    group, sub = slot >> 3, slot & 7
    at_y = (group >> (n_lon.bit_length() - 1)) ^ (lat // 2)
    at_lon = (group & (n_lon - 1)) ^ lax.axis_index("lon")

    def wrapped(lon):
        return jnp.where(lon < 0, lon + n_lon, jnp.where(lon >= n_lon, lon - n_lon, lon))

    def one_hot(hit):
        return jnp.where(hit, 1.0, 0.0).astype(jnp.bfloat16)

    def weights(to_core):
        lat = 2 * at_y + to_core
        owner = at_lon * n_lat + lat
        last = lat == n_lat - 1
        top = n_lat * rows - 1
        south = jnp.where(lat == 0, owner * rows, owner * rows - 1)
        north = jnp.where(last, wrapped(hinge_block - at_lon) * (n_lat * rows) + top, (owner + 1) * rows)
        third = jnp.where(last, wrapped(hinge_block - at_lon - 1) * (n_lat * rows) + top, -1)
        kind = sub >> 1
        extra_key = jnp.where(kind == 0, south, jnp.where(kind == 1, north, jnp.where(kind == 2, third, -1)))
        extra = key == extra_key
        beside = wrapped(at_lon + 1 - 2 * half) * n_lat + lat
        return (
            one_hot(key == owner * rows + sub),
            one_hot(key == owner * rows + DEEP + sub),
            one_hot(extra & ((sub & 1) == 0)),
            one_hot(extra & ((sub & 1) == 1)),
            one_hot(((key >> 4) == beside) & (sub == 6)),
        )

    def split(x):
        first = x.astype(jnp.bfloat16)
        rest = x - first.astype(F32)
        second = rest.astype(jnp.bfloat16)
        third = (rest - second.astype(F32)).astype(jnp.bfloat16)
        return first, second, third

    square = iota((tiles, tiles), 0) == iota((tiles, tiles), 1)
    row_of = jnp.sum(jnp.where(square, (key & (rows - 1)).astype(F32), 0.0), axis=1, keepdims=True).astype(I32)

    for copy in fluxes:
        copy.wait()
    x = x_ref[...]
    lane = iota((tiles, LANES), 1)
    edge = jnp.zeros((tiles, LANES), F32)
    for c in range(3):
        begin = c * half_cols
        value = jnp.where(half == 0, x[:, begin : begin + 1], x[:, begin + half_cols - 1 : begin + half_cols])
        edge = jnp.where(((lane >> 4) == c) & ((lane & 15) == row_of), value, edge)
    parts, edges = split(x), split(edge)
    wide = 3 * half_cols
    quarter = wide // 2

    def dot(hot, terms, begin, end):
        products = [
            jnp.dot(hot, term[:, begin:end], preferred_element_type=F32) for term in reversed(terms)
        ]
        return products[0] + products[1] + products[2]

    for out_ref, to_core in ((keep_ref, core), (send_ref, 1 - core)):
        low, high, even, odd, ring = weights(to_core)
        out_ref[:, 0:wide] = dot(low, parts, 0, wide)
        out_ref[:, wide : 2 * wide] = dot(high, parts, 0, wide)
        rest = dot(even, parts, 0, quarter) + dot(odd, parts, quarter, wide)
        beside = dot(ring, edges, 0, LANES)
        out_ref[:, 2 * wide : 2 * wide + LANES] = rest[:, 0:LANES] + beside
        out_ref[:, 2 * wide + LANES :] = rest[:, LANES:]

    for copy in fields:
        copy.wait()
    total = jnp.zeros(total_ref.shape, F32)
    for k in range(DEEP):
        at = slice(k * rows, (k + 1) * rows)
        total = total + buoyancy_of(state_ref[2, at, :], state_ref[3, at, :])
    total_ref[...] = total
    edge_columns(state_ref, mask_ref, west_ref, east_ref)


def merge_kernel(kept_ref, got_ref, keep_ref, send_ref):
    half = keep_ref.shape[0]
    send_ref[...] = kept_ref[half:, :] + got_ref[half:, :]
    keep_ref[...] = kept_ref[0:half, :] + got_ref[0:half, :]


def prepare(state, mask, flux_tiles, flux_owner, flux_row, fold_partner, n_lon, n_lat):
    tiles, _, cols = flux_tiles.shape
    wide = 3 * (cols // 2)
    slots = shape(n_lon * n_lat // 2 * DEEP, 2 * wide + wide // 2)
    side = shape(2 * DEEP, LANES)
    return call(
        functools.partial(prepare_kernel, n_lon, n_lat),
        (slots, slots, side, side, shape(2 * DEEP, cols)),
        [HBM] * 6,
        in_hbm(
            state,
            mask,
            flux_tiles.transpose(1, 0, 2),
            flux_owner.reshape(1, tiles),
            flux_row.reshape(1, tiles),
            fold_partner,
        ),
        [
            pltpu.VMEM(state.shape, F32),
            pltpu.VMEM(mask.shape, I32),
            pltpu.VMEM((tiles, wide), F32),
            pltpu.VMEM((1, tiles), I32),
            pltpu.VMEM((1, tiles), I32),
            pltpu.SMEM(fold_partner.shape, I32),
            pltpu.SemaphoreType.DMA((8,)),
        ],
        name="prepare",
    )


def level_rows(ref, row, rows):
    return jnp.concatenate([ref[k * rows + row : k * rows + row + 1, :] for k in range(DEEP)], axis=0)


def buoyancy_of(temper, saline):
    return ALPHA * temper - BETA * saline


def edge_rows(state_ref, mask_ref, out_ref, rows, near, far):
    for f in range(5):
        out_ref[2 * f] = level_rows(state_ref.at[f], near, rows)
        out_ref[2 * f + 1] = level_rows(state_ref.at[f], far, rows)
    out_ref[10] = level_rows(mask_ref, near, rows).astype(F32)


def edge_columns(state_ref, mask_ref, west_ref, east_ref):
    rows, cols = west_ref.shape[0], state_ref.shape[2]
    lane = iota((rows, LANES), 1)
    last = slice(cols - LANES, cols)
    west = jnp.zeros((rows, LANES), F32)
    east = jnp.zeros((rows, LANES), F32)
    for k in range(DEEP):
        at = slice(k * rows, (k + 1) * rows)
        for f in range(5):
            to = f * DEEP + k
            left, right = state_ref[f, at, 0:LANES], state_ref[f, at, last]
            west = jnp.where(lane == to, roll(left, to, 1), west)
            west = jnp.where(lane == FAR + to, roll(left, FAR + to - 1, 1), west)
            east = jnp.where(lane == to, roll(right, to + 1, 1), east)
            east = jnp.where(lane == FAR + to, roll(right, FAR + to + 2, 1), east)
        west = jnp.where(lane == WET + k, roll(mask_ref[at, 0:LANES].astype(F32), WET + k, 1), west)
        east = jnp.where(lane == WET + k, roll(mask_ref[at, last].astype(F32), WET + k + 1, 1), east)
    west_ref[...] = west
    east_ref[...] = east


def top_kernel(state_ref, mask_ref, prefix_ref, top_ref):
    rows, cols = prefix_ref.shape
    for slab in range(SLABS):
        if slab < 10:
            line = level_rows(state_ref.at[slab // 2], rows - 1 - slab % 2, rows)
        else:
            line = level_rows(mask_ref, rows - 1, rows).astype(F32)
        for piece in range(cols // LANES):
            top_ref[piece, slab] = line[:, piece * LANES : (piece + 1) * LANES]
    top_ref[:, CORNERS] = jnp.zeros((cols // LANES, DEEP, LANES), F32)
    for n in (1, 2):
        for piece in range(cols // LANES):
            top_ref[piece, CORNERS, 2 + n : 3 + n, :] = prefix_ref[rows - n : rows - n + 1, piece * LANES : (piece + 1) * LANES]


def columns_kernel(n_lat, west_ref, east_ref, prefix_ref, fold_ref, partner_ref, west_out_ref, east_out_ref):
    rows, cols = prefix_ref.shape
    lane = iota((rows, LANES), 1)
    for side, in_ref, out_ref in ((0, west_ref, west_out_ref), (1, east_ref, east_out_ref)):
        near, far = (0, 1) if side == 0 else (cols - 1, cols - 2)
        value = jnp.where(lane == ABOVE, prefix_ref[:, near : near + 1], in_ref[...])
        out_ref[0:rows, :] = jnp.where(lane == FAR + ABOVE, prefix_ref[:, far : far + 1], value)
        out_ref[rows:, :] = jnp.zeros((DEEP, LANES), F32)

    @pl.when(lax.axis_index("lat") == n_lat - 1)
    def _():
        within = partner_ref[0] & (LANES - 1)
        sub8, lane8 = iota((DEEP, LANES), 0), iota((DEEP, LANES), 1)
        for out_ref in (west_out_ref, east_out_ref):
            line = jnp.zeros((DEEP, LANES), F32)
            for slab in (0, 2, 4, 6, 8, CORNERS):
                if out_ref is west_out_ref:
                    cell = jnp.where(lane8 == within, fold_ref[fold_ref.shape[0] - 1, slab], 0.0)
                else:
                    cell = jnp.where(lane8 == within + 1, fold_ref[0, slab], 0.0)
                    cell = jnp.where((lane8 == 0) & (within == LANES - 1), fold_ref[1, slab], cell)
                cell = jnp.sum(cell, axis=1, keepdims=True)
                here = (lane8 == ABOVE) & (sub8 == 3) if slab == CORNERS else lane8 == (slab // 2) * DEEP + sub8
                line = jnp.where(here, -cell if slab < 4 else cell, line)
            out_ref[rows : rows + 1, :] = jnp.sum(line, axis=0, keepdims=True)


def corner_slab(out_ref, prefix_ref, turn_ref, from_west_ref, from_east_ref, near, far):
    out_ref[CORNERS] = jnp.full(out_ref.shape[1:], turn_ref[near], F32)
    out_ref[CORNERS, 0:1, 0:LANES] = from_west_ref[near : near + 1, :]
    out_ref[CORNERS, 1:2, 0:LANES] = from_east_ref[near : near + 1, :]
    out_ref[CORNERS, 3:4, :] = prefix_ref[near : near + 1, :]
    out_ref[CORNERS, 4:5, :] = prefix_ref[far : far + 1, :]


def rows_kernel(state_ref, mask_ref, prefix_ref, turn_ref, from_west_ref, from_east_ref, pair_ref, cross_ref):
    rows = prefix_ref.shape[0]
    odd = lax.rem(lax.axis_index("lat"), 2) == 1

    def fill(out_ref, near, far):
        edge_rows(state_ref, mask_ref, out_ref, rows, near, far)
        corner_slab(out_ref, prefix_ref, turn_ref, from_west_ref, from_east_ref, near, far)

    @pl.when(odd)
    def _():
        fill(pair_ref, 0, 1)
        fill(cross_ref, rows - 1, rows - 2)

    @pl.when(jnp.logical_not(odd))
    def _():
        fill(pair_ref, rows - 1, rows - 2)
        fill(cross_ref, 0, 1)


def around(value, west, east, south, north):
    rows, cols = value.shape
    row, col = iota((rows, cols), 0), iota((rows, cols), 1)
    return (
        jnp.where(col == cols - 1, east, roll(value, -1, 1)),
        jnp.where(col == 0, west, roll(value, 1, 1)),
        jnp.where(row == rows - 1, north, roll(value, -1, 0)),
        jnp.where(row == 0, south, roll(value, 1, 0)),
    )


def advanced(values, sides, wet, turn, pressed, heat=None):
    zonal, merid = values[0], values[1]
    sums = [(e + w) + (n + s) for e, w, n, s in sides]
    across = [(e - w, n - s) for e, w, n, s in sides]
    press_x, press_y = pressed(
        0.5 * buoyancy_of(across[2][0], across[3][0]), 0.5 * buoyancy_of(across[2][1], across[3][1])
    )
    out = []
    carry_x, carry_y = (0.5 * ADVECT) * zonal, (0.5 * ADVECT) * merid
    for f in range(5):
        spread = (VISCOUS if f < 2 else DIFFUSE) * (sums[f] - 4.0 * values[f])
        if f == 0:
            trend = spread + (turn * merid - press_x)
        elif f == 1:
            trend = spread - (turn * zonal + press_y)
        else:
            trend = spread - (carry_x * across[f][0] + carry_y * across[f][1])
        new = values[f] + wet * trend
        out.append(new if heat is None or f < 2 else new + heat[f - 2])
    return out


class Tiles:
    def __init__(self, grid, west=None, east=None, south=None, north=None):
        self.grid, self.ghosts, self.turned = grid, (west, east, south, north), {}
        self.lane, self.sub = iota((DEEP, LANES), 1), iota((DEEP, LANES), 0)

    def rolled(self, r, j, shift, axis):
        at = (r, j, shift, axis)
        if at not in self.turned:
            self.turned[at] = roll(self.grid[r][j], shift, axis)
        return self.turned[at]

    def side(self, r, j, shift, axis):
        here = self.rolled(r, j, shift, axis)
        r_from, j_from = (r, j - shift) if axis else (r - shift, j)
        edge = (0 if shift == 1 else LANES - 1) if axis else (0 if shift == 1 else DEEP - 1)
        if 0 <= r_from < len(self.grid) and 0 <= j_from < len(self.grid[0]):
            other = self.rolled(r_from, j_from, shift, axis)
        else:
            ghost = self.ghosts[(0 if shift == 1 else 1) + (0 if axis else 2)]
            if ghost is None:
                return here
            other = ghost[r if axis else j]
        return jnp.where((self.lane if axis else self.sub) == edge, other, here)

    def around(self, r, j):
        return self.side(r, j, -1, 1), self.side(r, j, 1, 1), self.side(r, j, -1, 0), self.side(r, j, 1, 0)


def tile(r, j, k, rows):
    return slice(k * rows + r * DEEP, k * rows + (r + 1) * DEEP), slice(j * LANES, (j + 1) * LANES)


def turn_column(turn_ref, rows):
    row = iota((rows, LANES), 0)
    column = jnp.zeros((rows, LANES), F32)
    for j in range(rows):
        column = jnp.where(row == j, turn_ref[j], column)
    return column


def mirrored(value, width):
    back = LANES - 1 - iota((value.shape[0], LANES), 1)
    blocks = [
        jnp.take_along_axis(value[:, begin : begin + LANES], back, axis=1)
        for begin in range(width - LANES, -1, -LANES)
    ]
    return jnp.concatenate(blocks, axis=1)


def scan_down(value):
    row = iota(value.shape, 0)
    for step in (1, 2, 4):
        value = value + jnp.where(row >= step, roll(value, step, 0), 0.0)
    return value


def scan_lanes(value):
    lane = iota(value.shape, 1) & 7
    for step in (1, 2, 4):
        value = value + jnp.where(lane >= step, roll(value, step, 1), 0.0)
    return value


def lanes_between(value, begin, end):
    lane = iota(value.shape, 1)
    return jnp.where((lane >= begin) & (lane < end), value, 0.0)


def buoyancy_sum(column):
    here = lanes_between(buoyancy_of(roll(column, -16, 1), roll(column, -24, 1)), 0, 8)
    return jnp.sum(here, axis=1, keepdims=True)


def inside_kernel(state_ref, mask_ref, prefix_ref, turn_ref, share_ref, new_ref, sums_ref):
    rows, cols = prefix_ref.shape
    n_r, n_j = rows // DEEP, cols // LANES
    turn = turn_column(turn_ref, rows)
    grid = [(r, j) for r in range(n_r) for j in range(n_j)]
    zero = jnp.zeros((DEEP, LANES), F32)
    prefix = Tiles([[prefix_ref[tile(r, j, 0, rows)] for j in range(n_j)] for r in range(n_r)])
    run = {}
    for at in grid:
        east, west, north, south = prefix.around(*at)
        run[at] = [0.5 * (east - west), 0.5 * (north - south), zero, zero]
    for k in range(DEEP):
        fields = [Tiles([[state_ref[(f, *tile(r, j, k, rows))] for j in range(n_j)] for r in range(n_r)]) for f in range(5)]
        for r, j in grid:
            at = tile(r, j, k, rows)
            above_x, above_y, total, absorbed = run[r, j]
            slopes = []

            def pressed(x, y):
                slopes.extend((x, y))
                return PRESS * (above_x + 0.5 * x), PRESS * (above_y + 0.5 * y)

            values = [field.grid[r][j] for field in fields]
            wet = mask_ref[at].astype(F32)
            new = advanced(
                values, [field.around(r, j) for field in fields], wet, turn[r * DEEP : (r + 1) * DEEP, 0:1], pressed
            )
            for f in range(5):
                new_ref[(f, *at)] = new[f]
            run[r, j] = [
                above_x + slopes[0],
                above_y + slopes[1],
                total + buoyancy_of(new[2], new[3]),
                absorbed + wet * share_ref[k],
            ]
    for r, j in grid:
        for kind in range(2):
            at = slice(kind * cols + j * LANES, kind * cols + (j + 1) * LANES)
            sums_ref[r * DEEP : (r + 1) * DEEP, at] = run[r, j][2 + kind]


def rim_kernel(
    n_lat, state_ref, mask_ref, prefix_ref, turn_ref, share_ref, partner_ref, own_west_ref, own_east_ref,
    from_west_ref, from_east_ref, pair_ref, cross_ref, fold_ref, inside_ref, ring_rows_ref, ring_cols_ref,
    edge_rows_ref, edge_cols_ref, sums_ref, south_ref, north_ref,
):
    rows, cols = prefix_ref.shape
    lat = lax.axis_index("lat")
    odd = lax.rem(lat, 2) == 1
    within = partner_ref[0] & (LANES - 1)
    at_top = lat == n_lat - 1

    @pl.when(odd)
    def _():
        south_ref[...] = pair_ref[...]

    @pl.when(jnp.logical_not(odd))
    def _():
        north_ref[...] = pair_ref[...]

    @pl.when(jnp.logical_not(odd) & (lat > 0))
    def _():
        south_ref[...] = cross_ref[...]

    @pl.when(odd & (lat < n_lat - 1))
    def _():
        north_ref[...] = cross_ref[...]

    @pl.when(lat == 0)
    def _():
        edge_rows(state_ref, mask_ref, south_ref, rows, 0, 0)
        corner_slab(south_ref, prefix_ref, turn_ref, from_west_ref, from_east_ref, 0, 0)

    sub8, lane8 = iota((DEEP, LANES), 0), iota((DEEP, LANES), 1)

    @pl.when(at_top)
    def _():
        for slab in range(SLABS + 1):
            row = jnp.concatenate([fold_ref[piece, slab] for piece in range(fold_ref.shape[0])], axis=1)
            row = pltpu.roll(row, cols + LANES - 1 - within, 1)
            if slab < 4:
                row = -row
            north_ref[slab] = mirrored(row, cols)
        north_ref[CORNERS, 0:1, 0:LANES] = from_west_ref[rows : rows + 1, :]
        north_ref[CORNERS, 1:2, 0:LANES] = from_east_ref[rows : rows + 1, :]
        north_ref[CORNERS, 2:3, :] = jnp.full((1, cols), turn_ref[rows - 1], F32)

    wide = cols + LANES
    sums_ref[rows:, :] = jnp.zeros((DEEP, 2 * wide), F32)
    for kind in range(2):
        sums_ref[0:rows, kind * wide : kind * wide + cols] = inside_ref[:, kind * cols : (kind + 1) * cols]

    share_down = jnp.zeros((DEEP, LANES), F32)
    for k in range(DEEP):
        share_down = jnp.where(sub8 == k, share_ref[k], share_down)

    def down(line, f):
        return jnp.sum(jnp.where(lane8 == f * DEEP + sub8, line, 0.0), axis=1, keepdims=True)

    def row_step(near, south, north, west_line, east_line, wet, turn, above, above_south, above_north):
        col = iota((DEEP, cols), 1)
        sides = [
            (
                jnp.where(col == cols - 1, down(east_line, f), roll(near[f], -1, 1)),
                jnp.where(col == 0, down(west_line, f), roll(near[f], 1, 1)),
                north[f],
                south[f],
            )
            for f in range(5)
        ]
        east = jnp.where(col[0:1] == cols - 1, east_line[:, ABOVE : ABOVE + 1], roll(above, -1, 1))
        west = jnp.where(col[0:1] == 0, west_line[:, ABOVE : ABOVE + 1], roll(above, 1, 1))
        above_x, above_y = 0.5 * (east - west), 0.5 * (above_north - above_south)

        def pressed(x, y):
            return PRESS * (above_x + scan_down(x) - 0.5 * x), PRESS * (above_y + scan_down(y) - 0.5 * y)

        return advanced(near, sides, wet, turn, pressed)

    for side, ghost_ref, edge, inner in ((0, south_ref, 0, 1), (1, north_ref, rows - 1, rows - 2)):
        near = [ghost_ref[2 * f] for f in range(5)]
        far = [ghost_ref[2 * f + 1] for f in range(5)]
        own = [level_rows(state_ref.at[f], edge, rows) for f in range(5)]
        own_next = [level_rows(state_ref.at[f], inner, rows) for f in range(5)]
        ring_wet = ghost_ref[10]
        corners = ghost_ref[CORNERS, :, 0:LANES]
        above_near, above_far = ghost_ref[CORNERS, 3:4, :], ghost_ref[CORNERS, 4:5, :]
        above_own, above_next = prefix_ref[edge : edge + 1, :], prefix_ref[inner : inner + 1, :]
        outward, inward = (far, above_far), (own, above_own)
        (south, above_south), (north, above_north) = (outward, inward) if side == 0 else (inward, outward)
        ring = row_step(
            near, south, north, corners[0:1, :], corners[1:2, :], ring_wet, corners[2:3, 0:1], above_near, above_south, above_north
        )
        outward, inward = (near, above_near), (own_next, above_next)
        (south, above_south), (north, above_north) = (outward, inward) if side == 0 else (inward, outward)
        wet = level_rows(mask_ref, edge, rows).astype(F32)
        edge_line = slice(edge, edge + 1)
        new = row_step(
            own, south, north, from_west_ref[edge_line, :], from_east_ref[edge_line, :], wet, turn_ref[edge],
            above_own, above_south, above_north,
        )
        for f in range(5):
            edge_rows_ref[side, f] = new[f]
            ring_rows_ref[side, f] = jnp.where(lat == 0, new[f], ring[f]) if side == 0 else ring[f]
        ring_rows_ref[side, 5] = ring_wet
        at = slice(rows + side, rows + side + 1)
        here = buoyancy_of(ring_rows_ref[side, 2], ring_rows_ref[side, 3])
        sums_ref[at, 0:cols] = jnp.sum(here, axis=0, keepdims=True)
        sums_ref[at, wide : wide + cols] = jnp.sum(ring_wet * share_down[:, 0:1], axis=0, keepdims=True)

    row, lane = iota((rows, LANES), 0), iota((rows, LANES), 1)
    turn = turn_column(turn_ref, rows)
    share_lanes = jnp.zeros((rows, LANES), F32)
    for k in range(DEEP):
        share_lanes = jnp.where((lane & 7) == k, share_ref[k], share_lanes)

    def column_step(near, east, west, north, south):
        dx, dy = 0.5 * (east - west), 0.5 * (north - south)
        lap = (east + west) + (north + south) - 4.0 * near
        zonal, merid = lanes_between(near, 0, 8), lanes_between(near, 8, 16)
        wet = lanes_between(near, WET, WET + 8)
        wet_all = sum(roll(wet, -8 * n, 1) for n in range(2, 7))
        zonal_all = sum(roll(zonal, 8 * n, 1) for n in (2, 3, 4))
        merid_all = sum(roll(merid, 8 * n, 1) for n in (1, 2, 3))
        bx = lanes_between(buoyancy_of(roll(dx, -16, 1), roll(dx, -24, 1)), 0, 8)
        by = lanes_between(buoyancy_of(roll(dy, -8, 1), roll(dy, -16, 1)), 8, 16)
        press_x = lanes_between(PRESS * (dx[:, ABOVE : ABOVE + 1] + scan_lanes(bx) - 0.5 * bx), 0, 8)
        press_y = lanes_between(PRESS * (dy[:, ABOVE : ABOVE + 1] + scan_lanes(by) - 0.5 * by), 8, 16)
        trend = VISCOUS * lap - ADVECT * (zonal_all * dx + merid_all * dy) - press_x - press_y
        trend = trend + lanes_between(turn * roll(near, -8, 1), 0, 8) - lanes_between(turn * roll(near, 8, 1), 8, 16)
        return near + wet_all * trend, wet

    blocks = [jnp.zeros((rows, LANES), F32)] * 2
    sides = ((0, from_west_ref, own_west_ref), (1, from_east_ref, own_east_ref))
    for side, ghost_ref, own_ref in sides:
        near, own = ghost_ref[0:rows, :], own_ref[0:rows, :]
        far, own_next = roll(near, -FAR, 1), roll(own, -FAR, 1)
        north = jnp.where(row == rows - 1, north_ref[CORNERS, side : side + 1, 0:LANES], roll(near, -1, 0))
        south = jnp.where(row == 0, south_ref[CORNERS, side : side + 1, 0:LANES], roll(near, 1, 0))
        east, west = (own, far) if side == 0 else (far, own)
        new, wet = column_step(near, east, west, north, south)
        ring_cols_ref[side] = new
        blocks[0] = jnp.where(lane == side, buoyancy_sum(new), blocks[0])
        blocks[1] = jnp.where(lane == side, jnp.sum(wet * share_lanes, axis=1, keepdims=True), blocks[1])
        east, west = (own_next, near) if side == 0 else (near, own_next)
        new, _ = column_step(own, east, west, roll(own, -1, 0), roll(own, 1, 0))
        edge_cols_ref[side] = new
        column = 0 if side == 0 else cols - 1
        sums_ref[0:rows, column : column + 1] = buoyancy_sum(new)
    for kind in range(2):
        sums_ref[0:rows, kind * wide + cols : (kind + 1) * wide] = blocks[kind]
    for side, edge in ((0, 0), (1, rows - 1)):
        here = buoyancy_of(edge_rows_ref[side, 2], edge_rows_ref[side, 3])
        sums_ref[edge : edge + 1, 0:cols] = jnp.sum(here, axis=0, keepdims=True)


def flux_kernel(n_lat, sums_ref, mine_ref, theirs_ref, partner_ref, flux_ref, flux_rows_ref, flux_cols_ref, above_ref):
    rows, cols = flux_ref.shape[1:]
    half_cols = cols // 2
    wide = 3 * half_cols
    mine, theirs = mine_ref[...], theirs_ref[...]
    first = lax.axis_index("lev") == 0
    halves = (jnp.where(first, mine, theirs), jnp.where(first, theirs, mine))
    at_top = lax.axis_index("lat") == n_lat - 1
    hinge = partner_ref[0]
    within = hinge - (hinge // cols) * cols

    def extra(kind, c):
        found = []
        for part in halves:
            line = jnp.concatenate(
                [part[2 * kind : 2 * kind + 1, 2 * wide :], part[2 * kind + 1 : 2 * kind + 2, 2 * wide :]], axis=1
            )
            found.append(line[:, c * half_cols : (c + 1) * half_cols])
        return jnp.concatenate(found, axis=1)

    flux, flux_south, flux_north, flux_west, flux_east = [], [], [], [], []
    crossed = jnp.zeros((DEEP, 2 * cols), F32)
    for c in range(3):
        pair = jnp.concatenate([extra(2, c), extra(1, c)], axis=1)
        crossed = jnp.where(iota(crossed.shape, 0) == c, pair, crossed)
    crossed = mirrored(pltpu.roll(crossed, 2 * cols - 1 - within, 1), cols)
    row, lane = iota((rows, LANES), 0), iota((rows, LANES), 1)
    for c in range(3):
        bands = [
            jnp.concatenate([part[:, b * wide + c * half_cols : b * wide + (c + 1) * half_cols] for part in halves], axis=1)
            for b in range(2)
        ]
        flux.append(jnp.concatenate(bands, axis=0))
        flux_south.append(extra(0, c))
        flux_north.append(jnp.where(at_top, crossed[c : c + 1, :], extra(1, c)))
        here = lane == c * 16 + row
        for side, part in ((flux_west, halves[1]), (flux_east, halves[0])):
            line = part[6:7, 2 * wide : 2 * wide + LANES]
            side.append(jnp.sum(jnp.where(here, line, 0.0), axis=1, keepdims=True))

    flux_cols = jnp.zeros((rows, LANES), F32)
    for c in range(3):
        flux_ref[c] = flux[c]
        flux_rows_ref[c : c + 1, :] = flux_south[c]
        flux_rows_ref[3 + c : 4 + c, :] = flux_north[c]
        flux_cols = jnp.where(lane == c, flux_west[c], jnp.where(lane == 3 + c, flux_east[c], flux_cols))
    flux_rows_ref[6:8, :] = jnp.zeros((2, cols), F32)
    flux_cols_ref[...] = flux_cols
    reach = cols + LANES
    above_ref[rows:, :] = jnp.zeros((DEEP, reach), F32)
    above_ref[0:rows, 0:cols] = sums_ref[0:rows, 0:cols] + sums_ref[0:rows, reach : reach + cols] * buoyancy_of(flux[0], flux[1])
    ends = jnp.zeros((rows, LANES), F32)
    for side, column, line in ((0, (flux_west[0], flux_west[1]), flux_south), (1, (flux_east[0], flux_east[1]), flux_north)):
        at = slice(rows + side, rows + side + 1)
        above_ref[at, 0:cols] = sums_ref[at, 0:cols] + sums_ref[at, reach : reach + cols] * buoyancy_of(line[0], line[1])
        before, taken = sums_ref[0:rows, cols:reach], sums_ref[0:rows, reach + cols :]
        ends = jnp.where(lane == side, before + taken * buoyancy_of(*column), ends)
    above_ref[0:rows, cols:reach] = ends


def second_kernel(
    state_ref, mask_ref, ring_rows_ref, ring_cols_ref, edge_rows_ref, edge_cols_ref, flux_ref, flux_rows_ref,
    flux_cols_ref, turn_ref, share_ref, out_hbm, flow_ref, tracers_ref, sem,
):
    rows, cols = flux_ref.shape[1:]
    n_r, n_j = rows // DEEP, cols // LANES
    sub8, lane8 = iota((DEEP, LANES), 0), iota((DEEP, LANES), 1)
    lane = iota((rows, LANES), 1)
    turn = turn_column(turn_ref, rows)
    share_down = jnp.zeros((DEEP, LANES), F32)
    share_lanes = jnp.zeros((rows, LANES), F32)
    for k in range(DEEP):
        share_down = jnp.where(sub8 == k, share_ref[k], share_down)
        share_lanes = jnp.where((lane & 7) == k, share_ref[k], share_lanes)

    ring_rows, ring_cols = [], []
    for side in range(2):
        taken = ring_rows_ref[side, 5] * share_down[:, 0:1]
        values = [ring_rows_ref[side, f] for f in range(2)]
        values += [ring_rows_ref[side, 2 + c] + taken * flux_rows_ref[3 * side + c : 3 * side + c + 1, :] for c in range(3)]
        ring_rows.append(values)
        found = ring_cols_ref[side]
        taken = lanes_between(found, WET, WET + 8) * share_lanes
        for c in range(3):
            found = found + roll(taken, 8 * (2 + c) - WET, 1) * flux_cols_ref[:, 3 * side + c : 3 * side + c + 1]
        ring_cols.append(found)

    grid = [(r, j) for r in range(n_r) for j in range(n_j)]

    def cut(value, r, j):
        return value[r * DEEP : (r + 1) * DEEP, j * LANES : (j + 1) * LANES]

    zero = jnp.zeros((DEEP, LANES), F32)
    run = {at: (zero, zero) for at in grid}
    edge_cols = [edge_cols_ref[side] for side in range(2)]
    copies = []

    def column(value, r, n):
        return jnp.broadcast_to(value[r * DEEP : (r + 1) * DEEP, n : n + 1], (DEEP, LANES))

    for k in range(DEEP):
        wets, heats, grids = {}, {}, [[[None] * n_j for _ in range(n_r)] for _ in range(5)]
        for r, j in grid:
            at = tile(r, j, k, rows)
            wet = mask_ref[at].astype(F32)
            taken = wet * share_ref[k]
            wets[r, j] = wet
            heats[r, j] = [taken * cut(flux_ref[c], r, j) for c in range(3)]
            for f in range(5):
                value = state_ref[(f, *at)]
                if j == 0:
                    value = jnp.where(lane8 == 0, column(edge_cols[0], r, f * DEEP + k), value)
                if j == n_j - 1:
                    value = jnp.where(lane8 == LANES - 1, column(edge_cols[1], r, f * DEEP + k), value)
                if r == 0:
                    value = jnp.where(sub8 == 0, edge_rows_ref[0, f, k : k + 1, at[1]], value)
                if r == n_r - 1:
                    value = jnp.where(sub8 == DEEP - 1, edge_rows_ref[1, f, k : k + 1, at[1]], value)
                if f >= 2:
                    value = value + heats[r, j][f - 2]
                grids[f][r][j] = value
        fields = [
            Tiles(
                grids[f],
                [column(ring_cols[0], r, f * DEEP + k) for r in range(n_r)],
                [column(ring_cols[1], r, f * DEEP + k) for r in range(n_r)],
                [ring_rows[0][f][k : k + 1, j * LANES : (j + 1) * LANES] for j in range(n_j)],
                [ring_rows[1][f][k : k + 1, j * LANES : (j + 1) * LANES] for j in range(n_j)],
            )
            for f in range(5)
        ]
        for r, j in grid:
            at = tile(r, j, k, rows)
            over_x, over_y = run[r, j]

            def pressed(x, y):
                run[r, j] = (over_x + x, over_y + y)
                return PRESS * (over_x + 0.5 * x), PRESS * (over_y + 0.5 * y)

            new = advanced(
                [field.grid[r][j] for field in fields],
                [field.around(r, j) for field in fields],
                wets[r, j],
                turn[r * DEEP : (r + 1) * DEEP, 0:1],
                pressed,
                heats[r, j],
            )
            for f in range(5):
                if f < 2:
                    flow_ref[(f, *at)] = new[f]
                else:
                    tracers_ref[(f - 2, *at)] = new[f]
        whole = pl.ds(k * rows, rows)
        copies.append(
            pltpu.make_async_copy(tracers_ref.at[:, whole, :], out_hbm.at[pl.ds(2, 3), whole, :], sem.at[k])
        )
        copies[-1].start()
    for copy in copies:
        copy.wait()


def last_kernel(out_in_hbm, flow_ref, mask_ref, above_ref, out_hbm, moved_ref, sem):
    del out_in_hbm
    rows, cols = mask_ref.shape[0] // DEEP, mask_ref.shape[1]
    above = above_ref[...]
    east, west, north, south = around(
        above[0:rows, 0:cols],
        above[0:rows, cols : cols + 1],
        above[0:rows, cols + 1 : cols + 2],
        above[rows : rows + 1, 0:cols],
        above[rows + 1 : rows + 2, 0:cols],
    )
    push_x, push_y = (0.5 * PRESS) * (east - west), (0.5 * PRESS) * (north - south)
    copies = []
    for k in range(DEEP):
        whole = pl.ds(k * rows, rows)
        wet = mask_ref[whole, :].astype(F32)
        moved_ref[0, whole, :] = flow_ref[0, whole, :] - wet * push_x
        moved_ref[1, whole, :] = flow_ref[1, whole, :] - wet * push_y
        copies.append(pltpu.make_async_copy(moved_ref.at[:, whole, :], out_hbm.at[pl.ds(0, 2), whole, :], sem.at[k]))
        copies[-1].start()
    for copy in copies:
        copy.wait()


def body(n_lon, n_lat, state, mask, coriolis, penetration, flux_tiles, flux_owner, flux_row, fold_partner):
    fields, levels, rows, cols = state.shape
    flat_state = state.reshape(fields, levels * rows, cols)
    flat_mask = mask.reshape(levels * rows, cols)
    last = n_lat - 1

    keep, send, west, east, total = prepare(
        flat_state, flat_mask, flux_tiles, flux_owner, flux_row, fold_partner, n_lon, n_lat
    )

    stages = []
    for axis, size, least in (("lat", n_lat, 2), ("lon", n_lon, 1)):
        bit = size // 2
        while bit >= least:
            stages.append((axis, size, bit))
            bit //= 2
    got = lax.ppermute(send, "lat", [(i, i ^ 1) for i in range(n_lat)])
    prefix = lax.ppermute(total, "lev", [(0, 1)])

    def merged(keep, got):
        half = shape(keep.shape[0] // 2, keep.shape[1])
        return call(merge_kernel, (half, half), [VMEM] * 2, (keep, got), name="merge_flux")

    def passed_on(send, stage):
        axis, size, bit = stage
        return lax.ppermute(send, axis, [(i, i ^ bit) for i in range(size)])

    pieces = cols // LANES
    hinge_piece = fold_partner[0] >> (LANES.bit_length() - 1)
    keep = after(keep, (prefix, hinge_piece))
    keep, send = merged(keep, got)
    got = passed_on(send, stages[0])

    message = shape(SLABS + 1, DEEP, cols)
    top_shape = shape(pieces, SLABS + 1, DEEP, LANES)
    top = call(top_kernel, top_shape, [VMEM] * 3, (flat_state, flat_mask, prefix), name="top_rows")
    top = after(top, send)

    def folded(hinge_piece):
        block, piece = divmod(hinge_piece, pieces)

        def swap(rows_out):
            def across(part, other):
                pairs = [(a * n_lat + last, (other - a) % n_lon * n_lat + last) for a in range(n_lon)]
                return lax.ppermute(part, ("lon", "lat"), pairs)

            return jnp.concatenate([across(rows_out[piece:], block - 1), across(rows_out[: piece + 1], block)], axis=0)

        return swap

    fold = lax.switch(hinge_piece, [folded(n) for n in range(n_lon * pieces)], top)
    side = shape(rows + DEEP, LANES)
    west, east = call(
        functools.partial(columns_kernel, n_lat),
        (side, side),
        [VMEM] * 4 + [SMEM],
        (west, east, prefix, fold, fold_partner),
        name="edge_columns",
    )
    from_west = lax.ppermute(east, "lon", [(i, (i + 1) % n_lon) for i in range(n_lon)])
    from_east = lax.ppermute(west, "lon", [((i + 1) % n_lon, i) for i in range(n_lon)])
    keep = after(keep, (from_west, from_east))
    keep, send = merged(keep, got)
    got = passed_on(send, stages[1])

    from_west, from_east = after((from_west, from_east), send)
    pair, cross = call(
        rows_kernel,
        (message, message),
        [VMEM, VMEM, VMEM, SMEM, VMEM, VMEM],
        (flat_state, flat_mask, prefix, coriolis, from_west, from_east),
        name="edge_rows",
    )
    from_pair = lax.ppermute(pair, "lat", [(i, i ^ 1) for i in range(n_lat)])
    from_cross = lax.ppermute(cross, "lat", [(i, i + 1 if i % 2 else i - 1) for i in range(1, last)])
    keep = after(keep, (pair, cross))
    for stage in stages[2:]:
        keep, send = merged(keep, got)
        got = passed_on(send, stage)

    near_state, near_mask = after((flat_state, flat_mask), send)
    new_state, inside = call(
        inside_kernel,
        (shape(fields, levels * rows, cols), shape(rows, 2 * cols)),
        [VMEM, VMEM, VMEM, SMEM, SMEM],
        (near_state, near_mask, prefix, coriolis, penetration),
        name="first_inside",
    )
    keep = after(keep, inside)
    mine = keep + got
    theirs = lax.ppermute(mine, "lev", [(0, 1), (1, 0)])

    inside = after(inside, mine)
    wide = cols + LANES
    *ring, sums = call(
        functools.partial(rim_kernel, n_lat),
        (
            shape(2, 6, DEEP, cols),
            shape(2, rows, LANES),
            shape(2, 5, DEEP, cols),
            shape(2, rows, LANES),
            shape(rows + DEEP, 2 * wide),
        ),
        [VMEM, VMEM, VMEM, SMEM, SMEM, SMEM] + [VMEM] * 8,
        (
            flat_state, flat_mask, prefix, coriolis, penetration, fold_partner, west, east, from_west, from_east, from_pair,
            from_cross, fold, inside,
        ),
        [pltpu.VMEM((SLABS + 1, DEEP, cols), F32), pltpu.VMEM((SLABS + 1, DEEP, cols), F32)],
        name="first_rim",
    )
    *flux, above = call(
        functools.partial(flux_kernel, n_lat),
        (shape(3, rows, cols), shape(DEEP, cols), shape(rows, LANES), shape(rows + DEEP, wide)),
        [VMEM] * 3 + [SMEM],
        (sums, mine, theirs, fold_partner),
        name="flux_parts",
    )
    above = lax.ppermute(above, "lev", [(0, 1)])

    out = jax.ShapeDtypeStruct(flat_state.shape, F32)
    result, flow = call(
        second_kernel,
        (out, shape(2, levels * rows, cols)),
        [VMEM] * 9 + [SMEM] * 2,
        (new_state, flat_mask, *ring, *flux, coriolis, penetration),
        [pltpu.VMEM((3, levels * rows, cols), F32), pltpu.SemaphoreType.DMA((DEEP,))],
        name="second_substep",
        out_specs=(ANY, VMEM),
    )
    result = call(
        last_kernel,
        out,
        [ANY] + [VMEM] * 3,
        (result, flow, flat_mask, above),
        [pltpu.VMEM((2, levels * rows, cols), F32), pltpu.SemaphoreType.DMA((DEEP,))],
        name="deeper_pressure",
        out_specs=ANY,
        aliases={0: 0},
    )
    return result.reshape(fields, levels, rows, cols)


def solution(mesh):
    n_lon, n_lat = mesh.shape["lon"], mesh.shape["lat"]
    assert mesh.shape["lev"] == 2 and n_lat % 2 == 0 and n_lon > 2
    return jax.shard_map(
        functools.partial(body, n_lon, n_lat),
        mesh=mesh,
        in_specs=(
            P(None, "lev", "lat", "lon"),
            P("lev", "lat", "lon"),
            P("lat"),
            P("lev"),
            P(("lon", "lat"), None, None),
            P(("lon", "lat"), None),
            P(("lon", "lat")),
            P(),
        ),
        out_specs=P(None, "lev", "lat", "lon"),
        check_vma=False,
    )
```

```python
import functools

import jax
import jax.numpy as jnp
from jax import lax
from jax.experimental import pallas as pl
from jax.experimental.pallas import tpu as pltpu
from jax.sharding import PartitionSpec as P

ALPHA = 0.2
BETA = 0.15
PRESS = 0.1
VISCOUS = 0.1
DIFFUSE = 0.1
ADVECT = 0.1

F32 = jnp.float32
I32 = jnp.int32
LANES = 128
DEEP = 8
FAR = 64
WET = 48
ABOVE = 56
SLABS = 11
CORNERS = SLABS
VMEM_BYTES = 16 * 1024 * 1024

VMEM = pl.BlockSpec(memory_space=pltpu.VMEM)
SMEM = pl.BlockSpec(memory_space=pltpu.SMEM)
ANY = pl.BlockSpec(memory_space=pl.ANY)
HBM = pl.BlockSpec(memory_space=pltpu.HBM)


def iota(shape, dim):
    return lax.broadcasted_iota(I32, shape, dim)


def roll(value, shift, axis):
    return pltpu.roll(value, shift % value.shape[axis], axis)


def call(kernel, out_shape, in_specs, args, scratch=(), name=None, out_specs=None, aliases=None):
    return pl.pallas_call(
        kernel,
        out_shape=out_shape,
        in_specs=in_specs,
        out_specs=out_specs or jax.tree.map(lambda _: VMEM, out_shape),
        input_output_aliases=aliases or {},
        scratch_shapes=list(scratch),
        compiler_params=pltpu.CompilerParams(vmem_limit_bytes=VMEM_BYTES),
        name=name,
    )(*args)


def after(values, *others):
    return lax.optimization_barrier((values, others))[0]


def shape(*dims):
    return pltpu.VMEM(dims, F32)


def in_hbm(*arrays):
    return tuple(pltpu.with_memory_space_constraint(array, pltpu.HBM) for array in arrays)


def prepare_kernel(
    n_lon, n_lat, state_hbm, mask_hbm, tiles_hbm, owner_hbm, row_hbm, partner_hbm, keep_ref, send_ref, west_ref, east_ref,
    total_ref, state_ref, mask_ref, x_ref, owners_ref, rows_ref, hinge_ref, sem,
):
    tiles, cols = tiles_hbm.shape[1], tiles_hbm.shape[2]
    half_cols = cols // 2
    rows = 2 * DEEP
    n_y = n_lat // 2
    half = lax.axis_index("lev")
    lat = lax.axis_index("lat")
    core = lax.rem(lat, 2)
    begin = pl.multiple_of(half * half_cols, LANES)
    indices = [
        pltpu.make_async_copy(owner_hbm, owners_ref, sem.at[0]),
        pltpu.make_async_copy(row_hbm, rows_ref, sem.at[1]),
        pltpu.make_async_copy(partner_hbm, hinge_ref, sem.at[2]),
    ]
    fluxes = [
        pltpu.make_async_copy(
            tiles_hbm.at[c, :, pl.ds(begin, half_cols)], x_ref.at[:, pl.ds(c * half_cols, half_cols)], sem.at[3 + c]
        )
        for c in range(3)
    ]
    fields = [
        pltpu.make_async_copy(state_hbm, state_ref, sem.at[6]),
        pltpu.make_async_copy(mask_hbm, mask_ref, sem.at[7]),
    ]
    for copy in indices + fluxes + fields:
        copy.start()
    for copy in indices:
        copy.wait()

    key = owners_ref[...] * rows + rows_ref[...]
    hinge_block = hinge_ref[0] // cols
    slots = keep_ref.shape[0]
    slot = iota((slots, tiles), 0)
    group, sub = slot >> 3, slot & 7
    at_y = (group >> (n_lon.bit_length() - 1)) ^ (lat // 2)
    at_lon = (group & (n_lon - 1)) ^ lax.axis_index("lon")

    def wrapped(lon):
        return jnp.where(lon < 0, lon + n_lon, jnp.where(lon >= n_lon, lon - n_lon, lon))

    def one_hot(hit):
        return jnp.where(hit, 1.0, 0.0).astype(jnp.bfloat16)

    def weights(to_core):
        lat = 2 * at_y + to_core
        owner = at_lon * n_lat + lat
        last = lat == n_lat - 1
        top = n_lat * rows - 1
        south = jnp.where(lat == 0, owner * rows, owner * rows - 1)
        north = jnp.where(last, wrapped(hinge_block - at_lon) * (n_lat * rows) + top, (owner + 1) * rows)
        third = jnp.where(last, wrapped(hinge_block - at_lon - 1) * (n_lat * rows) + top, -1)
        kind = sub >> 1
        extra_key = jnp.where(kind == 0, south, jnp.where(kind == 1, north, jnp.where(kind == 2, third, -1)))
        extra = key == extra_key
        beside = wrapped(at_lon + 1 - 2 * half) * n_lat + lat
        return (
            one_hot(key == owner * rows + sub),
            one_hot(key == owner * rows + DEEP + sub),
            one_hot(extra & ((sub & 1) == 0)),
            one_hot(extra & ((sub & 1) == 1)),
            one_hot(((key >> 4) == beside) & (sub == 6)),
        )

    def split(x):
        first = x.astype(jnp.bfloat16)
        rest = x - first.astype(F32)
        second = rest.astype(jnp.bfloat16)
        third = (rest - second.astype(F32)).astype(jnp.bfloat16)
        return first, second, third

    square = iota((tiles, tiles), 0) == iota((tiles, tiles), 1)
    row_of = jnp.sum(jnp.where(square, (key & (rows - 1)).astype(F32), 0.0), axis=1, keepdims=True).astype(I32)

    for copy in fluxes:
        copy.wait()
    x = x_ref[...]
    lane = iota((tiles, LANES), 1)
    edge = jnp.zeros((tiles, LANES), F32)
    for c in range(3):
        begin = c * half_cols
        value = jnp.where(half == 0, x[:, begin : begin + 1], x[:, begin + half_cols - 1 : begin + half_cols])
        edge = jnp.where(((lane >> 4) == c) & ((lane & 15) == row_of), value, edge)
    parts, edges = split(x), split(edge)
    wide = 3 * half_cols
    quarter = wide // 2

    def dot(hot, terms, begin, end):
        products = [
            jnp.dot(hot, term[:, begin:end], preferred_element_type=F32) for term in reversed(terms)
        ]
        return products[0] + products[1] + products[2]

    for out_ref, to_core in ((keep_ref, core), (send_ref, 1 - core)):
        low, high, even, odd, ring = weights(to_core)
        out_ref[:, 0:wide] = dot(low, parts, 0, wide)
        out_ref[:, wide : 2 * wide] = dot(high, parts, 0, wide)
        rest = dot(even, parts, 0, quarter) + dot(odd, parts, quarter, wide)
        beside = dot(ring, edges, 0, LANES)
        out_ref[:, 2 * wide : 2 * wide + LANES] = rest[:, 0:LANES] + beside
        out_ref[:, 2 * wide + LANES :] = rest[:, LANES:]

    for copy in fields:
        copy.wait()
    total = jnp.zeros(total_ref.shape, F32)
    for k in range(DEEP):
        at = slice(k * rows, (k + 1) * rows)
        total = total + buoyancy_of(state_ref[2, at, :], state_ref[3, at, :])
    total_ref[...] = total
    edge_columns(state_ref, mask_ref, west_ref, east_ref)


def merge_kernel(kept_ref, got_ref, keep_ref, send_ref):
    half = keep_ref.shape[0]
    send_ref[...] = kept_ref[half:, :] + got_ref[half:, :]
    keep_ref[...] = kept_ref[0:half, :] + got_ref[0:half, :]


def prepare(state, mask, flux_tiles, flux_owner, flux_row, fold_partner, n_lon, n_lat):
    tiles, _, cols = flux_tiles.shape
    wide = 3 * (cols // 2)
    slots = shape(n_lon * n_lat // 2 * DEEP, 2 * wide + wide // 2)
    side = shape(2 * DEEP, LANES)
    return call(
        functools.partial(prepare_kernel, n_lon, n_lat),
        (slots, slots, side, side, shape(2 * DEEP, cols)),
        [HBM] * 6,
        in_hbm(
            state,
            mask,
            flux_tiles.transpose(1, 0, 2),
            flux_owner.reshape(1, tiles),
            flux_row.reshape(1, tiles),
            fold_partner,
        ),
        [
            pltpu.VMEM(state.shape, F32),
            pltpu.VMEM(mask.shape, I32),
            pltpu.VMEM((tiles, wide), F32),
            pltpu.VMEM((1, tiles), I32),
            pltpu.VMEM((1, tiles), I32),
            pltpu.SMEM(fold_partner.shape, I32),
            pltpu.SemaphoreType.DMA((8,)),
        ],
        name="prepare",
    )


def cell(ref, n):
    return ref[0:1, n : n + 1]


def scalar_of(ref):
    row = ref[0:1, 0:LANES].astype(F32)
    return jnp.sum(jnp.where(iota(row.shape, 1) == 0, row, 0.0)).astype(I32)


def level_rows(ref, row, rows):
    return jnp.concatenate([ref[k * rows + row : k * rows + row + 1, :] for k in range(DEEP)], axis=0)


def buoyancy_of(temper, saline):
    return ALPHA * temper - BETA * saline


def edge_rows(state_ref, mask_ref, out_ref, rows, near, far):
    for f in range(5):
        out_ref[2 * f] = level_rows(state_ref.at[f], near, rows)
        out_ref[2 * f + 1] = level_rows(state_ref.at[f], far, rows)
    out_ref[10] = level_rows(mask_ref, near, rows).astype(F32)


def edge_columns(state_ref, mask_ref, west_ref, east_ref):
    rows, cols = west_ref.shape[0], state_ref.shape[2]
    lane = iota((rows, LANES), 1)
    last = slice(cols - LANES, cols)
    west = jnp.zeros((rows, LANES), F32)
    east = jnp.zeros((rows, LANES), F32)
    for k in range(DEEP):
        at = slice(k * rows, (k + 1) * rows)
        for f in range(5):
            to = f * DEEP + k
            left, right = state_ref[f, at, 0:LANES], state_ref[f, at, last]
            west = jnp.where(lane == to, roll(left, to, 1), west)
            west = jnp.where(lane == FAR + to, roll(left, FAR + to - 1, 1), west)
            east = jnp.where(lane == to, roll(right, to + 1, 1), east)
            east = jnp.where(lane == FAR + to, roll(right, FAR + to + 2, 1), east)
        west = jnp.where(lane == WET + k, roll(mask_ref[at, 0:LANES].astype(F32), WET + k, 1), west)
        east = jnp.where(lane == WET + k, roll(mask_ref[at, last].astype(F32), WET + k + 1, 1), east)
    west_ref[...] = west
    east_ref[...] = east


def top_kernel(state_ref, mask_ref, prefix_ref, top_ref):
    rows, cols = prefix_ref.shape
    for slab in range(SLABS):
        if slab < 10:
            line = level_rows(state_ref.at[slab // 2], rows - 1 - slab % 2, rows)
        else:
            line = level_rows(mask_ref, rows - 1, rows).astype(F32)
        for piece in range(cols // LANES):
            top_ref[piece, slab] = line[:, piece * LANES : (piece + 1) * LANES]
    top_ref[:, CORNERS] = jnp.zeros((cols // LANES, DEEP, LANES), F32)
    for n in (1, 2):
        for piece in range(cols // LANES):
            top_ref[piece, CORNERS, 2 + n : 3 + n, :] = prefix_ref[rows - n : rows - n + 1, piece * LANES : (piece + 1) * LANES]


def columns_kernel(n_lat, west_ref, east_ref, prefix_ref, fold_ref, partner_ref, west_out_ref, east_out_ref):
    rows, cols = prefix_ref.shape
    lane = iota((rows, LANES), 1)
    for side, in_ref, out_ref in ((0, west_ref, west_out_ref), (1, east_ref, east_out_ref)):
        near, far = (0, 1) if side == 0 else (cols - 1, cols - 2)
        value = jnp.where(lane == ABOVE, prefix_ref[:, near : near + 1], in_ref[...])
        out_ref[0:rows, :] = jnp.where(lane == FAR + ABOVE, prefix_ref[:, far : far + 1], value)
        out_ref[rows:, :] = jnp.zeros((DEEP, LANES), F32)

    @pl.when(lax.axis_index("lat") == n_lat - 1)
    def _():
        within = cell(partner_ref, 0) & (LANES - 1)
        sub8, lane8 = iota((DEEP, LANES), 0), iota((DEEP, LANES), 1)
        for out_ref in (west_out_ref, east_out_ref):
            line = jnp.zeros((DEEP, LANES), F32)
            for slab in (0, 2, 4, 6, 8, CORNERS):
                if out_ref is west_out_ref:
                    found = jnp.where(lane8 == within, fold_ref[fold_ref.shape[0] - 1, slab], 0.0)
                else:
                    found = jnp.where(lane8 == within + 1, fold_ref[0, slab], 0.0)
                    found = jnp.where(jnp.where(lane8 == 0, within, 0) == LANES - 1, fold_ref[1, slab], found)
                found = jnp.sum(found, axis=1, keepdims=True)
                here = (lane8 == ABOVE) & (sub8 == 3) if slab == CORNERS else lane8 == (slab // 2) * DEEP + sub8
                line = jnp.where(here, -found if slab < 4 else found, line)
            out_ref[rows : rows + 1, :] = jnp.sum(line, axis=0, keepdims=True)


def corner_slab(out_ref, prefix_ref, turn_ref, from_west_ref, from_east_ref, near, far):
    out_ref[CORNERS] = jnp.broadcast_to(cell(turn_ref, near), out_ref.shape[1:])
    out_ref[CORNERS, 0:1, 0:LANES] = from_west_ref[near : near + 1, :]
    out_ref[CORNERS, 1:2, 0:LANES] = from_east_ref[near : near + 1, :]
    out_ref[CORNERS, 3:4, :] = prefix_ref[near : near + 1, :]
    out_ref[CORNERS, 4:5, :] = prefix_ref[far : far + 1, :]


def rows_kernel(state_ref, mask_ref, prefix_ref, turn_ref, from_west_ref, from_east_ref, pair_ref, cross_ref):
    rows = prefix_ref.shape[0]
    odd = lax.rem(lax.axis_index("lat"), 2) == 1

    def fill(out_ref, near, far):
        edge_rows(state_ref, mask_ref, out_ref, rows, near, far)
        corner_slab(out_ref, prefix_ref, turn_ref, from_west_ref, from_east_ref, near, far)

    @pl.when(odd)
    def _():
        fill(pair_ref, 0, 1)
        fill(cross_ref, rows - 1, rows - 2)

    @pl.when(jnp.logical_not(odd))
    def _():
        fill(pair_ref, rows - 1, rows - 2)
        fill(cross_ref, 0, 1)


def around(value, west, east, south, north):
    rows, cols = value.shape
    row, col = iota((rows, cols), 0), iota((rows, cols), 1)
    return (
        jnp.where(col == cols - 1, east, roll(value, -1, 1)),
        jnp.where(col == 0, west, roll(value, 1, 1)),
        jnp.where(row == rows - 1, north, roll(value, -1, 0)),
        jnp.where(row == 0, south, roll(value, 1, 0)),
    )


def advanced(values, sides, wet, turn, pressed, heat=None):
    zonal, merid = values[0], values[1]
    sums = [(e + w) + (n + s) for e, w, n, s in sides]
    across = [(e - w, n - s) for e, w, n, s in sides]
    press_x, press_y = pressed(
        0.5 * buoyancy_of(across[2][0], across[3][0]), 0.5 * buoyancy_of(across[2][1], across[3][1])
    )
    out = []
    carry_x, carry_y = (0.5 * ADVECT) * zonal, (0.5 * ADVECT) * merid
    for f in range(5):
        spread = (VISCOUS if f < 2 else DIFFUSE) * (sums[f] - 4.0 * values[f])
        if f == 0:
            trend = spread + (turn * merid - press_x)
        elif f == 1:
            trend = spread - (turn * zonal + press_y)
        else:
            trend = spread - (carry_x * across[f][0] + carry_y * across[f][1])
        new = values[f] + wet * trend
        out.append(new if heat is None or f < 2 else new + heat[f - 2])
    return out


class Tiles:
    def __init__(self, grid, west=None, east=None, south=None, north=None):
        self.grid, self.ghosts, self.turned = grid, (west, east, south, north), {}
        self.lane, self.sub = iota((DEEP, LANES), 1), iota((DEEP, LANES), 0)

    def rolled(self, r, j, shift, axis):
        at = (r, j, shift, axis)
        if at not in self.turned:
            self.turned[at] = roll(self.grid[r][j], shift, axis)
        return self.turned[at]

    def side(self, r, j, shift, axis):
        here = self.rolled(r, j, shift, axis)
        r_from, j_from = (r, j - shift) if axis else (r - shift, j)
        edge = (0 if shift == 1 else LANES - 1) if axis else (0 if shift == 1 else DEEP - 1)
        if 0 <= r_from < len(self.grid) and 0 <= j_from < len(self.grid[0]):
            other = self.rolled(r_from, j_from, shift, axis)
        else:
            ghost = self.ghosts[(0 if shift == 1 else 1) + (0 if axis else 2)]
            if ghost is None:
                return here
            other = ghost[r if axis else j]
        return jnp.where((self.lane if axis else self.sub) == edge, other, here)

    def around(self, r, j):
        return self.side(r, j, -1, 1), self.side(r, j, 1, 1), self.side(r, j, -1, 0), self.side(r, j, 1, 0)


def tile(r, j, k, rows):
    return slice(k * rows + r * DEEP, k * rows + (r + 1) * DEEP), slice(j * LANES, (j + 1) * LANES)


def turn_column(turn_ref, rows):
    row = iota((rows, LANES), 0)
    column = jnp.zeros((rows, LANES), F32)
    for j in range(rows):
        column = jnp.where(row == j, cell(turn_ref, j), column)
    return column


def mirrored(value, width):
    back = LANES - 1 - iota((value.shape[0], LANES), 1)
    blocks = [
        jnp.take_along_axis(value[:, begin : begin + LANES], back, axis=1)
        for begin in range(width - LANES, -1, -LANES)
    ]
    return jnp.concatenate(blocks, axis=1)


def scan_down(value):
    row = iota(value.shape, 0)
    for step in (1, 2, 4):
        value = value + jnp.where(row >= step, roll(value, step, 0), 0.0)
    return value


def scan_lanes(value):
    lane = iota(value.shape, 1) & 7
    for step in (1, 2, 4):
        value = value + jnp.where(lane >= step, roll(value, step, 1), 0.0)
    return value


def lanes_between(value, begin, end):
    lane = iota(value.shape, 1)
    return jnp.where((lane >= begin) & (lane < end), value, 0.0)


def buoyancy_sum(column):
    here = lanes_between(buoyancy_of(roll(column, -16, 1), roll(column, -24, 1)), 0, 8)
    return jnp.sum(here, axis=1, keepdims=True)


def inside_kernel(state_ref, mask_ref, prefix_ref, turn_ref, share_ref, new_ref, sums_ref):
    rows, cols = prefix_ref.shape
    n_r, n_j = rows // DEEP, cols // LANES
    turn = turn_column(turn_ref, rows)
    grid = [(r, j) for r in range(n_r) for j in range(n_j)]
    zero = jnp.zeros((DEEP, LANES), F32)
    prefix = Tiles([[prefix_ref[tile(r, j, 0, rows)] for j in range(n_j)] for r in range(n_r)])
    run = {}
    for at in grid:
        east, west, north, south = prefix.around(*at)
        run[at] = [0.5 * (east - west), 0.5 * (north - south), zero, zero]
    for k in range(DEEP):
        fields = [Tiles([[state_ref[(f, *tile(r, j, k, rows))] for j in range(n_j)] for r in range(n_r)]) for f in range(5)]
        for r, j in grid:
            at = tile(r, j, k, rows)
            above_x, above_y, total, absorbed = run[r, j]
            slopes = []

            def pressed(x, y):
                slopes.extend((x, y))
                return PRESS * (above_x + 0.5 * x), PRESS * (above_y + 0.5 * y)

            values = [field.grid[r][j] for field in fields]
            wet = mask_ref[at].astype(F32)
            new = advanced(
                values, [field.around(r, j) for field in fields], wet, turn[r * DEEP : (r + 1) * DEEP, 0:1], pressed
            )
            for f in range(5):
                new_ref[(f, *at)] = new[f]
            run[r, j] = [
                above_x + slopes[0],
                above_y + slopes[1],
                total + buoyancy_of(new[2], new[3]),
                absorbed + wet * cell(share_ref, k),
            ]
    for r, j in grid:
        for kind in range(2):
            at = slice(kind * cols + j * LANES, kind * cols + (j + 1) * LANES)
            sums_ref[r * DEEP : (r + 1) * DEEP, at] = run[r, j][2 + kind]


def rim_kernel(
    n_lat, state_ref, mask_ref, prefix_ref, turn_ref, share_ref, partner_ref, own_west_ref, own_east_ref,
    from_west_ref, from_east_ref, pair_ref, cross_ref, fold_ref, inside_ref, ring_rows_ref, ring_cols_ref,
    edge_rows_ref, edge_cols_ref, sums_ref, south_ref, north_ref,
):
    rows, cols = prefix_ref.shape
    lat = lax.axis_index("lat")
    odd = lax.rem(lat, 2) == 1
    within = scalar_of(partner_ref) & (LANES - 1)
    at_top = lat == n_lat - 1

    @pl.when(odd)
    def _():
        south_ref[...] = pair_ref[...]

    @pl.when(jnp.logical_not(odd))
    def _():
        north_ref[...] = pair_ref[...]

    @pl.when(jnp.logical_not(odd) & (lat > 0))
    def _():
        south_ref[...] = cross_ref[...]

    @pl.when(odd & (lat < n_lat - 1))
    def _():
        north_ref[...] = cross_ref[...]

    @pl.when(lat == 0)
    def _():
        edge_rows(state_ref, mask_ref, south_ref, rows, 0, 0)
        corner_slab(south_ref, prefix_ref, turn_ref, from_west_ref, from_east_ref, 0, 0)

    sub8, lane8 = iota((DEEP, LANES), 0), iota((DEEP, LANES), 1)

    @pl.when(at_top)
    def _():
        for slab in range(SLABS + 1):
            row = jnp.concatenate([fold_ref[piece, slab] for piece in range(fold_ref.shape[0])], axis=1)
            row = pltpu.roll(row, cols + LANES - 1 - within, 1)
            if slab < 4:
                row = -row
            north_ref[slab] = mirrored(row, cols)
        north_ref[CORNERS, 0:1, 0:LANES] = from_west_ref[rows : rows + 1, :]
        north_ref[CORNERS, 1:2, 0:LANES] = from_east_ref[rows : rows + 1, :]
        north_ref[CORNERS, 2:3, :] = jnp.broadcast_to(cell(turn_ref, rows - 1), (1, cols))

    wide = cols + LANES
    sums_ref[rows:, :] = jnp.zeros((DEEP, 2 * wide), F32)
    for kind in range(2):
        sums_ref[0:rows, kind * wide : kind * wide + cols] = inside_ref[:, kind * cols : (kind + 1) * cols]

    share_down = jnp.zeros((DEEP, LANES), F32)
    for k in range(DEEP):
        share_down = jnp.where(sub8 == k, cell(share_ref, k), share_down)

    def down(line, f):
        return jnp.sum(jnp.where(lane8 == f * DEEP + sub8, line, 0.0), axis=1, keepdims=True)

    def row_step(near, south, north, west_line, east_line, wet, turn, above, above_south, above_north):
        col = iota((DEEP, cols), 1)
        sides = [
            (
                jnp.where(col == cols - 1, down(east_line, f), roll(near[f], -1, 1)),
                jnp.where(col == 0, down(west_line, f), roll(near[f], 1, 1)),
                north[f],
                south[f],
            )
            for f in range(5)
        ]
        east = jnp.where(col[0:1] == cols - 1, east_line[:, ABOVE : ABOVE + 1], roll(above, -1, 1))
        west = jnp.where(col[0:1] == 0, west_line[:, ABOVE : ABOVE + 1], roll(above, 1, 1))
        above_x, above_y = 0.5 * (east - west), 0.5 * (above_north - above_south)

        def pressed(x, y):
            return PRESS * (above_x + scan_down(x) - 0.5 * x), PRESS * (above_y + scan_down(y) - 0.5 * y)

        return advanced(near, sides, wet, turn, pressed)

    for side, ghost_ref, edge, inner in ((0, south_ref, 0, 1), (1, north_ref, rows - 1, rows - 2)):
        near = [ghost_ref[2 * f] for f in range(5)]
        far = [ghost_ref[2 * f + 1] for f in range(5)]
        own = [level_rows(state_ref.at[f], edge, rows) for f in range(5)]
        own_next = [level_rows(state_ref.at[f], inner, rows) for f in range(5)]
        ring_wet = ghost_ref[10]
        corners = ghost_ref[CORNERS, :, 0:LANES]
        above_near, above_far = ghost_ref[CORNERS, 3:4, :], ghost_ref[CORNERS, 4:5, :]
        above_own, above_next = prefix_ref[edge : edge + 1, :], prefix_ref[inner : inner + 1, :]
        outward, inward = (far, above_far), (own, above_own)
        (south, above_south), (north, above_north) = (outward, inward) if side == 0 else (inward, outward)
        ring = row_step(
            near, south, north, corners[0:1, :], corners[1:2, :], ring_wet, corners[2:3, 0:1], above_near, above_south, above_north
        )
        outward, inward = (near, above_near), (own_next, above_next)
        (south, above_south), (north, above_north) = (outward, inward) if side == 0 else (inward, outward)
        wet = level_rows(mask_ref, edge, rows).astype(F32)
        edge_line = slice(edge, edge + 1)
        new = row_step(
            own, south, north, from_west_ref[edge_line, :], from_east_ref[edge_line, :], wet, cell(turn_ref, edge),
            above_own, above_south, above_north,
        )
        for f in range(5):
            edge_rows_ref[side, f] = new[f]
            ring_rows_ref[side, f] = jnp.where(lat == 0, new[f], ring[f]) if side == 0 else ring[f]
        ring_rows_ref[side, 5] = ring_wet
        at = slice(rows + side, rows + side + 1)
        here = buoyancy_of(ring_rows_ref[side, 2], ring_rows_ref[side, 3])
        sums_ref[at, 0:cols] = jnp.sum(here, axis=0, keepdims=True)
        sums_ref[at, wide : wide + cols] = jnp.sum(ring_wet * share_down[:, 0:1], axis=0, keepdims=True)

    row, lane = iota((rows, LANES), 0), iota((rows, LANES), 1)
    turn = turn_column(turn_ref, rows)
    share_lanes = jnp.zeros((rows, LANES), F32)
    for k in range(DEEP):
        share_lanes = jnp.where((lane & 7) == k, cell(share_ref, k), share_lanes)

    def column_step(near, east, west, north, south):
        dx, dy = 0.5 * (east - west), 0.5 * (north - south)
        lap = (east + west) + (north + south) - 4.0 * near
        zonal, merid = lanes_between(near, 0, 8), lanes_between(near, 8, 16)
        wet = lanes_between(near, WET, WET + 8)
        wet_all = sum(roll(wet, -8 * n, 1) for n in range(2, 7))
        zonal_all = sum(roll(zonal, 8 * n, 1) for n in (2, 3, 4))
        merid_all = sum(roll(merid, 8 * n, 1) for n in (1, 2, 3))
        bx = lanes_between(buoyancy_of(roll(dx, -16, 1), roll(dx, -24, 1)), 0, 8)
        by = lanes_between(buoyancy_of(roll(dy, -8, 1), roll(dy, -16, 1)), 8, 16)
        press_x = lanes_between(PRESS * (dx[:, ABOVE : ABOVE + 1] + scan_lanes(bx) - 0.5 * bx), 0, 8)
        press_y = lanes_between(PRESS * (dy[:, ABOVE : ABOVE + 1] + scan_lanes(by) - 0.5 * by), 8, 16)
        trend = VISCOUS * lap - ADVECT * (zonal_all * dx + merid_all * dy) - press_x - press_y
        trend = trend + lanes_between(turn * roll(near, -8, 1), 0, 8) - lanes_between(turn * roll(near, 8, 1), 8, 16)
        return near + wet_all * trend, wet

    blocks = [jnp.zeros((rows, LANES), F32)] * 2
    sides = ((0, from_west_ref, own_west_ref), (1, from_east_ref, own_east_ref))
    for side, ghost_ref, own_ref in sides:
        near, own = ghost_ref[0:rows, :], own_ref[0:rows, :]
        far, own_next = roll(near, -FAR, 1), roll(own, -FAR, 1)
        north = jnp.where(row == rows - 1, north_ref[CORNERS, side : side + 1, 0:LANES], roll(near, -1, 0))
        south = jnp.where(row == 0, south_ref[CORNERS, side : side + 1, 0:LANES], roll(near, 1, 0))
        east, west = (own, far) if side == 0 else (far, own)
        new, wet = column_step(near, east, west, north, south)
        ring_cols_ref[side] = new
        blocks[0] = jnp.where(lane == side, buoyancy_sum(new), blocks[0])
        blocks[1] = jnp.where(lane == side, jnp.sum(wet * share_lanes, axis=1, keepdims=True), blocks[1])
        east, west = (own_next, near) if side == 0 else (near, own_next)
        new, _ = column_step(own, east, west, roll(own, -1, 0), roll(own, 1, 0))
        edge_cols_ref[side] = new
        column = 0 if side == 0 else cols - 1
        sums_ref[0:rows, column : column + 1] = buoyancy_sum(new)
    for kind in range(2):
        sums_ref[0:rows, kind * wide + cols : (kind + 1) * wide] = blocks[kind]
    for side, edge in ((0, 0), (1, rows - 1)):
        here = buoyancy_of(edge_rows_ref[side, 2], edge_rows_ref[side, 3])
        sums_ref[edge : edge + 1, 0:cols] = jnp.sum(here, axis=0, keepdims=True)


def flux_kernel(n_lat, sums_ref, mine_ref, theirs_ref, partner_ref, flux_ref, flux_rows_ref, flux_cols_ref, above_ref):
    rows, cols = flux_ref.shape[1:]
    half_cols = cols // 2
    wide = 3 * half_cols
    mine, theirs = mine_ref[...], theirs_ref[...]
    first = lax.axis_index("lev") == 0
    halves = (jnp.where(first, mine, theirs), jnp.where(first, theirs, mine))
    at_top = lax.axis_index("lat") == n_lat - 1
    within = scalar_of(partner_ref) & (cols - 1)

    def extra(kind, c):
        found = []
        for part in halves:
            line = jnp.concatenate(
                [part[2 * kind : 2 * kind + 1, 2 * wide :], part[2 * kind + 1 : 2 * kind + 2, 2 * wide :]], axis=1
            )
            found.append(line[:, c * half_cols : (c + 1) * half_cols])
        return jnp.concatenate(found, axis=1)

    flux, flux_south, flux_north, flux_west, flux_east = [], [], [], [], []
    crossed = jnp.zeros((DEEP, 2 * cols), F32)
    for c in range(3):
        pair = jnp.concatenate([extra(2, c), extra(1, c)], axis=1)
        crossed = jnp.where(iota(crossed.shape, 0) == c, pair, crossed)
    crossed = mirrored(pltpu.roll(crossed, 2 * cols - 1 - within, 1), cols)
    row, lane = iota((rows, LANES), 0), iota((rows, LANES), 1)
    for c in range(3):
        bands = [
            jnp.concatenate([part[:, b * wide + c * half_cols : b * wide + (c + 1) * half_cols] for part in halves], axis=1)
            for b in range(2)
        ]
        flux.append(jnp.concatenate(bands, axis=0))
        flux_south.append(extra(0, c))
        flux_north.append(jnp.where(at_top, crossed[c : c + 1, :], extra(1, c)))
        here = lane == c * 16 + row
        for side, part in ((flux_west, halves[1]), (flux_east, halves[0])):
            line = part[6:7, 2 * wide : 2 * wide + LANES]
            side.append(jnp.sum(jnp.where(here, line, 0.0), axis=1, keepdims=True))

    flux_cols = jnp.zeros((rows, LANES), F32)
    for c in range(3):
        flux_ref[c] = flux[c]
        flux_rows_ref[c : c + 1, :] = flux_south[c]
        flux_rows_ref[3 + c : 4 + c, :] = flux_north[c]
        flux_cols = jnp.where(lane == c, flux_west[c], jnp.where(lane == 3 + c, flux_east[c], flux_cols))
    flux_rows_ref[6:8, :] = jnp.zeros((2, cols), F32)
    flux_cols_ref[...] = flux_cols
    reach = cols + LANES
    above_ref[rows:, :] = jnp.zeros((DEEP, reach), F32)
    above_ref[0:rows, 0:cols] = sums_ref[0:rows, 0:cols] + sums_ref[0:rows, reach : reach + cols] * buoyancy_of(flux[0], flux[1])
    ends = jnp.zeros((rows, LANES), F32)
    for side, column, line in ((0, (flux_west[0], flux_west[1]), flux_south), (1, (flux_east[0], flux_east[1]), flux_north)):
        at = slice(rows + side, rows + side + 1)
        above_ref[at, 0:cols] = sums_ref[at, 0:cols] + sums_ref[at, reach : reach + cols] * buoyancy_of(line[0], line[1])
        before, taken = sums_ref[0:rows, cols:reach], sums_ref[0:rows, reach + cols :]
        ends = jnp.where(lane == side, before + taken * buoyancy_of(*column), ends)
    above_ref[0:rows, cols:reach] = ends


def second_kernel(
    state_ref, mask_ref, ring_rows_ref, ring_cols_ref, edge_rows_ref, edge_cols_ref, flux_ref, flux_rows_ref,
    flux_cols_ref, turn_ref, share_ref, out_hbm, flow_ref, tracers_ref, sem,
):
    rows, cols = flux_ref.shape[1:]
    n_r, n_j = rows // DEEP, cols // LANES
    sub8, lane8 = iota((DEEP, LANES), 0), iota((DEEP, LANES), 1)
    lane = iota((rows, LANES), 1)
    turn = turn_column(turn_ref, rows)
    share_down = jnp.zeros((DEEP, LANES), F32)
    share_lanes = jnp.zeros((rows, LANES), F32)
    for k in range(DEEP):
        share_down = jnp.where(sub8 == k, cell(share_ref, k), share_down)
        share_lanes = jnp.where((lane & 7) == k, cell(share_ref, k), share_lanes)

    ring_rows, ring_cols = [], []
    for side in range(2):
        taken = ring_rows_ref[side, 5] * share_down[:, 0:1]
        values = [ring_rows_ref[side, f] for f in range(2)]
        values += [ring_rows_ref[side, 2 + c] + taken * flux_rows_ref[3 * side + c : 3 * side + c + 1, :] for c in range(3)]
        ring_rows.append(values)
        found = ring_cols_ref[side]
        taken = lanes_between(found, WET, WET + 8) * share_lanes
        for c in range(3):
            found = found + roll(taken, 8 * (2 + c) - WET, 1) * flux_cols_ref[:, 3 * side + c : 3 * side + c + 1]
        ring_cols.append(found)

    grid = [(r, j) for r in range(n_r) for j in range(n_j)]

    def cut(value, r, j):
        return value[r * DEEP : (r + 1) * DEEP, j * LANES : (j + 1) * LANES]

    zero = jnp.zeros((DEEP, LANES), F32)
    run = {at: (zero, zero) for at in grid}
    edge_cols = [edge_cols_ref[side] for side in range(2)]
    copies = []

    def column(value, r, n):
        return jnp.broadcast_to(value[r * DEEP : (r + 1) * DEEP, n : n + 1], (DEEP, LANES))

    for k in range(DEEP):
        wets, heats, grids = {}, {}, [[[None] * n_j for _ in range(n_r)] for _ in range(5)]
        for r, j in grid:
            at = tile(r, j, k, rows)
            wet = mask_ref[at].astype(F32)
            taken = wet * cell(share_ref, k)
            wets[r, j] = wet
            heats[r, j] = [taken * cut(flux_ref[c], r, j) for c in range(3)]
            for f in range(5):
                value = state_ref[(f, *at)]
                if j == 0:
                    value = jnp.where(lane8 == 0, column(edge_cols[0], r, f * DEEP + k), value)
                if j == n_j - 1:
                    value = jnp.where(lane8 == LANES - 1, column(edge_cols[1], r, f * DEEP + k), value)
                if r == 0:
                    value = jnp.where(sub8 == 0, edge_rows_ref[0, f, k : k + 1, at[1]], value)
                if r == n_r - 1:
                    value = jnp.where(sub8 == DEEP - 1, edge_rows_ref[1, f, k : k + 1, at[1]], value)
                if f >= 2:
                    value = value + heats[r, j][f - 2]
                grids[f][r][j] = value
        fields = [
            Tiles(
                grids[f],
                [column(ring_cols[0], r, f * DEEP + k) for r in range(n_r)],
                [column(ring_cols[1], r, f * DEEP + k) for r in range(n_r)],
                [ring_rows[0][f][k : k + 1, j * LANES : (j + 1) * LANES] for j in range(n_j)],
                [ring_rows[1][f][k : k + 1, j * LANES : (j + 1) * LANES] for j in range(n_j)],
            )
            for f in range(5)
        ]
        for r, j in grid:
            at = tile(r, j, k, rows)
            over_x, over_y = run[r, j]

            def pressed(x, y):
                run[r, j] = (over_x + x, over_y + y)
                return PRESS * (over_x + 0.5 * x), PRESS * (over_y + 0.5 * y)

            new = advanced(
                [field.grid[r][j] for field in fields],
                [field.around(r, j) for field in fields],
                wets[r, j],
                turn[r * DEEP : (r + 1) * DEEP, 0:1],
                pressed,
                heats[r, j],
            )
            for f in range(5):
                if f < 2:
                    flow_ref[(f, *at)] = new[f]
                else:
                    tracers_ref[(f - 2, *at)] = new[f]
        whole = pl.ds(k * rows, rows)
        copies.append(
            pltpu.make_async_copy(tracers_ref.at[:, whole, :], out_hbm.at[pl.ds(2, 3), whole, :], sem.at[k])
        )
        copies[-1].start()
    for copy in copies:
        copy.wait()


def last_kernel(out_in_hbm, flow_ref, mask_ref, above_ref, out_hbm, moved_ref, sem):
    del out_in_hbm
    rows, cols = mask_ref.shape[0] // DEEP, mask_ref.shape[1]
    above = above_ref[...]
    east, west, north, south = around(
        above[0:rows, 0:cols],
        above[0:rows, cols : cols + 1],
        above[0:rows, cols + 1 : cols + 2],
        above[rows : rows + 1, 0:cols],
        above[rows + 1 : rows + 2, 0:cols],
    )
    push_x, push_y = (0.5 * PRESS) * (east - west), (0.5 * PRESS) * (north - south)
    copies = []
    for k in range(DEEP):
        whole = pl.ds(k * rows, rows)
        wet = mask_ref[whole, :].astype(F32)
        moved_ref[0, whole, :] = flow_ref[0, whole, :] - wet * push_x
        moved_ref[1, whole, :] = flow_ref[1, whole, :] - wet * push_y
        copies.append(pltpu.make_async_copy(moved_ref.at[:, whole, :], out_hbm.at[pl.ds(0, 2), whole, :], sem.at[k]))
        copies[-1].start()
    for copy in copies:
        copy.wait()


def body(n_lon, n_lat, state, mask, coriolis, penetration, flux_tiles, flux_owner, flux_row, fold_partner):
    fields, levels, rows, cols = state.shape
    flat_state = state.reshape(fields, levels * rows, cols)
    flat_mask = mask.reshape(levels * rows, cols)
    last = n_lat - 1
    turn, share, hinge = coriolis.reshape(1, -1), penetration.reshape(1, -1), fold_partner.reshape(1, -1)

    keep, send, west, east, total = prepare(
        flat_state, flat_mask, flux_tiles, flux_owner, flux_row, fold_partner, n_lon, n_lat
    )

    stages = []
    for axis, size, least in (("lat", n_lat, 2), ("lon", n_lon, 1)):
        bit = size // 2
        while bit >= least:
            stages.append((axis, size, bit))
            bit //= 2
    got = lax.ppermute(send, "lat", [(i, i ^ 1) for i in range(n_lat)])
    prefix = lax.ppermute(total, "lev", [(0, 1)])

    def merged(keep, got):
        half = shape(keep.shape[0] // 2, keep.shape[1])
        return call(merge_kernel, (half, half), [VMEM] * 2, (keep, got), name="merge_flux")

    def passed_on(send, stage):
        axis, size, bit = stage
        return lax.ppermute(send, axis, [(i, i ^ bit) for i in range(size)])

    pieces = cols // LANES
    hinge_piece = fold_partner[0] >> (LANES.bit_length() - 1)
    keep = after(keep, (prefix, hinge_piece))
    keep, send = merged(keep, got)
    got = passed_on(send, stages[0])

    message = shape(SLABS + 1, DEEP, cols)
    top_shape = shape(pieces, SLABS + 1, DEEP, LANES)
    top = call(top_kernel, top_shape, [VMEM] * 3, (flat_state, flat_mask, prefix), name="top_rows")
    top = after(top, send)

    def folded(hinge_piece):
        block, piece = divmod(hinge_piece, pieces)

        def swap(rows_out):
            def across(part, other):
                pairs = [(a * n_lat + last, (other - a) % n_lon * n_lat + last) for a in range(n_lon)]
                return lax.ppermute(part, ("lon", "lat"), pairs)

            return jnp.concatenate([across(rows_out[piece:], block - 1), across(rows_out[: piece + 1], block)], axis=0)

        return swap

    fold = lax.switch(hinge_piece, [folded(n) for n in range(n_lon * pieces)], top)
    side = shape(rows + DEEP, LANES)
    west, east = call(
        functools.partial(columns_kernel, n_lat),
        (side, side),
        [VMEM] * 4 + [VMEM],
        (west, east, prefix, fold, hinge),
        name="edge_columns",
    )
    from_west = lax.ppermute(east, "lon", [(i, (i + 1) % n_lon) for i in range(n_lon)])
    from_east = lax.ppermute(west, "lon", [((i + 1) % n_lon, i) for i in range(n_lon)])
    keep = after(keep, (from_west, from_east))
    keep, send = merged(keep, got)
    got = passed_on(send, stages[1])

    from_west, from_east = after((from_west, from_east), send)
    pair, cross = call(
        rows_kernel,
        (message, message),
        [VMEM, VMEM, VMEM, VMEM, VMEM, VMEM],
        (flat_state, flat_mask, prefix, turn, from_west, from_east),
        name="edge_rows",
    )
    from_pair = lax.ppermute(pair, "lat", [(i, i ^ 1) for i in range(n_lat)])
    from_cross = lax.ppermute(cross, "lat", [(i, i + 1 if i % 2 else i - 1) for i in range(1, last)])
    keep = after(keep, (pair, cross))
    for stage in stages[2:]:
        keep, send = merged(keep, got)
        got = passed_on(send, stage)

    near_state, near_mask = after((flat_state, flat_mask), send)
    new_state, inside = call(
        inside_kernel,
        (shape(fields, levels * rows, cols), shape(rows, 2 * cols)),
        [VMEM, VMEM, VMEM, VMEM, VMEM],
        (near_state, near_mask, prefix, turn, share),
        name="first_inside",
    )
    keep = after(keep, inside)
    mine = keep + got
    theirs = lax.ppermute(mine, "lev", [(0, 1), (1, 0)])

    inside = after(inside, mine)
    wide = cols + LANES
    *ring, sums = call(
        functools.partial(rim_kernel, n_lat),
        (
            shape(2, 6, DEEP, cols),
            shape(2, rows, LANES),
            shape(2, 5, DEEP, cols),
            shape(2, rows, LANES),
            shape(rows + DEEP, 2 * wide),
        ),
        [VMEM, VMEM, VMEM, VMEM, VMEM, VMEM] + [VMEM] * 8,
        (
            flat_state, flat_mask, prefix, turn, share, hinge, west, east, from_west, from_east, from_pair,
            from_cross, fold, inside,
        ),
        [pltpu.VMEM((SLABS + 1, DEEP, cols), F32), pltpu.VMEM((SLABS + 1, DEEP, cols), F32)],
        name="first_rim",
    )
    *flux, above = call(
        functools.partial(flux_kernel, n_lat),
        (shape(3, rows, cols), shape(DEEP, cols), shape(rows, LANES), shape(rows + DEEP, wide)),
        [VMEM] * 3 + [VMEM],
        (sums, mine, theirs, hinge),
        name="flux_parts",
    )
    above = lax.ppermute(above, "lev", [(0, 1)])

    out = jax.ShapeDtypeStruct(flat_state.shape, F32)
    result, flow = call(
        second_kernel,
        (out, shape(2, levels * rows, cols)),
        [VMEM] * 9 + [VMEM] * 2,
        (new_state, flat_mask, *ring, *flux, turn, share),
        [pltpu.VMEM((3, levels * rows, cols), F32), pltpu.SemaphoreType.DMA((DEEP,))],
        name="second_substep",
        out_specs=(ANY, VMEM),
    )
    result = call(
        last_kernel,
        out,
        [ANY] + [VMEM] * 3,
        (result, flow, flat_mask, above),
        [pltpu.VMEM((2, levels * rows, cols), F32), pltpu.SemaphoreType.DMA((DEEP,))],
        name="deeper_pressure",
        out_specs=ANY,
        aliases={0: 0},
    )
    return result.reshape(fields, levels, rows, cols)


def solution(mesh):
    n_lon, n_lat = mesh.shape["lon"], mesh.shape["lat"]
    assert mesh.shape["lev"] == 2 and n_lat % 2 == 0 and n_lon > 2
    return jax.shard_map(
        functools.partial(body, n_lon, n_lat),
        mesh=mesh,
        in_specs=(
            P(None, "lev", "lat", "lon"),
            P("lev", "lat", "lon"),
            P("lat"),
            P("lev"),
            P(("lon", "lat"), None, None),
            P(("lon", "lat"), None),
            P(("lon", "lat")),
            P(),
        ),
        out_specs=P(None, "lev", "lat", "lon"),
        check_vma=False,
    )
```
